32 devices in a mesh: grp: 2 (over y), blk: 4 (over z), rep: 2 (over x), sub: 2 (over core).
Axes of the slice: x: 2, y: 2, z: 4, core: 2. Of those that a mesh axis runs over, the one named last changes fastest.
Arguments:
- states: bfloat16 [4096, 256], P(('grp', 'blk', 'sub')), parts along dimension 0, may hold values from -6 to 6
- goal_distance: int32 [4096, 1], P(('grp', 'blk', 'sub')), parts along dimension 0, may hold values from 0 to 7; in each aligned block of 256 rows (0 to 255, 256 to 511, ...) at most 128 rows name the same one
- goal_row: int32 [4096], P(('grp', 'blk', 'sub')), parts along dimension 0, may hold values from 0 to 255
- episode: int32 [4096], P(('grp', 'blk', 'sub')), parts along dimension 0, may hold values from 0 to 15, never falling along the last dimension, each value on 1 to 256 neighbouring positions
- state_first: bfloat16 [256, 4096], P(None, 'rep'), may hold values from -0.375 to 0.375
- state_second: bfloat16 [4096, 256], P('rep'), may hold values from -0.09375 to 0.09375
- goal_first: bfloat16 [256, 4096], P(None, 'rep'), may hold values from -0.375 to 0.375
- goal_second: bfloat16 [4096, 256], P('rep'), may hold values from -0.09375 to 0.09375
Outputs:
- grad_state_first: float32 [512, 4096], P('grp', 'rep'), parts along dimension 0
- grad_state_second: float32 [8192, 256], P(('grp', 'rep')), parts along dimension 0
- grad_goal_first: float32 [512, 4096], P('grp', 'rep'), parts along dimension 0
- grad_goal_second: float32 [8192, 256], P(('grp', 'rep')), parts along dimension 0
The draws below stay inside these ranges and needn't reach their ends.
There are 2 independent parts, one for each index of `grp`. The reference program is written for one: setup_inputs(seed, part) draws one part's arguments, and reference() takes and returns one part's arrays. A program takes and returns all parts, laid end to end along the dimension named above; an argument that names none is the same for every part. Nothing has to cross between parts.
Inputs may be any that keep to these rules, and one draw needn't show every extreme that they name: `goal_distance`: in the rows of one device each distance is named by at most 128 rows. Numbers never fall along the rows; an episode covers at most 256 rows.
All inputs are finite; a program needn't handle non-finite values.
Results may differ from the reference program's by a relative error of at most 0.0084.
Values may be sent and summed in bfloat16 or wider, within the bound.
No kernel may reach another device: no remote copies, remote signals or barrier semaphores. Data moves between devices by JAX's collectives and lax.ppermute only.
A program may use at most 64 MiB of HBM per device.

```python
import math
import jax
import jax.numpy as jnp
import numpy as np
from jax import lax

STATE = 256
HID = 4096
EMB = 256
SLAB = 128
ROWS_DEV = 256
BATCH = 512
ROWS = 2048
CAP = 128
EPISODES = 16
N_BLK = 4
N_SUB = 2


def place_ends(values, key, least, top_value):
    longest = values.shape.index(max(values.shape))
    spots = []
    for shift in (0, 1):
        where = [jax.random.randint(jax.random.fold_in(key, axis), (), 0, length) for axis, length in enumerate(values.shape)]
        where[longest] = (where[longest] + shift) % values.shape[longest]
        spots.append(tuple(where))
    return values.at[spots[0]].set(least).at[spots[1]].set(top_value)


def levels(key, shape, cuts, least, high):
    level, own = 1.0, jax.random.fold_in(key, 6)
    for dim, shards_of in cuts:
        heights = jnp.exp(jax.random.uniform(jax.random.fold_in(own, dim), (shards_of,), jnp.float32, least / len(cuts), high / len(cuts)))
        level = level * jnp.repeat(heights, shape[dim] // shards_of).reshape([-1 if axis == dim else 1 for axis in range(len(shape))])
    return level


def profile(count, total, bound, slope):
    portions = [(1 << 20) // math.isqrt(rank ** slope) + 1 for rank in range(2, count + 1)]
    rest, counts = total - bound - (count - 1), [1] * (count - 1)
    while rest > 0:
        free = [i for i in range(count - 1) if counts[i] < bound]
        mass, left = sum([portions[i] for i in free]), rest
        for i in free:
            more = min(bound - counts[i], max(1, left * portions[i] // mass), rest)
            counts[i] = counts[i] + more
            rest = rest - more
    return np.array([bound] + counts)


def uneven(stream_key, amount, total, reach, skew):
    if amount == 2:
        one = jax.random.randint(stream_key, (), max(1, total - reach), min(reach, total - 1) + 1)
        return jnp.stack([one, total - one])
    lengths = jnp.asarray(profile(amount, total, reach, skew), jnp.int32)
    couples = (amount - 1) // 2
    source_of, receiver = lengths[1:1 + 2 * couples:2], lengths[2:2 + 2 * couples:2]
    slack = jnp.minimum(source_of - 1, reach - receiver)
    shifted = jax.random.randint(jax.random.fold_in(stream_key, 1), (couples,), 0, 1 << 20) % (slack + 1)
    lengths = lengths.at[1:1 + 2 * couples:2].set(source_of - shifted).at[2:2 + 2 * couples:2].set(receiver + shifted)
    return lengths[jax.random.permutation(jax.random.fold_in(stream_key, 2), amount)]


def assign_block(stream_key, own, number, rows, count, top, limit, slope):
    sequence = jax.random.permutation(stream_key, count)
    crowded, ordinary = load_shares(count, rows * top, limit, slope, True), load_shares(count, rows * top, limit, slope, False)
    places = jnp.arange(count)

    def named(tallies, rotation):
        used = int((tallies > 0).sum())
        fixed = max(1, used // 4)
        shifted = fixed + (places - fixed + rotation * (used - fixed)) % max(1, count - fixed)
        return jnp.zeros((count,), jnp.int32).at[sequence[jnp.where(places < fixed, places, shifted)]].set(jnp.asarray(tallies, jnp.int32))

    tallies = jnp.where(number % 4 == 0, named(crowded, number // 4), named(ordinary, number - number // 4 - 1))
    mixed = jax.random.permutation(jax.random.fold_in(own, 3), count)
    source_of, taker = mixed[0:count // 2 * 2:2], mixed[1:count // 2 * 2:2]
    room = jnp.minimum(tallies[source_of] - 1, limit - tallies[taker]) // 2
    room = jnp.where((source_of == sequence[0]) | (taker == sequence[0]) | (tallies[taker] == 0), 0, jnp.maximum(room, 0))
    shifted = jax.random.randint(jax.random.fold_in(own, 4), (count // 2,), 0, 1 << 20) % (room + 1)
    tallies = tallies.at[source_of].add(-shifted).at[taker].add(shifted)
    labels = jnp.searchsorted(jnp.cumsum(tallies), jnp.arange(rows * top), side="right").astype(jnp.int32)
    table = labels.reshape(top, rows).T
    table = table[jax.random.permutation(jax.random.fold_in(own, 1), rows)]
    rotation = jax.random.randint(jax.random.fold_in(own, 2), (rows, 1), 0, top)
    return jnp.take_along_axis(table, (jnp.arange(top)[None, :] + rotation) % top, axis=1)


def load_shares(amount, total, limit, slope, full):
    portions = [(1 << 20) // math.isqrt(grade ** slope) + 1 for grade in range(1, amount + 1)]
    largest = limit if full else min(limit, max(-(-total // amount), total * portions[0] // sum(portions)))
    least = 1 if total - largest >= amount - 1 else 0
    given, spare = [largest] + [least] * (amount - 1), total - largest - least * (amount - 1)
    while spare > 0:
        movable = [i for i in range(1, amount) if given[i] < largest] or [i for i in range(1, amount) if given[i] < limit]
        mass, remaining = sum([portions[i] for i in movable]), spare
        for i in movable:
            extra = min(limit - given[i], max(1, remaining * portions[i] // mass), spare)
            given[i] = given[i] + extra
            spare = spare - extra
    return np.array(given)


def scatter_about(own_key, dims, scale, bound, cuts=(), kind=jnp.bfloat16):
    values = scale * jax.random.normal(own_key, dims, jnp.float32)
    if cuts:
        values = values * levels(own_key, dims, cuts, -0.22, 0.18)
    return jnp.clip(values, -bound, bound).astype(kind)


def setup_inputs(seed: int = 0, part: int = 0) -> dict:
    streams_of = jax.random.split(jax.random.key(seed), 9)
    part_splits = jax.random.split(jax.random.fold_in(streams_of[8], part), 9)
    states = scatter_about(part_splits[0], (ROWS, STATE), 1.0, 6.0, ((0, 8),))
    goal_distance_keys = jax.random.split(jax.random.fold_in(part_splits[1], 1), ROWS // ROWS_DEV)
    goal_distance_turns = jax.random.permutation(jax.random.fold_in(part_splits[1], 3), ROWS // ROWS_DEV)
    goal_distance = jax.vmap(lambda own, number: assign_block(jax.random.fold_in(part_splits[1], 2), own, number, ROWS_DEV, N_BLK * N_SUB, 1, CAP, 2))(goal_distance_keys, goal_distance_turns).reshape((ROWS, 1))
    goal_row = place_ends(jax.random.randint(part_splits[2], (ROWS,), 0, ROWS_DEV), jax.random.fold_in(part_splits[2], 1), 0, ROWS_DEV - 1).astype(jnp.int32)
    episode = jnp.searchsorted(jnp.cumsum(uneven(part_splits[3], EPISODES, ROWS, ROWS_DEV, 1)), jnp.arange(ROWS), side="right").astype(jnp.int32)
    state_first = scatter_about(streams_of[4], (STATE, HID), STATE ** -0.5, 0.375, ((1, 2),))
    state_second = scatter_about(streams_of[5], (HID, EMB), HID ** -0.5, 0.09375, ((0, 2),))
    goal_first = scatter_about(streams_of[6], (STATE, HID), STATE ** -0.5, 0.375, ((1, 2),))
    goal_second = scatter_about(streams_of[7], (HID, EMB), HID ** -0.5, 0.09375, ((0, 2),))
    return {"states": states, "goal_distance": goal_distance, "goal_row": goal_row, "episode": episode, "state_first": state_first, "state_second": state_second, "goal_first": goal_first, "goal_second": goal_second}


def silu_slope(hidden):
    sig = jax.nn.sigmoid(hidden)
    return sig * (1.0 + hidden * (1.0 - sig))

def encode(rows_in, first, second):
    hidden = jnp.dot(rows_in, first, preferred_element_type=jnp.float32)
    active = jax.nn.silu(hidden).astype(jnp.bfloat16)
    return jnp.dot(active, second, preferred_element_type=jnp.float32).astype(jnp.bfloat16)

def embed_rows(rows_in, first, second):
    blocks = rows_in.reshape(-1, ROWS_DEV, STATE)
    return lax.map(lambda block: encode(block, first, second), blocks).reshape(ROWS, EMB)

def encoder_grads(rows_in, first, second, emb_grad):

    def one_block(carry, pair):
        block_rows, block_grad = pair
        hidden = jnp.dot(block_rows, first, preferred_element_type=jnp.float32)
        active = jax.nn.silu(hidden).astype(jnp.bfloat16)
        grad_second = jnp.dot(active.T, block_grad, preferred_element_type=jnp.float32)
        back = jnp.dot(block_grad, second.T, preferred_element_type=jnp.float32)
        back_rows = (back * silu_slope(hidden)).astype(jnp.bfloat16)
        grad_first = jnp.dot(block_rows.T, back_rows, preferred_element_type=jnp.float32)
        return ((carry[0] + grad_first, carry[1] + grad_second), None)
    start_value = (jnp.zeros((STATE, HID), jnp.float32), jnp.zeros((HID, EMB), jnp.float32))
    blocks = rows_in.reshape(-1, ROWS_DEV, STATE)
    grads = emb_grad.reshape(-1, ROWS_DEV, EMB)
    result, unused = lax.scan(one_block, start_value, (blocks, grads))
    return result

def to_groups(values):
    shaped = values.reshape((N_BLK, ROWS // BATCH, SLAB) + values.shape[1:])
    moved = jnp.swapaxes(shaped, 0, 1)
    return moved.reshape((ROWS // BATCH, BATCH) + values.shape[1:])

def from_groups(values):
    shaped = values.reshape((ROWS // BATCH, N_BLK, SLAB) + values.shape[2:])
    moved = jnp.swapaxes(shaped, 0, 1)
    return moved.reshape((ROWS,) + values.shape[2:])

def contrast(triple):
    phi, psi, episode_ids = triple
    logit_scale = 4.0 / math.sqrt(EMB)
    scores = jnp.dot(phi, psi.T, preferred_element_type=jnp.float32) * logit_scale
    index = jnp.arange(BATCH, dtype=jnp.int32)
    diagonal = index[:, None] == index[None, :]
    excluded = (episode_ids[:, None] == episode_ids[None, :]) & ~diagonal
    exponent = jnp.where(excluded, 0.0, jnp.exp(scores))
    totals = lax.optimization_barrier(jnp.sum(exponent, axis=1, keepdims=True))
    delta = (exponent / totals - diagonal.astype(jnp.float32)).astype(jnp.bfloat16)
    phi_grad = (jnp.dot(delta, psi, preferred_element_type=jnp.float32) * logit_scale).astype(jnp.bfloat16)
    psi_grad = (jnp.dot(delta.T, phi, preferred_element_type=jnp.float32) * logit_scale).astype(jnp.bfloat16)
    return (phi_grad, psi_grad)

def reference(states, goal_distance, goal_row, episode, state_first, state_second, goal_first, goal_second):
    row_ids = jnp.arange(ROWS, dtype=jnp.int32)
    owners = (row_ids // ROWS_DEV + goal_distance[:, 0]) % (ROWS // ROWS_DEV)
    goal_index = (owners * ROWS_DEV + goal_row).astype(jnp.int32)
    goal_states = states[goal_index]
    phi = embed_rows(states, state_first, state_second)
    psi = embed_rows(goal_states, goal_first, goal_second)
    phi_grad, psi_grad = lax.map(contrast, (to_groups(phi), to_groups(psi), to_groups(episode)))
    phi_grad = from_groups(phi_grad)
    psi_grad = from_groups(psi_grad)
    grad_state_first, grad_state_second = encoder_grads(states, state_first, state_second, phi_grad)
    grad_goal_first, grad_goal_second = encoder_grads(goal_states, goal_first, goal_second, psi_grad)
    return (grad_state_first, grad_state_second, grad_goal_first, grad_goal_second)
```

```python
import functools
import math

import jax
import jax.numpy as jnp
from jax import lax
from jax.experimental import pallas as pl
from jax.experimental.pallas import tpu as pltpu
from jax.sharding import PartitionSpec as P

BF = jnp.bfloat16
F32 = jnp.float32
VMEM = 56 * 1024 * 1024


def dot(a, b):
    return jnp.dot(a, b, preferred_element_type=F32)


def sigmoid(v):
    return 0.5 * jnp.tanh(0.5 * v) + 0.5


def whole(shape):
    return pl.BlockSpec(shape, lambda *_: (0,) * len(shape))


def forward_kernel(x_ref, sf_ref, gf_ref, ss_ref, gs_ref, out_ref, acc):
    step = pl.program_id(0)
    emb = ss_ref.shape[1]

    @pl.when(step == 0)
    def _():
        acc[...] = jnp.zeros_like(acc)

    x = x_ref[...]
    for k, (first, second) in enumerate(((sf_ref, ss_ref), (gf_ref, gs_ref))):
        hidden = dot(x, first[...])
        active = (hidden * sigmoid(hidden)).astype(BF)
        acc[:, k * emb : (k + 1) * emb] += dot(active, second[...])

    @pl.when(step == pl.num_programs(0) - 1)
    def _():
        out_ref[...] = acc[...].astype(BF)


def forward(x, rows, sf, gf, ss, gs):
    width, hid = sf.shape
    emb = ss.shape[1]
    tile = 512
    return pl.pallas_call(
        forward_kernel,
        grid=(hid // tile,),
        in_specs=[
            pl.BlockSpec((rows, width), lambda i: (0, 0)),
            pl.BlockSpec((width, tile), lambda i: (0, i)),
            pl.BlockSpec((width, tile), lambda i: (0, i)),
            pl.BlockSpec((tile, emb), lambda i: (i, 0)),
            pl.BlockSpec((tile, emb), lambda i: (i, 0)),
        ],
        out_specs=pl.BlockSpec((rows, 2 * emb), lambda i: (0, 0)),
        out_shape=jax.ShapeDtypeStruct((rows, 2 * emb), BF),
        scratch_shapes=[pltpu.VMEM((rows, 2 * emb), F32)],
        compiler_params=pltpu.CompilerParams(vmem_limit_bytes=VMEM),
        cost_estimate=pl.CostEstimate(
            flops=8 * rows * width * hid, bytes_accessed=8 * width * hid, transcendentals=2 * rows * hid
        ),
        name="forward",
    )(x, sf, gf, ss, gs)


def place_blocks(pos_ref, mine, other, put, n_blk, n_rep, slab):
    b, s = pos_ref[0], pos_ref[1]
    for side, blocks in ((s, mine), (1 - s, other)):
        for k, block in enumerate(blocks):
            at = jnp.bitwise_xor(b, k)
            for r in range(n_rep):
                off = ((side * n_rep + r) * n_blk + at) * slab
                put(pl.multiple_of(off, slab), block(r))


def hidden_kernel(n_blk, n_rep, slab, pos_ref, *refs):
    mine = refs[:n_blk]
    other = refs[n_blk]
    first_ref, all_ref, active_ref, slope_ref, states_t = refs[n_blk + 1 :]
    rows = slab * n_rep
    pad = other.shape[0] // n_blk

    @pl.when(pl.program_id(0) == 0)
    def _():
        def put(off, value):
            all_ref[pl.ds(off, slab), :] = value
            states_t[:, pl.ds(off, slab)] = value.T

        place_blocks(
            pos_ref,
            [functools.partial(lambda ref, r: ref[r * slab : (r + 1) * slab, :], ref) for ref in mine],
            [
                functools.partial(lambda k, r: other[k * pad + r * slab : k * pad + (r + 1) * slab, :], k)
                for k in range(n_blk)
            ],
            put,
            n_blk,
            n_rep,
            slab,
        )

    first_t = first_ref[...].T
    chunk = 512
    for c in range(all_ref.shape[0] // chunk):
        cols = slice(c * chunk, (c + 1) * chunk)
        hidden = dot(first_t, states_t[:, cols])
        sig = sigmoid(hidden)
        active = hidden * sig
        active_ref[:, cols] = active.astype(BF)
        slope_ref[:, cols] = (sig + active * (1.0 - sig)).astype(BF)


def hidden_all(pos, mine, other, first, n_blk, n_rep, slab, quarter):
    width = first.shape[0]
    rows = 2 * n_blk * n_rep * slab
    tile = 256
    steps = quarter // tile
    return pl.pallas_call(
        functools.partial(hidden_kernel, n_blk, n_rep, slab),
        grid_spec=pltpu.PrefetchScalarGridSpec(
            num_scalar_prefetch=1,
            grid=(steps,),
            in_specs=[whole(m.shape) for m in mine]
            + [whole(other.shape)]
            + [pl.BlockSpec((width, tile), lambda i, p: (0, p[1] * steps + i))],
            out_specs=[
                whole((rows, width)),
                pl.BlockSpec((tile, rows), lambda i, p: (i, 0)),
                pl.BlockSpec((tile, rows), lambda i, p: (i, 0)),
            ],
            scratch_shapes=[pltpu.VMEM((width, rows), BF)],
        ),
        out_shape=[
            jax.ShapeDtypeStruct((rows, width), BF),
            jax.ShapeDtypeStruct((quarter, rows), BF),
            jax.ShapeDtypeStruct((quarter, rows), BF),
        ],
        compiler_params=pltpu.CompilerParams(vmem_limit_bytes=VMEM),
        cost_estimate=pl.CostEstimate(
            flops=2 * rows * width * quarter, bytes_accessed=4 * rows * quarter, transcendentals=rows * quarter
        ),
        name="hidden_all",
    )(pos, *mine, other, first)


def contrast_kernel(n_blk, n_rep, slab, scale, pos_ref, *refs):
    mine = refs[:n_blk]
    other = refs[n_blk : 2 * n_blk]
    (goal_row_ref, goal_col_ref, ep_row_ref, ep_col_ref) = refs[2 * n_blk : 2 * n_blk + 4]
    phi_grad_ref, phi_grad_t_ref, sum_ref, sum_t_ref, phi_all, psi_all, total = refs[2 * n_blk + 4 :]
    emb = phi_all.shape[1]
    batch = n_blk * slab
    rows = phi_all.shape[0]

    def put(off, value):
        phi_all[pl.ds(off, slab), :] = value[:, :emb]
        psi_all[pl.ds(off, slab), :] = value[:, emb:]

    def slabs(refs_):
        return [functools.partial(lambda ref, r: ref[r * slab : (r + 1) * slab, :], ref) for ref in refs_]

    place_blocks(pos_ref, slabs(mine), slabs(other), put, n_blk, n_rep, slab)

    for j in range(rows // batch):
        own = slice(j * batch, (j + 1) * batch)
        pick = (
            goal_col_ref[own, :1] == lax.broadcasted_iota(jnp.int32, (batch, rows), 1)
        ).astype(F32).astype(BF)
        psi = dot(pick, psi_all[...]).astype(BF)
        phi = phi_all[own, :]
        scores = lax.dot_general(phi, psi, (((1,), (1,)), ((), ())), preferred_element_type=F32) * scale
        diagonal = lax.broadcasted_iota(jnp.int32, (batch, batch), 0) == lax.broadcasted_iota(
            jnp.int32, (batch, batch), 1
        )
        same = ep_col_ref[own, :1] == ep_row_ref[:1, own]
        exponent = jnp.where(same & ~diagonal, 0.0, jnp.exp(scores))
        totals = jnp.sum(exponent, axis=1, keepdims=True)
        delta = (exponent / totals - diagonal.astype(F32)).astype(BF)
        phi_grad = dot(delta, psi) * scale
        phi_grad_ref[own, :] = phi_grad.astype(BF)
        phi_grad_t_ref[:, own] = phi_grad.T.astype(BF)
        psi_grad = (dot(delta.T, phi) * scale).astype(BF)
        put_back = (
            goal_row_ref[:1, own] == lax.broadcasted_iota(jnp.int32, (rows, batch), 0)
        ).astype(F32).astype(BF)
        add = dot(put_back, psi_grad)
        if j == 0:
            total[...] = add
        else:
            total[...] += add
    sum_ref[...] = total[...].astype(BF)
    sum_t_ref[...] = total[...].T.astype(BF)


def contrast(pos, mine, other, goal_row, goal_col, ep_row, ep_col, n_blk, n_rep, slab, emb):
    rows = 2 * n_blk * n_rep * slab
    args = (*mine, *other, goal_row, goal_col, ep_row, ep_col)
    return pl.pallas_call(
        functools.partial(contrast_kernel, n_blk, n_rep, slab, 4.0 / math.sqrt(emb)),
        grid_spec=pltpu.PrefetchScalarGridSpec(
            num_scalar_prefetch=1,
            grid=(1,),
            in_specs=[whole(a.shape) for a in args],
            out_specs=[whole((rows, emb)), whole((emb, rows)), whole((rows, emb)), whole((emb, rows))],
            scratch_shapes=[
                pltpu.VMEM((rows, emb), BF),
                pltpu.VMEM((rows, emb), BF),
                pltpu.VMEM((rows, emb), F32),
            ],
        ),
        out_shape=[
            jax.ShapeDtypeStruct((rows, emb), BF),
            jax.ShapeDtypeStruct((emb, rows), BF),
            jax.ShapeDtypeStruct((rows, emb), BF),
            jax.ShapeDtypeStruct((emb, rows), BF),
        ],
        compiler_params=pltpu.CompilerParams(vmem_limit_bytes=VMEM),
        name="contrast",
    )(pos, *args)


def backward_kernel(second_ref, grad_ref, grad_t_ref, states_ref, active_ref, slope_ref, gf_ref, gs_ref):
    gs_ref[...] = dot(active_ref[...], grad_ref[...])
    back = (dot(second_ref[...], grad_t_ref[...]) * slope_ref[...].astype(F32)).astype(BF)
    gf_ref[...] = dot(back, states_ref[...]).T


def backward(pos, second, grad, grad_t, states, active, slope):
    rows, width = states.shape
    quarter = active.shape[0]
    emb = second.shape[1]
    tile = 256
    steps = quarter // tile

    def body(pos_ref, *refs):
        backward_kernel(*refs)

    return pl.pallas_call(
        body,
        grid_spec=pltpu.PrefetchScalarGridSpec(
            num_scalar_prefetch=1,
            grid=(steps,),
            in_specs=[
                pl.BlockSpec((tile, emb), lambda i, p: (p[1] * steps + i, 0)),
                whole((rows, emb)),
                whole((emb, rows)),
                whole((rows, width)),
                pl.BlockSpec((tile, rows), lambda i, p: (i, 0)),
                pl.BlockSpec((tile, rows), lambda i, p: (i, 0)),
            ],
            out_specs=[
                pl.BlockSpec((width, tile), lambda i, p: (0, i)),
                pl.BlockSpec((tile, emb), lambda i, p: (i, 0)),
            ],
        ),
        out_shape=[
            jax.ShapeDtypeStruct((width, quarter), F32),
            jax.ShapeDtypeStruct((quarter, emb), F32),
        ],
        compiler_params=pltpu.CompilerParams(vmem_limit_bytes=VMEM),
        cost_estimate=pl.CostEstimate(
            flops=6 * rows * width * quarter, bytes_accessed=4 * rows * quarter, transcendentals=0
        ),
        name="backward",
    )(pos, second, grad, grad_t, states, active, slope)


def gathered(
    states, goal_distance, goal_row, episode, state_first, state_second, goal_first, goal_second
):
    rows_dev, width = states.shape
    n_blk, n_rep, n_sub = (lax.axis_size(a) for a in ("blk", "rep", "sub"))
    owners = n_blk * n_sub
    slab = rows_dev // n_rep
    rows_all = owners * rows_dev
    emb = state_second.shape[1]
    b, s = lax.axis_index("blk"), lax.axis_index("sub")
    pos = jnp.stack([b, s]).astype(jnp.int32)
    quarter = state_first.shape[1] // n_sub

    def across(x, k):
        return lax.ppermute(x, "blk", [(i, i ^ k) for i in range(n_blk)])

    def swap(x, axis):
        return lax.ppermute(x, axis, [(0, 1), (1, 0)])

    owner = (b * n_sub + s + goal_distance[:, 0]) % owners
    goal = (((owner % n_sub) * n_rep + goal_row // slab) * n_blk + owner // n_sub) * slab + goal_row % slab
    meta = jnp.stack([goal // 256, goal % 256, episode]).astype(BF)
    own = jnp.concatenate([states, jnp.pad(meta, ((0, 13), (0, 0)))], axis=0)
    got = {0: own, 3: across(own, 3)}
    got[1] = across(own, 1)
    got[2] = across(own, 2)

    weights = (state_first, goal_first, state_second, goal_second)
    sums = {}
    for k in (0, 3):
        part = forward(states if k == 0 else got[k], rows_dev, *weights)
        there = swap(part, "rep")
        sums[k] = (part.astype(F32) + there.astype(F32)).astype(BF)
    sums[1] = across(sums[0], 1)
    sums[2] = across(sums[3], 1)

    mine = [got[k] for k in range(n_blk)]
    other = swap(jnp.concatenate(mine, axis=0), "sub")
    all_states, active_s, slope_s = hidden_all(pos, mine, other, state_first, n_blk, n_rep, slab, quarter)
    _, active_g, slope_g = hidden_all(pos, mine, other, goal_first, n_blk, n_rep, slab, quarter)

    metas = jnp.stack(
        [jnp.stack([m[rows_dev : rows_dev + 3] for m in mine])]
        + [other.reshape(n_blk, -1, width)[:, rows_dev : rows_dev + 3]]
    )
    metas = metas.astype(F32).astype(jnp.int32)
    metas = jnp.where(s == 0, metas, metas[::-1])
    metas = jnp.take(metas, jnp.bitwise_xor(b, jnp.arange(n_blk)), axis=1)
    metas = metas.reshape(n_sub, n_blk, 3, n_rep, slab).transpose(2, 0, 3, 1, 4).reshape(3, rows_all)
    goal_all = metas[0] * 256 + metas[1]
    ep_all = metas[2]

    others = [swap(sums[k], "sub") for k in range(n_blk)]
    phi_grad, phi_grad_t, psi_sum, psi_sum_t = contrast(
        pos,
        [sums[k] for k in range(n_blk)],
        others,
        goal_all[None, :],
        goal_all[:, None],
        ep_all[None, :],
        ep_all[:, None],
        n_blk,
        n_rep,
        slab,
        emb,
    )

    outs = []
    for second, grad, grad_t, active, slope in (
        (state_second, phi_grad, phi_grad_t, active_s, slope_s),
        (goal_second, psi_sum, psi_sum_t, active_g, slope_g),
    ):
        gf, gs = backward(pos, second, grad, grad_t, all_states, active, slope)
        gf2, gs2 = swap(gf, "sub"), swap(gs, "sub")
        outs.append(
            jnp.where(s == 0, jnp.concatenate([gf, gf2], axis=1), jnp.concatenate([gf2, gf], axis=1))
        )
        outs.append(
            jnp.where(s == 0, jnp.concatenate([gs, gs2], axis=0), jnp.concatenate([gs2, gs], axis=0))
        )
    return tuple(outs)


def silu_slope(hidden):
    sig = jax.nn.sigmoid(hidden)
    return sig * (1.0 + hidden * (1.0 - sig))


def encoder_grads(rows_in, hidden, active, second, emb_grad):
    grad_second = jnp.einsum("nh,ne->he", active, emb_grad, preferred_element_type=jnp.float32)
    back = jnp.einsum("ne,he->nh", emb_grad, second, preferred_element_type=jnp.float32)
    back_rows = (back * silu_slope(hidden)).astype(jnp.bfloat16)
    grad_first = jnp.einsum("ns,nh->sh", rows_in, back_rows, preferred_element_type=jnp.float32)
    return (grad_first, grad_second)


def exchanged(
    states, goal_distance, goal_row, episode, state_first, state_second, goal_first, goal_second
):
    rows_dev, width = states.shape
    owners = lax.axis_size(("blk", "sub"))
    position = lax.axis_index(("blk", "sub"))
    capacity = 4 * rows_dev // owners
    target = (position + goal_distance[:, 0]) % owners
    onehot = (target[:, None] == jnp.arange(owners, dtype=jnp.int32)[None, :]).astype(jnp.int32)
    slot_rank = jnp.sum((jnp.cumsum(onehot, axis=0) - onehot) * onehot, axis=1)
    requests = jnp.zeros((owners, capacity), jnp.int32).at[target, slot_rank].set(goal_row)
    wanted = lax.all_to_all(requests, ("blk", "sub"), split_axis=0, concat_axis=0, tiled=True)
    fetched = jnp.take(states, wanted.reshape(-1), axis=0).reshape(wanted.shape + (width,))
    replies = lax.all_to_all(fetched, ("blk", "sub"), split_axis=0, concat_axis=0, tiled=True)
    goal_states = jnp.take(
        replies.reshape(owners * capacity, width), target * capacity + slot_rank, axis=0
    )
    slab_rows = rows_dev // lax.axis_size("rep")
    state_hidden = jnp.dot(states, state_first, preferred_element_type=jnp.float32)
    state_active = jax.nn.silu(state_hidden).astype(jnp.bfloat16)
    goal_hidden = jnp.dot(goal_states, goal_first, preferred_element_type=jnp.float32)
    goal_active = jax.nn.silu(goal_hidden).astype(jnp.bfloat16)
    phi = lax.psum_scatter(
        jnp.dot(state_active, state_second, preferred_element_type=jnp.float32),
        "rep",
        scatter_dimension=0,
        tiled=True,
    ).astype(jnp.bfloat16)
    psi = lax.psum_scatter(
        jnp.dot(goal_active, goal_second, preferred_element_type=jnp.float32),
        "rep",
        scatter_dimension=0,
        tiled=True,
    ).astype(jnp.bfloat16)
    episode_own = lax.dynamic_slice_in_dim(episode, lax.axis_index("rep") * slab_rows, slab_rows, 0)
    psi_all, episode_all = (
        lax.all_gather(psi, "blk", axis=0, tiled=True),
        lax.all_gather(episode_own, "blk", axis=0, tiled=True),
    )
    batch_rows = psi_all.shape[0]
    logit_scale = 4.0 / math.sqrt(psi.shape[1])
    own_rows = lax.axis_index("blk") * slab_rows + jnp.arange(slab_rows, dtype=jnp.int32)
    columns = jnp.arange(batch_rows, dtype=jnp.int32)
    diagonal = own_rows[:, None] == columns[None, :]
    excluded = (episode_own[:, None] == episode_all[None, :]) & ~diagonal
    scores = jnp.einsum("ie,je->ij", phi, psi_all, preferred_element_type=jnp.float32) * logit_scale
    exponent = jnp.where(excluded, 0.0, jnp.exp(scores))
    totals = jnp.sum(exponent, axis=1)
    delta = (exponent / totals[:, None] - diagonal.astype(jnp.float32)).astype(jnp.bfloat16)
    phi_grad = (jnp.dot(delta, psi_all, preferred_element_type=jnp.float32) * logit_scale).astype(
        jnp.bfloat16
    )
    psi_grad = lax.psum_scatter(
        jnp.einsum("ij,ie->je", delta, phi, preferred_element_type=jnp.float32) * logit_scale,
        "blk",
        scatter_dimension=0,
        tiled=True,
    ).astype(jnp.bfloat16)
    phi_full, psi_full = (
        lax.all_gather(phi_grad, "rep", axis=0, tiled=True),
        lax.all_gather(psi_grad, "rep", axis=0, tiled=True),
    )
    state_parts = encoder_grads(states, state_hidden, state_active, state_second, phi_full)
    goal_parts = encoder_grads(goal_states, goal_hidden, goal_active, goal_second, psi_full)
    summed = lax.psum(
        (state_parts[0], state_parts[1], goal_parts[0], goal_parts[1]), ("blk", "sub")
    )
    return (summed[0], summed[1], summed[2], summed[3])


def solution(mesh):
    in_specs = (
        P(("grp", "blk", "sub"), None),
        P(("grp", "blk", "sub"), None),
        P(("grp", "blk", "sub")),
        P(("grp", "blk", "sub")),
        P(None, "rep"),
        P("rep", None),
        P(None, "rep"),
        P("rep", None),
    )
    out_specs = (P("grp", "rep"), P(("grp", "rep"), None), P("grp", "rep"), P(("grp", "rep"), None))
    shape = mesh.shape
    local = gathered if (shape["blk"], shape["rep"], shape["sub"]) == (4, 2, 2) else exchanged
    return jax.shard_map(local, mesh=mesh, in_specs=in_specs, out_specs=out_specs, check_vma=False)
```

```python
import functools
import math

import jax
import jax.numpy as jnp
from jax import lax
from jax.experimental import pallas as pl
from jax.experimental.pallas import tpu as pltpu
from jax.sharding import PartitionSpec as P

BF = jnp.bfloat16
F32 = jnp.float32
MIB = 1024 * 1024


def dot(a, b):
    return jnp.dot(a, b, preferred_element_type=F32)


def sigmoid(v):
    return 0.5 * jnp.tanh(0.5 * v) + 0.5


def in_vmem(body, name, out_shape, args, scratch=(), limit=32, pos=None, flops=0):
    vmem = pl.BlockSpec(memory_space=pltpu.VMEM)
    smem = pl.BlockSpec(memory_space=pltpu.SMEM)
    specs = [vmem] * len(args)
    if pos is not None:
        args = (pos, *args)
        specs = [smem] + specs
    return pl.pallas_call(
        body,
        in_specs=specs,
        out_specs=jax.tree.map(lambda _: vmem, out_shape),
        out_shape=out_shape,
        scratch_shapes=scratch,
        compiler_params=pltpu.CompilerParams(vmem_limit_bytes=limit * MIB),
        cost_estimate=pl.CostEstimate(flops=flops, bytes_accessed=0, transcendentals=0),
        name=name,
    )(*args)


def forward_kernel(x_ref, sf_ref, gf_ref, ss_ref, gs_ref, out_ref, active):
    emb = ss_ref.shape[1]
    for k, (first, second) in enumerate(((sf_ref, ss_ref), (gf_ref, gs_ref))):
        for c in range(0, active.shape[1], 512):
            hidden = dot(x_ref[...], first[:, c : c + 512])
            active[:, c : c + 512] = (hidden * sigmoid(hidden)).astype(BF)
        out_ref[:, k * emb : (k + 1) * emb] = dot(active[...], second[...]).astype(BF)


def forward(x, sf, gf, ss, gs):
    rows, width = x.shape
    hid, emb = ss.shape
    return in_vmem(
        forward_kernel,
        "forward",
        jax.ShapeDtypeStruct((rows, 2 * emb), BF),
        (x, sf, gf, ss, gs),
        [pltpu.VMEM((rows, hid), BF)],
        limit=16,
        flops=8 * rows * width * hid,
    )


def place_blocks(pos_ref, mine, other, put, n_blk, n_rep, slab):
    b, s = pos_ref[0], pos_ref[1]
    for side, blocks in ((s, mine), (1 - s, other)):
        for k, block in enumerate(blocks):
            at = jnp.bitwise_xor(b, k)
            for r in range(n_rep):
                off = ((side * n_rep + r) * n_blk + at) * slab
                put(pl.multiple_of(off, slab), block[r * slab : (r + 1) * slab, :])


def arrange_kernel(n_blk, n_rep, slab, pos_ref, *refs):
    mine, other = refs[:n_blk], refs[n_blk : 2 * n_blk]
    all_ref, all_t_ref = refs[2 * n_blk :]

    def put(off, value):
        all_ref[pl.ds(off, slab), :] = value
        all_t_ref[:, pl.ds(off, slab)] = value.T

    place_blocks(pos_ref, mine, other, put, n_blk, n_rep, slab)


def column(row):
    return jnp.broadcast_to(row, (128, row.shape[1])).T[:, :1]


def contrast_kernel(n_blk, n_rep, slab, scale, pos_ref, *refs):
    mine, other = refs[:n_blk], refs[n_blk : 2 * n_blk]
    meta_ref = refs[2 * n_blk]
    phi_grad_ref, phi_grad_t_ref, sum_ref, sum_t_ref, phi_all, psi_all, total = refs[2 * n_blk + 1 :]
    emb = phi_all.shape[1]
    batch = n_blk * slab
    rows = phi_all.shape[0]

    def put(off, value):
        phi_all[pl.ds(off, slab), :] = value[:, :emb]
        psi_all[pl.ds(off, slab), :] = value[:, emb:]

    place_blocks(pos_ref, mine, other, put, n_blk, n_rep, slab)

    for j in range(rows // batch):
        own = slice(j * batch, (j + 1) * batch)
        side, r = j // n_rep, j % n_rep

        def meta_row(which):
            parts = [
                meta_ref[(blk * 2 + side) * 8 + which : (blk * 2 + side) * 8 + which + 1, r * slab : (r + 1) * slab]
                for blk in range(n_blk)
            ]
            return jnp.concatenate(parts, axis=1)

        goal_row, ep_row = meta_row(0), meta_row(1)
        goal_col, ep_col = column(goal_row.astype(F32)), column(ep_row.astype(F32))
        pick = jnp.where(
            goal_col.astype(jnp.int32) == lax.broadcasted_iota(jnp.int32, (batch, rows), 1), 1.0, 0.0
        ).astype(BF)
        psi = dot(pick, psi_all[...]).astype(BF)
        phi = phi_all[own, :]
        scores = lax.dot_general(phi, psi, (((1,), (1,)), ((), ())), preferred_element_type=F32) * scale
        diagonal = lax.broadcasted_iota(jnp.int32, (batch, batch), 0) == lax.broadcasted_iota(
            jnp.int32, (batch, batch), 1
        )
        same = ep_col == ep_row.astype(F32)
        exponent = jnp.where(same & ~diagonal, 0.0, jnp.exp(scores))
        totals = jnp.sum(exponent, axis=1, keepdims=True)
        delta = (exponent / totals - diagonal.astype(F32)).astype(BF)
        phi_grad = dot(delta, psi) * scale
        phi_grad_ref[own, :] = phi_grad.astype(BF)
        phi_grad_t_ref[:, own] = phi_grad.astype(BF).T
        psi_grad = (dot(delta.T, phi) * scale).astype(BF)
        put_back = jnp.where(
            goal_row == lax.broadcasted_iota(jnp.int32, (rows, batch), 0), 1.0, 0.0
        ).astype(BF)
        add = dot(put_back, psi_grad)
        if j == 0:
            total[...] = add
        else:
            total[...] += add
    sum_ref[...] = total[...].astype(BF)
    sum_t_ref[...] = total[...].astype(BF).T


def backward_kernel(pos_ref, first_ref, second_ref, grad_ref, grad_t_ref, states_ref, states_t_ref, gf_ref, gs_ref, active, back):
    quarter, rows = active.shape
    at = pl.multiple_of(pos_ref[1] * quarter, quarter)
    first_t = first_ref[:, pl.ds(at, quarter)].T
    second = second_ref[pl.ds(at, quarter), :]
    chunk = 512
    for c in range(0, rows, chunk):
        cols = slice(c, c + chunk)
        hidden = dot(first_t, states_t_ref[:, cols])
        sig = sigmoid(hidden)
        act = hidden * sig
        active[:, cols] = act.astype(BF)
        slope = sig + act * (1.0 - sig)
        back[:, cols] = (dot(second, grad_t_ref[:, cols]) * slope).astype(BF)
    gs_ref[...] = dot(active[...], grad_ref[...])
    gf_ref[...] = dot(back[...], states_ref[...]).T


def backward(pos, first, second, grad, grad_t, states, states_t, quarter):
    rows, width = states.shape
    emb = second.shape[1]
    return in_vmem(
        backward_kernel,
        "backward",
        [jax.ShapeDtypeStruct((width, quarter), F32), jax.ShapeDtypeStruct((quarter, emb), F32)],
        (first, second, grad, grad_t, states, states_t),
        [pltpu.VMEM((quarter, rows), BF), pltpu.VMEM((quarter, rows), BF)],
        limit=32,
        pos=pos,
        flops=8 * rows * width * quarter,
    )


def gathered(
    states, goal_distance, goal_row, episode, state_first, state_second, goal_first, goal_second
):
    rows_dev, width = states.shape
    n_blk, n_rep, n_sub = (lax.axis_size(a) for a in ("blk", "rep", "sub"))
    owners = n_blk * n_sub
    slab = rows_dev // n_rep
    rows_all = owners * rows_dev
    emb = state_second.shape[1]
    b, s = lax.axis_index("blk"), lax.axis_index("sub")
    pos = jnp.stack([b, s]).astype(jnp.int32)
    quarter = state_first.shape[1] // n_sub
    weights = (state_first, goal_first, state_second, goal_second)

    def across(x, k):
        return lax.ppermute(x, "blk", [(i, i ^ k) for i in range(n_blk)])

    def swap(x, axis):
        return lax.ppermute(x, axis, [(0, 1), (1, 0)])

    def after(x, *first):
        return lax.optimization_barrier((x, *first))[0]

    def both(part, there):
        return (part.astype(F32) + there.astype(F32)).astype(BF)

    got = {0: states, 3: across(states, 3)}
    part0 = forward(states, *weights)
    there0 = swap(part0, "rep")
    got[2] = across(after(states, part0), 2)
    part3 = forward(got[3], *weights)
    there3 = swap(part3, "rep")
    got[1] = across(after(states, part3), 1)

    distance = after(goal_distance, part3)
    owner = (b * n_sub + s + distance[:, 0]) % owners
    goal = (((owner % n_sub) * n_rep + goal_row // slab) * n_blk + owner // n_sub) * slab + goal_row % slab
    meta = jnp.pad(jnp.stack([goal, episode]), ((0, 6), (0, 0)))
    meta_all = lax.all_gather(meta, ("blk", "sub"), axis=0, tiled=True)

    sums = {0: both(part0, there0)}
    sums[1] = across(sums[0], 1)
    part2 = forward(got[2], *weights)
    there2 = swap(part2, "rep")
    sums[3] = both(part3, there3)
    sums[2] = both(part2, there2)

    others = [swap(got[k], "sub") for k in range(n_blk)]
    all_states, all_states_t = in_vmem(
        functools.partial(arrange_kernel, n_blk, n_rep, slab),
        "arrange",
        [jax.ShapeDtypeStruct((rows_all, width), BF), jax.ShapeDtypeStruct((width, rows_all), BF)],
        (*(got[k] for k in range(n_blk)), *others),
        pos=pos,
        limit=16,
    )

    other_sums = [swap(sums[k], "sub") for k in range(n_blk)]
    phi_grad, phi_grad_t, psi_sum, psi_sum_t = in_vmem(
        functools.partial(contrast_kernel, n_blk, n_rep, slab, 4.0 / math.sqrt(emb)),
        "contrast",
        [
            jax.ShapeDtypeStruct((rows_all, emb), BF),
            jax.ShapeDtypeStruct((emb, rows_all), BF),
            jax.ShapeDtypeStruct((rows_all, emb), BF),
            jax.ShapeDtypeStruct((emb, rows_all), BF),
        ],
        (*(sums[k] for k in range(n_blk)), *other_sums, meta_all),
        [pltpu.VMEM((rows_all, emb), BF), pltpu.VMEM((rows_all, emb), BF), pltpu.VMEM((rows_all, emb), F32)],
        pos=pos,
        limit=24,
        flops=2 * rows_all * emb * (2 * rows_all + 3 * n_blk * slab),
    )

    outs = []
    for first, second, grad, grad_t in (
        (state_first, state_second, phi_grad, phi_grad_t),
        (goal_first, goal_second, psi_sum, psi_sum_t),
    ):
        gf, gs = backward(pos, first, second, grad, grad_t, all_states, all_states_t, quarter)
        gf2, gs2 = swap(gf, "sub"), swap(gs, "sub")
        outs.append(
            jnp.where(s == 0, jnp.concatenate([gf, gf2], axis=1), jnp.concatenate([gf2, gf], axis=1))
        )
        outs.append(
            jnp.where(s == 0, jnp.concatenate([gs, gs2], axis=0), jnp.concatenate([gs2, gs], axis=0))
        )
    return tuple(outs)


def silu_slope(hidden):
    sig = jax.nn.sigmoid(hidden)
    return sig * (1.0 + hidden * (1.0 - sig))


def encoder_grads(rows_in, hidden, active, second, emb_grad):
    grad_second = jnp.einsum("nh,ne->he", active, emb_grad, preferred_element_type=jnp.float32)
    back = jnp.einsum("ne,he->nh", emb_grad, second, preferred_element_type=jnp.float32)
    back_rows = (back * silu_slope(hidden)).astype(jnp.bfloat16)
    grad_first = jnp.einsum("ns,nh->sh", rows_in, back_rows, preferred_element_type=jnp.float32)
    return (grad_first, grad_second)


def exchanged(
    states, goal_distance, goal_row, episode, state_first, state_second, goal_first, goal_second
):
    rows_dev, width = states.shape
    owners = lax.axis_size(("blk", "sub"))
    position = lax.axis_index(("blk", "sub"))
    capacity = 4 * rows_dev // owners
    target = (position + goal_distance[:, 0]) % owners
    onehot = (target[:, None] == jnp.arange(owners, dtype=jnp.int32)[None, :]).astype(jnp.int32)
    slot_rank = jnp.sum((jnp.cumsum(onehot, axis=0) - onehot) * onehot, axis=1)
    requests = jnp.zeros((owners, capacity), jnp.int32).at[target, slot_rank].set(goal_row)
    wanted = lax.all_to_all(requests, ("blk", "sub"), split_axis=0, concat_axis=0, tiled=True)
    fetched = jnp.take(states, wanted.reshape(-1), axis=0).reshape(wanted.shape + (width,))
    replies = lax.all_to_all(fetched, ("blk", "sub"), split_axis=0, concat_axis=0, tiled=True)
    goal_states = jnp.take(
        replies.reshape(owners * capacity, width), target * capacity + slot_rank, axis=0
    )
    slab_rows = rows_dev // lax.axis_size("rep")
    state_hidden = jnp.dot(states, state_first, preferred_element_type=jnp.float32)
    state_active = jax.nn.silu(state_hidden).astype(jnp.bfloat16)
    goal_hidden = jnp.dot(goal_states, goal_first, preferred_element_type=jnp.float32)
    goal_active = jax.nn.silu(goal_hidden).astype(jnp.bfloat16)
    phi = lax.psum_scatter(
        jnp.dot(state_active, state_second, preferred_element_type=jnp.float32),
        "rep",
        scatter_dimension=0,
        tiled=True,
    ).astype(jnp.bfloat16)
    psi = lax.psum_scatter(
        jnp.dot(goal_active, goal_second, preferred_element_type=jnp.float32),
        "rep",
        scatter_dimension=0,
        tiled=True,
    ).astype(jnp.bfloat16)
    episode_own = lax.dynamic_slice_in_dim(episode, lax.axis_index("rep") * slab_rows, slab_rows, 0)
    psi_all, episode_all = (
        lax.all_gather(psi, "blk", axis=0, tiled=True),
        lax.all_gather(episode_own, "blk", axis=0, tiled=True),
    )
    batch_rows = psi_all.shape[0]
    logit_scale = 4.0 / math.sqrt(psi.shape[1])
    own_rows = lax.axis_index("blk") * slab_rows + jnp.arange(slab_rows, dtype=jnp.int32)
    columns = jnp.arange(batch_rows, dtype=jnp.int32)
    diagonal = own_rows[:, None] == columns[None, :]
    excluded = (episode_own[:, None] == episode_all[None, :]) & ~diagonal
    scores = jnp.einsum("ie,je->ij", phi, psi_all, preferred_element_type=jnp.float32) * logit_scale
    exponent = jnp.where(excluded, 0.0, jnp.exp(scores))
    totals = jnp.sum(exponent, axis=1)
    delta = (exponent / totals[:, None] - diagonal.astype(jnp.float32)).astype(jnp.bfloat16)
    phi_grad = (jnp.dot(delta, psi_all, preferred_element_type=jnp.float32) * logit_scale).astype(
        jnp.bfloat16
    )
    psi_grad = lax.psum_scatter(
        jnp.einsum("ij,ie->je", delta, phi, preferred_element_type=jnp.float32) * logit_scale,
        "blk",
        scatter_dimension=0,
        tiled=True,
    ).astype(jnp.bfloat16)
    phi_full, psi_full = (
        lax.all_gather(phi_grad, "rep", axis=0, tiled=True),
        lax.all_gather(psi_grad, "rep", axis=0, tiled=True),
    )
    state_parts = encoder_grads(states, state_hidden, state_active, state_second, phi_full)
    goal_parts = encoder_grads(goal_states, goal_hidden, goal_active, goal_second, psi_full)
    summed = lax.psum(
        (state_parts[0], state_parts[1], goal_parts[0], goal_parts[1]), ("blk", "sub")
    )
    return (summed[0], summed[1], summed[2], summed[3])


def solution(mesh):
    in_specs = (
        P(("grp", "blk", "sub"), None),
        P(("grp", "blk", "sub"), None),
        P(("grp", "blk", "sub")),
        P(("grp", "blk", "sub")),
        P(None, "rep"),
        P("rep", None),
        P(None, "rep"),
        P("rep", None),
    )
    out_specs = (P("grp", "rep"), P(("grp", "rep"), None), P("grp", "rep"), P(("grp", "rep"), None))
    shape = mesh.shape
    local = gathered if (shape["blk"], shape["rep"], shape["sub"]) == (4, 2, 2) else exchanged
    return jax.shard_map(local, mesh=mesh, in_specs=in_specs, out_specs=out_specs, check_vma=False)
```

```python
import functools
import math

import jax
import jax.numpy as jnp
from jax import lax
from jax.experimental import pallas as pl
from jax.experimental.pallas import tpu as pltpu
from jax.sharding import PartitionSpec as P

BF = jnp.bfloat16
F32 = jnp.float32
MIB = 1024 * 1024


def dot(a, b):
    return jnp.dot(a, b, preferred_element_type=F32)


def sigmoid(v):
    return 0.5 * jnp.tanh(0.5 * v) + 0.5


HBM = pl.BlockSpec(memory_space=pl.ANY)
VMEM = pl.BlockSpec(memory_space=pltpu.VMEM)
SMEM = pl.BlockSpec(memory_space=pltpu.SMEM)


def kernel(body, name, outs, args, scratch=(), limit=16, pos=None, flops=0, hbm=(), hbm_out=(), aliases={}):
    specs = [HBM if i in hbm else VMEM for i in range(len(args))]
    if pos is not None:
        args, specs = (pos, *args), [SMEM, *specs]
        aliases = {i + 1: o for i, o in aliases.items()}
    return pl.pallas_call(
        body,
        in_specs=specs,
        out_specs=[HBM if i in hbm_out else VMEM for i in range(len(outs))],
        out_shape=[jax.ShapeDtypeStruct(shape, dtype) for shape, dtype in outs],
        scratch_shapes=scratch,
        input_output_aliases=aliases,
        compiler_params=pltpu.CompilerParams(vmem_limit_bytes=limit * MIB),
        cost_estimate=pl.CostEstimate(flops=flops, bytes_accessed=0, transcendentals=0),
        name=name,
    )(*args)


def encode(x_ref, weights, out_ref, active):
    emb = weights[2].shape[1]
    for k in range(2):
        first, second = weights[k], weights[2 + k]
        for c in range(0, active.shape[1], 512):
            hidden = dot(x_ref[...], first[:, c : c + 512])
            active[:, c : c + 512] = (hidden * sigmoid(hidden)).astype(BF)
        out_ref[:, k * emb : (k + 1) * emb] = dot(active[...], second[...]).astype(BF)


def first_kernel(x_ref, *refs):
    weights, out_ref, held, active, sems = refs[:4], refs[4], refs[5:9], refs[9], refs[10]
    copies = [pltpu.make_async_copy(w, h, sems.at[i]) for i, (w, h) in enumerate(zip(weights, held))]
    for i in (0, 2, 1, 3):
        copies[i].start()
    for c in copies:
        c.wait()
    encode(x_ref, held, out_ref, active)


def forward_kernel(x_ref, *refs):
    encode(x_ref, refs[:4], refs[4], refs[5])


def forward(x, weights, load=False):
    rows, width = x.shape
    hid, emb = weights[2].shape
    outs = [((rows, 2 * emb), BF)] + [(w.shape, w.dtype) for w in weights] * load
    got = kernel(
        first_kernel if load else forward_kernel,
        "forward",
        outs,
        (x, *weights),
        [pltpu.VMEM((rows, hid), BF)] + [pltpu.SemaphoreType.DMA((4,))] * load,
        flops=8 * rows * width * hid,
        hbm=(1, 2, 3, 4) if load else (),
    )
    return (got[0], got[1:]) if load else got[0]


def place_blocks(pos_ref, mine, other, put, n_blk, n_rep, slab):
    b, s = pos_ref[0], pos_ref[1]
    for side, blocks in ((s, mine), (1 - s, other)):
        for k, block in enumerate(blocks):
            at = jnp.bitwise_xor(b, k)
            for r in range(n_rep):
                off = ((side * n_rep + r) * n_blk + at) * slab
                put(pl.multiple_of(off, slab), block[r * slab : (r + 1) * slab, :])


def column(row):
    return jnp.broadcast_to(row, (128, row.shape[1])).T[:, :1]


def meta_row(pos_ref, meta_mine, meta_other, which, j, n_blk, n_rep, slab):
    side, r = j // n_rep, j % n_rep
    parts = []
    for blk in range(n_blk):
        at = pl.multiple_of(jnp.bitwise_xor(blk, pos_ref[0]) * 8, 8)
        cols = slice(r * slab, (r + 1) * slab)
        pair = [ref[pl.ds(at, 8), cols][which : which + 1, :] for ref in (meta_mine, meta_other)]
        parts.append(jnp.where(pos_ref[1] == side, pair[0], pair[1]))
    return jnp.concatenate(parts, axis=1).astype(F32)


def arrange_kernel(n_blk, n_rep, slab, pos_ref, *refs):
    mine, other = refs[:n_blk], refs[n_blk : 2 * n_blk]
    meta_mine, meta_other, all_ref, all_t_ref, goals_ref, goals_t_ref, pick_ref = refs[2 * n_blk :]
    rows = all_ref.shape[0]
    batch = n_blk * slab

    def put(off, value):
        all_ref[pl.ds(off, slab), :] = value
        all_t_ref[:, pl.ds(off, slab)] = value.T

    place_blocks(pos_ref, mine, other, put, n_blk, n_rep, slab)
    for j in range(rows // batch):
        own = slice(j * batch, (j + 1) * batch)
        goal = column(meta_row(pos_ref, meta_mine, meta_other, 0, j, n_blk, n_rep, slab)).astype(jnp.int32)
        pick_ref[own, :] = jnp.where(
            goal == lax.broadcasted_iota(jnp.int32, (batch, rows), 1), 1.0, 0.0
        ).astype(BF)
    goals = dot(pick_ref[...], all_ref[...]).astype(BF)
    goals_ref[...] = goals
    goals_t_ref[...] = goals.T


def contrast_kernel(n_blk, n_rep, slab, scale, pos_ref, *refs):
    mine, other = refs[:n_blk], refs[n_blk : 2 * n_blk]
    meta_mine, meta_other, pick_ref = refs[2 * n_blk : 2 * n_blk + 3]
    phi_grad_ref, phi_grad_t_ref, psi_grad_ref, psi_grad_t_ref, phi_all, psi_all = refs[2 * n_blk + 3 :]
    emb = phi_all.shape[1]
    batch = n_blk * slab
    rows = phi_all.shape[0]

    def put(off, value):
        phi_all[pl.ds(off, slab), :] = value[:, :emb]
        psi_all[pl.ds(off, slab), :] = value[:, emb:]

    place_blocks(pos_ref, mine, other, put, n_blk, n_rep, slab)

    for j in range(rows // batch):
        own = slice(j * batch, (j + 1) * batch)
        ep_row = meta_row(pos_ref, meta_mine, meta_other, 1, j, n_blk, n_rep, slab)
        psi = dot(pick_ref[own, :], psi_all[...]).astype(BF)
        phi = phi_all[own, :]
        scores = lax.dot_general(phi, psi, (((1,), (1,)), ((), ())), preferred_element_type=F32) * scale
        diagonal = lax.broadcasted_iota(jnp.int32, (batch, batch), 0) == lax.broadcasted_iota(
            jnp.int32, (batch, batch), 1
        )
        same = column(ep_row) == ep_row
        exponent = jnp.where(same & ~diagonal, 0.0, jnp.exp(scores))
        totals = jnp.sum(exponent, axis=1, keepdims=True)
        delta = (exponent / totals - diagonal.astype(F32)).astype(BF)
        phi_grad = (dot(delta, psi) * scale).astype(BF)
        phi_grad_ref[own, :] = phi_grad
        phi_grad_t_ref[:, own] = phi_grad.T
        psi_grad = (dot(delta.T, phi) * scale).astype(BF)
        psi_grad_ref[own, :] = psi_grad
        psi_grad_t_ref[:, own] = psi_grad.T


def backward_kernel(n_put, pos_ref, first_ref, second_ref, grad_ref, grad_t_ref, states_ref, states_t_ref, *refs):
    done, (gf_ref, gs_ref), outs, (active, back), sems = (
        refs[:n_put],
        refs[n_put : n_put + 2],
        refs[n_put + 2 : 2 * n_put + 2],
        refs[2 * n_put + 2 : 2 * n_put + 4],
        refs[2 * n_put + 4 :],
    )
    copies = [put_half(pos_ref[1], x, o, sems[0].at[i]) for i, (x, o) in enumerate(zip(done, outs))]
    for c in copies:
        c.start()
    quarter, rows = active.shape
    at = pl.multiple_of(pos_ref[1] * quarter, quarter)
    first_t = first_ref[:, pl.ds(at, quarter)].T
    second = second_ref[pl.ds(at, quarter), :]
    chunk = 512
    for c in range(0, rows, chunk):
        cols = slice(c, c + chunk)
        hidden = dot(first_t, states_t_ref[:, cols])
        sig = sigmoid(hidden)
        act = hidden * sig
        active[:, cols] = act.astype(BF)
        slope = sig + act * (1.0 - sig)
        back[:, cols] = (dot(second, grad_t_ref[:, cols]) * slope).astype(BF)
    gs_ref[...] = dot(active[...], grad_ref[...])
    gf_ref[...] = dot(back[...], states_ref[...]).T
    for c in copies:
        c.wait()


def put_half(side, half, out, sem):
    n, m = half.shape
    if out.shape[0] == n:
        to = out.at[:, pl.ds(pl.multiple_of(side * m, m), m)]
    else:
        to = out.at[pl.ds(pl.multiple_of(side * n, n), n), :]
    return pltpu.make_async_copy(half, to, sem)


def backward(pos, first, second, grad, grad_t, states, states_t, quarter, done=()):
    rows, width = states.shape
    emb = second.shape[1]
    halves = [((width, quarter), F32), ((quarter, emb), F32)]
    return kernel(
        functools.partial(backward_kernel, len(done)),
        "backward",
        halves + [((width, 2 * quarter), F32), ((2 * quarter, emb), F32)][: len(done)],
        (first, second, grad, grad_t, states, states_t, *done),
        [pltpu.VMEM((quarter, rows), BF), pltpu.VMEM((quarter, rows), BF)]
        + [pltpu.SemaphoreType.DMA((2,))] * bool(done),
        limit=28,
        pos=pos,
        flops=8 * rows * width * quarter,
        hbm_out=(2, 3),
    )


def finish_kernel(old, new, pos_ref, *refs):
    halves = refs[: old + new]
    outs = refs[2 * old + new : 2 * (old + new) + old]
    sems = refs[-1]
    copies = [
        put_half(1 - pos_ref[1] if i < old else pos_ref[1], x, o, sems.at[i])
        for i, (x, o) in enumerate(zip(halves, outs))
    ]
    for c in copies:
        c.start()
    for c in copies:
        c.wait()


def finish(pos, halves, wholes, shapes):
    old, new = len(wholes), len(shapes)
    n = old + new
    return kernel(
        functools.partial(finish_kernel, old, new),
        "finish",
        [(w.shape, w.dtype) for w in wholes] + shapes,
        (*halves, *wholes),
        [pltpu.SemaphoreType.DMA((n,))],
        pos=pos,
        hbm=range(n, n + old),
        hbm_out=range(n),
        aliases={n + i: i for i in range(old)},
    )


def gathered(
    states, goal_distance, goal_row, episode, state_first, state_second, goal_first, goal_second
):
    rows_dev, width = states.shape
    n_blk, n_rep, n_sub = (lax.axis_size(a) for a in ("blk", "rep", "sub"))
    owners = n_blk * n_sub
    slab = rows_dev // n_rep
    rows_all = owners * rows_dev
    hid, emb = state_second.shape
    b, s = lax.axis_index("blk"), lax.axis_index("sub")
    pos = jnp.stack([b, s]).astype(jnp.int32)
    quarter = hid // n_sub

    def across(x, k):
        return lax.ppermute(x, "blk", [(i, i ^ k) for i in range(n_blk)])

    def swap(x, axis):
        return lax.ppermute(x, axis, [(0, 1), (1, 0)])

    def after(x, *first):
        return lax.optimization_barrier((x, *first))[0]

    def both(part, there):
        return (part.astype(F32) + there.astype(F32)).astype(BF)

    got = {0: states, 3: across(states, 3), 2: across(states, 2)}
    part0, weights = forward(states, (state_first, goal_first, state_second, goal_second), load=True)
    there0 = swap(part0, "rep")
    part3 = forward(got[3], weights)
    there3 = swap(part3, "rep")

    distance = after(goal_distance, part0)
    owner = (b * n_sub + s + distance[:, 0]) % owners
    goal = (((owner % n_sub) * n_rep + goal_row // slab) * n_blk + owner // n_sub) * slab + goal_row % slab
    meta = jnp.pad(jnp.stack([goal, episode]), ((0, 6), (0, 0)))
    meta = jnp.concatenate([meta, across(meta, 1)], axis=0)
    meta = jnp.concatenate([meta, across(meta, 2)], axis=0)
    meta_other = swap(meta, "sub")

    sums = {0: both(part0, there0)}
    sums[1] = across(sums[0], 1)
    part2 = forward(after(got[2], sums[0]), weights)
    there2 = swap(part2, "rep")
    got[1] = across(after(states, part2), 1)
    sums[3] = both(part3, there3)
    sums[2] = both(part2, there2)

    others = [swap(got[k], "sub") for k in range(n_blk)]
    wide, tall = ((rows_all, width), BF), ((width, rows_all), BF)
    all_states, all_states_t, goals, goals_t, pick = kernel(
        functools.partial(arrange_kernel, n_blk, n_rep, slab),
        "arrange",
        [wide, tall, wide, tall, ((rows_all, rows_all), BF)],
        (*(got[k] for k in range(n_blk)), *others, meta, meta_other),
        pos=pos,
        flops=2 * rows_all * rows_all * width,
    )

    other_sums = [swap(sums[k], "sub") for k in range(n_blk)]
    wide, tall = ((rows_all, emb), BF), ((emb, rows_all), BF)
    phi_grad, phi_grad_t, psi_grad, psi_grad_t = kernel(
        functools.partial(contrast_kernel, n_blk, n_rep, slab, 4.0 / math.sqrt(emb)),
        "contrast",
        [wide, tall, wide, tall],
        (*(sums[k] for k in range(n_blk)), *other_sums, meta, meta_other, pick),
        [pltpu.VMEM((rows_all, emb), BF), pltpu.VMEM((rows_all, emb), BF)],
        pos=pos,
        flops=2 * rows_all * emb * (rows_all + 3 * n_blk * slab),
    )

    sf, gf, ss, gs = weights
    state_first_half, state_second_half = backward(
        pos, sf, ss, phi_grad, phi_grad_t, all_states, all_states_t, quarter
    )
    state_there = [swap(x, "sub") for x in (state_first_half, state_second_half)]
    goal_first_half, goal_second_half, out0, out1 = backward(
        pos, gf, gs, psi_grad, psi_grad_t, goals, goals_t, quarter, (state_first_half, state_second_half)
    )
    goal_there = [swap(x, "sub") for x in (goal_first_half, goal_second_half)]
    out0, out1, out2, out3 = finish(
        pos,
        (*state_there, goal_first_half, goal_second_half),
        (out0, out1),
        [((width, hid), F32), ((hid, emb), F32)],
    )
    out2, out3 = finish(pos, goal_there, (out2, out3), [])
    return (out0, out1, out2, out3)


def silu_slope(hidden):
    sig = jax.nn.sigmoid(hidden)
    return sig * (1.0 + hidden * (1.0 - sig))


def encoder_grads(rows_in, hidden, active, second, emb_grad):
    grad_second = jnp.einsum("nh,ne->he", active, emb_grad, preferred_element_type=jnp.float32)
    back = jnp.einsum("ne,he->nh", emb_grad, second, preferred_element_type=jnp.float32)
    back_rows = (back * silu_slope(hidden)).astype(jnp.bfloat16)
    grad_first = jnp.einsum("ns,nh->sh", rows_in, back_rows, preferred_element_type=jnp.float32)
    return (grad_first, grad_second)


def exchanged(
    states, goal_distance, goal_row, episode, state_first, state_second, goal_first, goal_second
):
    rows_dev, width = states.shape
    owners = lax.axis_size(("blk", "sub"))
    position = lax.axis_index(("blk", "sub"))
    capacity = 4 * rows_dev // owners
    target = (position + goal_distance[:, 0]) % owners
    onehot = (target[:, None] == jnp.arange(owners, dtype=jnp.int32)[None, :]).astype(jnp.int32)
    slot_rank = jnp.sum((jnp.cumsum(onehot, axis=0) - onehot) * onehot, axis=1)
    requests = jnp.zeros((owners, capacity), jnp.int32).at[target, slot_rank].set(goal_row)
    wanted = lax.all_to_all(requests, ("blk", "sub"), split_axis=0, concat_axis=0, tiled=True)
    fetched = jnp.take(states, wanted.reshape(-1), axis=0).reshape(wanted.shape + (width,))
    replies = lax.all_to_all(fetched, ("blk", "sub"), split_axis=0, concat_axis=0, tiled=True)
    goal_states = jnp.take(
        replies.reshape(owners * capacity, width), target * capacity + slot_rank, axis=0
    )
    slab_rows = rows_dev // lax.axis_size("rep")
    state_hidden = jnp.dot(states, state_first, preferred_element_type=jnp.float32)
    state_active = jax.nn.silu(state_hidden).astype(jnp.bfloat16)
    goal_hidden = jnp.dot(goal_states, goal_first, preferred_element_type=jnp.float32)
    goal_active = jax.nn.silu(goal_hidden).astype(jnp.bfloat16)
    phi = lax.psum_scatter(
        jnp.dot(state_active, state_second, preferred_element_type=jnp.float32),
        "rep",
        scatter_dimension=0,
        tiled=True,
    ).astype(jnp.bfloat16)
    psi = lax.psum_scatter(
        jnp.dot(goal_active, goal_second, preferred_element_type=jnp.float32),
        "rep",
        scatter_dimension=0,
        tiled=True,
    ).astype(jnp.bfloat16)
    episode_own = lax.dynamic_slice_in_dim(episode, lax.axis_index("rep") * slab_rows, slab_rows, 0)
    psi_all, episode_all = (
        lax.all_gather(psi, "blk", axis=0, tiled=True),
        lax.all_gather(episode_own, "blk", axis=0, tiled=True),
    )
    batch_rows = psi_all.shape[0]
    logit_scale = 4.0 / math.sqrt(psi.shape[1])
    own_rows = lax.axis_index("blk") * slab_rows + jnp.arange(slab_rows, dtype=jnp.int32)
    columns = jnp.arange(batch_rows, dtype=jnp.int32)
    diagonal = own_rows[:, None] == columns[None, :]
    excluded = (episode_own[:, None] == episode_all[None, :]) & ~diagonal
    scores = jnp.einsum("ie,je->ij", phi, psi_all, preferred_element_type=jnp.float32) * logit_scale
    exponent = jnp.where(excluded, 0.0, jnp.exp(scores))
    totals = jnp.sum(exponent, axis=1)
    delta = (exponent / totals[:, None] - diagonal.astype(jnp.float32)).astype(jnp.bfloat16)
    phi_grad = (jnp.dot(delta, psi_all, preferred_element_type=jnp.float32) * logit_scale).astype(
        jnp.bfloat16
    )
    psi_grad = lax.psum_scatter(
        jnp.einsum("ij,ie->je", delta, phi, preferred_element_type=jnp.float32) * logit_scale,
        "blk",
        scatter_dimension=0,
        tiled=True,
    ).astype(jnp.bfloat16)
    phi_full, psi_full = (
        lax.all_gather(phi_grad, "rep", axis=0, tiled=True),
        lax.all_gather(psi_grad, "rep", axis=0, tiled=True),
    )
    state_parts = encoder_grads(states, state_hidden, state_active, state_second, phi_full)
    goal_parts = encoder_grads(goal_states, goal_hidden, goal_active, goal_second, psi_full)
    summed = lax.psum(
        (state_parts[0], state_parts[1], goal_parts[0], goal_parts[1]), ("blk", "sub")
    )
    return (summed[0], summed[1], summed[2], summed[3])


def solution(mesh):
    in_specs = (
        P(("grp", "blk", "sub"), None),
        P(("grp", "blk", "sub"), None),
        P(("grp", "blk", "sub")),
        P(("grp", "blk", "sub")),
        P(None, "rep"),
        P("rep", None),
        P(None, "rep"),
        P("rep", None),
    )
    out_specs = (P("grp", "rep"), P(("grp", "rep"), None), P("grp", "rep"), P(("grp", "rep"), None))
    shape = mesh.shape
    local = gathered if (shape["blk"], shape["rep"], shape["sub"]) == (4, 2, 2) else exchanged
    return jax.shard_map(local, mesh=mesh, in_specs=in_specs, out_specs=out_specs, check_vma=False)
```

```python
import functools
import math

import jax
import jax.numpy as jnp
from jax import lax
from jax.experimental import pallas as pl
from jax.experimental.pallas import tpu as pltpu
from jax.sharding import PartitionSpec as P

BF = jnp.bfloat16
F32 = jnp.float32
MIB = 1024 * 1024


def dot(a, b):
    return jnp.dot(a, b, preferred_element_type=F32)


def sigmoid(v):
    return 0.5 * jnp.tanh(0.5 * v) + 0.5


HBM = pl.BlockSpec(memory_space=pltpu.HBM)
VMEM = pl.BlockSpec(memory_space=pltpu.VMEM)
SMEM = pl.BlockSpec(memory_space=pltpu.SMEM)


def kernel(body, name, outs, args, scratch=(), limit=16, pos=None, flops=0, hbm=(), hbm_out=(), aliases={}):
    specs = [HBM if i in hbm else VMEM for i in range(len(args))]
    if pos is not None:
        args, specs = (pos, *args), [SMEM, *specs]
        aliases = {i + 1: o for i, o in aliases.items()}
    return pl.pallas_call(
        body,
        in_specs=specs,
        out_specs=[HBM if i in hbm_out else VMEM for i in range(len(outs))],
        out_shape=[jax.ShapeDtypeStruct(shape, dtype) for shape, dtype in outs],
        scratch_shapes=scratch,
        input_output_aliases=aliases,
        compiler_params=pltpu.CompilerParams(vmem_limit_bytes=limit * MIB),
        cost_estimate=pl.CostEstimate(flops=flops, bytes_accessed=0, transcendentals=0),
        name=name,
    )(*args)


def encode(x_ref, weights, out_ref, active):
    emb = weights[2].shape[1]
    for k in range(2):
        first, second = weights[k], weights[2 + k]
        for c in range(0, active.shape[1], 512):
            hidden = dot(x_ref[...], first[:, c : c + 512])
            active[:, c : c + 512] = (hidden * sigmoid(hidden)).astype(BF)
        out_ref[:, k * emb : (k + 1) * emb] = dot(active[...], second[...]).astype(BF)


def first_kernel(x_ref, *refs):
    weights, out_ref, held, active, sems = refs[:4], refs[4], refs[5:9], refs[9], refs[10]
    copies = [pltpu.make_async_copy(w, h, sems.at[i]) for i, (w, h) in enumerate(zip(weights, held))]
    for i in (0, 2, 1, 3):
        copies[i].start()
    for c in copies:
        c.wait()
    encode(x_ref, held, out_ref, active)


def forward_kernel(x_ref, *refs):
    encode(x_ref, refs[:4], refs[4], refs[5])


def forward(x, weights, load=False):
    rows, width = x.shape
    hid, emb = weights[2].shape
    outs = [((rows, 2 * emb), BF)] + [(w.shape, w.dtype) for w in weights] * load
    got = kernel(
        first_kernel if load else forward_kernel,
        "forward",
        outs,
        (x, *weights),
        [pltpu.VMEM((rows, hid), BF)] + [pltpu.SemaphoreType.DMA((4,))] * load,
        flops=8 * rows * width * hid,
        hbm=(1, 2, 3, 4) if load else (),
    )
    return (got[0], got[1:]) if load else got[0]


def add_kernel(a_ref, b_ref, out_ref):
    out_ref[...] = (a_ref[...].astype(F32) + b_ref[...].astype(F32)).astype(BF)


def both(part, there):
    return kernel(add_kernel, "both", [(part.shape, BF)], (part, there), limit=4)[0]


def place_blocks(pos_ref, blocks, put, n_blk, n_rep, slab):
    for k, block in enumerate(blocks):
        at = jnp.bitwise_xor(pos_ref[0], k)
        for r in range(n_rep):
            off = (r * n_blk + at) * slab
            put(pl.multiple_of(off, slab), block[r * slab : (r + 1) * slab, :])


def column(row):
    return jnp.broadcast_to(row, (128, row.shape[1])).T[:, :1]


def meta_row(pos_ref, meta_ref, which, r, n_blk, slab):
    parts = []
    for blk in range(n_blk):
        at = pl.multiple_of(jnp.bitwise_xor(blk, pos_ref[0]) * 8, 8)
        parts.append(meta_ref[pl.ds(at, 8), r * slab : (r + 1) * slab][which : which + 1, :])
    return jnp.concatenate(parts, axis=1).astype(F32)


def arrange_kernel(n_blk, n_rep, slab, pos_ref, *refs):
    mine, other, metas = refs[:n_blk], refs[n_blk : 2 * n_blk], refs[2 * n_blk : 2 * n_blk + 2]
    rows_mine, rows_other, goals_mine, goals_other, pick_ref, both_sides, pick_other = refs[2 * n_blk + 2 :]
    half = rows_mine.shape[0]
    rows = 2 * half
    batch = n_blk * slab
    for i, (blocks, to) in enumerate(((mine, rows_mine), (other, rows_other))):

        def put(off, value, i=i, to=to):
            to[pl.ds(off, slab), :] = value
            both_sides[pl.ds(i * half + off, slab), :] = value

        place_blocks(pos_ref, blocks, put, n_blk, n_rep, slab)
    for meta, pick, goals in ((metas[0], pick_ref, goals_mine), (metas[1], pick_other, goals_other)):
        for r in range(n_rep):
            own = slice(r * batch, (r + 1) * batch)
            goal = column(meta_row(pos_ref, meta, 0, r, n_blk, slab)).astype(jnp.int32) + pos_ref[1] * half
            goal = jnp.where(goal >= rows, goal - rows, goal)
            pick[own, :] = jnp.where(
                goal == lax.broadcasted_iota(jnp.int32, (batch, rows), 1), 1.0, 0.0
            ).astype(BF)
        goals[...] = dot(pick[...], both_sides[...]).astype(BF)


def contrast_kernel(n_blk, n_rep, slab, scale, pos_ref, *refs):
    n = n_blk + 1
    mine, other, meta_ref, pick_ref = refs[:n], refs[n : 2 * n], refs[2 * n], refs[2 * n + 1]
    grads_ref, phi_all, psi_all = refs[2 * n + 2 :]
    half, emb = phi_all.shape
    batch = n_blk * slab
    last = n_blk - 2

    def sums(parts):
        blocks = list(parts[:n_blk])
        blocks[last] = (parts[last][...].astype(F32) + parts[n_blk][...].astype(F32)).astype(BF)
        return blocks

    def put_mine(off, value):
        phi_all[pl.ds(off, slab), :] = value[:, :emb]
        psi_all[pl.ds(off, slab), :] = value[:, emb:]

    def put_other(off, value):
        psi_all[pl.ds(half + off, slab), :] = value[:, emb:]

    place_blocks(pos_ref, sums(mine), put_mine, n_blk, n_rep, slab)
    place_blocks(pos_ref, sums(other), put_other, n_blk, n_rep, slab)
    diagonal = lax.broadcasted_iota(jnp.int32, (batch, batch), 0) == lax.broadcasted_iota(
        jnp.int32, (batch, batch), 1
    )
    for r in range(n_rep):
        own = slice(r * batch, (r + 1) * batch)
        ep_row = meta_row(pos_ref, meta_ref, 1, r, n_blk, slab)
        psi = dot(pick_ref[own, :], psi_all[...]).astype(BF)
        phi = phi_all[own, :]
        scores = lax.dot_general(phi, psi, (((1,), (1,)), ((), ())), preferred_element_type=F32)
        kept = (column(ep_row) != ep_row) | diagonal
        exponent = jnp.where(kept, jnp.exp(scores * scale), 0.0)
        totals = jnp.sum(exponent, axis=1, keepdims=True)
        power = jnp.where(totals > 1.0, 2.0**-32, 1.0)
        shares = (exponent * power) * (1.0 / (totals * power))
        delta = jnp.where(diagonal, shares - 1.0, shares).astype(BF)
        grads_ref[own, :emb] = (dot(delta, psi) * scale).astype(BF)
        grads_ref[own, emb:] = (dot(delta.T, phi) * scale).astype(BF)


def rows_grads(at, first_ref, second_ref, grads_ref, k, rows_ref, active, back):
    quarter, rows = active.shape
    emb = second_ref.shape[1]
    first_t = first_ref[:, pl.ds(at, quarter)].T
    second = second_ref[pl.ds(at, quarter), :]
    grad = grads_ref[:, k * emb : (k + 1) * emb]
    chunk = 512
    for c in range(0, rows, chunk):
        cols = slice(c, c + chunk)
        hidden = dot(first_t, rows_ref[cols, :].T)
        sig = sigmoid(hidden)
        act = hidden * sig
        active[:, cols] = act.astype(BF)
        slope = sig + act * (1.0 - sig)
        back[:, cols] = (dot(second, grad[cols, :].T) * slope).astype(BF)
    return dot(active[...], grad), dot(back[...], rows_ref[...])


def mine_kernel(pos_ref, sf, gf, ss, gs, grads_ref, rows_ref, goals_ref, *refs):
    outs, (active, back) = refs[:4], refs[4:]
    quarter = active.shape[0]
    at = pl.multiple_of(pos_ref[1] * quarter, quarter)
    outs[0][...], outs[1][...] = rows_grads(at, sf, ss, grads_ref, 0, rows_ref, active, back)
    outs[2][...], outs[3][...] = rows_grads(at, gf, gs, grads_ref, 1, goals_ref, active, back)


def other_kernel(k, n_put, pos_ref, first, second, grads_ref, rows_ref, sum_second, sum_first, *refs):
    done, (gf_ref, gs_ref), outs, (active, back), sems = (
        refs[:n_put],
        refs[n_put : n_put + 2],
        refs[n_put + 2 : 2 * n_put + 2],
        refs[2 * n_put + 2 : 2 * n_put + 4],
        refs[2 * n_put + 4 :],
    )
    copies = [put_half(pos_ref[1], x, o, sems[0].at[i]) for i, (x, o) in enumerate(zip(done, outs))]
    for c in copies:
        c.start()
    quarter = active.shape[0]
    at = pl.multiple_of(pos_ref[1] * quarter, quarter)
    grad_second, grad_first = rows_grads(at, first, second, grads_ref, k, rows_ref, active, back)
    gs_ref[...] = sum_second[...] + grad_second
    gf_ref[...] = (sum_first[...] + grad_first).T
    for c in copies:
        c.wait()


def put_half(side, half, out, sem):
    n, m = half.shape
    if out.shape[0] == n:
        to = out.at[:, pl.ds(pl.multiple_of(side * m, m), m)]
    else:
        to = out.at[pl.ds(pl.multiple_of(side * n, n), n), :]
    return pltpu.make_async_copy(half, to, sem)


def finish_kernel(old, new, pos_ref, *refs):
    halves = refs[: old + new]
    outs = refs[2 * old + new : 2 * (old + new) + old]
    sems = refs[-1]
    copies = [
        put_half(1 - pos_ref[1] if i < old else pos_ref[1], x, o, sems.at[i])
        for i, (x, o) in enumerate(zip(halves, outs))
    ]
    for c in copies:
        c.start()
    for c in copies:
        c.wait()


def finish(pos, halves, wholes, shapes):
    old, new = len(wholes), len(shapes)
    n = old + new
    return kernel(
        functools.partial(finish_kernel, old, new),
        "finish",
        [(w.shape, w.dtype) for w in wholes] + shapes,
        (*halves, *wholes),
        [pltpu.SemaphoreType.DMA((n,))],
        pos=pos,
        hbm=range(n, n + old),
        hbm_out=range(n),
        aliases={n + i: i for i in range(old)},
    )


def gathered(
    states, goal_distance, goal_row, episode, state_first, state_second, goal_first, goal_second
):
    rows_dev, width = states.shape
    n_blk, n_rep, n_sub = (lax.axis_size(a) for a in ("blk", "rep", "sub"))
    owners = n_blk * n_sub
    slab = rows_dev // n_rep
    rows_all = owners * rows_dev
    hid, emb = state_second.shape
    b, s = lax.axis_index("blk"), lax.axis_index("sub")
    pos = jnp.stack([b, s]).astype(jnp.int32)
    quarter = hid // n_sub

    def across(x, k):
        return lax.ppermute(x, "blk", [(i, i ^ k) for i in range(n_blk)])

    def swap(x, axis):
        return lax.ppermute(x, axis, [(0, 1), (1, 0)])

    def after(x, *first):
        return lax.optimization_barrier((x, *first))[0]

    got = {0: states, 3: across(states, 3), 2: across(states, 2)}
    part0, weights = forward(states, (state_first, goal_first, state_second, goal_second), load=True)
    there0 = swap(part0, "rep")
    got[1] = across(after(states, part0), 1)
    part3 = forward(got[3], weights)
    there3 = swap(part3, "rep")

    distance = after(goal_distance, part0)
    owner = (b * n_sub + s + distance[:, 0]) % owners
    goal = (((owner % n_sub) * n_rep + goal_row // slab) * n_blk + owner // n_sub) * slab + goal_row % slab
    meta = jnp.pad(jnp.stack([goal, episode]), ((0, 6), (0, 0)))
    meta = jnp.concatenate([meta, across(meta, 1)], axis=0)
    meta = jnp.concatenate([meta, across(meta, 2)], axis=0)
    meta_other = swap(meta, "sub")

    sums = {0: both(part0, there0)}
    sums[1] = across(sums[0], 1)
    part2 = forward(after(got[2], sums[0]), weights)
    there2 = swap(part2, "rep")
    sums[3] = both(part3, there3)
    embedded = [sums[0], sums[1], part2, sums[3], there2]

    side = ((rows_all // 2, width), BF)
    mine, other, goals_mine, goals_other, pick = kernel(
        functools.partial(arrange_kernel, n_blk, n_rep, slab),
        "arrange",
        [side, side, side, side, ((rows_all // 2, rows_all), BF)],
        (*(got[k] for k in range(n_blk)), *(swap(got[k], "sub") for k in range(n_blk)), meta, meta_other),
        [pltpu.VMEM((rows_all, width), BF), pltpu.VMEM((rows_all // 2, rows_all), BF)],
        pos=pos,
        flops=2 * rows_all * rows_all * width,
    )
    (grads_mine,) = kernel(
        functools.partial(contrast_kernel, n_blk, n_rep, slab, 4.0 / math.sqrt(emb)),
        "contrast",
        [((rows_all // 2, 2 * emb), BF)],
        (*embedded, *(swap(x, "sub") for x in embedded), meta, pick),
        [pltpu.VMEM((rows_all // 2, emb), BF), pltpu.VMEM((rows_all, emb), BF)],
        pos=pos,
        flops=rows_all * emb * (rows_all + 3 * n_blk * slab),
    )
    grads_other = swap(grads_mine, "sub")

    sf, gf, ss, gs = weights
    work = [pltpu.VMEM((quarter, rows_all // 2), BF), pltpu.VMEM((quarter, rows_all // 2), BF)]
    flops = 4 * rows_all * width * quarter
    sums_s2, sums_s1, sums_g2, sums_g1 = kernel(
        mine_kernel,
        "mine",
        [((quarter, emb), F32), ((quarter, width), F32)] * 2,
        (sf, gf, ss, gs, grads_mine, mine, goals_mine),
        work,
        pos=pos,
        flops=2 * flops,
    )
    halves = [((width, quarter), F32), ((quarter, emb), F32)]
    wholes = [((width, hid), F32), ((hid, emb), F32)]
    state_halves = kernel(
        functools.partial(other_kernel, 0, 0),
        "other_state",
        halves,
        (sf, ss, grads_other, other, sums_s2, sums_s1),
        work,
        pos=pos,
        flops=flops,
    )
    state_there = [swap(x, "sub") for x in state_halves]
    *goal_halves, out0, out1 = kernel(
        functools.partial(other_kernel, 1, 2),
        "other_goal",
        halves + wholes,
        (gf, gs, grads_other, goals_other, sums_g2, sums_g1, *state_halves),
        work + [pltpu.SemaphoreType.DMA((2,))],
        pos=pos,
        flops=flops,
        hbm_out=(2, 3),
    )
    goal_there = [swap(x, "sub") for x in goal_halves]
    out0, out1, out2, out3 = finish(pos, (*state_there, *goal_halves), (out0, out1), wholes)
    out2, out3 = finish(pos, goal_there, (out2, out3), [])
    return (out0, out1, out2, out3)


def silu_slope(hidden):
    sig = jax.nn.sigmoid(hidden)
    return sig * (1.0 + hidden * (1.0 - sig))


def encoder_grads(rows_in, hidden, active, second, emb_grad):
    grad_second = jnp.einsum("nh,ne->he", active, emb_grad, preferred_element_type=jnp.float32)
    back = jnp.einsum("ne,he->nh", emb_grad, second, preferred_element_type=jnp.float32)
    back_rows = (back * silu_slope(hidden)).astype(jnp.bfloat16)
    grad_first = jnp.einsum("ns,nh->sh", rows_in, back_rows, preferred_element_type=jnp.float32)
    return (grad_first, grad_second)


def exchanged(
    states, goal_distance, goal_row, episode, state_first, state_second, goal_first, goal_second
):
    rows_dev, width = states.shape
    owners = lax.axis_size(("blk", "sub"))
    position = lax.axis_index(("blk", "sub"))
    capacity = 4 * rows_dev // owners
    target = (position + goal_distance[:, 0]) % owners
    onehot = (target[:, None] == jnp.arange(owners, dtype=jnp.int32)[None, :]).astype(jnp.int32)
    slot_rank = jnp.sum((jnp.cumsum(onehot, axis=0) - onehot) * onehot, axis=1)
    requests = jnp.zeros((owners, capacity), jnp.int32).at[target, slot_rank].set(goal_row)
    wanted = lax.all_to_all(requests, ("blk", "sub"), split_axis=0, concat_axis=0, tiled=True)
    fetched = jnp.take(states, wanted.reshape(-1), axis=0).reshape(wanted.shape + (width,))
    replies = lax.all_to_all(fetched, ("blk", "sub"), split_axis=0, concat_axis=0, tiled=True)
    goal_states = jnp.take(
        replies.reshape(owners * capacity, width), target * capacity + slot_rank, axis=0
    )
    slab_rows = rows_dev // lax.axis_size("rep")
    state_hidden = jnp.dot(states, state_first, preferred_element_type=jnp.float32)
    state_active = jax.nn.silu(state_hidden).astype(jnp.bfloat16)
    goal_hidden = jnp.dot(goal_states, goal_first, preferred_element_type=jnp.float32)
    goal_active = jax.nn.silu(goal_hidden).astype(jnp.bfloat16)
    phi = lax.psum_scatter(
        jnp.dot(state_active, state_second, preferred_element_type=jnp.float32),
        "rep",
        scatter_dimension=0,
        tiled=True,
    ).astype(jnp.bfloat16)
    psi = lax.psum_scatter(
        jnp.dot(goal_active, goal_second, preferred_element_type=jnp.float32),
        "rep",
        scatter_dimension=0,
        tiled=True,
    ).astype(jnp.bfloat16)
    episode_own = lax.dynamic_slice_in_dim(episode, lax.axis_index("rep") * slab_rows, slab_rows, 0)
    psi_all, episode_all = (
        lax.all_gather(psi, "blk", axis=0, tiled=True),
        lax.all_gather(episode_own, "blk", axis=0, tiled=True),
    )
    batch_rows = psi_all.shape[0]
    logit_scale = 4.0 / math.sqrt(psi.shape[1])
    own_rows = lax.axis_index("blk") * slab_rows + jnp.arange(slab_rows, dtype=jnp.int32)
    columns = jnp.arange(batch_rows, dtype=jnp.int32)
    diagonal = own_rows[:, None] == columns[None, :]
    excluded = (episode_own[:, None] == episode_all[None, :]) & ~diagonal
    scores = jnp.einsum("ie,je->ij", phi, psi_all, preferred_element_type=jnp.float32) * logit_scale
    exponent = jnp.where(excluded, 0.0, jnp.exp(scores))
    totals = jnp.sum(exponent, axis=1)
    delta = (exponent / totals[:, None] - diagonal.astype(jnp.float32)).astype(jnp.bfloat16)
    phi_grad = (jnp.dot(delta, psi_all, preferred_element_type=jnp.float32) * logit_scale).astype(
        jnp.bfloat16
    )
    psi_grad = lax.psum_scatter(
        jnp.einsum("ij,ie->je", delta, phi, preferred_element_type=jnp.float32) * logit_scale,
        "blk",
        scatter_dimension=0,
        tiled=True,
    ).astype(jnp.bfloat16)
    phi_full, psi_full = (
        lax.all_gather(phi_grad, "rep", axis=0, tiled=True),
        lax.all_gather(psi_grad, "rep", axis=0, tiled=True),
    )
    state_parts = encoder_grads(states, state_hidden, state_active, state_second, phi_full)
    goal_parts = encoder_grads(goal_states, goal_hidden, goal_active, goal_second, psi_full)
    summed = lax.psum(
        (state_parts[0], state_parts[1], goal_parts[0], goal_parts[1]), ("blk", "sub")
    )
    return (summed[0], summed[1], summed[2], summed[3])


def solution(mesh):
    in_specs = (
        P(("grp", "blk", "sub"), None),
        P(("grp", "blk", "sub"), None),
        P(("grp", "blk", "sub")),
        P(("grp", "blk", "sub")),
        P(None, "rep"),
        P("rep", None),
        P(None, "rep"),
        P("rep", None),
    )
    out_specs = (P("grp", "rep"), P(("grp", "rep"), None), P("grp", "rep"), P(("grp", "rep"), None))
    shape = mesh.shape
    local = gathered if (shape["blk"], shape["rep"], shape["sub"]) == (4, 2, 2) else exchanged
    return jax.shard_map(local, mesh=mesh, in_specs=in_specs, out_specs=out_specs, check_vma=False)
```

```python
import functools
import math

import jax
import jax.numpy as jnp
from jax import lax
from jax.experimental import pallas as pl
from jax.experimental.pallas import tpu as pltpu
from jax.sharding import PartitionSpec as P

BF = jnp.bfloat16
F32 = jnp.float32
MIB = 1024 * 1024


def dot(a, b):
    return jnp.dot(a, b, preferred_element_type=F32)


def sigmoid(v):
    return 0.5 * jnp.tanh(0.5 * v) + 0.5


HBM = pl.BlockSpec(memory_space=pltpu.HBM)
VMEM = pl.BlockSpec(memory_space=pltpu.VMEM)
SMEM = pl.BlockSpec(memory_space=pltpu.SMEM)


def kernel(body, name, outs, args, scratch=(), limit=16, pos=None, flops=0, hbm=(), hbm_out=(), aliases={}):
    specs = [HBM if i in hbm else VMEM for i in range(len(args))]
    if pos is not None:
        args, specs = (pos, *args), [SMEM, *specs]
        aliases = {i + 1: o for i, o in aliases.items()}
    return pl.pallas_call(
        body,
        in_specs=specs,
        out_specs=[HBM if i in hbm_out else VMEM for i in range(len(outs))],
        out_shape=[jax.ShapeDtypeStruct(shape, dtype) for shape, dtype in outs],
        scratch_shapes=scratch,
        input_output_aliases=aliases,
        compiler_params=pltpu.CompilerParams(vmem_limit_bytes=limit * MIB),
        cost_estimate=pl.CostEstimate(flops=flops, bytes_accessed=0, transcendentals=0),
        name=name,
    )(*args)


def forward_kernel(x_ref, *refs):
    weights, out_ref, held, active, sems = refs[:4], refs[4], refs[5:9], refs[9], refs[10]
    hid, emb = weights[2].shape
    part = hid // 2

    def piece(ref, i, p):
        at = pl.ds(p * part, part)
        return ref.at[:, at] if i < 2 else ref.at[at, :]

    copies = {}
    for k in range(2):
        for p in range(2):
            for i in (k, 2 + k):
                copies[i, p] = pltpu.make_async_copy(
                    piece(weights[i], i, p), piece(held[i], i, p), sems.at[2 * i + p]
                )
                copies[i, p].start()
    for k in range(2):
        for p in range(2):
            copies[k, p].wait()
            for c in range(p * part, (p + 1) * part, 512):
                hidden = dot(x_ref[...], held[k][:, c : c + 512])
                active[:, c : c + 512] = (hidden * sigmoid(hidden)).astype(BF)
        for p in range(2):
            copies[2 + k, p].wait()
        out_ref[:, k * emb : (k + 1) * emb] = dot(active[...], held[2 + k][...]).astype(BF)


def forward(x, weights):
    rows, width = x.shape
    hid, emb = weights[2].shape
    return kernel(
        forward_kernel,
        "forward",
        [((rows, 2 * emb), BF)],
        (x, *weights),
        [pltpu.VMEM(w.shape, w.dtype) for w in weights]
        + [pltpu.VMEM((rows, hid), BF), pltpu.SemaphoreType.DMA((8,))],
        limit=56,
        hbm=(1, 2, 3, 4),
    )[0]


def add_kernel(a_ref, b_ref, out_ref):
    out_ref[...] = (a_ref[...].astype(F32) + b_ref[...].astype(F32)).astype(BF)


def both(part, there):
    return kernel(add_kernel, "both", [(part.shape, BF)], (part, there), limit=4)[0]


def place_blocks(pos_ref, blocks, put, n_blk, n_rep, slab):
    for k, block in enumerate(blocks):
        at = jnp.bitwise_xor(pos_ref[0], k)
        for r in range(n_rep):
            off = (r * n_blk + at) * slab
            put(pl.multiple_of(off, slab), block[r * slab : (r + 1) * slab, :])


def column(row):
    return jnp.broadcast_to(row, (128, row.shape[1])).T[:, :1]


def meta_row(pos_ref, meta_ref, which, r, n_blk, slab):
    parts = []
    for blk in range(n_blk):
        at = pl.multiple_of(jnp.bitwise_xor(blk, pos_ref[0]) * 8, 8)
        parts.append(meta_ref[pl.ds(at, 8), r * slab : (r + 1) * slab][which : which + 1, :])
    return jnp.concatenate(parts, axis=1).astype(F32)


def arrange_kernel(n_blk, n_rep, slab, pos_ref, *refs):
    mine, other, metas = refs[:n_blk], refs[n_blk : 2 * n_blk], refs[2 * n_blk : 2 * n_blk + 2]
    rows_mine, rows_other, goals_mine, goals_other, pick_ref, both_sides, pick_other = refs[2 * n_blk + 2 :]
    half = rows_mine.shape[0]
    rows = 2 * half
    batch = n_blk * slab
    for i, (blocks, to) in enumerate(((mine, rows_mine), (other, rows_other))):

        def put(off, value, i=i, to=to):
            to[pl.ds(off, slab), :] = value
            both_sides[pl.ds(i * half + off, slab), :] = value

        place_blocks(pos_ref, blocks, put, n_blk, n_rep, slab)
    for meta, pick, goals in ((metas[0], pick_ref, goals_mine), (metas[1], pick_other, goals_other)):
        for r in range(n_rep):
            own = slice(r * batch, (r + 1) * batch)
            goal = column(meta_row(pos_ref, meta, 0, r, n_blk, slab)).astype(jnp.int32) + pos_ref[1] * half
            goal = jnp.where(goal >= rows, goal - rows, goal)
            pick[own, :] = jnp.where(
                goal == lax.broadcasted_iota(jnp.int32, (batch, rows), 1), 1.0, 0.0
            ).astype(BF)
        goals[...] = dot(pick[...], both_sides[...]).astype(BF)


def contrast_kernel(n_blk, n_rep, slab, scale, pos_ref, *refs):
    n = n_blk + 1
    mine, other, meta_ref, pick_ref = refs[:n], refs[n : 2 * n], refs[2 * n], refs[2 * n + 1]
    grads_ref, phi_all, psi_all = refs[2 * n + 2 :]
    half, emb = phi_all.shape
    batch = n_blk * slab
    last = n_blk - 2

    def sums(parts):
        blocks = list(parts[:n_blk])
        blocks[last] = (parts[last][...].astype(F32) + parts[n_blk][...].astype(F32)).astype(BF)
        return blocks

    def put_mine(off, value):
        phi_all[pl.ds(off, slab), :] = value[:, :emb]
        psi_all[pl.ds(off, slab), :] = value[:, emb:]

    def put_other(off, value):
        psi_all[pl.ds(half + off, slab), :] = value[:, emb:]

    place_blocks(pos_ref, sums(mine), put_mine, n_blk, n_rep, slab)
    place_blocks(pos_ref, sums(other), put_other, n_blk, n_rep, slab)
    diagonal = lax.broadcasted_iota(jnp.int32, (batch, batch), 0) == lax.broadcasted_iota(
        jnp.int32, (batch, batch), 1
    )
    for r in range(n_rep):
        own = slice(r * batch, (r + 1) * batch)
        ep_row = meta_row(pos_ref, meta_ref, 1, r, n_blk, slab)
        psi = dot(pick_ref[own, :], psi_all[...]).astype(BF)
        phi = phi_all[own, :]
        scores = lax.dot_general(phi, psi, (((1,), (1,)), ((), ())), preferred_element_type=F32)
        kept = (column(ep_row) != ep_row) | diagonal
        exponent = jnp.where(kept, jnp.exp(scores * scale), 0.0)
        totals = jnp.sum(exponent, axis=1, keepdims=True)
        power = jnp.where(totals > 1.0, 2.0**-32, 1.0)
        shares = (exponent * power) * (1.0 / (totals * power))
        delta = jnp.where(diagonal, shares - 1.0, shares).astype(BF)
        grads_ref[own, :emb] = (dot(delta, psi) * scale).astype(BF)
        grads_ref[own, emb:] = (dot(delta.T, phi) * scale).astype(BF)


def rows_grads(at, first_ref, second_ref, grads_ref, k, rows_ref, active, back):
    quarter, rows = active.shape
    emb = second_ref.shape[1]
    first_t = first_ref[:, pl.ds(at, quarter)].T
    second = second_ref[pl.ds(at, quarter), :]
    grad = grads_ref[:, k * emb : (k + 1) * emb]
    chunk = 512
    for c in range(0, rows, chunk):
        cols = slice(c, c + chunk)
        hidden = dot(first_t, rows_ref[cols, :].T)
        sig = sigmoid(hidden)
        act = hidden * sig
        active[:, cols] = act.astype(BF)
        slope = sig + act * (1.0 - sig)
        back[:, cols] = (dot(second, grad[cols, :].T) * slope).astype(BF)
    return dot(active[...], grad), dot(back[...], rows_ref[...])


def mine_kernel(pos_ref, sf, gf, ss, gs, grads_ref, rows_ref, goals_ref, *refs):
    outs, (active, back) = refs[:4], refs[4:]
    quarter = active.shape[0]
    at = pl.multiple_of(pos_ref[1] * quarter, quarter)
    outs[0][...], outs[1][...] = rows_grads(at, sf, ss, grads_ref, 0, rows_ref, active, back)
    outs[2][...], outs[3][...] = rows_grads(at, gf, gs, grads_ref, 1, goals_ref, active, back)


def other_kernel(k, n_put, pos_ref, first, second, grads_ref, rows_ref, sum_second, sum_first, *refs):
    done, (gf_ref, gs_ref), outs, (active, back), sems = (
        refs[:n_put],
        refs[n_put : n_put + 2],
        refs[n_put + 2 : 2 * n_put + 2],
        refs[2 * n_put + 2 : 2 * n_put + 4],
        refs[2 * n_put + 4 :],
    )
    copies = [put_half(pos_ref[1], x, o, sems[0].at[i]) for i, (x, o) in enumerate(zip(done, outs))]
    for c in copies:
        c.start()
    quarter = active.shape[0]
    at = pl.multiple_of(pos_ref[1] * quarter, quarter)
    grad_second, grad_first = rows_grads(at, first, second, grads_ref, k, rows_ref, active, back)
    gs_ref[...] = sum_second[...] + grad_second
    gf_ref[...] = (sum_first[...] + grad_first).T
    for c in copies:
        c.wait()


def put_half(side, half, out, sem):
    n, m = half.shape
    if out.shape[0] == n:
        to = out.at[:, pl.ds(pl.multiple_of(side * m, m), m)]
    else:
        to = out.at[pl.ds(pl.multiple_of(side * n, n), n), :]
    return pltpu.make_async_copy(half, to, sem)


def finish_kernel(old, new, pos_ref, *refs):
    halves = refs[: old + new]
    outs = refs[2 * old + new : 2 * (old + new) + old]
    sems = refs[-1]
    copies = [
        put_half(1 - pos_ref[1] if i < old else pos_ref[1], x, o, sems.at[i])
        for i, (x, o) in enumerate(zip(halves, outs))
    ]
    for c in copies:
        c.start()
    for c in copies:
        c.wait()


def finish(pos, halves, wholes, shapes):
    old, new = len(wholes), len(shapes)
    n = old + new
    return kernel(
        functools.partial(finish_kernel, old, new),
        "finish",
        [(w.shape, w.dtype) for w in wholes] + shapes,
        (*halves, *wholes),
        [pltpu.SemaphoreType.DMA((n,))],
        pos=pos,
        hbm=range(n, n + old),
        hbm_out=range(n),
        aliases={n + i: i for i in range(old)},
    )


def gathered(
    states, goal_distance, goal_row, episode, state_first, state_second, goal_first, goal_second
):
    rows_dev, width = states.shape
    n_blk, n_rep, n_sub = (lax.axis_size(a) for a in ("blk", "rep", "sub"))
    owners = n_blk * n_sub
    slab = rows_dev // n_rep
    rows_all = owners * rows_dev
    hid, emb = state_second.shape
    b, s = lax.axis_index("blk"), lax.axis_index("sub")
    pos = jnp.stack([b, s]).astype(jnp.int32)
    quarter = hid // n_sub

    def across(x, k):
        return lax.ppermute(x, "blk", [(i, i ^ k) for i in range(n_blk)])

    def swap(x, axis):
        return lax.ppermute(x, axis, [(0, 1), (1, 0)])

    def after(x, *first):
        return lax.optimization_barrier((x, *first))[0]

    got = {0: states, 3: across(states, 3), 2: across(states, 2)}
    weights = (state_first, goal_first, state_second, goal_second)
    part0 = forward(states, weights)
    there0 = swap(part0, "rep")
    got[1] = across(after(states, part0), 1)
    part3 = forward(got[3], weights)
    there3 = swap(part3, "rep")

    distance = after(goal_distance, part0)
    owner = (b * n_sub + s + distance[:, 0]) % owners
    goal = (((owner % n_sub) * n_rep + goal_row // slab) * n_blk + owner // n_sub) * slab + goal_row % slab
    meta = jnp.pad(jnp.stack([goal, episode]), ((0, 6), (0, 0)))
    meta = jnp.concatenate([meta, across(meta, 1)], axis=0)
    meta = jnp.concatenate([meta, across(meta, 2)], axis=0)
    meta_other = swap(meta, "sub")

    sums = {0: both(part0, there0)}
    sums[1] = across(sums[0], 1)
    part2 = forward(after(got[2], sums[0]), weights)
    there2 = swap(part2, "rep")
    sums[3] = both(part3, there3)
    embedded = [sums[0], sums[1], part2, sums[3], there2]

    side = ((rows_all // 2, width), BF)
    mine, other, goals_mine, goals_other, pick = kernel(
        functools.partial(arrange_kernel, n_blk, n_rep, slab),
        "arrange",
        [side, side, side, side, ((rows_all // 2, rows_all), BF)],
        (*(got[k] for k in range(n_blk)), *(swap(got[k], "sub") for k in range(n_blk)), meta, meta_other),
        [pltpu.VMEM((rows_all, width), BF), pltpu.VMEM((rows_all // 2, rows_all), BF)],
        pos=pos,
    )
    (grads_mine,) = kernel(
        functools.partial(contrast_kernel, n_blk, n_rep, slab, 4.0 / math.sqrt(emb)),
        "contrast",
        [((rows_all // 2, 2 * emb), BF)],
        (*embedded, *(swap(x, "sub") for x in embedded), meta, pick),
        [pltpu.VMEM((rows_all // 2, emb), BF), pltpu.VMEM((rows_all, emb), BF)],
        pos=pos,
        flops=rows_all * emb * (rows_all + 3 * n_blk * slab),
    )
    grads_other = swap(grads_mine, "sub")

    sf, gf, ss, gs = weights
    work = [pltpu.VMEM((quarter, rows_all // 2), BF), pltpu.VMEM((quarter, rows_all // 2), BF)]
    flops = 4 * rows_all * width * quarter
    sums_s2, sums_s1, sums_g2, sums_g1 = kernel(
        mine_kernel,
        "mine",
        [((quarter, emb), F32), ((quarter, width), F32)] * 2,
        (sf, gf, ss, gs, grads_mine, mine, goals_mine),
        work,
        pos=pos,
        flops=2 * flops,
    )
    halves = [((width, quarter), F32), ((quarter, emb), F32)]
    wholes = [((width, hid), F32), ((hid, emb), F32)]
    state_halves = kernel(
        functools.partial(other_kernel, 0, 0),
        "other_state",
        halves,
        (sf, ss, grads_other, other, sums_s2, sums_s1),
        work,
        pos=pos,
        flops=flops,
    )
    state_there = [swap(x, "sub") for x in state_halves]
    *goal_halves, out0, out1 = kernel(
        functools.partial(other_kernel, 1, 2),
        "other_goal",
        halves + wholes,
        (gf, gs, grads_other, goals_other, sums_g2, sums_g1, *state_halves),
        work + [pltpu.SemaphoreType.DMA((2,))],
        pos=pos,
        flops=flops,
        hbm_out=(2, 3),
    )
    goal_there = [swap(x, "sub") for x in goal_halves]
    out0, out1, out2, out3 = finish(pos, (*state_there, *goal_halves), (out0, out1), wholes)
    out2, out3 = finish(pos, goal_there, (out2, out3), [])
    return (out0, out1, out2, out3)


def silu_slope(hidden):
    sig = jax.nn.sigmoid(hidden)
    return sig * (1.0 + hidden * (1.0 - sig))


def encoder_grads(rows_in, hidden, active, second, emb_grad):
    grad_second = jnp.einsum("nh,ne->he", active, emb_grad, preferred_element_type=jnp.float32)
    back = jnp.einsum("ne,he->nh", emb_grad, second, preferred_element_type=jnp.float32)
    back_rows = (back * silu_slope(hidden)).astype(jnp.bfloat16)
    grad_first = jnp.einsum("ns,nh->sh", rows_in, back_rows, preferred_element_type=jnp.float32)
    return (grad_first, grad_second)


def exchanged(
    states, goal_distance, goal_row, episode, state_first, state_second, goal_first, goal_second
):
    rows_dev, width = states.shape
    owners = lax.axis_size(("blk", "sub"))
    position = lax.axis_index(("blk", "sub"))
    capacity = 4 * rows_dev // owners
    target = (position + goal_distance[:, 0]) % owners
    onehot = (target[:, None] == jnp.arange(owners, dtype=jnp.int32)[None, :]).astype(jnp.int32)
    slot_rank = jnp.sum((jnp.cumsum(onehot, axis=0) - onehot) * onehot, axis=1)
    requests = jnp.zeros((owners, capacity), jnp.int32).at[target, slot_rank].set(goal_row)
    wanted = lax.all_to_all(requests, ("blk", "sub"), split_axis=0, concat_axis=0, tiled=True)
    fetched = jnp.take(states, wanted.reshape(-1), axis=0).reshape(wanted.shape + (width,))
    replies = lax.all_to_all(fetched, ("blk", "sub"), split_axis=0, concat_axis=0, tiled=True)
    goal_states = jnp.take(
        replies.reshape(owners * capacity, width), target * capacity + slot_rank, axis=0
    )
    slab_rows = rows_dev // lax.axis_size("rep")
    state_hidden = jnp.dot(states, state_first, preferred_element_type=jnp.float32)
    state_active = jax.nn.silu(state_hidden).astype(jnp.bfloat16)
    goal_hidden = jnp.dot(goal_states, goal_first, preferred_element_type=jnp.float32)
    goal_active = jax.nn.silu(goal_hidden).astype(jnp.bfloat16)
    phi = lax.psum_scatter(
        jnp.dot(state_active, state_second, preferred_element_type=jnp.float32),
        "rep",
        scatter_dimension=0,
        tiled=True,
    ).astype(jnp.bfloat16)
    psi = lax.psum_scatter(
        jnp.dot(goal_active, goal_second, preferred_element_type=jnp.float32),
        "rep",
        scatter_dimension=0,
        tiled=True,
    ).astype(jnp.bfloat16)
    episode_own = lax.dynamic_slice_in_dim(episode, lax.axis_index("rep") * slab_rows, slab_rows, 0)
    psi_all, episode_all = (
        lax.all_gather(psi, "blk", axis=0, tiled=True),
        lax.all_gather(episode_own, "blk", axis=0, tiled=True),
    )
    batch_rows = psi_all.shape[0]
    logit_scale = 4.0 / math.sqrt(psi.shape[1])
    own_rows = lax.axis_index("blk") * slab_rows + jnp.arange(slab_rows, dtype=jnp.int32)
    columns = jnp.arange(batch_rows, dtype=jnp.int32)
    diagonal = own_rows[:, None] == columns[None, :]
    excluded = (episode_own[:, None] == episode_all[None, :]) & ~diagonal
    scores = jnp.einsum("ie,je->ij", phi, psi_all, preferred_element_type=jnp.float32) * logit_scale
    exponent = jnp.where(excluded, 0.0, jnp.exp(scores))
    totals = jnp.sum(exponent, axis=1)
    delta = (exponent / totals[:, None] - diagonal.astype(jnp.float32)).astype(jnp.bfloat16)
    phi_grad = (jnp.dot(delta, psi_all, preferred_element_type=jnp.float32) * logit_scale).astype(
        jnp.bfloat16
    )
    psi_grad = lax.psum_scatter(
        jnp.einsum("ij,ie->je", delta, phi, preferred_element_type=jnp.float32) * logit_scale,
        "blk",
        scatter_dimension=0,
        tiled=True,
    ).astype(jnp.bfloat16)
    phi_full, psi_full = (
        lax.all_gather(phi_grad, "rep", axis=0, tiled=True),
        lax.all_gather(psi_grad, "rep", axis=0, tiled=True),
    )
    state_parts = encoder_grads(states, state_hidden, state_active, state_second, phi_full)
    goal_parts = encoder_grads(goal_states, goal_hidden, goal_active, goal_second, psi_full)
    summed = lax.psum(
        (state_parts[0], state_parts[1], goal_parts[0], goal_parts[1]), ("blk", "sub")
    )
    return (summed[0], summed[1], summed[2], summed[3])


def solution(mesh):
    in_specs = (
        P(("grp", "blk", "sub"), None),
        P(("grp", "blk", "sub"), None),
        P(("grp", "blk", "sub")),
        P(("grp", "blk", "sub")),
        P(None, "rep"),
        P("rep", None),
        P(None, "rep"),
        P("rep", None),
    )
    out_specs = (P("grp", "rep"), P(("grp", "rep"), None), P("grp", "rep"), P(("grp", "rep"), None))
    shape = mesh.shape
    local = gathered if (shape["blk"], shape["rep"], shape["sub"]) == (4, 2, 2) else exchanged
    return jax.shard_map(local, mesh=mesh, in_specs=in_specs, out_specs=out_specs, check_vma=False)
```

```python
import functools
import math

import jax
import jax.numpy as jnp
from jax import lax
from jax.experimental import pallas as pl
from jax.experimental.pallas import tpu as pltpu
from jax.sharding import PartitionSpec as P

BF = jnp.bfloat16
F32 = jnp.float32
MIB = 1024 * 1024


def dot(a, b):
    return jnp.dot(a, b, preferred_element_type=F32)


def sigmoid(v):
    return 0.5 * jnp.tanh(0.5 * v) + 0.5


HBM = pl.BlockSpec(memory_space=pltpu.HBM)
VMEM = pl.BlockSpec(memory_space=pltpu.VMEM)
SMEM = pl.BlockSpec(memory_space=pltpu.SMEM)


def kernel(body, name, outs, args, scratch=(), limit=16, pos=None, flops=0, hbm=(), hbm_out=(), aliases={}):
    specs = [HBM if i in hbm else VMEM for i in range(len(args))]
    if pos is not None:
        args, specs = (pos, *args), [SMEM, *specs]
        aliases = {i + 1: o for i, o in aliases.items()}
    return pl.pallas_call(
        body,
        in_specs=specs,
        out_specs=[HBM if i in hbm_out else VMEM for i in range(len(outs))],
        out_shape=[jax.ShapeDtypeStruct(shape, dtype) for shape, dtype in outs],
        scratch_shapes=scratch,
        input_output_aliases=aliases,
        compiler_params=pltpu.CompilerParams(vmem_limit_bytes=limit * MIB),
        cost_estimate=pl.CostEstimate(flops=flops, bytes_accessed=0, transcendentals=0),
        name=name,
    )(*args)


def encode(x_ref, weights, out_ref, active):
    emb = weights[2].shape[1]
    for k in range(2):
        first, second = weights[k], weights[2 + k]
        for c in range(0, active.shape[1], 512):
            hidden = dot(x_ref[...], first[:, c : c + 512])
            active[:, c : c + 512] = (hidden * sigmoid(hidden)).astype(BF)
        out_ref[:, k * emb : (k + 1) * emb] = dot(active[...], second[...]).astype(BF)


def first_kernel(n_rep, n_blk, n_sub, pos_ref, x_hbm, *refs):
    weights, (distance_ref, place_ref, episode_ref) = refs[:4], refs[4:7]
    out_ref, pack_ref, held, active, x_ref, sems = refs[7], refs[8], refs[9:13], refs[13], refs[14], refs[15]
    copies = [pltpu.make_async_copy(x_hbm, x_ref, sems.at[4])]
    copies += [pltpu.make_async_copy(weights[i], held[i], sems.at[i]) for i in (0, 2, 1, 3)]
    for c in copies:
        c.start()
    rows = x_ref.shape[0]
    slab = rows // n_rep

    def bits(n):
        return n.bit_length() - 1

    owner = (pos_ref[0] * n_sub + pos_ref[1] + distance_ref[...]) & (n_blk * n_sub - 1)
    place = place_ref[...]
    batch = ((owner & (n_sub - 1)) << bits(n_rep)) + (place >> bits(slab))
    goal = (((batch << bits(n_blk)) + (owner >> bits(n_sub))) << bits(slab)) + (place & (slab - 1))
    digits = (goal >> 8, goal & 255, episode_ref[...])
    table = jnp.concatenate([d.astype(F32) for d in digits] + [jnp.zeros((13, rows), F32)], axis=0)
    pack_ref[rows:, :] = table.astype(BF)
    copies[0].wait()
    pack_ref[:rows, :] = x_ref[...]
    for c in copies[1:]:
        c.wait()
    encode(x_ref, held, out_ref, active)


def first_forward(pos, x, weights, meta, n_rep, n_blk, n_sub):
    rows, width = x.shape
    hid, emb = weights[2].shape
    part, pack, *held = kernel(
        functools.partial(first_kernel, n_rep, n_blk, n_sub),
        "forward",
        [((rows, 2 * emb), BF), ((rows + 16, width), BF)] + [(w.shape, w.dtype) for w in weights],
        (x, *weights, *meta),
        [pltpu.VMEM((rows, hid), BF), pltpu.VMEM(x.shape, x.dtype), pltpu.SemaphoreType.DMA((5,))],
        limit=49,
        pos=pos,
        hbm=range(5),
    )
    return part, pack, held


def forward_kernel(x_ref, *refs):
    encode(x_ref.at[: refs[4].shape[0]], refs[:4], refs[4], refs[5])


def forward(x, weights, rows):
    hid, emb = weights[2].shape
    return kernel(
        forward_kernel,
        "forward",
        [((rows, 2 * emb), BF)],
        (x, *weights),
        [pltpu.VMEM((rows, hid), BF)],
        limit=8,
    )[0]


def add_kernel(a_ref, b_ref, out_ref):
    out_ref[...] = (a_ref[...].astype(F32) + b_ref[...].astype(F32)).astype(BF)


def both(part, there):
    return kernel(add_kernel, "both", [(part.shape, BF)], (part, there), limit=4)[0]


def place_blocks(pos_ref, blocks, put, n_blk, n_rep, slab):
    for k, block in enumerate(blocks):
        at = jnp.bitwise_xor(pos_ref[0], k)
        for r in range(n_rep):
            off = (r * n_blk + at) * slab
            put(pl.multiple_of(off, slab), block[r * slab : (r + 1) * slab, :])


def column(row):
    return jnp.broadcast_to(row, (128, row.shape[1])).T[:, :1]


def arrange_kernel(n_blk, n_rep, slab, pos_ref, *refs):
    mine, other = refs[:n_blk], refs[n_blk : 2 * n_blk]
    rows_mine, rows_other, goals_mine, goals_other, pick_ref, ep_ref, both_sides, pick_other, meta = refs[2 * n_blk :]
    half = rows_mine.shape[0]
    rows = 2 * half
    batch = n_blk * slab
    for i, (blocks, to) in enumerate(((mine, rows_mine), (other, rows_other))):

        def put(off, value, i=i, to=to):
            to[pl.ds(off, slab), :] = value
            both_sides[pl.ds(i * half + off, slab), :] = value

        place_blocks(pos_ref, blocks, put, n_blk, n_rep, slab)
        for k, block in enumerate(blocks):
            at = jnp.bitwise_xor(pos_ref[0], k)
            for r in range(n_rep):
                off = pl.multiple_of((r * n_blk + at) * slab, slab)
                meta[i, :, pl.ds(off, slab)] = block[n_rep * slab :, r * slab : (r + 1) * slab].astype(F32)
    ep_ref[...] = meta[0, 2:3, :]
    for i, (pick, goals) in enumerate(((pick_ref, goals_mine), (pick_other, goals_other))):
        for r in range(n_rep):
            own = slice(r * batch, (r + 1) * batch)
            goal = column(meta[i, 0:1, own] * 256.0 + meta[i, 1:2, own]).astype(jnp.int32) + pos_ref[1] * half
            goal = jnp.where(goal >= rows, goal - rows, goal)
            pick[own, :] = jnp.where(
                goal == lax.broadcasted_iota(jnp.int32, (batch, rows), 1), 1.0, 0.0
            ).astype(BF)
        goals[...] = dot(pick[...], both_sides[...]).astype(BF)


def contrast_kernel(n_blk, n_rep, slab, scale, pos_ref, *refs):
    n = n_blk + 1
    mine, other, ep_ref, pick_ref = refs[:n], refs[n : 2 * n], refs[2 * n], refs[2 * n + 1]
    grads_ref, phi_all, psi_all = refs[2 * n + 2 :]
    half, emb = phi_all.shape
    batch = n_blk * slab
    last = n_blk - 2

    def sums(parts):
        blocks = list(parts[:n_blk])
        blocks[last] = (parts[last][...].astype(F32) + parts[n_blk][...].astype(F32)).astype(BF)
        return blocks

    def put_mine(off, value):
        phi_all[pl.ds(off, slab), :] = value[:, :emb]
        psi_all[pl.ds(off, slab), :] = value[:, emb:]

    def put_other(off, value):
        psi_all[pl.ds(half + off, slab), :] = value[:, emb:]

    place_blocks(pos_ref, sums(mine), put_mine, n_blk, n_rep, slab)
    place_blocks(pos_ref, sums(other), put_other, n_blk, n_rep, slab)
    diagonal = lax.broadcasted_iota(jnp.int32, (batch, batch), 0) == lax.broadcasted_iota(
        jnp.int32, (batch, batch), 1
    )
    for r in range(n_rep):
        own = slice(r * batch, (r + 1) * batch)
        ep_row = ep_ref[:, own]
        psi = dot(pick_ref[own, :], psi_all[...]).astype(BF)
        phi = phi_all[own, :]
        scores = lax.dot_general(phi, psi, (((1,), (1,)), ((), ())), preferred_element_type=F32)
        kept = (column(ep_row) != ep_row) | diagonal
        exponent = jnp.where(kept, jnp.exp(scores * scale), 0.0)
        totals = jnp.sum(exponent, axis=1, keepdims=True)
        power = jnp.where(totals > 1.0, 2.0**-32, 1.0)
        shares = (exponent * power) * (1.0 / (totals * power))
        delta = jnp.where(diagonal, shares - 1.0, shares).astype(BF)
        grads_ref[own, :emb] = (dot(delta, psi) * scale).astype(BF)
        grads_ref[own, emb:] = (dot(delta.T, phi) * scale).astype(BF)


def rows_grads(at, first_ref, second_ref, grads_ref, k, rows_ref, active, back):
    quarter, rows = active.shape
    emb = second_ref.shape[1]
    first_t = first_ref[:, pl.ds(at, quarter)].T
    second = second_ref[pl.ds(at, quarter), :]
    grad = grads_ref[:, k * emb : (k + 1) * emb]
    chunk = 512
    for c in range(0, rows, chunk):
        cols = slice(c, c + chunk)
        hidden = dot(first_t, rows_ref[cols, :].T)
        sig = sigmoid(hidden)
        act = hidden * sig
        active[:, cols] = act.astype(BF)
        slope = sig + act * (1.0 - sig)
        back[:, cols] = (dot(second, grad[cols, :].T) * slope).astype(BF)
    return dot(active[...], grad), dot(back[...], rows_ref[...])


def mine_kernel(pos_ref, sf, gf, ss, gs, grads_ref, rows_ref, goals_ref, *refs):
    outs, (active, back) = refs[:4], refs[4:]
    quarter = active.shape[0]
    at = pl.multiple_of(pos_ref[1] * quarter, quarter)
    outs[0][...], outs[1][...] = rows_grads(at, sf, ss, grads_ref, 0, rows_ref, active, back)
    outs[2][...], outs[3][...] = rows_grads(at, gf, gs, grads_ref, 1, goals_ref, active, back)


def other_kernel(k, n_put, pos_ref, first, second, grads_ref, rows_ref, sum_second, sum_first, *refs):
    done, (gf_ref, gs_ref), outs, (active, back), sems = (
        refs[:n_put],
        refs[n_put : n_put + 2],
        refs[n_put + 2 : 2 * n_put + 2],
        refs[2 * n_put + 2 : 2 * n_put + 4],
        refs[2 * n_put + 4 :],
    )
    copies = [put_half(pos_ref[1], x, o, sems[0].at[i]) for i, (x, o) in enumerate(zip(done, outs))]
    for c in copies:
        c.start()
    quarter = active.shape[0]
    at = pl.multiple_of(pos_ref[1] * quarter, quarter)
    grad_second, grad_first = rows_grads(at, first, second, grads_ref, k, rows_ref, active, back)
    gs_ref[...] = sum_second[...] + grad_second
    gf_ref[...] = (sum_first[...] + grad_first).T
    for c in copies:
        c.wait()


def put_half(side, half, out, sem):
    n, m = half.shape
    if out.shape[0] == n:
        to = out.at[:, pl.ds(pl.multiple_of(side * m, m), m)]
    else:
        to = out.at[pl.ds(pl.multiple_of(side * n, n), n), :]
    return pltpu.make_async_copy(half, to, sem)


def finish_kernel(old, new, pos_ref, *refs):
    halves = refs[: old + new]
    outs = refs[2 * old + new : 2 * (old + new) + old]
    sems = refs[-1]
    copies = [
        put_half(1 - pos_ref[1] if i < old else pos_ref[1], x, o, sems.at[i])
        for i, (x, o) in enumerate(zip(halves, outs))
    ]
    for c in copies:
        c.start()
    for c in copies:
        c.wait()


def finish(pos, halves, wholes, shapes):
    old, new = len(wholes), len(shapes)
    n = old + new
    return kernel(
        functools.partial(finish_kernel, old, new),
        "finish",
        [(w.shape, w.dtype) for w in wholes] + shapes,
        (*halves, *wholes),
        [pltpu.SemaphoreType.DMA((n,))],
        pos=pos,
        hbm=range(n, n + old),
        hbm_out=range(n),
        aliases={n + i: i for i in range(old)},
    )


def gathered(
    states, goal_distance, goal_row, episode, state_first, state_second, goal_first, goal_second
):
    rows_dev, width = states.shape
    n_blk, n_rep, n_sub = (lax.axis_size(a) for a in ("blk", "rep", "sub"))
    owners = n_blk * n_sub
    slab = rows_dev // n_rep
    rows_all = owners * rows_dev
    hid, emb = state_second.shape
    b, s = lax.axis_index("blk"), lax.axis_index("sub")
    pos = jnp.stack([b, s]).astype(jnp.int32)
    quarter = hid // n_sub

    def across(x, k):
        return lax.ppermute(x, "blk", [(i, i ^ k) for i in range(n_blk)])

    def swap(x, axis):
        return lax.ppermute(x, axis, [(0, 1), (1, 0)])

    def after(x, *first):
        return lax.optimization_barrier((x, *first))[0]

    weights = (state_first, goal_first, state_second, goal_second)
    meta = (goal_distance.reshape(1, rows_dev), goal_row.reshape(1, rows_dev), episode.reshape(1, rows_dev))
    part0, pack, held = first_forward(pos, states, weights, meta, n_rep, n_blk, n_sub)
    got = {k: across(pack, k) if k else pack for k in (0, 3, 2, 1)}
    there0 = swap(part0, "rep")
    part3 = forward(got[3], held, rows_dev)
    there3 = swap(part3, "rep")

    sums = {0: both(part0, there0)}
    sums[1] = across(sums[0], 1)
    part2 = forward(after(got[2], sums[0]), held, rows_dev)
    there2 = swap(part2, "rep")
    sums[3] = both(part3, there3)
    embedded = [sums[0], sums[1], part2, sums[3], there2]

    side = ((rows_all // 2, width), BF)
    mine, other, goals_mine, goals_other, pick, episodes = kernel(
        functools.partial(arrange_kernel, n_blk, n_rep, slab),
        "arrange",
        [side, side, side, side, ((rows_all // 2, rows_all), BF), ((1, rows_all // 2), F32)],
        (*(got[k] for k in range(n_blk)), *(swap(got[k], "sub") for k in range(n_blk))),
        [
            pltpu.VMEM((rows_all, width), BF),
            pltpu.VMEM((rows_all // 2, rows_all), BF),
            pltpu.VMEM((2, 16, rows_all // 2), F32),
        ],
        pos=pos,
    )
    (grads_mine,) = kernel(
        functools.partial(contrast_kernel, n_blk, n_rep, slab, 4.0 / math.sqrt(emb)),
        "contrast",
        [((rows_all // 2, 2 * emb), BF)],
        (*embedded, *(swap(x, "sub") for x in embedded), episodes, pick),
        [pltpu.VMEM((rows_all // 2, emb), BF), pltpu.VMEM((rows_all, emb), BF)],
        pos=pos,
    )
    grads_other = swap(grads_mine, "sub")

    sf, gf, ss, gs = weights
    work = [pltpu.VMEM((quarter, rows_all // 2), BF), pltpu.VMEM((quarter, rows_all // 2), BF)]
    flops = 4 * rows_all * width * quarter
    sums_s2, sums_s1, sums_g2, sums_g1 = kernel(
        mine_kernel,
        "mine",
        [((quarter, emb), F32), ((quarter, width), F32)] * 2,
        (sf, gf, ss, gs, grads_mine, mine, goals_mine),
        work,
        pos=pos,
        flops=2 * flops,
    )
    halves = [((width, quarter), F32), ((quarter, emb), F32)]
    wholes = [((width, hid), F32), ((hid, emb), F32)]
    state_halves = kernel(
        functools.partial(other_kernel, 0, 0),
        "other_state",
        halves,
        (sf, ss, grads_other, other, sums_s2, sums_s1),
        work,
        pos=pos,
        flops=flops,
    )
    state_there = [swap(x, "sub") for x in state_halves]
    *goal_halves, out0, out1 = kernel(
        functools.partial(other_kernel, 1, 2),
        "other_goal",
        halves + wholes,
        (gf, gs, grads_other, goals_other, sums_g2, sums_g1, *state_halves),
        work + [pltpu.SemaphoreType.DMA((2,))],
        pos=pos,
        flops=flops,
        hbm_out=(2, 3),
    )
    goal_there = [swap(x, "sub") for x in goal_halves]
    out0, out1, out2, out3 = finish(pos, (*state_there, *goal_halves), (out0, out1), wholes)
    out2, out3 = finish(pos, goal_there, (out2, out3), [])
    return (out0, out1, out2, out3)


def silu_slope(hidden):
    sig = jax.nn.sigmoid(hidden)
    return sig * (1.0 + hidden * (1.0 - sig))


def encoder_grads(rows_in, hidden, active, second, emb_grad):
    grad_second = jnp.einsum("nh,ne->he", active, emb_grad, preferred_element_type=jnp.float32)
    back = jnp.einsum("ne,he->nh", emb_grad, second, preferred_element_type=jnp.float32)
    back_rows = (back * silu_slope(hidden)).astype(jnp.bfloat16)
    grad_first = jnp.einsum("ns,nh->sh", rows_in, back_rows, preferred_element_type=jnp.float32)
    return (grad_first, grad_second)


def exchanged(
    states, goal_distance, goal_row, episode, state_first, state_second, goal_first, goal_second
):
    rows_dev, width = states.shape
    owners = lax.axis_size(("blk", "sub"))
    position = lax.axis_index(("blk", "sub"))
    capacity = 4 * rows_dev // owners
    target = (position + goal_distance[:, 0]) % owners
    onehot = (target[:, None] == jnp.arange(owners, dtype=jnp.int32)[None, :]).astype(jnp.int32)
    slot_rank = jnp.sum((jnp.cumsum(onehot, axis=0) - onehot) * onehot, axis=1)
    requests = jnp.zeros((owners, capacity), jnp.int32).at[target, slot_rank].set(goal_row)
    wanted = lax.all_to_all(requests, ("blk", "sub"), split_axis=0, concat_axis=0, tiled=True)
    fetched = jnp.take(states, wanted.reshape(-1), axis=0).reshape(wanted.shape + (width,))
    replies = lax.all_to_all(fetched, ("blk", "sub"), split_axis=0, concat_axis=0, tiled=True)
    goal_states = jnp.take(
        replies.reshape(owners * capacity, width), target * capacity + slot_rank, axis=0
    )
    slab_rows = rows_dev // lax.axis_size("rep")
    state_hidden = jnp.dot(states, state_first, preferred_element_type=jnp.float32)
    state_active = jax.nn.silu(state_hidden).astype(jnp.bfloat16)
    goal_hidden = jnp.dot(goal_states, goal_first, preferred_element_type=jnp.float32)
    goal_active = jax.nn.silu(goal_hidden).astype(jnp.bfloat16)
    phi = lax.psum_scatter(
        jnp.dot(state_active, state_second, preferred_element_type=jnp.float32),
        "rep",
        scatter_dimension=0,
        tiled=True,
    ).astype(jnp.bfloat16)
    psi = lax.psum_scatter(
        jnp.dot(goal_active, goal_second, preferred_element_type=jnp.float32),
        "rep",
        scatter_dimension=0,
        tiled=True,
    ).astype(jnp.bfloat16)
    episode_own = lax.dynamic_slice_in_dim(episode, lax.axis_index("rep") * slab_rows, slab_rows, 0)
    psi_all, episode_all = (
        lax.all_gather(psi, "blk", axis=0, tiled=True),
        lax.all_gather(episode_own, "blk", axis=0, tiled=True),
    )
    batch_rows = psi_all.shape[0]
    logit_scale = 4.0 / math.sqrt(psi.shape[1])
    own_rows = lax.axis_index("blk") * slab_rows + jnp.arange(slab_rows, dtype=jnp.int32)
    columns = jnp.arange(batch_rows, dtype=jnp.int32)
    diagonal = own_rows[:, None] == columns[None, :]
    excluded = (episode_own[:, None] == episode_all[None, :]) & ~diagonal
    scores = jnp.einsum("ie,je->ij", phi, psi_all, preferred_element_type=jnp.float32) * logit_scale
    exponent = jnp.where(excluded, 0.0, jnp.exp(scores))
    totals = jnp.sum(exponent, axis=1)
    delta = (exponent / totals[:, None] - diagonal.astype(jnp.float32)).astype(jnp.bfloat16)
    phi_grad = (jnp.dot(delta, psi_all, preferred_element_type=jnp.float32) * logit_scale).astype(
        jnp.bfloat16
    )
    psi_grad = lax.psum_scatter(
        jnp.einsum("ij,ie->je", delta, phi, preferred_element_type=jnp.float32) * logit_scale,
        "blk",
        scatter_dimension=0,
        tiled=True,
    ).astype(jnp.bfloat16)
    phi_full, psi_full = (
        lax.all_gather(phi_grad, "rep", axis=0, tiled=True),
        lax.all_gather(psi_grad, "rep", axis=0, tiled=True),
    )
    state_parts = encoder_grads(states, state_hidden, state_active, state_second, phi_full)
    goal_parts = encoder_grads(goal_states, goal_hidden, goal_active, goal_second, psi_full)
    summed = lax.psum(
        (state_parts[0], state_parts[1], goal_parts[0], goal_parts[1]), ("blk", "sub")
    )
    return (summed[0], summed[1], summed[2], summed[3])


def solution(mesh):
    in_specs = (
        P(("grp", "blk", "sub"), None),
        P(("grp", "blk", "sub"), None),
        P(("grp", "blk", "sub")),
        P(("grp", "blk", "sub")),
        P(None, "rep"),
        P("rep", None),
        P(None, "rep"),
        P("rep", None),
    )
    out_specs = (P("grp", "rep"), P(("grp", "rep"), None), P("grp", "rep"), P(("grp", "rep"), None))
    shape = mesh.shape
    local = gathered if (shape["blk"], shape["rep"], shape["sub"]) == (4, 2, 2) else exchanged
    return jax.shard_map(local, mesh=mesh, in_specs=in_specs, out_specs=out_specs, check_vma=False)
```

```python
import functools
import math

import jax
import jax.numpy as jnp
from jax import lax
from jax.experimental import pallas as pl
from jax.experimental.pallas import tpu as pltpu
from jax.sharding import PartitionSpec as P

BF = jnp.bfloat16
F32 = jnp.float32
MIB = 1024 * 1024


def dot(a, b):
    return jnp.dot(a, b, preferred_element_type=F32)


def sigmoid(v):
    return 0.5 * jnp.tanh(0.5 * v) + 0.5


HBM = pl.BlockSpec(memory_space=pltpu.HBM)
VMEM = pl.BlockSpec(memory_space=pltpu.VMEM)
SMEM = pl.BlockSpec(memory_space=pltpu.SMEM)


def kernel(body, name, outs, args, scratch=(), limit=16, pos=None, flops=0, hbm=(), hbm_out=(), aliases={}):
    specs = [HBM if i in hbm else VMEM for i in range(len(args))]
    if pos is not None:
        args, specs = (pos, *args), [SMEM, *specs]
        aliases = {i + 1: o for i, o in aliases.items()}
    return pl.pallas_call(
        body,
        in_specs=specs,
        out_specs=[HBM if i in hbm_out else VMEM for i in range(len(outs))],
        out_shape=[jax.ShapeDtypeStruct(shape, dtype) for shape, dtype in outs],
        scratch_shapes=scratch,
        input_output_aliases=aliases,
        compiler_params=pltpu.CompilerParams(vmem_limit_bytes=int(limit * MIB)),
        cost_estimate=pl.CostEstimate(flops=flops, bytes_accessed=0, transcendentals=0),
        name=name,
    )(*args)


def encode(x_ref, weights, out_ref, active, ready=lambda i: None):
    emb = weights[2].shape[1]
    for k in range(2):
        first, second = weights[k], weights[2 + k]
        ready(k)
        for c in range(0, active.shape[1], 512):
            hidden = dot(x_ref[...], first[:, c : c + 512])
            active[:, c : c + 512] = (hidden * sigmoid(hidden)).astype(BF)
        ready(2 + k)
        out_ref[:, k * emb : (k + 1) * emb] = dot(active[...], second[...]).astype(BF)


def first_kernel(pos_ref, x_ref, *refs):
    weights, out_ref, held, active, sems = refs[:4], refs[4], refs[5:9], refs[9], refs[10]
    copies = [pltpu.make_async_copy(weights[i], held[i], sems.at[i]) for i in range(4)]
    for i in (0, 2, 1, 3):
        copies[i].start()
    encode(x_ref, held, out_ref, active, lambda i: copies[i].wait())


def first_forward(pos, x, weights):
    rows, width = x.shape
    hid, emb = weights[2].shape
    part, *held = kernel(
        first_kernel,
        "forward",
        [((rows, 2 * emb), BF)] + [(w.shape, w.dtype) for w in weights],
        (x, *weights),
        [pltpu.VMEM((rows, hid), BF), pltpu.SemaphoreType.DMA((4,))],
        limit=49,
        pos=pos,
        hbm=range(1, 5),
    )
    return part, held


def pack_kernel(n_rep, n_blk, n_sub, pos_ref, x_ref, distance_ref, place_ref, episode_ref, pack_ref, meta_ref):
    rows = x_ref.shape[0]
    slab = rows // n_rep

    def bits(n):
        return n.bit_length() - 1

    owner = (pos_ref[0] * n_sub + pos_ref[1] + distance_ref[...]) & (n_blk * n_sub - 1)
    place = place_ref[...]
    batch = ((owner & (n_sub - 1)) << bits(n_rep)) + (place >> bits(slab))
    goal = (((batch << bits(n_blk)) + (owner >> bits(n_sub))) << bits(slab)) + (place & (slab - 1))
    digits = (goal >> 8, goal & 255, episode_ref[...])
    table = jnp.concatenate([d.astype(F32) for d in digits] + [jnp.zeros((13, rows), F32)], axis=0).astype(BF)
    pack_ref[:rows, :] = x_ref[...]
    pack_ref[rows:, :] = table
    meta_ref[...] = table


def forward_kernel(x_ref, *refs):
    encode(x_ref.at[: refs[4].shape[0]], refs[:4], refs[4], refs[5])


def forward(x, weights, rows):
    hid, emb = weights[2].shape
    return kernel(
        forward_kernel,
        "forward",
        [((rows, 2 * emb), BF)],
        (x, *weights),
        [pltpu.VMEM((rows, hid), BF)],
        limit=8,
    )[0]


def add_kernel(a_ref, b_ref, out_ref):
    out_ref[...] = (a_ref[...].astype(F32) + b_ref[...].astype(F32)).astype(BF)


def both(part, there):
    return kernel(add_kernel, "both", [(part.shape, BF)], (part, there), limit=4)[0]


def place_blocks(pos_ref, blocks, put, n_blk, n_rep, slab):
    for k, block in enumerate(blocks):
        at = jnp.bitwise_xor(pos_ref[0], k)
        for r in range(n_rep):
            off = (r * n_blk + at) * slab
            put(pl.multiple_of(off, slab), block[r * slab : (r + 1) * slab, :])


def column(row):
    return jnp.broadcast_to(row, (128, row.shape[1])).T[:, :1]


def arrange_kernel(n_blk, n_rep, slab, pos_ref, *refs):
    n = n_blk + 1
    mine, other = refs[:n], refs[n : 2 * n]
    rows_mine, rows_other, goals_mine, goals_other, pick_ref, ep_ref, both_sides, pick_other, meta = refs[2 * n :]
    half = rows_mine.shape[0]
    rows = 2 * half
    batch = n_blk * slab
    for i, (blocks, to) in enumerate(((mine, rows_mine), (other, rows_other))):

        def put(off, value, i=i, to=to):
            to[pl.ds(off, slab), :] = value
            both_sides[pl.ds(i * half + off, slab), :] = value

        place_blocks(pos_ref, blocks[:n_blk], put, n_blk, n_rep, slab)
        tables = [block.at[n_rep * slab :] for block in blocks[: n_blk - 1]] + [blocks[n_blk]]
        for k, table in enumerate(tables):
            at = jnp.bitwise_xor(pos_ref[0], k)
            for r in range(n_rep):
                off = pl.multiple_of((r * n_blk + at) * slab, slab)
                meta[i, :, pl.ds(off, slab)] = table[:, r * slab : (r + 1) * slab].astype(F32)
    ep_ref[...] = meta[0, 2:3, :]
    for i, (pick, goals) in enumerate(((pick_ref, goals_mine), (pick_other, goals_other))):
        for r in range(n_rep):
            own = slice(r * batch, (r + 1) * batch)
            goal = column(meta[i, 0:1, own] * 256.0 + meta[i, 1:2, own]).astype(jnp.int32) + pos_ref[1] * half
            goal = jnp.where(goal >= rows, goal - rows, goal)
            pick[own, :] = jnp.where(
                goal == lax.broadcasted_iota(jnp.int32, (batch, rows), 1), 1.0, 0.0
            ).astype(BF)
        goals[...] = dot(pick[...], both_sides[...]).astype(BF)


def contrast_kernel(n_blk, n_rep, slab, scale, pos_ref, *refs):
    n = n_blk + 1
    mine, other, ep_ref, pick_ref = refs[:n], refs[n : 2 * n], refs[2 * n], refs[2 * n + 1]
    grads_ref, phi_all, psi_all = refs[2 * n + 2 :]
    half, emb = phi_all.shape
    batch = n_blk * slab
    last = n_blk - 2

    def sums(parts):
        blocks = list(parts[:n_blk])
        blocks[last] = (parts[last][...].astype(F32) + parts[n_blk][...].astype(F32)).astype(BF)
        return blocks

    def put_mine(off, value):
        phi_all[pl.ds(off, slab), :] = value[:, :emb]
        psi_all[pl.ds(off, slab), :] = value[:, emb:]

    def put_other(off, value):
        psi_all[pl.ds(half + off, slab), :] = value[:, emb:]

    place_blocks(pos_ref, sums(mine), put_mine, n_blk, n_rep, slab)
    place_blocks(pos_ref, sums(other), put_other, n_blk, n_rep, slab)
    diagonal = lax.broadcasted_iota(jnp.int32, (batch, batch), 0) == lax.broadcasted_iota(
        jnp.int32, (batch, batch), 1
    )
    for r in range(n_rep):
        own = slice(r * batch, (r + 1) * batch)
        ep_row = ep_ref[:, own]
        psi = dot(pick_ref[own, :], psi_all[...]).astype(BF)
        phi = phi_all[own, :]
        scores = lax.dot_general(phi, psi, (((1,), (1,)), ((), ())), preferred_element_type=F32)
        kept = (column(ep_row) != ep_row) | diagonal
        exponent = jnp.where(kept, jnp.exp(scores * scale), 0.0)
        totals = jnp.sum(exponent, axis=1, keepdims=True)
        power = jnp.where(totals > 1.0, 2.0**-32, 1.0)
        shares = (exponent * power) * (1.0 / (totals * power))
        delta = jnp.where(diagonal, shares - 1.0, shares).astype(BF)
        grads_ref[own, :emb] = (dot(delta, psi) * scale).astype(BF)
        grads_ref[own, emb:] = (dot(delta.T, phi) * scale).astype(BF)


def rows_grads(at, first_ref, second_ref, grads_ref, k, rows_ref, active, back):
    quarter, rows = active.shape
    emb = second_ref.shape[1]
    first_t = first_ref[:, pl.ds(at, quarter)].T
    second = second_ref[pl.ds(at, quarter), :]
    grad = grads_ref[:, k * emb : (k + 1) * emb]
    chunk = 512
    for c in range(0, rows, chunk):
        cols = slice(c, c + chunk)
        hidden = dot(first_t, rows_ref[cols, :].T)
        sig = sigmoid(hidden)
        act = hidden * sig
        active[:, cols] = act.astype(BF)
        slope = sig + act * (1.0 - sig)
        back[:, cols] = (dot(second, grad[cols, :].T) * slope).astype(BF)
    return dot(active[...], grad), dot(back[...], rows_ref[...])


def mine_kernel(pos_ref, sf, gf, ss, gs, grads_ref, rows_ref, goals_ref, *refs):
    outs, (active, back) = refs[:4], refs[4:]
    quarter = active.shape[0]
    at = pl.multiple_of(pos_ref[1] * quarter, quarter)
    outs[0][...], outs[1][...] = rows_grads(at, sf, ss, grads_ref, 0, rows_ref, active, back)
    outs[2][...], outs[3][...] = rows_grads(at, gf, gs, grads_ref, 1, goals_ref, active, back)


def other_kernel(k, n_put, pos_ref, first, second, grads_ref, rows_ref, sum_second, sum_first, *refs):
    done, (gf_ref, gs_ref), outs, (active, back), sems = (
        refs[:n_put],
        refs[n_put : n_put + 2],
        refs[n_put + 2 : 2 * n_put + 2],
        refs[2 * n_put + 2 : 2 * n_put + 4],
        refs[2 * n_put + 4 :],
    )
    copies = [put_half(pos_ref[1], x, o, sems[0].at[i]) for i, (x, o) in enumerate(zip(done, outs))]
    for c in copies:
        c.start()
    quarter = active.shape[0]
    at = pl.multiple_of(pos_ref[1] * quarter, quarter)
    grad_second, grad_first = rows_grads(at, first, second, grads_ref, k, rows_ref, active, back)
    gs_ref[...] = sum_second[...] + grad_second
    gf_ref[...] = (sum_first[...] + grad_first).T
    for c in copies:
        c.wait()


def put_half(side, half, out, sem):
    n, m = half.shape
    if out.shape[0] == n:
        to = out.at[:, pl.ds(pl.multiple_of(side * m, m), m)]
    else:
        to = out.at[pl.ds(pl.multiple_of(side * n, n), n), :]
    return pltpu.make_async_copy(half, to, sem)


def finish_kernel(old, new, pos_ref, *refs):
    halves = refs[: old + new]
    outs = refs[2 * old + new : 2 * (old + new) + old]
    sems = refs[-1]
    copies = [
        put_half(1 - pos_ref[1] if i < old else pos_ref[1], x, o, sems.at[i])
        for i, (x, o) in enumerate(zip(halves, outs))
    ]
    for c in copies:
        c.start()
    for c in copies:
        c.wait()


def finish(pos, halves, wholes, shapes):
    old, new = len(wholes), len(shapes)
    n = old + new
    return kernel(
        functools.partial(finish_kernel, old, new),
        "finish",
        [(w.shape, w.dtype) for w in wholes] + shapes,
        (*halves, *wholes),
        [pltpu.SemaphoreType.DMA((n,))],
        pos=pos,
        hbm=range(n, n + old),
        hbm_out=range(n),
        aliases={n + i: i for i in range(old)},
    )


def gathered(
    states, goal_distance, goal_row, episode, state_first, state_second, goal_first, goal_second
):
    rows_dev, width = states.shape
    n_blk, n_rep, n_sub = (lax.axis_size(a) for a in ("blk", "rep", "sub"))
    owners = n_blk * n_sub
    slab = rows_dev // n_rep
    rows_all = owners * rows_dev
    hid, emb = state_second.shape
    b, s = lax.axis_index("blk"), lax.axis_index("sub")
    pos = jnp.stack([b, s]).astype(jnp.int32)
    quarter = hid // n_sub

    def across(x, k):
        return lax.ppermute(x, "blk", [(i, i ^ k) for i in range(n_blk)])

    def swap(x, axis):
        return lax.ppermute(x, axis, [(0, 1), (1, 0)])

    def after(x, *first):
        return lax.optimization_barrier((x, *first))[0]

    weights = (state_first, goal_first, state_second, goal_second)
    meta = (goal_distance.reshape(1, rows_dev), goal_row.reshape(1, rows_dev), episode.reshape(1, rows_dev))
    got = {3: across(states, 3)}
    part0, held = first_forward(pos, states, weights)
    there0 = swap(part0, "rep")
    pack, table = kernel(
        functools.partial(pack_kernel, n_rep, n_blk, n_sub),
        "pack",
        [((rows_dev + 16, width), BF), ((16, width), BF)],
        (after(states, part0), *meta),
        pos=pos,
        limit=4,
    )
    got[0], got[1] = pack, across(pack, 1)
    got[2] = across(after(pack, got[3]), 2)
    got[4] = across(after(table, got[3]), 3)
    part3 = forward(got[3], held, rows_dev)
    there3 = swap(part3, "rep")

    sums = {0: both(part0, there0)}
    sums[1] = across(sums[0], 1)
    part2 = forward(after(got[2], sums[0]), held, rows_dev)
    there2 = swap(part2, "rep")
    sums[3] = both(part3, there3)

    side = ((rows_all // 2, width), BF)
    mine, other, goals_mine, goals_other, pick, episodes = kernel(
        functools.partial(arrange_kernel, n_blk, n_rep, slab),
        "arrange",
        [side, side, side, side, ((rows_all // 2, rows_all), BF), ((1, rows_all // 2), F32)],
        (*(got[k] for k in range(n_blk + 1)), *(swap(got[k], "sub") for k in range(n_blk + 1))),
        [
            pltpu.VMEM((rows_all, width), BF),
            pltpu.VMEM((rows_all // 2, rows_all), BF),
            pltpu.VMEM((2, 16, rows_all // 2), F32),
        ],
        pos=pos,
    )
    embedded = [sums[0], sums[1], part2, sums[3], after(there2, pick)]
    (grads_mine,) = kernel(
        functools.partial(contrast_kernel, n_blk, n_rep, slab, 4.0 / math.sqrt(emb)),
        "contrast",
        [((rows_all // 2, 2 * emb), BF)],
        (*embedded, *(swap(x, "sub") for x in embedded), episodes, pick),
        [pltpu.VMEM((rows_all // 2, emb), BF), pltpu.VMEM((rows_all, emb), BF)],
        pos=pos,
    )
    grads_other = swap(grads_mine, "sub")

    sf, gf, ss, gs = weights
    work = [pltpu.VMEM((quarter, rows_all // 2), BF), pltpu.VMEM((quarter, rows_all // 2), BF)]
    flops = 4 * rows_all * width * quarter
    sums_s2, sums_s1, sums_g2, sums_g1 = kernel(
        mine_kernel,
        "mine",
        [((quarter, emb), F32), ((quarter, width), F32)] * 2,
        (sf, gf, ss, gs, grads_mine, mine, goals_mine),
        work,
        pos=pos,
        flops=2 * flops,
    )
    halves = [((width, quarter), F32), ((quarter, emb), F32)]
    wholes = [((width, hid), F32), ((hid, emb), F32)]
    state_halves = kernel(
        functools.partial(other_kernel, 0, 0),
        "other_state",
        halves,
        (sf, ss, grads_other, other, sums_s2, sums_s1),
        work,
        pos=pos,
        flops=flops,
    )
    state_there = [swap(x, "sub") for x in state_halves]
    *goal_halves, out0, out1 = kernel(
        functools.partial(other_kernel, 1, 2),
        "other_goal",
        halves + wholes,
        (gf, gs, grads_other, goals_other, sums_g2, sums_g1, *state_halves),
        work + [pltpu.SemaphoreType.DMA((2,))],
        pos=pos,
        flops=flops,
        hbm_out=(2, 3),
    )
    goal_there = [swap(x, "sub") for x in goal_halves]
    out0, out1, out2, out3 = finish(pos, (*state_there, *goal_halves), (out0, out1), wholes)
    out2, out3 = finish(pos, goal_there, (out2, out3), [])
    return (out0, out1, out2, out3)


def silu_slope(hidden):
    sig = jax.nn.sigmoid(hidden)
    return sig * (1.0 + hidden * (1.0 - sig))


def encoder_grads(rows_in, hidden, active, second, emb_grad):
    grad_second = jnp.einsum("nh,ne->he", active, emb_grad, preferred_element_type=jnp.float32)
    back = jnp.einsum("ne,he->nh", emb_grad, second, preferred_element_type=jnp.float32)
    back_rows = (back * silu_slope(hidden)).astype(jnp.bfloat16)
    grad_first = jnp.einsum("ns,nh->sh", rows_in, back_rows, preferred_element_type=jnp.float32)
    return (grad_first, grad_second)


def exchanged(
    states, goal_distance, goal_row, episode, state_first, state_second, goal_first, goal_second
):
    rows_dev, width = states.shape
    owners = lax.axis_size(("blk", "sub"))
    position = lax.axis_index(("blk", "sub"))
    capacity = 4 * rows_dev // owners
    target = (position + goal_distance[:, 0]) % owners
    onehot = (target[:, None] == jnp.arange(owners, dtype=jnp.int32)[None, :]).astype(jnp.int32)
    slot_rank = jnp.sum((jnp.cumsum(onehot, axis=0) - onehot) * onehot, axis=1)
    requests = jnp.zeros((owners, capacity), jnp.int32).at[target, slot_rank].set(goal_row)
    wanted = lax.all_to_all(requests, ("blk", "sub"), split_axis=0, concat_axis=0, tiled=True)
    fetched = jnp.take(states, wanted.reshape(-1), axis=0).reshape(wanted.shape + (width,))
    replies = lax.all_to_all(fetched, ("blk", "sub"), split_axis=0, concat_axis=0, tiled=True)
    goal_states = jnp.take(
        replies.reshape(owners * capacity, width), target * capacity + slot_rank, axis=0
    )
    slab_rows = rows_dev // lax.axis_size("rep")
    state_hidden = jnp.dot(states, state_first, preferred_element_type=jnp.float32)
    state_active = jax.nn.silu(state_hidden).astype(jnp.bfloat16)
    goal_hidden = jnp.dot(goal_states, goal_first, preferred_element_type=jnp.float32)
    goal_active = jax.nn.silu(goal_hidden).astype(jnp.bfloat16)
    phi = lax.psum_scatter(
        jnp.dot(state_active, state_second, preferred_element_type=jnp.float32),
        "rep",
        scatter_dimension=0,
        tiled=True,
    ).astype(jnp.bfloat16)
    psi = lax.psum_scatter(
        jnp.dot(goal_active, goal_second, preferred_element_type=jnp.float32),
        "rep",
        scatter_dimension=0,
        tiled=True,
    ).astype(jnp.bfloat16)
    episode_own = lax.dynamic_slice_in_dim(episode, lax.axis_index("rep") * slab_rows, slab_rows, 0)
    psi_all, episode_all = (
        lax.all_gather(psi, "blk", axis=0, tiled=True),
        lax.all_gather(episode_own, "blk", axis=0, tiled=True),
    )
    batch_rows = psi_all.shape[0]
    logit_scale = 4.0 / math.sqrt(psi.shape[1])
    own_rows = lax.axis_index("blk") * slab_rows + jnp.arange(slab_rows, dtype=jnp.int32)
    columns = jnp.arange(batch_rows, dtype=jnp.int32)
    diagonal = own_rows[:, None] == columns[None, :]
    excluded = (episode_own[:, None] == episode_all[None, :]) & ~diagonal
    scores = jnp.einsum("ie,je->ij", phi, psi_all, preferred_element_type=jnp.float32) * logit_scale
    exponent = jnp.where(excluded, 0.0, jnp.exp(scores))
    totals = jnp.sum(exponent, axis=1)
    delta = (exponent / totals[:, None] - diagonal.astype(jnp.float32)).astype(jnp.bfloat16)
    phi_grad = (jnp.dot(delta, psi_all, preferred_element_type=jnp.float32) * logit_scale).astype(
        jnp.bfloat16
    )
    psi_grad = lax.psum_scatter(
        jnp.einsum("ij,ie->je", delta, phi, preferred_element_type=jnp.float32) * logit_scale,
        "blk",
        scatter_dimension=0,
        tiled=True,
    ).astype(jnp.bfloat16)
    phi_full, psi_full = (
        lax.all_gather(phi_grad, "rep", axis=0, tiled=True),
        lax.all_gather(psi_grad, "rep", axis=0, tiled=True),
    )
    state_parts = encoder_grads(states, state_hidden, state_active, state_second, phi_full)
    goal_parts = encoder_grads(goal_states, goal_hidden, goal_active, goal_second, psi_full)
    summed = lax.psum(
        (state_parts[0], state_parts[1], goal_parts[0], goal_parts[1]), ("blk", "sub")
    )
    return (summed[0], summed[1], summed[2], summed[3])


def solution(mesh):
    in_specs = (
        P(("grp", "blk", "sub"), None),
        P(("grp", "blk", "sub"), None),
        P(("grp", "blk", "sub")),
        P(("grp", "blk", "sub")),
        P(None, "rep"),
        P("rep", None),
        P(None, "rep"),
        P("rep", None),
    )
    out_specs = (P("grp", "rep"), P(("grp", "rep"), None), P("grp", "rep"), P(("grp", "rep"), None))
    shape = mesh.shape
    local = gathered if (shape["blk"], shape["rep"], shape["sub"]) == (4, 2, 2) else exchanged
    return jax.shard_map(local, mesh=mesh, in_specs=in_specs, out_specs=out_specs, check_vma=False)
```

```python
import functools
import math

import jax
import jax.numpy as jnp
from jax import lax
from jax.experimental import pallas as pl
from jax.experimental.pallas import tpu as pltpu
from jax.sharding import PartitionSpec as P

BF = jnp.bfloat16
F32 = jnp.float32
MIB = 1024 * 1024


def dot(a, b):
    return jnp.dot(a, b, preferred_element_type=F32)


def sigmoid(v):
    return 0.5 * jnp.tanh(0.5 * v) + 0.5


HBM = pl.BlockSpec(memory_space=pltpu.HBM)
VMEM = pl.BlockSpec(memory_space=pltpu.VMEM)
SMEM = pl.BlockSpec(memory_space=pltpu.SMEM)


def kernel(body, name, outs, args, scratch=(), limit=16, pos=None, flops=0, hbm=(), hbm_out=(), aliases={}):
    specs = [HBM if i in hbm else VMEM for i in range(len(args))]
    if pos is not None:
        args, specs = (pos, *args), [SMEM, *specs]
        aliases = {i + 1: o for i, o in aliases.items()}
    return pl.pallas_call(
        body,
        in_specs=specs,
        out_specs=[HBM if i in hbm_out else VMEM for i in range(len(outs))],
        out_shape=[jax.ShapeDtypeStruct(shape, dtype) for shape, dtype in outs],
        scratch_shapes=scratch,
        input_output_aliases=aliases,
        compiler_params=pltpu.CompilerParams(vmem_limit_bytes=int(limit * MIB)),
        cost_estimate=pl.CostEstimate(flops=flops, bytes_accessed=0, transcendentals=0),
        name=name,
    )(*args)


def encode(x_ref, weights, out_ref, active, ready=lambda i: None):
    emb = weights[2].shape[1]
    for k in range(2):
        first, second = weights[k], weights[2 + k]
        ready(k)
        for c in range(0, active.shape[1], 512):
            hidden = dot(x_ref[...], first[:, c : c + 512])
            active[:, c : c + 512] = (hidden * sigmoid(hidden)).astype(BF)
        ready(2 + k)
        out_ref[:, k * emb : (k + 1) * emb] = dot(active[...], second[...]).astype(BF)


def first_kernel(pos_ref, x_ref, *refs):
    weights, out_ref, held, active, sems = refs[:4], refs[4], refs[5:9], refs[9], refs[10]
    copies = [pltpu.make_async_copy(weights[i], held[i], sems.at[i]) for i in range(4)]
    for i in (0, 2, 1, 3):
        copies[i].start()
    encode(x_ref, held, out_ref, active, lambda i: copies[i].wait())


def first_forward(pos, x, weights):
    rows, width = x.shape
    hid, emb = weights[2].shape
    part, *held = kernel(
        first_kernel,
        "forward",
        [((rows, 2 * emb), BF)] + [(w.shape, w.dtype) for w in weights],
        (x, *weights),
        [pltpu.VMEM((rows, hid), BF), pltpu.SemaphoreType.DMA((4,))],
        limit=49,
        pos=pos,
        hbm=range(1, 5),
    )
    return part, held


def pack_kernel(n_rep, n_blk, n_sub, pos_ref, x_ref, distance_ref, place_ref, episode_ref, pack_ref, meta_ref):
    rows = x_ref.shape[0]
    slab = rows // n_rep

    def bits(n):
        return n.bit_length() - 1

    owner = (pos_ref[0] * n_sub + pos_ref[1] + distance_ref[...]) & (n_blk * n_sub - 1)
    place = place_ref[...]
    batch = ((owner & (n_sub - 1)) << bits(n_rep)) + (place >> bits(slab))
    goal = (((batch << bits(n_blk)) + (owner >> bits(n_sub))) << bits(slab)) + (place & (slab - 1))
    digits = (goal >> 8, goal & 255, episode_ref[...])
    table = jnp.concatenate([d.astype(F32) for d in digits] + [jnp.zeros((13, rows), F32)], axis=0).astype(BF)
    pack_ref[:rows, :] = x_ref[...]
    pack_ref[rows:, :] = table
    meta_ref[...] = table


def forward_kernel(x_ref, *refs):
    encode(x_ref.at[: refs[4].shape[0]], refs[:4], refs[4], refs[5])


def forward(x, weights, rows):
    hid, emb = weights[2].shape
    return kernel(
        forward_kernel,
        "forward",
        [((rows, 2 * emb), BF)],
        (x, *weights),
        [pltpu.VMEM((rows, hid), BF)],
        limit=8,
    )[0]


def add_kernel(a_ref, b_ref, out_ref):
    out_ref[...] = (a_ref[...].astype(F32) + b_ref[...].astype(F32)).astype(BF)


def both(part, there):
    return kernel(add_kernel, "both", [(part.shape, BF)], (part, there), limit=4)[0]


def place_blocks(pos_ref, blocks, put, n_blk, n_rep, slab):
    for k, block in enumerate(blocks):
        at = jnp.bitwise_xor(pos_ref[0], k)
        for r in range(n_rep):
            off = (r * n_blk + at) * slab
            put(pl.multiple_of(off, slab), block[r * slab : (r + 1) * slab, :])


def column(row):
    return jnp.broadcast_to(row, (128, row.shape[1])).T[:, :1]


def arrange_kernel(n_blk, n_rep, slab, pos_ref, *refs):
    n = n_blk + 1
    mine, other = refs[:n], refs[n : 2 * n - 1]
    rows_mine, rows_other, goals_ref, pick_ref, ep_ref, both_sides, meta = refs[2 * n - 1 :]
    half = rows_mine.shape[0]
    rows = 2 * half
    batch = n_blk * slab
    for i, (blocks, to) in enumerate(((mine, rows_mine), (other, rows_other))):

        def put(off, value, i=i, to=to):
            to[pl.ds(off, slab), :] = value
            both_sides[pl.ds(i * half + off, slab), :] = value

        place_blocks(pos_ref, blocks[:n_blk], put, n_blk, n_rep, slab)
    tables = [block.at[n_rep * slab :] for block in mine[: n_blk - 1]] + [mine[n_blk]]
    for k, table in enumerate(tables):
        at = jnp.bitwise_xor(pos_ref[0], k)
        for r in range(n_rep):
            off = pl.multiple_of((r * n_blk + at) * slab, slab)
            meta[:, pl.ds(off, slab)] = table[:, r * slab : (r + 1) * slab].astype(F32)
    ep_ref[...] = meta[2:3, :]
    for r in range(n_rep):
        own = slice(r * batch, (r + 1) * batch)
        goal = column(meta[0:1, own] * 256.0 + meta[1:2, own]).astype(jnp.int32) + pos_ref[1] * half
        goal = jnp.where(goal >= rows, goal - rows, goal)
        pick_ref[own, :] = jnp.where(
            goal == lax.broadcasted_iota(jnp.int32, (batch, rows), 1), 1.0, 0.0
        ).astype(BF)
    goals_ref[...] = dot(pick_ref[...], both_sides[...]).astype(BF)


def contrast_kernel(n_blk, n_rep, slab, scale, pos_ref, *refs):
    n = n_blk + 1
    mine, other, ep_ref, pick_ref = refs[:n], refs[n : 2 * n], refs[2 * n], refs[2 * n + 1]
    grads_ref, phi_all, psi_all = refs[2 * n + 2 :]
    half, emb = phi_all.shape
    batch = n_blk * slab
    last = n_blk - 2

    def sums(parts):
        blocks = list(parts[:n_blk])
        blocks[last] = (parts[last][...].astype(F32) + parts[n_blk][...].astype(F32)).astype(BF)
        return blocks

    def put_mine(off, value):
        phi_all[pl.ds(off, slab), :] = value[:, :emb]
        psi_all[pl.ds(off, slab), :] = value[:, emb:]

    def put_other(off, value):
        psi_all[pl.ds(half + off, slab), :] = value[:, emb:]

    place_blocks(pos_ref, sums(mine), put_mine, n_blk, n_rep, slab)
    place_blocks(pos_ref, sums(other), put_other, n_blk, n_rep, slab)
    diagonal = lax.broadcasted_iota(jnp.int32, (batch, batch), 0) == lax.broadcasted_iota(
        jnp.int32, (batch, batch), 1
    )
    for r in range(n_rep):
        own = slice(r * batch, (r + 1) * batch)
        ep_row = ep_ref[:, own]
        psi = dot(pick_ref[own, :], psi_all[...]).astype(BF)
        phi = phi_all[own, :]
        scores = lax.dot_general(phi, psi, (((1,), (1,)), ((), ())), preferred_element_type=F32)
        kept = (column(ep_row) != ep_row) | diagonal
        exponent = jnp.where(kept, jnp.exp(scores * scale), 0.0)
        totals = jnp.sum(exponent, axis=1, keepdims=True)
        power = jnp.where(totals > 1.0, 2.0**-32, 1.0)
        shares = (exponent * power) * (1.0 / (totals * power))
        delta = jnp.where(diagonal, shares - 1.0, shares).astype(BF)
        grads_ref[own, :emb] = (dot(delta, psi) * scale).astype(BF)
        grads_ref[own, emb:] = (dot(delta.T, phi) * scale).astype(BF)


def rows_grads(at, first_ref, second_ref, grads_ref, k, rows_ref, active, back):
    quarter, rows = active.shape
    emb = second_ref.shape[1]
    first_t = first_ref[:, pl.ds(at, quarter)].T
    second = second_ref[pl.ds(at, quarter), :]
    grad = grads_ref[:, k * emb : (k + 1) * emb]
    chunk = 512
    for c in range(0, rows, chunk):
        cols = slice(c, c + chunk)
        hidden = dot(first_t, rows_ref[cols, :].T)
        sig = sigmoid(hidden)
        act = hidden * sig
        active[:, cols] = act.astype(BF)
        slope = sig + act * (1.0 - sig)
        back[:, cols] = (dot(second, grad[cols, :].T) * slope).astype(BF)
    return dot(active[...], grad), dot(back[...], rows_ref[...])


def mine_kernel(pos_ref, sf, gf, ss, gs, grads_ref, rows_ref, goals_ref, *refs):
    outs, (active, back) = refs[:4], refs[4:]
    quarter = active.shape[0]
    at = pl.multiple_of(pos_ref[1] * quarter, quarter)
    outs[0][...], outs[1][...] = rows_grads(at, sf, ss, grads_ref, 0, rows_ref, active, back)
    outs[2][...], outs[3][...] = rows_grads(at, gf, gs, grads_ref, 1, goals_ref, active, back)


def other_kernel(k, n_put, pos_ref, first, second, grads_ref, rows_ref, sum_second, sum_first, *refs):
    done, (gf_ref, gs_ref), outs, (active, back), rest = (
        refs[:n_put],
        refs[n_put : n_put + 2],
        refs[n_put + 2 : 2 * n_put + 2],
        refs[2 * n_put + 2 : 2 * n_put + 4],
        refs[2 * n_put + 4 :],
    )
    copies = put_halves([pos_ref[1]] * n_put, done, outs, rest)
    quarter = active.shape[0]
    at = pl.multiple_of(pos_ref[1] * quarter, quarter)
    grad_second, grad_first = rows_grads(at, first, second, grads_ref, k, rows_ref, active, back)
    gs_ref[...] = (sum_second[...] + grad_second).astype(BF)
    gf_ref[...] = (sum_first[...] + grad_first).astype(BF).T
    for c in copies:
        c.wait()


def put_halves(sides, halves, outs, rest):
    copies = []
    for i, (side, half, out) in enumerate(zip(sides, halves, outs)):
        rest[i][...] = half[...].astype(F32)
        copies.append(put_half(side, rest[i], out, rest[-1].at[i]))
        copies[-1].start()
    return copies


def put_half(side, half, out, sem):
    n, m = half.shape
    if out.shape[0] == n:
        to = out.at[:, pl.ds(pl.multiple_of(side * m, m), m)]
    else:
        to = out.at[pl.ds(pl.multiple_of(side * n, n), n), :]
    return pltpu.make_async_copy(half, to, sem)


def finish_kernel(old, new, pos_ref, *refs):
    n = old + new
    sides = [1 - pos_ref[1]] * old + [pos_ref[1]] * new
    for c in put_halves(sides, refs[:n], refs[n + old : 2 * n + old], refs[2 * n + old :]):
        c.wait()


def finish(pos, halves, wholes, shapes):
    old, new = len(wholes), len(shapes)
    n = old + new
    return kernel(
        functools.partial(finish_kernel, old, new),
        "finish",
        [(w.shape, w.dtype) for w in wholes] + shapes,
        (*halves, *wholes),
        [*(pltpu.VMEM(x.shape, F32) for x in halves), pltpu.SemaphoreType.DMA((n,))],
        pos=pos,
        hbm=range(n, n + old),
        hbm_out=range(n),
        aliases={n + i: i for i in range(old)},
    )


def gathered(
    states, goal_distance, goal_row, episode, state_first, state_second, goal_first, goal_second
):
    rows_dev, width = states.shape
    n_blk, n_rep, n_sub = (lax.axis_size(a) for a in ("blk", "rep", "sub"))
    owners = n_blk * n_sub
    slab = rows_dev // n_rep
    rows_all = owners * rows_dev
    hid, emb = state_second.shape
    b, s = lax.axis_index("blk"), lax.axis_index("sub")
    pos = jnp.stack([b, s]).astype(jnp.int32)
    quarter = hid // n_sub

    def across(x, k):
        return lax.ppermute(x, "blk", [(i, i ^ k) for i in range(n_blk)])

    def swap(x, axis):
        return lax.ppermute(x, axis, [(0, 1), (1, 0)])

    def after(x, *first):
        return lax.optimization_barrier((x, *first))[0]

    weights = (state_first, goal_first, state_second, goal_second)
    meta = (goal_distance.reshape(1, rows_dev), goal_row.reshape(1, rows_dev), episode.reshape(1, rows_dev))
    got = {3: across(states, 3)}
    part0, held = first_forward(pos, states, weights)
    there0 = swap(part0, "rep")
    pack, table = kernel(
        functools.partial(pack_kernel, n_rep, n_blk, n_sub),
        "pack",
        [((rows_dev + 16, width), BF), ((16, width), BF)],
        (after(states, part0), *meta),
        pos=pos,
        limit=4,
    )
    got[0], got[1] = pack, across(pack, 1)
    got[2] = across(after(pack, got[3]), 2)
    part3 = forward(got[3], held, rows_dev)
    there3 = swap(part3, "rep")

    sums = {0: both(part0, there0)}
    sums[1] = across(sums[0], 1)
    part2 = forward(after(got[2], sums[0]), held, rows_dev)
    there2 = swap(part2, "rep")
    got[4] = across(after(table, part2), 3)
    sums[3] = both(part3, there3)

    side = ((rows_all // 2, width), BF)
    mine, other, goals_mine, pick, episodes = kernel(
        functools.partial(arrange_kernel, n_blk, n_rep, slab),
        "arrange",
        [side, side, side, ((rows_all // 2, rows_all), BF), ((1, rows_all // 2), F32)],
        (*(got[k] for k in range(n_blk + 1)), *(swap(got[k], "sub") for k in range(n_blk))),
        [
            pltpu.VMEM((rows_all, width), BF),
            pltpu.VMEM((16, rows_all // 2), F32),
        ],
        pos=pos,
    )
    embedded = [sums[0], sums[1], part2, sums[3], after(there2, pick)]
    (grads_mine,) = kernel(
        functools.partial(contrast_kernel, n_blk, n_rep, slab, 4.0 / math.sqrt(emb)),
        "contrast",
        [((rows_all // 2, 2 * emb), BF)],
        (*embedded, *(swap(x, "sub") for x in embedded), episodes, pick),
        [pltpu.VMEM((rows_all // 2, emb), BF), pltpu.VMEM((rows_all, emb), BF)],
        pos=pos,
    )
    grads_other = swap(grads_mine, "sub")
    goals_other = swap(goals_mine, "sub")

    sf, gf, ss, gs = weights
    work = [pltpu.VMEM((quarter, rows_all // 2), BF), pltpu.VMEM((quarter, rows_all // 2), BF)]
    flops = 4 * rows_all * width * quarter
    sums_s2, sums_s1, sums_g2, sums_g1 = kernel(
        mine_kernel,
        "mine",
        [((quarter, emb), F32), ((quarter, width), F32)] * 2,
        (sf, gf, ss, gs, grads_mine, mine, goals_mine),
        work,
        pos=pos,
        flops=2 * flops,
    )
    halves = [((width, quarter), BF), ((quarter, emb), BF)]
    wholes = [((width, hid), F32), ((hid, emb), F32)]
    state_halves = kernel(
        functools.partial(other_kernel, 0, 0),
        "other_state",
        halves,
        (sf, ss, grads_other, other, sums_s2, sums_s1),
        work,
        pos=pos,
        flops=flops,
    )
    state_there = [swap(x, "sub") for x in state_halves]
    *goal_halves, out0, out1 = kernel(
        functools.partial(other_kernel, 1, 2),
        "other_goal",
        halves + wholes,
        (gf, gs, grads_other, goals_other, sums_g2, sums_g1, *state_halves),
        work + [*(pltpu.VMEM(shape, F32) for shape, _ in halves), pltpu.SemaphoreType.DMA((2,))],
        pos=pos,
        flops=flops,
        hbm_out=(2, 3),
    )
    goal_there = [swap(x, "sub") for x in goal_halves]
    out0, out1, out2, out3 = finish(pos, (*state_there, *goal_halves), (out0, out1), wholes)
    out2, out3 = finish(pos, goal_there, (out2, out3), [])
    return (out0, out1, out2, out3)


def silu_slope(hidden):
    sig = jax.nn.sigmoid(hidden)
    return sig * (1.0 + hidden * (1.0 - sig))


def encoder_grads(rows_in, hidden, active, second, emb_grad):
    grad_second = jnp.einsum("nh,ne->he", active, emb_grad, preferred_element_type=jnp.float32)
    back = jnp.einsum("ne,he->nh", emb_grad, second, preferred_element_type=jnp.float32)
    back_rows = (back * silu_slope(hidden)).astype(jnp.bfloat16)
    grad_first = jnp.einsum("ns,nh->sh", rows_in, back_rows, preferred_element_type=jnp.float32)
    return (grad_first, grad_second)


def exchanged(
    states, goal_distance, goal_row, episode, state_first, state_second, goal_first, goal_second
):
    rows_dev, width = states.shape
    owners = lax.axis_size(("blk", "sub"))
    position = lax.axis_index(("blk", "sub"))
    capacity = 4 * rows_dev // owners
    target = (position + goal_distance[:, 0]) % owners
    onehot = (target[:, None] == jnp.arange(owners, dtype=jnp.int32)[None, :]).astype(jnp.int32)
    slot_rank = jnp.sum((jnp.cumsum(onehot, axis=0) - onehot) * onehot, axis=1)
    requests = jnp.zeros((owners, capacity), jnp.int32).at[target, slot_rank].set(goal_row)
    wanted = lax.all_to_all(requests, ("blk", "sub"), split_axis=0, concat_axis=0, tiled=True)
    fetched = jnp.take(states, wanted.reshape(-1), axis=0).reshape(wanted.shape + (width,))
    replies = lax.all_to_all(fetched, ("blk", "sub"), split_axis=0, concat_axis=0, tiled=True)
    goal_states = jnp.take(
        replies.reshape(owners * capacity, width), target * capacity + slot_rank, axis=0
    )
    slab_rows = rows_dev // lax.axis_size("rep")
    state_hidden = jnp.dot(states, state_first, preferred_element_type=jnp.float32)
    state_active = jax.nn.silu(state_hidden).astype(jnp.bfloat16)
    goal_hidden = jnp.dot(goal_states, goal_first, preferred_element_type=jnp.float32)
    goal_active = jax.nn.silu(goal_hidden).astype(jnp.bfloat16)
    phi = lax.psum_scatter(
        jnp.dot(state_active, state_second, preferred_element_type=jnp.float32),
        "rep",
        scatter_dimension=0,
        tiled=True,
    ).astype(jnp.bfloat16)
    psi = lax.psum_scatter(
        jnp.dot(goal_active, goal_second, preferred_element_type=jnp.float32),
        "rep",
        scatter_dimension=0,
        tiled=True,
    ).astype(jnp.bfloat16)
    episode_own = lax.dynamic_slice_in_dim(episode, lax.axis_index("rep") * slab_rows, slab_rows, 0)
    psi_all, episode_all = (
        lax.all_gather(psi, "blk", axis=0, tiled=True),
        lax.all_gather(episode_own, "blk", axis=0, tiled=True),
    )
    batch_rows = psi_all.shape[0]
    logit_scale = 4.0 / math.sqrt(psi.shape[1])
    own_rows = lax.axis_index("blk") * slab_rows + jnp.arange(slab_rows, dtype=jnp.int32)
    columns = jnp.arange(batch_rows, dtype=jnp.int32)
    diagonal = own_rows[:, None] == columns[None, :]
    excluded = (episode_own[:, None] == episode_all[None, :]) & ~diagonal
    scores = jnp.einsum("ie,je->ij", phi, psi_all, preferred_element_type=jnp.float32) * logit_scale
    exponent = jnp.where(excluded, 0.0, jnp.exp(scores))
    totals = jnp.sum(exponent, axis=1)
    delta = (exponent / totals[:, None] - diagonal.astype(jnp.float32)).astype(jnp.bfloat16)
    phi_grad = (jnp.dot(delta, psi_all, preferred_element_type=jnp.float32) * logit_scale).astype(
        jnp.bfloat16
    )
    psi_grad = lax.psum_scatter(
        jnp.einsum("ij,ie->je", delta, phi, preferred_element_type=jnp.float32) * logit_scale,
        "blk",
        scatter_dimension=0,
        tiled=True,
    ).astype(jnp.bfloat16)
    phi_full, psi_full = (
        lax.all_gather(phi_grad, "rep", axis=0, tiled=True),
        lax.all_gather(psi_grad, "rep", axis=0, tiled=True),
    )
    state_parts = encoder_grads(states, state_hidden, state_active, state_second, phi_full)
    goal_parts = encoder_grads(goal_states, goal_hidden, goal_active, goal_second, psi_full)
    summed = lax.psum(
        (state_parts[0], state_parts[1], goal_parts[0], goal_parts[1]), ("blk", "sub")
    )
    return (summed[0], summed[1], summed[2], summed[3])


def solution(mesh):
    in_specs = (
        P(("grp", "blk", "sub"), None),
        P(("grp", "blk", "sub"), None),
        P(("grp", "blk", "sub")),
        P(("grp", "blk", "sub")),
        P(None, "rep"),
        P("rep", None),
        P(None, "rep"),
        P("rep", None),
    )
    out_specs = (P("grp", "rep"), P(("grp", "rep"), None), P("grp", "rep"), P(("grp", "rep"), None))
    shape = mesh.shape
    local = gathered if (shape["blk"], shape["rep"], shape["sub"]) == (4, 2, 2) else exchanged
    return jax.shard_map(local, mesh=mesh, in_specs=in_specs, out_specs=out_specs, check_vma=False)
```

```python
import functools
import math

import jax
import jax.numpy as jnp
from jax import lax
from jax.experimental import pallas as pl
from jax.experimental.pallas import tpu as pltpu
from jax.sharding import PartitionSpec as P

BF = jnp.bfloat16
F32 = jnp.float32
MIB = 1024 * 1024


def dot(a, b):
    return jnp.dot(a, b, preferred_element_type=F32)


def sigmoid(v):
    return 0.5 * jnp.tanh(0.5 * v) + 0.5


HBM = pl.BlockSpec(memory_space=pltpu.HBM)
VMEM = pl.BlockSpec(memory_space=pltpu.VMEM)
SMEM = pl.BlockSpec(memory_space=pltpu.SMEM)


def kernel(body, name, outs, args, scratch=(), limit=16, pos=None, flops=0, hbm=(), hbm_out=(), aliases={}):
    specs = [HBM if i in hbm else VMEM for i in range(len(args))]
    if pos is not None:
        args, specs = (pos, *args), [SMEM, *specs]
        aliases = {i + 1: o for i, o in aliases.items()}
    return pl.pallas_call(
        body,
        in_specs=specs,
        out_specs=[HBM if i in hbm_out else VMEM for i in range(len(outs))],
        out_shape=[jax.ShapeDtypeStruct(shape, dtype) for shape, dtype in outs],
        scratch_shapes=scratch,
        input_output_aliases=aliases,
        compiler_params=pltpu.CompilerParams(vmem_limit_bytes=int(limit * MIB)),
        cost_estimate=pl.CostEstimate(flops=flops, bytes_accessed=0, transcendentals=0),
        name=name,
    )(*args)


def encode(x_ref, weights, out_ref, active, ready=lambda i: None):
    emb = weights[2].shape[1]
    for k in range(2):
        first, second = weights[k], weights[2 + k]
        ready(k)
        for c in range(0, active.shape[1], 512):
            hidden = dot(x_ref[...], first[:, c : c + 512])
            active[:, c : c + 512] = (hidden * sigmoid(hidden)).astype(BF)
        ready(2 + k)
        out_ref[:, k * emb : (k + 1) * emb] = dot(active[...], second[...]).astype(BF)


def first_kernel(pos_ref, x_ref, *refs):
    weights, out_ref, held, active, sems = refs[:4], refs[4], refs[5:9], refs[9], refs[10]
    copies = [pltpu.make_async_copy(weights[i], held[i], sems.at[i]) for i in range(4)]
    for i in (0, 2, 1, 3):
        copies[i].start()
    encode(x_ref.at[: out_ref.shape[0]], held, out_ref, active, lambda i: copies[i].wait())


def first_forward(pos, x, weights, rows):
    hid, emb = weights[2].shape
    part, *held = kernel(
        first_kernel,
        "forward",
        [((rows, 2 * emb), BF)] + [(w.shape, w.dtype) for w in weights],
        (x, *weights),
        [pltpu.VMEM((rows, hid), BF), pltpu.SemaphoreType.DMA((4,))],
        limit=49,
        pos=pos,
        hbm=range(1, 5),
    )
    return part, held


def pack_kernel(n_rep, n_blk, n_sub, pos_ref, x_ref, own_ref, pack_ref):
    rows = x_ref.shape[0]
    slab = rows // n_rep

    def bits(n):
        return n.bit_length() - 1

    owner = (pos_ref[0] * n_sub + pos_ref[1] + own_ref[0:1, :]) & (n_blk * n_sub - 1)
    place = own_ref[1:2, :]
    batch = ((owner & (n_sub - 1)) << bits(n_rep)) + (place >> bits(slab))
    goal = (((batch << bits(n_blk)) + (owner >> bits(n_sub))) << bits(slab)) + (place & (slab - 1))
    digits = (goal >> 8, goal & 255, own_ref[2:3, :])
    table = jnp.concatenate([d.astype(F32) for d in digits] + [jnp.zeros((13, rows), F32)], axis=0).astype(BF)
    pack_ref[:rows, :] = x_ref[...]
    pack_ref[rows:, :] = table


def forward_kernel(x_ref, *refs):
    encode(x_ref.at[: refs[4].shape[0]], refs[:4], refs[4], refs[5])


def forward(x, weights, rows):
    hid, emb = weights[2].shape
    return kernel(
        forward_kernel,
        "forward",
        [((rows, 2 * emb), BF)],
        (x, *weights),
        [pltpu.VMEM((rows, hid), BF)],
        limit=8,
    )[0]


def add_kernel(a_ref, b_ref, out_ref):
    out_ref[...] = (a_ref[...].astype(F32) + b_ref[...].astype(F32)).astype(BF)


def both(part, there):
    return kernel(add_kernel, "both", [(part.shape, BF)], (part, there), limit=4)[0]


def place_blocks(pos_ref, blocks, put, n_blk, n_rep, slab):
    for k, block in enumerate(blocks):
        at = jnp.bitwise_xor(pos_ref[0], k)
        for r in range(n_rep):
            off = (r * n_blk + at) * slab
            put(pl.multiple_of(off, slab), block[r * slab : (r + 1) * slab, :])


def column(row):
    return jnp.broadcast_to(row, (128, row.shape[1])).T[:, :1]


def arrange_kernel(n_blk, n_rep, slab, pos_ref, *refs):
    mine, other = refs[:n_blk], refs[n_blk : 2 * n_blk]
    rows_mine, rows_other, goals_ref, pick_ref, ep_ref, both_sides, meta = refs[2 * n_blk :]
    half = rows_mine.shape[0]
    rows = 2 * half
    batch = n_blk * slab
    for i, (blocks, to) in enumerate(((mine, rows_mine), (other, rows_other))):

        def put(off, value, i=i, to=to):
            to[pl.ds(off, slab), :] = value
            both_sides[pl.ds(i * half + off, slab), :] = value

        place_blocks(pos_ref, blocks, put, n_blk, n_rep, slab)
    for k, block in enumerate(mine):
        at = jnp.bitwise_xor(pos_ref[0], k)
        for r in range(n_rep):
            off = pl.multiple_of((r * n_blk + at) * slab, slab)
            meta[:, pl.ds(off, slab)] = block[n_rep * slab :, r * slab : (r + 1) * slab].astype(F32)
    ep_ref[...] = meta[2:3, :]
    for r in range(n_rep):
        own = slice(r * batch, (r + 1) * batch)
        goal = column(meta[0:1, own] * 256.0 + meta[1:2, own]).astype(jnp.int32) + pos_ref[1] * half
        goal = jnp.where(goal >= rows, goal - rows, goal)
        pick_ref[own, :] = jnp.where(
            goal == lax.broadcasted_iota(jnp.int32, (batch, rows), 1), 1.0, 0.0
        ).astype(BF)
    goals_ref[...] = dot(pick_ref[...], both_sides[...]).astype(BF)


def contrast_kernel(n_blk, n_rep, slab, scale, pos_ref, *refs):
    n = n_blk + 1
    mine, other, ep_ref, pick_ref = refs[:n], refs[n : 2 * n], refs[2 * n], refs[2 * n + 1]
    grads_ref, phi_all, psi_all = refs[2 * n + 2 :]
    half, emb = phi_all.shape
    batch = n_blk * slab
    last = n_blk - 2

    def sums(parts):
        blocks = list(parts[:n_blk])
        blocks[last] = (parts[last][...].astype(F32) + parts[n_blk][...].astype(F32)).astype(BF)
        return blocks

    def put_mine(off, value):
        phi_all[pl.ds(off, slab), :] = value[:, :emb]
        psi_all[pl.ds(off, slab), :] = value[:, emb:]

    def put_other(off, value):
        psi_all[pl.ds(half + off, slab), :] = value[:, emb:]

    place_blocks(pos_ref, sums(mine), put_mine, n_blk, n_rep, slab)
    place_blocks(pos_ref, sums(other), put_other, n_blk, n_rep, slab)
    diagonal = lax.broadcasted_iota(jnp.int32, (batch, batch), 0) == lax.broadcasted_iota(
        jnp.int32, (batch, batch), 1
    )
    for r in range(n_rep):
        own = slice(r * batch, (r + 1) * batch)
        ep_row = ep_ref[:, own]
        psi = dot(pick_ref[own, :], psi_all[...]).astype(BF)
        phi = phi_all[own, :]
        scores = lax.dot_general(phi, psi, (((1,), (1,)), ((), ())), preferred_element_type=F32)
        kept = (column(ep_row) != ep_row) | diagonal
        exponent = jnp.where(kept, jnp.exp(scores * scale), 0.0)
        totals = jnp.sum(exponent, axis=1, keepdims=True)
        power = jnp.where(totals > 1.0, 2.0**-32, 1.0)
        shares = (exponent * power) * (1.0 / (totals * power))
        delta = jnp.where(diagonal, shares - 1.0, shares).astype(BF)
        grads_ref[own, :emb] = (dot(delta, psi) * scale).astype(BF)
        grads_ref[own, emb:] = (dot(delta.T, phi) * scale).astype(BF)


def rows_grads(at, first_ref, second_ref, grads_ref, k, rows_ref, active, back):
    quarter, rows = active.shape
    emb = second_ref.shape[1]
    first_t = first_ref[:, pl.ds(at, quarter)].T
    second = second_ref[pl.ds(at, quarter), :]
    grad = grads_ref[:, k * emb : (k + 1) * emb]
    chunk = 512
    for c in range(0, rows, chunk):
        cols = slice(c, c + chunk)
        hidden = dot(first_t, rows_ref[cols, :].T)
        sig = sigmoid(hidden)
        act = hidden * sig
        active[:, cols] = act.astype(BF)
        slope = sig + act * (1.0 - sig)
        back[:, cols] = (dot(second, grad[cols, :].T) * slope).astype(BF)
    return dot(active[...], grad), dot(back[...], rows_ref[...])


def mine_kernel(pos_ref, sf, gf, ss, gs, grads_ref, rows_ref, goals_ref, *refs):
    outs, (active, back) = refs[:4], refs[4:]
    quarter = active.shape[0]
    at = pl.multiple_of(pos_ref[1] * quarter, quarter)
    outs[0][...], outs[1][...] = rows_grads(at, sf, ss, grads_ref, 0, rows_ref, active, back)
    outs[2][...], outs[3][...] = rows_grads(at, gf, gs, grads_ref, 1, goals_ref, active, back)


def other_kernel(k, n_put, pos_ref, first, second, grads_ref, rows_ref, sum_second, sum_first, *refs):
    done, (gf_ref, gs_ref), outs, (active, back), rest = (
        refs[:n_put],
        refs[n_put : n_put + 2],
        refs[n_put + 2 : 2 * n_put + 2],
        refs[2 * n_put + 2 : 2 * n_put + 4],
        refs[2 * n_put + 4 :],
    )
    copies = put_halves([pos_ref[1]] * n_put, done, outs, rest)
    quarter = active.shape[0]
    at = pl.multiple_of(pos_ref[1] * quarter, quarter)
    grad_second, grad_first = rows_grads(at, first, second, grads_ref, k, rows_ref, active, back)
    gs_ref[...] = (sum_second[...] + grad_second).astype(BF)
    gf_ref[...] = (sum_first[...] + grad_first).astype(BF).T
    for c in copies:
        c.wait()


def put_halves(sides, halves, outs, rest):
    copies = []
    for i, (side, half, out) in enumerate(zip(sides, halves, outs)):
        rest[i][...] = half[...].astype(F32)
        copies.append(put_half(side, rest[i], out, rest[-1].at[i]))
        copies[-1].start()
    return copies


def put_half(side, half, out, sem):
    n, m = half.shape
    if out.shape[0] == n:
        to = out.at[:, pl.ds(pl.multiple_of(side * m, m), m)]
    else:
        to = out.at[pl.ds(pl.multiple_of(side * n, n), n), :]
    return pltpu.make_async_copy(half, to, sem)


def finish_kernel(old, new, pos_ref, *refs):
    n = old + new
    sides = [1 - pos_ref[1]] * old + [pos_ref[1]] * new
    for c in put_halves(sides, refs[:n], refs[n + old : 2 * n + old], refs[2 * n + old :]):
        c.wait()


def finish(pos, halves, wholes, shapes):
    old, new = len(wholes), len(shapes)
    n = old + new
    return kernel(
        functools.partial(finish_kernel, old, new),
        "finish",
        [(w.shape, w.dtype) for w in wholes] + shapes,
        (*halves, *wholes),
        [*(pltpu.VMEM(x.shape, F32) for x in halves), pltpu.SemaphoreType.DMA((n,))],
        pos=pos,
        hbm=range(n, n + old),
        hbm_out=range(n),
        aliases={n + i: i for i in range(old)},
    )


def gathered(
    states, goal_distance, goal_row, episode, state_first, state_second, goal_first, goal_second
):
    rows_dev, width = states.shape
    n_blk, n_rep, n_sub = (lax.axis_size(a) for a in ("blk", "rep", "sub"))
    owners = n_blk * n_sub
    slab = rows_dev // n_rep
    rows_all = owners * rows_dev
    hid, emb = state_second.shape
    b, s = lax.axis_index("blk"), lax.axis_index("sub")
    pos = jnp.stack([b, s]).astype(jnp.int32)
    quarter = hid // n_sub

    def across(x, k):
        return lax.ppermute(x, "blk", [(i, i ^ k) for i in range(n_blk)])

    def swap(x, axis):
        return lax.ppermute(x, axis, [(0, 1), (1, 0)])

    def after(x, *first):
        return lax.optimization_barrier((x, *first))[0]

    weights = (state_first, goal_first, state_second, goal_second)
    (pack,) = kernel(
        functools.partial(pack_kernel, n_rep, n_blk, n_sub),
        "pack",
        [((rows_dev + 16, width), BF)],
        (states, jnp.stack([goal_distance.reshape(rows_dev), goal_row, episode])),
        pos=pos,
        limit=4,
    )
    got = {0: pack, 3: across(pack, 3)}
    part0, held = first_forward(pos, pack, weights, rows_dev)
    got[1] = across(after(pack, part0), 1)
    got[2] = across(after(pack, got[3]), 2)
    there0 = swap(part0, "rep")
    part3 = forward(got[3], held, rows_dev)
    there3 = swap(part3, "rep")

    sums = {0: both(part0, there0)}
    sums[1] = across(sums[0], 1)
    part2 = forward(after(got[2], sums[0]), held, rows_dev)
    there2 = swap(part2, "rep")
    sums[3] = both(part3, there3)

    side = ((rows_all // 2, width), BF)
    mine, other, goals_mine, pick, episodes = kernel(
        functools.partial(arrange_kernel, n_blk, n_rep, slab),
        "arrange",
        [side, side, side, ((rows_all // 2, rows_all), BF), ((1, rows_all // 2), F32)],
        (*(got[k] for k in range(n_blk)), *(swap(got[k], "sub") for k in range(n_blk))),
        [
            pltpu.VMEM((rows_all, width), BF),
            pltpu.VMEM((16, rows_all // 2), F32),
        ],
        pos=pos,
    )
    embedded = [sums[0], sums[1], part2, sums[3], after(there2, pick)]
    (grads_mine,) = kernel(
        functools.partial(contrast_kernel, n_blk, n_rep, slab, 4.0 / math.sqrt(emb)),
        "contrast",
        [((rows_all // 2, 2 * emb), BF)],
        (*embedded, *(swap(x, "sub") for x in embedded), episodes, pick),
        [pltpu.VMEM((rows_all // 2, emb), BF), pltpu.VMEM((rows_all, emb), BF)],
        pos=pos,
    )
    grads_other = swap(grads_mine, "sub")
    goals_other = swap(goals_mine, "sub")

    sf, gf, ss, gs = weights
    work = [pltpu.VMEM((quarter, rows_all // 2), BF), pltpu.VMEM((quarter, rows_all // 2), BF)]
    flops = 4 * rows_all * width * quarter
    sums_s2, sums_s1, sums_g2, sums_g1 = kernel(
        mine_kernel,
        "mine",
        [((quarter, emb), F32), ((quarter, width), F32)] * 2,
        (sf, gf, ss, gs, grads_mine, mine, goals_mine),
        work,
        pos=pos,
        flops=2 * flops,
    )
    halves = [((width, quarter), BF), ((quarter, emb), BF)]
    wholes = [((width, hid), F32), ((hid, emb), F32)]
    state_halves = kernel(
        functools.partial(other_kernel, 0, 0),
        "other_state",
        halves,
        (sf, ss, grads_other, other, sums_s2, sums_s1),
        work,
        pos=pos,
        flops=flops,
    )
    state_there = [swap(x, "sub") for x in state_halves]
    *goal_halves, out0, out1 = kernel(
        functools.partial(other_kernel, 1, 2),
        "other_goal",
        halves + wholes,
        (gf, gs, grads_other, goals_other, sums_g2, sums_g1, *state_halves),
        work + [*(pltpu.VMEM(shape, F32) for shape, _ in halves), pltpu.SemaphoreType.DMA((2,))],
        pos=pos,
        flops=flops,
        hbm_out=(2, 3),
    )
    goal_there = [swap(x, "sub") for x in goal_halves]
    out0, out1, out2, out3 = finish(pos, (*state_there, *goal_halves), (out0, out1), wholes)
    out2, out3 = finish(pos, goal_there, (out2, out3), [])
    return (out0, out1, out2, out3)


def silu_slope(hidden):
    sig = jax.nn.sigmoid(hidden)
    return sig * (1.0 + hidden * (1.0 - sig))


def encoder_grads(rows_in, hidden, active, second, emb_grad):
    grad_second = jnp.einsum("nh,ne->he", active, emb_grad, preferred_element_type=jnp.float32)
    back = jnp.einsum("ne,he->nh", emb_grad, second, preferred_element_type=jnp.float32)
    back_rows = (back * silu_slope(hidden)).astype(jnp.bfloat16)
    grad_first = jnp.einsum("ns,nh->sh", rows_in, back_rows, preferred_element_type=jnp.float32)
    return (grad_first, grad_second)


def exchanged(
    states, goal_distance, goal_row, episode, state_first, state_second, goal_first, goal_second
):
    rows_dev, width = states.shape
    owners = lax.axis_size(("blk", "sub"))
    position = lax.axis_index(("blk", "sub"))
    capacity = 4 * rows_dev // owners
    target = (position + goal_distance[:, 0]) % owners
    onehot = (target[:, None] == jnp.arange(owners, dtype=jnp.int32)[None, :]).astype(jnp.int32)
    slot_rank = jnp.sum((jnp.cumsum(onehot, axis=0) - onehot) * onehot, axis=1)
    requests = jnp.zeros((owners, capacity), jnp.int32).at[target, slot_rank].set(goal_row)
    wanted = lax.all_to_all(requests, ("blk", "sub"), split_axis=0, concat_axis=0, tiled=True)
    fetched = jnp.take(states, wanted.reshape(-1), axis=0).reshape(wanted.shape + (width,))
    replies = lax.all_to_all(fetched, ("blk", "sub"), split_axis=0, concat_axis=0, tiled=True)
    goal_states = jnp.take(
        replies.reshape(owners * capacity, width), target * capacity + slot_rank, axis=0
    )
    slab_rows = rows_dev // lax.axis_size("rep")
    state_hidden = jnp.dot(states, state_first, preferred_element_type=jnp.float32)
    state_active = jax.nn.silu(state_hidden).astype(jnp.bfloat16)
    goal_hidden = jnp.dot(goal_states, goal_first, preferred_element_type=jnp.float32)
    goal_active = jax.nn.silu(goal_hidden).astype(jnp.bfloat16)
    phi = lax.psum_scatter(
        jnp.dot(state_active, state_second, preferred_element_type=jnp.float32),
        "rep",
        scatter_dimension=0,
        tiled=True,
    ).astype(jnp.bfloat16)
    psi = lax.psum_scatter(
        jnp.dot(goal_active, goal_second, preferred_element_type=jnp.float32),
        "rep",
        scatter_dimension=0,
        tiled=True,
    ).astype(jnp.bfloat16)
    episode_own = lax.dynamic_slice_in_dim(episode, lax.axis_index("rep") * slab_rows, slab_rows, 0)
    psi_all, episode_all = (
        lax.all_gather(psi, "blk", axis=0, tiled=True),
        lax.all_gather(episode_own, "blk", axis=0, tiled=True),
    )
    batch_rows = psi_all.shape[0]
    logit_scale = 4.0 / math.sqrt(psi.shape[1])
    own_rows = lax.axis_index("blk") * slab_rows + jnp.arange(slab_rows, dtype=jnp.int32)
    columns = jnp.arange(batch_rows, dtype=jnp.int32)
    diagonal = own_rows[:, None] == columns[None, :]
    excluded = (episode_own[:, None] == episode_all[None, :]) & ~diagonal
    scores = jnp.einsum("ie,je->ij", phi, psi_all, preferred_element_type=jnp.float32) * logit_scale
    exponent = jnp.where(excluded, 0.0, jnp.exp(scores))
    totals = jnp.sum(exponent, axis=1)
    delta = (exponent / totals[:, None] - diagonal.astype(jnp.float32)).astype(jnp.bfloat16)
    phi_grad = (jnp.dot(delta, psi_all, preferred_element_type=jnp.float32) * logit_scale).astype(
        jnp.bfloat16
    )
    psi_grad = lax.psum_scatter(
        jnp.einsum("ij,ie->je", delta, phi, preferred_element_type=jnp.float32) * logit_scale,
        "blk",
        scatter_dimension=0,
        tiled=True,
    ).astype(jnp.bfloat16)
    phi_full, psi_full = (
        lax.all_gather(phi_grad, "rep", axis=0, tiled=True),
        lax.all_gather(psi_grad, "rep", axis=0, tiled=True),
    )
    state_parts = encoder_grads(states, state_hidden, state_active, state_second, phi_full)
    goal_parts = encoder_grads(goal_states, goal_hidden, goal_active, goal_second, psi_full)
    summed = lax.psum(
        (state_parts[0], state_parts[1], goal_parts[0], goal_parts[1]), ("blk", "sub")
    )
    return (summed[0], summed[1], summed[2], summed[3])


def solution(mesh):
    in_specs = (
        P(("grp", "blk", "sub"), None),
        P(("grp", "blk", "sub"), None),
        P(("grp", "blk", "sub")),
        P(("grp", "blk", "sub")),
        P(None, "rep"),
        P("rep", None),
        P(None, "rep"),
        P("rep", None),
    )
    out_specs = (P("grp", "rep"), P(("grp", "rep"), None), P("grp", "rep"), P(("grp", "rep"), None))
    shape = mesh.shape
    local = gathered if (shape["blk"], shape["rep"], shape["sub"]) == (4, 2, 2) else exchanged
    return jax.shard_map(local, mesh=mesh, in_specs=in_specs, out_specs=out_specs, check_vma=False)
```

```python
import functools
import math

import jax
import jax.numpy as jnp
from jax import lax
from jax.experimental import pallas as pl
from jax.experimental.pallas import tpu as pltpu
from jax.sharding import PartitionSpec as P

BF = jnp.bfloat16
F32 = jnp.float32
MIB = 1024 * 1024


def dot(a, b):
    return jnp.dot(a, b, preferred_element_type=F32)


def sigmoid(v):
    return 0.5 * jnp.tanh(0.5 * v) + 0.5


HBM = pl.BlockSpec(memory_space=pltpu.HBM)
VMEM = pl.BlockSpec(memory_space=pltpu.VMEM)
SMEM = pl.BlockSpec(memory_space=pltpu.SMEM)


def kernel(body, name, outs, args, scratch=(), limit=16, pos=None, flops=0, hbm=(), hbm_out=(), aliases={}):
    specs = [HBM if i in hbm else VMEM for i in range(len(args))]
    if pos is not None:
        args, specs = (pos, *args), [SMEM, *specs]
        aliases = {i + 1: o for i, o in aliases.items()}
    return pl.pallas_call(
        body,
        in_specs=specs,
        out_specs=[HBM if i in hbm_out else VMEM for i in range(len(outs))],
        out_shape=[jax.ShapeDtypeStruct(shape, dtype) for shape, dtype in outs],
        scratch_shapes=scratch,
        input_output_aliases=aliases,
        compiler_params=pltpu.CompilerParams(vmem_limit_bytes=int(limit * MIB)),
        cost_estimate=pl.CostEstimate(flops=flops, bytes_accessed=0, transcendentals=0),
        name=name,
    )(*args)


def encode(x_ref, weights, out_ref, active, ready=lambda i: None):
    emb = weights[2].shape[1]
    for k in range(2):
        first, second = weights[k], weights[2 + k]
        ready(k)
        for c in range(0, active.shape[1], 512):
            hidden = dot(x_ref[...], first[:, c : c + 512])
            active[:, c : c + 512] = (hidden * sigmoid(hidden)).astype(BF)
        ready(2 + k)
        out_ref[:, k * emb : (k + 1) * emb] = dot(active[...], second[...]).astype(BF)


def first_kernel(pos_ref, x_ref, *refs):
    weights, out_ref, held, active, sems = refs[:4], refs[4], refs[5:9], refs[9], refs[10]
    copies = [pltpu.make_async_copy(weights[i], held[i], sems.at[i]) for i in range(4)]
    for i in (0, 2, 1, 3):
        copies[i].start()
    encode(x_ref.at[: out_ref.shape[0]], held, out_ref, active, lambda i: copies[i].wait())


def first_forward(pos, x, weights, rows):
    hid, emb = weights[2].shape
    part, *held = kernel(
        first_kernel,
        "forward",
        [((rows, 2 * emb), BF)] + [(w.shape, w.dtype) for w in weights],
        (x, *weights),
        [pltpu.VMEM((rows, hid), BF), pltpu.SemaphoreType.DMA((4,))],
        limit=49,
        pos=pos,
        hbm=range(1, 5),
    )
    return part, held


def pack_kernel(n_rep, n_blk, n_sub, pos_ref, x_ref, own_ref, pack_ref):
    rows = x_ref.shape[0]
    slab = rows // n_rep

    def bits(n):
        return n.bit_length() - 1

    owner = (pos_ref[0] * n_sub + pos_ref[1] + own_ref[0:1, :]) & (n_blk * n_sub - 1)
    place = own_ref[1:2, :]
    batch = ((owner & (n_sub - 1)) << bits(n_rep)) + (place >> bits(slab))
    goal = (((batch << bits(n_blk)) + (owner >> bits(n_sub))) << bits(slab)) + (place & (slab - 1))
    digits = (goal >> 8, goal & 255, own_ref[2:3, :])
    table = jnp.concatenate([d.astype(F32) for d in digits] + [jnp.zeros((13, rows), F32)], axis=0).astype(BF)
    pack_ref[:rows, :] = x_ref[...]
    pack_ref[rows:, :] = table


def forward_kernel(x_ref, *refs):
    encode(x_ref.at[: refs[4].shape[0]], refs[:4], refs[4], refs[5])


def forward(x, weights, rows):
    hid, emb = weights[2].shape
    return kernel(
        forward_kernel,
        "forward",
        [((rows, 2 * emb), BF)],
        (x, *weights),
        [pltpu.VMEM((rows, hid), BF)],
        limit=8,
    )[0]


def add_kernel(a_ref, b_ref, out_ref):
    out_ref[...] = (a_ref[...].astype(F32) + b_ref[...].astype(F32)).astype(BF)


def both(part, there):
    return kernel(add_kernel, "both", [(part.shape, BF)], (part, there), limit=4)[0]


def place_blocks(pos_ref, blocks, put, n_blk, n_rep, slab):
    for k, block in enumerate(blocks):
        at = jnp.bitwise_xor(pos_ref[0], k)
        for r in range(n_rep):
            off = (r * n_blk + at) * slab
            put(pl.multiple_of(off, slab), block[r * slab : (r + 1) * slab, :])


def column(row):
    return jnp.broadcast_to(row, (128, row.shape[1])).T[:, :1]


def arrange_kernel(n_blk, n_rep, slab, pos_ref, *refs):
    mine, other = refs[:n_blk], refs[n_blk : 2 * n_blk]
    rows_mine, rows_other, goals_ref, pick_ref, ep_ref, both_sides, meta = refs[2 * n_blk :]
    half = rows_mine.shape[0]
    rows = 2 * half
    batch = n_blk * slab
    for i, (blocks, to) in enumerate(((mine, rows_mine), (other, rows_other))):

        def put(off, value, i=i, to=to):
            to[pl.ds(off, slab), :] = value
            both_sides[pl.ds(i * half + off, slab), :] = value

        place_blocks(pos_ref, blocks, put, n_blk, n_rep, slab)
    for k, block in enumerate(mine):
        at = jnp.bitwise_xor(pos_ref[0], k)
        for r in range(n_rep):
            off = pl.multiple_of((r * n_blk + at) * slab, slab)
            meta[:, pl.ds(off, slab)] = block[n_rep * slab :, r * slab : (r + 1) * slab].astype(F32)
    ep_ref[...] = meta[2:3, :]
    for r in range(n_rep):
        own = slice(r * batch, (r + 1) * batch)
        goal = column(meta[0:1, own] * 256.0 + meta[1:2, own]).astype(jnp.int32) + pos_ref[1] * half
        goal = jnp.where(goal >= rows, goal - rows, goal)
        pick_ref[own, :] = jnp.where(
            goal == lax.broadcasted_iota(jnp.int32, (batch, rows), 1), 1.0, 0.0
        ).astype(BF)
    goals_ref[...] = dot(pick_ref[...], both_sides[...]).astype(BF)


def contrast_kernel(n_blk, n_rep, slab, scale, pos_ref, *refs):
    n = n_blk + 1
    mine, other, ep_ref, pick_ref = refs[:n], refs[n : 2 * n], refs[2 * n], refs[2 * n + 1]
    grads_ref, phi_all, psi_all = refs[2 * n + 2 :]
    half, emb = phi_all.shape
    batch = n_blk * slab
    last = n_blk - 2

    def sums(parts):
        blocks = list(parts[:n_blk])
        blocks[last] = (parts[last][...].astype(F32) + parts[n_blk][...].astype(F32)).astype(BF)
        return blocks

    def put_mine(off, value):
        phi_all[pl.ds(off, slab), :] = value[:, :emb]
        psi_all[pl.ds(off, slab), :] = value[:, emb:]

    def put_other(off, value):
        psi_all[pl.ds(half + off, slab), :] = value[:, emb:]

    place_blocks(pos_ref, sums(mine), put_mine, n_blk, n_rep, slab)
    place_blocks(pos_ref, sums(other), put_other, n_blk, n_rep, slab)
    diagonal = lax.broadcasted_iota(jnp.int32, (batch, batch), 0) == lax.broadcasted_iota(
        jnp.int32, (batch, batch), 1
    )
    psi_all[:half, :] = dot(pick_ref[...], psi_all[...]).astype(BF)
    for r in range(n_rep):
        own = slice(r * batch, (r + 1) * batch)
        ep_row = ep_ref[:, own]
        psi = psi_all[own, :]
        phi = phi_all[own, :]
        scores = lax.dot_general(phi, psi, (((1,), (1,)), ((), ())), preferred_element_type=F32)
        kept = (column(ep_row) != ep_row) | diagonal
        exponent = jnp.where(kept, jnp.exp(scores * scale), 0.0)
        totals = jnp.sum(exponent, axis=1, keepdims=True)
        power = jnp.where(totals > 1.0, 2.0**-32, 1.0)
        shares = (exponent * power) * (1.0 / (totals * power))
        delta = jnp.where(diagonal, shares - 1.0, shares).astype(BF)
        grads_ref[own, :emb] = (dot(delta, psi) * scale).astype(BF)
        grads_ref[own, emb:] = (dot(delta.T, phi) * scale).astype(BF)


def rows_grads(at, first_ref, second_ref, grads_ref, k, rows_ref, active, back):
    quarter, rows = active.shape
    emb = second_ref.shape[1]
    first_t = first_ref[:, pl.ds(at, quarter)].T
    second = second_ref[pl.ds(at, quarter), :]
    grad = grads_ref[:, k * emb : (k + 1) * emb]
    chunk = 256
    for c in range(0, rows, chunk):
        cols = slice(c, c + chunk)
        hidden = dot(first_t, rows_ref[cols, :].T)
        sig = sigmoid(hidden)
        act = hidden * sig
        active[:, cols] = act.astype(BF)
        slope = sig + act * (1.0 - sig)
        back[:, cols] = (dot(second, grad[cols, :].T) * slope).astype(BF)
    return dot(active[...], grad), dot(back[...], rows_ref[...])


def mine_kernel(pos_ref, sf, gf, ss, gs, grads_ref, rows_ref, goals_ref, *refs):
    outs, (active, back) = refs[:4], refs[4:]
    quarter = active.shape[0]
    at = pl.multiple_of(pos_ref[1] * quarter, quarter)
    outs[0][...], outs[1][...] = rows_grads(at, sf, ss, grads_ref, 0, rows_ref, active, back)
    outs[2][...], outs[3][...] = rows_grads(at, gf, gs, grads_ref, 1, goals_ref, active, back)


def other_kernel(k, n_put, pos_ref, first, second, grads_ref, rows_ref, sum_second, sum_first, *refs):
    done, (gf_ref, gs_ref), outs, (active, back), rest = (
        refs[:n_put],
        refs[n_put : n_put + 2],
        refs[n_put + 2 : 2 * n_put + 2],
        refs[2 * n_put + 2 : 2 * n_put + 4],
        refs[2 * n_put + 4 :],
    )
    copies = put_halves([pos_ref[1]] * n_put, done, outs, rest)
    quarter = active.shape[0]
    at = pl.multiple_of(pos_ref[1] * quarter, quarter)
    grad_second, grad_first = rows_grads(at, first, second, grads_ref, k, rows_ref, active, back)
    gs_ref[...] = (sum_second[...] + grad_second).astype(BF)
    gf_ref[...] = (sum_first[...] + grad_first).astype(BF).T
    for c in copies:
        c.wait()


def put_halves(sides, halves, outs, rest):
    copies = []
    for i, (side, half, out) in enumerate(zip(sides, halves, outs)):
        rest[i][...] = half[...].astype(F32)
        copies.append(put_half(side, rest[i], out, rest[-1].at[i]))
        copies[-1].start()
    return copies


def put_half(side, half, out, sem):
    n, m = half.shape
    if out.shape[0] == n:
        to = out.at[:, pl.ds(pl.multiple_of(side * m, m), m)]
    else:
        to = out.at[pl.ds(pl.multiple_of(side * n, n), n), :]
    return pltpu.make_async_copy(half, to, sem)


def finish_kernel(old, new, pos_ref, *refs):
    n = old + new
    sides = [1 - pos_ref[1]] * old + [pos_ref[1]] * new
    for c in put_halves(sides, refs[:n], refs[n + old : 2 * n + old], refs[2 * n + old :]):
        c.wait()


def finish(pos, halves, wholes, shapes):
    old, new = len(wholes), len(shapes)
    n = old + new
    return kernel(
        functools.partial(finish_kernel, old, new),
        "finish",
        [(w.shape, w.dtype) for w in wholes] + shapes,
        (*halves, *wholes),
        [*(pltpu.VMEM(x.shape, F32) for x in halves), pltpu.SemaphoreType.DMA((n,))],
        pos=pos,
        hbm=range(n, n + old),
        hbm_out=range(n),
        aliases={n + i: i for i in range(old)},
    )


def gathered(
    states, goal_distance, goal_row, episode, state_first, state_second, goal_first, goal_second
):
    rows_dev, width = states.shape
    n_blk, n_rep, n_sub = (lax.axis_size(a) for a in ("blk", "rep", "sub"))
    owners = n_blk * n_sub
    slab = rows_dev // n_rep
    rows_all = owners * rows_dev
    hid, emb = state_second.shape
    b, s = lax.axis_index("blk"), lax.axis_index("sub")
    pos = jnp.stack([b, s]).astype(jnp.int32)
    quarter = hid // n_sub

    def across(x, k):
        return lax.ppermute(x, "blk", [(i, i ^ k) for i in range(n_blk)])

    def swap(x, axis):
        return lax.ppermute(x, axis, [(0, 1), (1, 0)])

    def after(x, *first):
        return lax.optimization_barrier((x, *first))[0]

    weights = (state_first, goal_first, state_second, goal_second)
    (pack,) = kernel(
        functools.partial(pack_kernel, n_rep, n_blk, n_sub),
        "pack",
        [((rows_dev + 16, width), BF)],
        (states, jnp.stack([goal_distance.reshape(rows_dev), goal_row, episode])),
        pos=pos,
        limit=4,
    )
    got = {0: pack, 3: across(pack, 3)}
    part0, held = first_forward(pos, pack, weights, rows_dev)
    got[1] = across(after(pack, part0), 1)
    got[2] = across(after(pack, got[3]), 2)
    there0 = swap(part0, "rep")
    part3 = forward(got[3], held, rows_dev)
    there3 = swap(part3, "rep")

    sums = {0: both(part0, there0)}
    sums[1] = across(after(sums[0], got[2]), 1)
    part2 = forward(after(got[2], sums[0]), held, rows_dev)
    there2 = swap(part2, "rep")
    sums[3] = both(part3, there3)

    side = ((rows_all // 2, width), BF)
    mine, other, goals_mine, pick, episodes = kernel(
        functools.partial(arrange_kernel, n_blk, n_rep, slab),
        "arrange",
        [side, side, side, ((rows_all // 2, rows_all), BF), ((1, rows_all // 2), F32)],
        (*(got[k] for k in range(n_blk)), *(swap(got[k], "sub") for k in range(n_blk))),
        [
            pltpu.VMEM((rows_all, width), BF),
            pltpu.VMEM((16, rows_all // 2), F32),
        ],
        pos=pos,
    )
    embedded = [sums[0], sums[1], part2, sums[3], after(there2, pick)]
    (grads_mine,) = kernel(
        functools.partial(contrast_kernel, n_blk, n_rep, slab, 4.0 / math.sqrt(emb)),
        "contrast",
        [((rows_all // 2, 2 * emb), BF)],
        (*embedded, *(swap(x, "sub") for x in embedded), episodes, pick),
        [pltpu.VMEM((rows_all // 2, emb), BF), pltpu.VMEM((rows_all, emb), BF)],
        pos=pos,
    )
    grads_other = swap(grads_mine, "sub")
    goals_other = swap(goals_mine, "sub")

    sf, gf, ss, gs = weights
    work = [pltpu.VMEM((quarter, rows_all // 2), BF), pltpu.VMEM((quarter, rows_all // 2), BF)]
    flops = 4 * rows_all * width * quarter
    sums_s2, sums_s1, sums_g2, sums_g1 = kernel(
        mine_kernel,
        "mine",
        [((quarter, emb), F32), ((quarter, width), F32)] * 2,
        (sf, gf, ss, gs, grads_mine, mine, goals_mine),
        work,
        pos=pos,
        flops=2 * flops,
    )
    halves = [((width, quarter), BF), ((quarter, emb), BF)]
    wholes = [((width, hid), F32), ((hid, emb), F32)]
    state_halves = kernel(
        functools.partial(other_kernel, 0, 0),
        "other_state",
        halves,
        (sf, ss, grads_other, other, sums_s2, sums_s1),
        work,
        pos=pos,
        flops=flops,
    )
    state_there = [swap(x, "sub") for x in state_halves]
    *goal_halves, out0, out1 = kernel(
        functools.partial(other_kernel, 1, 2),
        "other_goal",
        halves + wholes,
        (gf, gs, grads_other, goals_other, sums_g2, sums_g1, *state_halves),
        work + [*(pltpu.VMEM(shape, F32) for shape, _ in halves), pltpu.SemaphoreType.DMA((2,))],
        pos=pos,
        flops=flops,
        hbm_out=(2, 3),
    )
    goal_there = [swap(x, "sub") for x in goal_halves]
    out0, out1, out2, out3 = finish(pos, (*state_there, *goal_halves), (out0, out1), wholes)
    out2, out3 = finish(pos, goal_there, (out2, out3), [])
    return (out0, out1, out2, out3)


def silu_slope(hidden):
    sig = jax.nn.sigmoid(hidden)
    return sig * (1.0 + hidden * (1.0 - sig))


def encoder_grads(rows_in, hidden, active, second, emb_grad):
    grad_second = jnp.einsum("nh,ne->he", active, emb_grad, preferred_element_type=jnp.float32)
    back = jnp.einsum("ne,he->nh", emb_grad, second, preferred_element_type=jnp.float32)
    back_rows = (back * silu_slope(hidden)).astype(jnp.bfloat16)
    grad_first = jnp.einsum("ns,nh->sh", rows_in, back_rows, preferred_element_type=jnp.float32)
    return (grad_first, grad_second)


def exchanged(
    states, goal_distance, goal_row, episode, state_first, state_second, goal_first, goal_second
):
    rows_dev, width = states.shape
    owners = lax.axis_size(("blk", "sub"))
    position = lax.axis_index(("blk", "sub"))
    capacity = 4 * rows_dev // owners
    target = (position + goal_distance[:, 0]) % owners
    onehot = (target[:, None] == jnp.arange(owners, dtype=jnp.int32)[None, :]).astype(jnp.int32)
    slot_rank = jnp.sum((jnp.cumsum(onehot, axis=0) - onehot) * onehot, axis=1)
    requests = jnp.zeros((owners, capacity), jnp.int32).at[target, slot_rank].set(goal_row)
    wanted = lax.all_to_all(requests, ("blk", "sub"), split_axis=0, concat_axis=0, tiled=True)
    fetched = jnp.take(states, wanted.reshape(-1), axis=0).reshape(wanted.shape + (width,))
    replies = lax.all_to_all(fetched, ("blk", "sub"), split_axis=0, concat_axis=0, tiled=True)
    goal_states = jnp.take(
        replies.reshape(owners * capacity, width), target * capacity + slot_rank, axis=0
    )
    slab_rows = rows_dev // lax.axis_size("rep")
    state_hidden = jnp.dot(states, state_first, preferred_element_type=jnp.float32)
    state_active = jax.nn.silu(state_hidden).astype(jnp.bfloat16)
    goal_hidden = jnp.dot(goal_states, goal_first, preferred_element_type=jnp.float32)
    goal_active = jax.nn.silu(goal_hidden).astype(jnp.bfloat16)
    phi = lax.psum_scatter(
        jnp.dot(state_active, state_second, preferred_element_type=jnp.float32),
        "rep",
        scatter_dimension=0,
        tiled=True,
    ).astype(jnp.bfloat16)
    psi = lax.psum_scatter(
        jnp.dot(goal_active, goal_second, preferred_element_type=jnp.float32),
        "rep",
        scatter_dimension=0,
        tiled=True,
    ).astype(jnp.bfloat16)
    episode_own = lax.dynamic_slice_in_dim(episode, lax.axis_index("rep") * slab_rows, slab_rows, 0)
    psi_all, episode_all = (
        lax.all_gather(psi, "blk", axis=0, tiled=True),
        lax.all_gather(episode_own, "blk", axis=0, tiled=True),
    )
    batch_rows = psi_all.shape[0]
    logit_scale = 4.0 / math.sqrt(psi.shape[1])
    own_rows = lax.axis_index("blk") * slab_rows + jnp.arange(slab_rows, dtype=jnp.int32)
    columns = jnp.arange(batch_rows, dtype=jnp.int32)
    diagonal = own_rows[:, None] == columns[None, :]
    excluded = (episode_own[:, None] == episode_all[None, :]) & ~diagonal
    scores = jnp.einsum("ie,je->ij", phi, psi_all, preferred_element_type=jnp.float32) * logit_scale
    exponent = jnp.where(excluded, 0.0, jnp.exp(scores))
    totals = jnp.sum(exponent, axis=1)
    delta = (exponent / totals[:, None] - diagonal.astype(jnp.float32)).astype(jnp.bfloat16)
    phi_grad = (jnp.dot(delta, psi_all, preferred_element_type=jnp.float32) * logit_scale).astype(
        jnp.bfloat16
    )
    psi_grad = lax.psum_scatter(
        jnp.einsum("ij,ie->je", delta, phi, preferred_element_type=jnp.float32) * logit_scale,
        "blk",
        scatter_dimension=0,
        tiled=True,
    ).astype(jnp.bfloat16)
    phi_full, psi_full = (
        lax.all_gather(phi_grad, "rep", axis=0, tiled=True),
        lax.all_gather(psi_grad, "rep", axis=0, tiled=True),
    )
    state_parts = encoder_grads(states, state_hidden, state_active, state_second, phi_full)
    goal_parts = encoder_grads(goal_states, goal_hidden, goal_active, goal_second, psi_full)
    summed = lax.psum(
        (state_parts[0], state_parts[1], goal_parts[0], goal_parts[1]), ("blk", "sub")
    )
    return (summed[0], summed[1], summed[2], summed[3])


def solution(mesh):
    in_specs = (
        P(("grp", "blk", "sub"), None),
        P(("grp", "blk", "sub"), None),
        P(("grp", "blk", "sub")),
        P(("grp", "blk", "sub")),
        P(None, "rep"),
        P("rep", None),
        P(None, "rep"),
        P("rep", None),
    )
    out_specs = (P("grp", "rep"), P(("grp", "rep"), None), P("grp", "rep"), P(("grp", "rep"), None))
    shape = mesh.shape
    local = gathered if (shape["blk"], shape["rep"], shape["sub"]) == (4, 2, 2) else exchanged
    return jax.shard_map(local, mesh=mesh, in_specs=in_specs, out_specs=out_specs, check_vma=False)
```

```python
import functools
import math

import jax
import jax.numpy as jnp
from jax import lax
from jax.experimental import pallas as pl
from jax.experimental.pallas import tpu as pltpu
from jax.sharding import PartitionSpec as P

BF = jnp.bfloat16
F32 = jnp.float32
MIB = 1024 * 1024


def dot(a, b):
    return jnp.dot(a, b, preferred_element_type=F32)


def sigmoid(v):
    return 0.5 * jnp.tanh(0.5 * v) + 0.5


HBM = pl.BlockSpec(memory_space=pltpu.HBM)
VMEM = pl.BlockSpec(memory_space=pltpu.VMEM)
SMEM = pl.BlockSpec(memory_space=pltpu.SMEM)


def kernel(body, name, outs, args, scratch=(), limit=16, pos=None, flops=0, hbm=(), hbm_out=(), aliases={}):
    specs = [HBM if i in hbm else VMEM for i in range(len(args))]
    if pos is not None:
        args, specs = (pos, *args), [SMEM, *specs]
        aliases = {i + 1: o for i, o in aliases.items()}
    return pl.pallas_call(
        body,
        in_specs=specs,
        out_specs=[HBM if i in hbm_out else VMEM for i in range(len(outs))],
        out_shape=[jax.ShapeDtypeStruct(shape, dtype) for shape, dtype in outs],
        scratch_shapes=scratch,
        input_output_aliases=aliases,
        compiler_params=pltpu.CompilerParams(vmem_limit_bytes=int(limit * MIB)),
        cost_estimate=pl.CostEstimate(flops=flops, bytes_accessed=0, transcendentals=0),
        name=name,
    )(*args)


def encode(x_ref, weights, out_ref, active, ready=lambda i: None):
    emb = weights[2].shape[1]
    for k in range(2):
        first, second = weights[k], weights[2 + k]
        ready(k)
        for c in range(0, active.shape[1], 512):
            hidden = dot(x_ref[...], first[:, c : c + 512])
            active[:, c : c + 512] = (hidden * sigmoid(hidden)).astype(BF)
        ready(2 + k)
        out_ref[:, k * emb : (k + 1) * emb] = dot(active[...], second[...]).astype(BF)


def pack_kernel(n_rep, n_blk, n_sub, pos_ref, x_ref, own_ref, pack_ref):
    rows = x_ref.shape[0]
    slab = rows // n_rep

    def bits(n):
        return n.bit_length() - 1

    owner = (pos_ref[0] * n_sub + pos_ref[1] + own_ref[0:1, :]) & (n_blk * n_sub - 1)
    place = own_ref[1:2, :]
    batch = ((owner & (n_sub - 1)) << bits(n_rep)) + (place >> bits(slab))
    goal = (((batch << bits(n_blk)) + (owner >> bits(n_sub))) << bits(slab)) + (place & (slab - 1))
    digits = (goal >> 8, goal & 255, own_ref[2:3, :])
    table = jnp.concatenate([d.astype(F32) for d in digits] + [jnp.zeros((13, rows), F32)], axis=0).astype(BF)
    pack_ref[:rows, :] = x_ref[...]
    pack_ref[rows:, :] = table


def forward_kernel(x_ref, *refs):
    encode(x_ref.at[: refs[4].shape[0]], refs[:4], refs[4], refs[5])


def forward(x, weights, rows):
    hid, emb = weights[2].shape
    return kernel(
        forward_kernel,
        "forward",
        [((rows, 2 * emb), BF)],
        (x, *weights),
        [pltpu.VMEM((rows, hid), BF)],
        limit=8,
    )[0]


def add_kernel(a_ref, b_ref, out_ref):
    out_ref[...] = (a_ref[...].astype(F32) + b_ref[...].astype(F32)).astype(BF)


def both(part, there):
    return kernel(add_kernel, "both", [(part.shape, BF)], (part, there), limit=4)[0]


def place_blocks(pos_ref, blocks, put, n_blk, n_rep, slab):
    for k, block in enumerate(blocks):
        at = jnp.bitwise_xor(pos_ref[0], k)
        for r in range(n_rep):
            off = (r * n_blk + at) * slab
            put(pl.multiple_of(off, slab), block[r * slab : (r + 1) * slab, :])


def column(row):
    return jnp.broadcast_to(row, (128, row.shape[1])).T[:, :1]


def arrange_kernel(n_blk, n_rep, slab, pos_ref, *refs):
    mine, other = refs[:n_blk], refs[n_blk : 2 * n_blk]
    rows_mine, rows_other, goals_ref, pick_ref, ep_ref, both_sides, meta = refs[2 * n_blk :]
    half = rows_mine.shape[0]
    rows = 2 * half
    batch = n_blk * slab
    for i, (blocks, to) in enumerate(((mine, rows_mine), (other, rows_other))):

        def put(off, value, i=i, to=to):
            to[pl.ds(off, slab), :] = value
            both_sides[pl.ds(i * half + off, slab), :] = value

        place_blocks(pos_ref, blocks, put, n_blk, n_rep, slab)
    for k, block in enumerate(mine):
        at = jnp.bitwise_xor(pos_ref[0], k)
        for r in range(n_rep):
            off = pl.multiple_of((r * n_blk + at) * slab, slab)
            meta[:, pl.ds(off, slab)] = block[n_rep * slab :, r * slab : (r + 1) * slab].astype(F32)
    ep_ref[...] = meta[2:3, :]
    for r in range(n_rep):
        own = slice(r * batch, (r + 1) * batch)
        goal = column(meta[0:1, own] * 256.0 + meta[1:2, own]).astype(jnp.int32) + pos_ref[1] * half
        goal = jnp.where(goal >= rows, goal - rows, goal)
        pick_ref[own, :] = jnp.where(
            goal == lax.broadcasted_iota(jnp.int32, (batch, rows), 1), 1.0, 0.0
        ).astype(BF)
    goals_ref[...] = dot(pick_ref[...], both_sides[...]).astype(BF)


def contrast_kernel(n_blk, n_rep, slab, scale, pos_ref, *refs):
    n = n_blk + 1
    mine, other, ep_ref, pick_ref = refs[:n], refs[n : 2 * n], refs[2 * n], refs[2 * n + 1]
    grads_ref, phi_all, psi_all = refs[2 * n + 2 :]
    half, emb = phi_all.shape
    batch = n_blk * slab
    last = n_blk - 2

    def sums(parts):
        blocks = list(parts[:n_blk])
        blocks[last] = (parts[last][...].astype(F32) + parts[n_blk][...].astype(F32)).astype(BF)
        return blocks

    def put_mine(off, value):
        phi_all[pl.ds(off, slab), :] = value[:, :emb]
        psi_all[pl.ds(off, slab), :] = value[:, emb:]

    def put_other(off, value):
        psi_all[pl.ds(half + off, slab), :] = value[:, emb:]

    place_blocks(pos_ref, sums(mine), put_mine, n_blk, n_rep, slab)
    place_blocks(pos_ref, sums(other), put_other, n_blk, n_rep, slab)
    diagonal = lax.broadcasted_iota(jnp.int32, (batch, batch), 0) == lax.broadcasted_iota(
        jnp.int32, (batch, batch), 1
    )
    psi_all[:half, :] = dot(pick_ref[...], psi_all[...]).astype(BF)
    for r in range(n_rep):
        own = slice(r * batch, (r + 1) * batch)
        ep_row = ep_ref[:, own]
        psi = psi_all[own, :]
        phi = phi_all[own, :]
        scores = lax.dot_general(phi, psi, (((1,), (1,)), ((), ())), preferred_element_type=F32)
        kept = (column(ep_row) != ep_row) | diagonal
        exponent = jnp.where(kept, jnp.exp(scores * scale), 0.0)
        totals = jnp.sum(exponent, axis=1, keepdims=True)
        power = jnp.where(totals > 1.0, 2.0**-32, 1.0)
        shares = (exponent * power) * (1.0 / (totals * power))
        delta = jnp.where(diagonal, shares - 1.0, shares).astype(BF)
        grads_ref[own, :emb] = (dot(delta, psi) * scale).astype(BF)
        grads_ref[own, emb:] = (dot(delta.T, phi) * scale).astype(BF)


def rows_grads(at, first_ref, second_ref, grads_ref, k, rows_ref, active, back):
    quarter, rows = active.shape
    emb = second_ref.shape[1]
    first_t = first_ref[:, pl.ds(at, quarter)].T
    second = second_ref[pl.ds(at, quarter), :]
    grad = grads_ref[:, k * emb : (k + 1) * emb]
    chunk = 256
    for c in range(0, rows, chunk):
        cols = slice(c, c + chunk)
        hidden = dot(first_t, rows_ref[cols, :].T)
        sig = sigmoid(hidden)
        act = hidden * sig
        active[:, cols] = act.astype(BF)
        slope = sig + act * (1.0 - sig)
        back[:, cols] = (dot(second, grad[cols, :].T) * slope).astype(BF)
    return dot(active[...], grad), dot(back[...], rows_ref[...])


def mine_kernel(pos_ref, sf, gf, ss, gs, grads_ref, rows_ref, goals_ref, *refs):
    outs, (active, back) = refs[:4], refs[4:]
    quarter = active.shape[0]
    at = pl.multiple_of(pos_ref[1] * quarter, quarter)
    outs[0][...], outs[1][...] = rows_grads(at, sf, ss, grads_ref, 0, rows_ref, active, back)
    outs[2][...], outs[3][...] = rows_grads(at, gf, gs, grads_ref, 1, goals_ref, active, back)


def other_kernel(k, n_put, pos_ref, first, second, grads_ref, rows_ref, sum_second, sum_first, *refs):
    done, outs, puts, (active, back), sems = (
        refs[:n_put],
        refs[n_put : n_put + 4],
        refs[n_put + 4 : 2 * n_put + 4],
        refs[2 * n_put + 4 : 2 * n_put + 6],
        refs[2 * n_put + 6 :],
    )
    copies = [put_half(pos_ref[1], x, o, sems[0].at[i]) for i, (x, o) in enumerate(zip(done, puts))]
    for c in copies:
        c.start()
    quarter = active.shape[0]
    at = pl.multiple_of(pos_ref[1] * quarter, quarter)
    grad_second, grad_first = rows_grads(at, first, second, grads_ref, k, rows_ref, active, back)
    halves = ((sum_first[...] + grad_first).astype(BF).T, (sum_second[...] + grad_second).astype(BF))
    for half, out16, out32 in zip(halves, outs[:2], outs[2:]):
        out16[...] = half
        out32[...] = half.astype(F32)
    for c in copies:
        c.wait()


def put_half(side, half, out, sem):
    n, m = half.shape
    if out.shape[0] == n:
        to = out.at[:, pl.ds(pl.multiple_of(side * m, m), m)]
    else:
        to = out.at[pl.ds(pl.multiple_of(side * n, n), n), :]
    return pltpu.make_async_copy(half, to, sem)


def finish_kernel(old, new, pos_ref, *refs):
    n = old + new
    halves, outs, scratch, sems = refs[:n], refs[n + old : 2 * n + old], refs[2 * n + old : -1], refs[-1]
    copies = [put_half(pos_ref[1], x, o, sems.at[old + i]) for i, (x, o) in enumerate(zip(halves[old:], outs[old:]))]
    for c in copies:
        c.start()
    for i in range(old):
        scratch[i][...] = halves[i][...].astype(F32)
        copies.append(put_half(1 - pos_ref[1], scratch[i], outs[i], sems.at[i]))
        copies[-1].start()
    for c in copies:
        c.wait()


def finish(pos, there, own, wholes, shapes):
    old, new = len(wholes), len(shapes)
    n = old + new
    return kernel(
        functools.partial(finish_kernel, old, new),
        "finish",
        [(w.shape, w.dtype) for w in wholes] + shapes,
        (*there, *own, *wholes),
        [*(pltpu.VMEM(x.shape, F32) for x in there), pltpu.SemaphoreType.DMA((n,))],
        pos=pos,
        hbm=range(n, n + old),
        hbm_out=range(n),
        aliases={n + i: i for i in range(old)},
    )


def gathered(
    states, goal_distance, goal_row, episode, state_first, state_second, goal_first, goal_second
):
    rows_dev, width = states.shape
    n_blk, n_rep, n_sub = (lax.axis_size(a) for a in ("blk", "rep", "sub"))
    owners = n_blk * n_sub
    slab = rows_dev // n_rep
    rows_all = owners * rows_dev
    hid, emb = state_second.shape
    b, s = lax.axis_index("blk"), lax.axis_index("sub")
    pos = jnp.stack([b, s]).astype(jnp.int32)
    quarter = hid // n_sub

    def across(x, k):
        return lax.ppermute(x, "blk", [(i, i ^ k) for i in range(n_blk)])

    def swap(x, axis):
        return lax.ppermute(x, axis, [(0, 1), (1, 0)])

    def after(x, *first):
        return lax.optimization_barrier((x, *first))[0]

    weights = (state_first, goal_first, state_second, goal_second)
    (pack,) = kernel(
        functools.partial(pack_kernel, n_rep, n_blk, n_sub),
        "pack",
        [((rows_dev + 16, width), BF)],
        (states, jnp.stack([goal_distance.reshape(rows_dev), goal_row, episode])),
        pos=pos,
        limit=4,
        flops=2**32,
    )
    got = {0: pack, 3: across(pack, 3)}
    held = weights
    part0 = forward(pack, held, rows_dev)
    got[1] = across(after(pack, part0), 1)
    got[2] = across(after(pack, got[3]), 2)
    there0 = swap(part0, "rep")
    part3 = forward(got[3], held, rows_dev)
    there3 = swap(part3, "rep")

    sums = {0: both(part0, there0)}
    sums[1] = across(after(sums[0], got[2]), 1)
    part2 = forward(after(got[2], sums[0]), held, rows_dev)
    there2 = swap(part2, "rep")
    sums[3] = both(part3, there3)

    side = ((rows_all // 2, width), BF)
    mine, other, goals_mine, pick, episodes = kernel(
        functools.partial(arrange_kernel, n_blk, n_rep, slab),
        "arrange",
        [side, side, side, ((rows_all // 2, rows_all), BF), ((1, rows_all // 2), F32)],
        (*(got[k] for k in range(n_blk)), *(swap(got[k], "sub") for k in range(n_blk))),
        [
            pltpu.VMEM((rows_all, width), BF),
            pltpu.VMEM((16, rows_all // 2), F32),
        ],
        pos=pos,
    )
    embedded = [sums[0], sums[1], part2, sums[3], after(there2, pick)]
    (grads_mine,) = kernel(
        functools.partial(contrast_kernel, n_blk, n_rep, slab, 4.0 / math.sqrt(emb)),
        "contrast",
        [((rows_all // 2, 2 * emb), BF)],
        (*embedded, *(swap(x, "sub") for x in embedded), episodes, pick),
        [pltpu.VMEM((rows_all // 2, emb), BF), pltpu.VMEM((rows_all, emb), BF)],
        pos=pos,
    )
    grads_other = swap(grads_mine, "sub")
    goals_other = swap(goals_mine, "sub")

    sf, gf, ss, gs = weights
    work = [pltpu.VMEM((quarter, rows_all // 2), BF), pltpu.VMEM((quarter, rows_all // 2), BF)]
    flops = 4 * rows_all * width * quarter
    sums_s2, sums_s1, sums_g2, sums_g1 = kernel(
        mine_kernel,
        "mine",
        [((quarter, emb), F32), ((quarter, width), F32)] * 2,
        (sf, gf, ss, gs, grads_mine, mine, goals_mine),
        work,
        pos=pos,
        flops=2 * flops,
    )
    halves = [(shape, kind) for kind in (BF, F32) for shape in ((width, quarter), (quarter, emb))]
    wholes = [((width, hid), F32), ((hid, emb), F32)]
    *state_halves, state_first_own, state_second_own = kernel(
        functools.partial(other_kernel, 0, 0),
        "other_state",
        halves,
        (sf, ss, grads_other, other, sums_s2, sums_s1),
        work,
        pos=pos,
        flops=flops,
    )
    state_there = [swap(x, "sub") for x in state_halves]
    *goal_halves, goal_first_own, goal_second_own, out0, out1 = kernel(
        functools.partial(other_kernel, 1, 2),
        "other_goal",
        halves + wholes,
        (gf, gs, grads_other, goals_other, sums_g2, sums_g1, state_first_own, state_second_own),
        work + [pltpu.SemaphoreType.DMA((2,))],
        pos=pos,
        flops=flops,
        hbm_out=(4, 5),
    )
    goal_there = [swap(x, "sub") for x in goal_halves]
    out0, out1, out2, out3 = finish(pos, state_there, (goal_first_own, goal_second_own), (out0, out1), wholes)
    out2, out3 = finish(pos, goal_there, (), (out2, out3), [])
    return (out0, out1, out2, out3)


def silu_slope(hidden):
    sig = jax.nn.sigmoid(hidden)
    return sig * (1.0 + hidden * (1.0 - sig))


def encoder_grads(rows_in, hidden, active, second, emb_grad):
    grad_second = jnp.einsum("nh,ne->he", active, emb_grad, preferred_element_type=jnp.float32)
    back = jnp.einsum("ne,he->nh", emb_grad, second, preferred_element_type=jnp.float32)
    back_rows = (back * silu_slope(hidden)).astype(jnp.bfloat16)
    grad_first = jnp.einsum("ns,nh->sh", rows_in, back_rows, preferred_element_type=jnp.float32)
    return (grad_first, grad_second)


def exchanged(
    states, goal_distance, goal_row, episode, state_first, state_second, goal_first, goal_second
):
    rows_dev, width = states.shape
    owners = lax.axis_size(("blk", "sub"))
    position = lax.axis_index(("blk", "sub"))
    capacity = 4 * rows_dev // owners
    target = (position + goal_distance[:, 0]) % owners
    onehot = (target[:, None] == jnp.arange(owners, dtype=jnp.int32)[None, :]).astype(jnp.int32)
    slot_rank = jnp.sum((jnp.cumsum(onehot, axis=0) - onehot) * onehot, axis=1)
    requests = jnp.zeros((owners, capacity), jnp.int32).at[target, slot_rank].set(goal_row)
    wanted = lax.all_to_all(requests, ("blk", "sub"), split_axis=0, concat_axis=0, tiled=True)
    fetched = jnp.take(states, wanted.reshape(-1), axis=0).reshape(wanted.shape + (width,))
    replies = lax.all_to_all(fetched, ("blk", "sub"), split_axis=0, concat_axis=0, tiled=True)
    goal_states = jnp.take(
        replies.reshape(owners * capacity, width), target * capacity + slot_rank, axis=0
    )
    slab_rows = rows_dev // lax.axis_size("rep")
    state_hidden = jnp.dot(states, state_first, preferred_element_type=jnp.float32)
    state_active = jax.nn.silu(state_hidden).astype(jnp.bfloat16)
    goal_hidden = jnp.dot(goal_states, goal_first, preferred_element_type=jnp.float32)
    goal_active = jax.nn.silu(goal_hidden).astype(jnp.bfloat16)
    phi = lax.psum_scatter(
        jnp.dot(state_active, state_second, preferred_element_type=jnp.float32),
        "rep",
        scatter_dimension=0,
        tiled=True,
    ).astype(jnp.bfloat16)
    psi = lax.psum_scatter(
        jnp.dot(goal_active, goal_second, preferred_element_type=jnp.float32),
        "rep",
        scatter_dimension=0,
        tiled=True,
    ).astype(jnp.bfloat16)
    episode_own = lax.dynamic_slice_in_dim(episode, lax.axis_index("rep") * slab_rows, slab_rows, 0)
    psi_all, episode_all = (
        lax.all_gather(psi, "blk", axis=0, tiled=True),
        lax.all_gather(episode_own, "blk", axis=0, tiled=True),
    )
    batch_rows = psi_all.shape[0]
    logit_scale = 4.0 / math.sqrt(psi.shape[1])
    own_rows = lax.axis_index("blk") * slab_rows + jnp.arange(slab_rows, dtype=jnp.int32)
    columns = jnp.arange(batch_rows, dtype=jnp.int32)
    diagonal = own_rows[:, None] == columns[None, :]
    excluded = (episode_own[:, None] == episode_all[None, :]) & ~diagonal
    scores = jnp.einsum("ie,je->ij", phi, psi_all, preferred_element_type=jnp.float32) * logit_scale
    exponent = jnp.where(excluded, 0.0, jnp.exp(scores))
    totals = jnp.sum(exponent, axis=1)
    delta = (exponent / totals[:, None] - diagonal.astype(jnp.float32)).astype(jnp.bfloat16)
    phi_grad = (jnp.dot(delta, psi_all, preferred_element_type=jnp.float32) * logit_scale).astype(
        jnp.bfloat16
    )
    psi_grad = lax.psum_scatter(
        jnp.einsum("ij,ie->je", delta, phi, preferred_element_type=jnp.float32) * logit_scale,
        "blk",
        scatter_dimension=0,
        tiled=True,
    ).astype(jnp.bfloat16)
    phi_full, psi_full = (
        lax.all_gather(phi_grad, "rep", axis=0, tiled=True),
        lax.all_gather(psi_grad, "rep", axis=0, tiled=True),
    )
    state_parts = encoder_grads(states, state_hidden, state_active, state_second, phi_full)
    goal_parts = encoder_grads(goal_states, goal_hidden, goal_active, goal_second, psi_full)
    summed = lax.psum(
        (state_parts[0], state_parts[1], goal_parts[0], goal_parts[1]), ("blk", "sub")
    )
    return (summed[0], summed[1], summed[2], summed[3])


def solution(mesh):
    in_specs = (
        P(("grp", "blk", "sub"), None),
        P(("grp", "blk", "sub"), None),
        P(("grp", "blk", "sub")),
        P(("grp", "blk", "sub")),
        P(None, "rep"),
        P("rep", None),
        P(None, "rep"),
        P("rep", None),
    )
    out_specs = (P("grp", "rep"), P(("grp", "rep"), None), P("grp", "rep"), P(("grp", "rep"), None))
    shape = mesh.shape
    local = gathered if (shape["blk"], shape["rep"], shape["sub"]) == (4, 2, 2) else exchanged
    return jax.shard_map(local, mesh=mesh, in_specs=in_specs, out_specs=out_specs, check_vma=False)
```

```python
import functools
import math

import jax
import jax.numpy as jnp
from jax import lax
from jax.experimental import pallas as pl
from jax.experimental.pallas import tpu as pltpu
from jax.sharding import PartitionSpec as P

BF = jnp.bfloat16
F32 = jnp.float32
MIB = 1024 * 1024


def dot(a, b):
    return jnp.dot(a, b, preferred_element_type=F32)


def sigmoid(v):
    return 0.5 * jnp.tanh(0.5 * v) + 0.5


HBM = pl.BlockSpec(memory_space=pltpu.HBM)
VMEM = pl.BlockSpec(memory_space=pltpu.VMEM)
SMEM = pl.BlockSpec(memory_space=pltpu.SMEM)


def kernel(body, name, outs, args, scratch=(), limit=16, pos=False, flops=0, hbm=(), hbm_out=(), aliases={}):
    specs = [HBM if i in hbm else VMEM for i in range(len(args))]
    if pos:
        inner = body

        def body(*refs):
            inner((lax.axis_index("blk"), lax.axis_index("sub")), *refs)

    return pl.pallas_call(
        body,
        in_specs=specs,
        out_specs=[HBM if i in hbm_out else VMEM for i in range(len(outs))],
        out_shape=[jax.ShapeDtypeStruct(shape, dtype) for shape, dtype in outs],
        scratch_shapes=scratch,
        input_output_aliases=aliases,
        compiler_params=pltpu.CompilerParams(vmem_limit_bytes=int(limit * MIB)),
        cost_estimate=pl.CostEstimate(flops=flops, bytes_accessed=0, transcendentals=0),
        name=name,
    )(*args)


def encode(x_ref, weights, out_ref, active, ready=lambda i: None):
    emb = weights[2].shape[1]
    for k in range(2):
        first, second = weights[k], weights[2 + k]
        ready(k)
        for c in range(0, active.shape[1], 512):
            hidden = dot(x_ref[...], first[:, c : c + 512])
            active[:, c : c + 512] = (hidden * sigmoid(hidden)).astype(BF)
        ready(2 + k)
        out_ref[:, k * emb : (k + 1) * emb] = dot(active[...], second[...]).astype(BF)


def pack_kernel(n_rep, n_blk, n_sub, pos, x_ref, own_ref, pack_ref):
    rows = x_ref.shape[0]
    slab = rows // n_rep

    def bits(n):
        return n.bit_length() - 1

    owner = (pos[0] * n_sub + pos[1] + own_ref[0:1, :]) & (n_blk * n_sub - 1)
    place = own_ref[1:2, :]
    batch = ((owner & (n_sub - 1)) << bits(n_rep)) + (place >> bits(slab))
    goal = (((batch << bits(n_blk)) + (owner >> bits(n_sub))) << bits(slab)) + (place & (slab - 1))
    digits = (goal >> 8, goal & 255, own_ref[2:3, :])
    table = jnp.concatenate([d.astype(F32) for d in digits] + [jnp.zeros((13, rows), F32)], axis=0).astype(BF)
    pack_ref[:rows, :] = x_ref[...]
    pack_ref[rows:, :] = table


def forward_kernel(x_ref, *refs):
    encode(x_ref.at[: refs[4].shape[0]], refs[:4], refs[4], refs[5])


def forward(x, weights, rows):
    hid, emb = weights[2].shape
    return kernel(
        forward_kernel,
        "forward",
        [((rows, 2 * emb), BF)],
        (x, *weights),
        [pltpu.VMEM((rows, hid), BF)],
        limit=8,
    )[0]


def add_kernel(a_ref, b_ref, out_ref):
    out_ref[...] = (a_ref[...].astype(F32) + b_ref[...].astype(F32)).astype(BF)


def both(part, there):
    return kernel(add_kernel, "both", [(part.shape, BF)], (part, there), limit=4)[0]


def place_blocks(pos, blocks, put, n_blk, n_rep, slab):
    for k, block in enumerate(blocks):
        at = jnp.bitwise_xor(pos[0], k)
        for r in range(n_rep):
            off = (r * n_blk + at) * slab
            put(pl.multiple_of(off, slab), block[r * slab : (r + 1) * slab, :])


def column(row):
    return jnp.broadcast_to(row, (128, row.shape[1])).T[:, :1]


def arrange_kernel(n_blk, n_rep, slab, pos, *refs):
    mine, other = refs[:n_blk], refs[n_blk : 2 * n_blk]
    rows_mine, rows_other, goals_ref, pick_ref, ep_ref, both_sides, meta = refs[2 * n_blk :]
    half = rows_mine.shape[0]
    rows = 2 * half
    batch = n_blk * slab
    for i, (blocks, to) in enumerate(((mine, rows_mine), (other, rows_other))):

        def put(off, value, i=i, to=to):
            to[pl.ds(off, slab), :] = value
            both_sides[pl.ds(i * half + off, slab), :] = value

        place_blocks(pos, blocks, put, n_blk, n_rep, slab)
    for k, block in enumerate(mine):
        at = jnp.bitwise_xor(pos[0], k)
        for r in range(n_rep):
            off = pl.multiple_of((r * n_blk + at) * slab, slab)
            meta[:, pl.ds(off, slab)] = block[n_rep * slab :, r * slab : (r + 1) * slab].astype(F32)
    ep_ref[...] = meta[2:3, :]
    for r in range(n_rep):
        own = slice(r * batch, (r + 1) * batch)
        goal = column(meta[0:1, own] * 256.0 + meta[1:2, own]).astype(jnp.int32) + pos[1] * half
        goal = jnp.where(goal >= rows, goal - rows, goal)
        pick_ref[own, :] = jnp.where(
            goal == lax.broadcasted_iota(jnp.int32, (batch, rows), 1), 1.0, 0.0
        ).astype(BF)
    goals_ref[...] = dot(pick_ref[...], both_sides[...]).astype(BF)


def contrast_kernel(n_blk, n_rep, slab, scale, pos, *refs):
    n = n_blk + 1
    mine, other, ep_ref, pick_ref = refs[:n], refs[n : 2 * n], refs[2 * n], refs[2 * n + 1]
    grads_ref, phi_all, psi_all = refs[2 * n + 2 :]
    half, emb = phi_all.shape
    batch = n_blk * slab
    last = n_blk - 2

    def sums(parts):
        blocks = list(parts[:n_blk])
        blocks[last] = (parts[last][...].astype(F32) + parts[n_blk][...].astype(F32)).astype(BF)
        return blocks

    def put_mine(off, value):
        phi_all[pl.ds(off, slab), :] = value[:, :emb]
        psi_all[pl.ds(off, slab), :] = value[:, emb:]

    def put_other(off, value):
        psi_all[pl.ds(half + off, slab), :] = value[:, emb:]

    place_blocks(pos, sums(mine), put_mine, n_blk, n_rep, slab)
    place_blocks(pos, sums(other), put_other, n_blk, n_rep, slab)
    diagonal = lax.broadcasted_iota(jnp.int32, (batch, batch), 0) == lax.broadcasted_iota(
        jnp.int32, (batch, batch), 1
    )
    psi_all[:half, :] = dot(pick_ref[...], psi_all[...]).astype(BF)
    for r in range(n_rep):
        own = slice(r * batch, (r + 1) * batch)
        ep_row = ep_ref[:, own]
        psi = psi_all[own, :]
        phi = phi_all[own, :]
        scores = lax.dot_general(phi, psi, (((1,), (1,)), ((), ())), preferred_element_type=F32)
        kept = (column(ep_row) != ep_row) | diagonal
        exponent = jnp.where(kept, jnp.exp(scores * scale), 0.0)
        totals = jnp.sum(exponent, axis=1, keepdims=True)
        power = jnp.where(totals > 1.0, 2.0**-32, 1.0)
        shares = (exponent * power) * (1.0 / (totals * power))
        delta = jnp.where(diagonal, shares - 1.0, shares).astype(BF)
        grads_ref[own, :emb] = (dot(delta, psi) * scale).astype(BF)
        grads_ref[own, emb:] = (dot(delta.T, phi) * scale).astype(BF)


def rows_grads(at, first_ref, second_ref, grads_ref, k, rows_ref, active, back):
    quarter, rows = active.shape
    emb = second_ref.shape[1]
    first_t = first_ref[:, pl.ds(at, quarter)].T
    second = second_ref[pl.ds(at, quarter), :]
    grad = grads_ref[:, k * emb : (k + 1) * emb]
    chunk = 256
    for c in range(0, rows, chunk):
        cols = slice(c, c + chunk)
        hidden = dot(first_t, rows_ref[cols, :].T)
        sig = sigmoid(hidden)
        act = hidden * sig
        active[:, cols] = act.astype(BF)
        slope = sig + act * (1.0 - sig)
        back[:, cols] = (dot(second, grad[cols, :].T) * slope).astype(BF)
    return dot(active[...], grad), dot(back[...], rows_ref[...])


def mine_kernel(pos, sf, gf, ss, gs, grads_ref, rows_ref, goals_ref, *refs):
    outs, (active, back) = refs[:4], refs[4:]
    quarter = active.shape[0]
    at = pl.multiple_of(pos[1] * quarter, quarter)
    outs[0][...], outs[1][...] = rows_grads(at, sf, ss, grads_ref, 0, rows_ref, active, back)
    outs[2][...], outs[3][...] = rows_grads(at, gf, gs, grads_ref, 1, goals_ref, active, back)


def other_kernel(k, n_put, pos, first, second, grads_ref, rows_ref, sum_second, sum_first, *refs):
    done, outs, puts, (active, back), sems = (
        refs[:n_put],
        refs[n_put : n_put + 4],
        refs[n_put + 4 : 2 * n_put + 4],
        refs[2 * n_put + 4 : 2 * n_put + 6],
        refs[2 * n_put + 6 :],
    )
    copies = [put_half(pos[1], x, o, sems[0].at[i]) for i, (x, o) in enumerate(zip(done, puts))]
    for c in copies:
        c.start()
    quarter = active.shape[0]
    at = pl.multiple_of(pos[1] * quarter, quarter)
    grad_second, grad_first = rows_grads(at, first, second, grads_ref, k, rows_ref, active, back)
    halves = ((sum_first[...] + grad_first).astype(BF).T, (sum_second[...] + grad_second).astype(BF))
    for half, out16, out32 in zip(halves, outs[:2], outs[2:]):
        out16[...] = half
        out32[...] = half.astype(F32)
    for c in copies:
        c.wait()


def put_half(side, half, out, sem):
    n, m = half.shape
    if out.shape[0] == n:
        to = out.at[:, pl.ds(pl.multiple_of(side * m, m), m)]
    else:
        to = out.at[pl.ds(pl.multiple_of(side * n, n), n), :]
    return pltpu.make_async_copy(half, to, sem)


def finish_kernel(old, new, pos, *refs):
    n = old + new
    halves, outs, scratch, sems = refs[:n], refs[n + old : 2 * n + old], refs[2 * n + old : -1], refs[-1]
    copies = [put_half(pos[1], x, o, sems.at[old + i]) for i, (x, o) in enumerate(zip(halves[old:], outs[old:]))]
    for c in copies:
        c.start()
    for i in range(old):
        scratch[i][...] = halves[i][...].astype(F32)
        copies.append(put_half(1 - pos[1], scratch[i], outs[i], sems.at[i]))
        copies[-1].start()
    for c in copies:
        c.wait()


def finish(there, own, wholes, shapes):
    old, new = len(wholes), len(shapes)
    n = old + new
    return kernel(
        functools.partial(finish_kernel, old, new),
        "finish",
        [(w.shape, w.dtype) for w in wholes] + shapes,
        (*there, *own, *wholes),
        [*(pltpu.VMEM(x.shape, F32) for x in there), pltpu.SemaphoreType.DMA((n,))],
        pos=True,
        hbm=range(n, n + old),
        hbm_out=range(n),
        aliases={n + i: i for i in range(old)},
    )


def gathered(
    states, goal_distance, goal_row, episode, state_first, state_second, goal_first, goal_second
):
    rows_dev, width = states.shape
    n_blk, n_rep, n_sub = (lax.axis_size(a) for a in ("blk", "rep", "sub"))
    slab = rows_dev // n_rep
    rows_all = n_blk * n_sub * rows_dev
    hid, emb = state_second.shape
    quarter = hid // n_sub

    def across(x, k):
        return lax.ppermute(x, "blk", [(i, i ^ k) for i in range(n_blk)])

    def swap(x, axis):
        return lax.ppermute(x, axis, [(0, 1), (1, 0)])

    def after(x, *first):
        return lax.optimization_barrier((x, *first))[0]

    weights = (state_first, goal_first, state_second, goal_second)
    (pack,) = kernel(
        functools.partial(pack_kernel, n_rep, n_blk, n_sub),
        "pack",
        [((rows_dev + 16, width), BF)],
        (states, jnp.stack([goal_distance.reshape(rows_dev), goal_row, episode])),
        pos=True,
        limit=4,
        flops=2**32,
    )
    got = {0: pack, 3: across(pack, 3)}
    held = weights
    part0 = forward(pack, held, rows_dev)
    got[1] = across(after(pack, part0), 1)
    got[2] = across(after(pack, got[3]), 2)
    there0 = swap(part0, "rep")
    part3 = forward(got[3], held, rows_dev)
    there3 = swap(part3, "rep")

    sums = {0: both(part0, there0)}
    sums[1] = across(after(sums[0], got[2]), 1)
    part2 = forward(after(got[2], sums[0]), held, rows_dev)
    there2 = swap(part2, "rep")
    sums[3] = both(part3, there3)

    side = ((rows_all // 2, width), BF)
    mine, other, goals_mine, pick, episodes = kernel(
        functools.partial(arrange_kernel, n_blk, n_rep, slab),
        "arrange",
        [side, side, side, ((rows_all // 2, rows_all), BF), ((1, rows_all // 2), F32)],
        (*(got[k] for k in range(n_blk)), *(swap(got[k], "sub") for k in range(n_blk))),
        [
            pltpu.VMEM((rows_all, width), BF),
            pltpu.VMEM((16, rows_all // 2), F32),
        ],
        pos=True,
    )
    embedded = [sums[0], sums[1], part2, sums[3], after(there2, pick)]
    (grads_mine,) = kernel(
        functools.partial(contrast_kernel, n_blk, n_rep, slab, 4.0 / math.sqrt(emb)),
        "contrast",
        [((rows_all // 2, 2 * emb), BF)],
        (*embedded, *(swap(x, "sub") for x in embedded), episodes, pick),
        [pltpu.VMEM((rows_all // 2, emb), BF), pltpu.VMEM((rows_all, emb), BF)],
        pos=True,
    )
    grads_other = swap(grads_mine, "sub")
    goals_other = swap(goals_mine, "sub")

    sf, gf, ss, gs = weights
    work = [pltpu.VMEM((quarter, rows_all // 2), BF), pltpu.VMEM((quarter, rows_all // 2), BF)]
    flops = 4 * rows_all * width * quarter
    sums_s2, sums_s1, sums_g2, sums_g1 = kernel(
        mine_kernel,
        "mine",
        [((quarter, emb), F32), ((quarter, width), F32)] * 2,
        (sf, gf, ss, gs, grads_mine, mine, goals_mine),
        work,
        pos=True,
        flops=2 * flops,
    )
    halves = [(shape, kind) for kind in (BF, F32) for shape in ((width, quarter), (quarter, emb))]
    wholes = [((width, hid), F32), ((hid, emb), F32)]
    *state_halves, state_first_own, state_second_own = kernel(
        functools.partial(other_kernel, 0, 0),
        "other_state",
        halves,
        (sf, ss, grads_other, other, sums_s2, sums_s1),
        work,
        pos=True,
        flops=flops,
    )
    state_there = [swap(x, "sub") for x in state_halves]
    *goal_halves, goal_first_own, goal_second_own, out0, out1 = kernel(
        functools.partial(other_kernel, 1, 2),
        "other_goal",
        halves + wholes,
        (gf, gs, grads_other, goals_other, sums_g2, sums_g1, state_first_own, state_second_own),
        work + [pltpu.SemaphoreType.DMA((2,))],
        pos=True,
        flops=flops,
        hbm_out=(4, 5),
    )
    goal_there = [swap(x, "sub") for x in goal_halves]
    out0, out1, out2, out3 = finish(state_there, (goal_first_own, goal_second_own), (out0, out1), wholes)
    out2, out3 = finish(goal_there, (), (out2, out3), [])
    return (out0, out1, out2, out3)


def silu_slope(hidden):
    sig = jax.nn.sigmoid(hidden)
    return sig * (1.0 + hidden * (1.0 - sig))


def encoder_grads(rows_in, hidden, active, second, emb_grad):
    grad_second = jnp.einsum("nh,ne->he", active, emb_grad, preferred_element_type=jnp.float32)
    back = jnp.einsum("ne,he->nh", emb_grad, second, preferred_element_type=jnp.float32)
    back_rows = (back * silu_slope(hidden)).astype(jnp.bfloat16)
    grad_first = jnp.einsum("ns,nh->sh", rows_in, back_rows, preferred_element_type=jnp.float32)
    return (grad_first, grad_second)


def exchanged(
    states, goal_distance, goal_row, episode, state_first, state_second, goal_first, goal_second
):
    rows_dev, width = states.shape
    owners = lax.axis_size(("blk", "sub"))
    position = lax.axis_index(("blk", "sub"))
    capacity = 4 * rows_dev // owners
    target = (position + goal_distance[:, 0]) % owners
    onehot = (target[:, None] == jnp.arange(owners, dtype=jnp.int32)[None, :]).astype(jnp.int32)
    slot_rank = jnp.sum((jnp.cumsum(onehot, axis=0) - onehot) * onehot, axis=1)
    requests = jnp.zeros((owners, capacity), jnp.int32).at[target, slot_rank].set(goal_row)
    wanted = lax.all_to_all(requests, ("blk", "sub"), split_axis=0, concat_axis=0, tiled=True)
    fetched = jnp.take(states, wanted.reshape(-1), axis=0).reshape(wanted.shape + (width,))
    replies = lax.all_to_all(fetched, ("blk", "sub"), split_axis=0, concat_axis=0, tiled=True)
    goal_states = jnp.take(
        replies.reshape(owners * capacity, width), target * capacity + slot_rank, axis=0
    )
    slab_rows = rows_dev // lax.axis_size("rep")
    state_hidden = jnp.dot(states, state_first, preferred_element_type=jnp.float32)
    state_active = jax.nn.silu(state_hidden).astype(jnp.bfloat16)
    goal_hidden = jnp.dot(goal_states, goal_first, preferred_element_type=jnp.float32)
    goal_active = jax.nn.silu(goal_hidden).astype(jnp.bfloat16)
    phi = lax.psum_scatter(
        jnp.dot(state_active, state_second, preferred_element_type=jnp.float32),
        "rep",
        scatter_dimension=0,
        tiled=True,
    ).astype(jnp.bfloat16)
    psi = lax.psum_scatter(
        jnp.dot(goal_active, goal_second, preferred_element_type=jnp.float32),
        "rep",
        scatter_dimension=0,
        tiled=True,
    ).astype(jnp.bfloat16)
    episode_own = lax.dynamic_slice_in_dim(episode, lax.axis_index("rep") * slab_rows, slab_rows, 0)
    psi_all, episode_all = (
        lax.all_gather(psi, "blk", axis=0, tiled=True),
        lax.all_gather(episode_own, "blk", axis=0, tiled=True),
    )
    batch_rows = psi_all.shape[0]
    logit_scale = 4.0 / math.sqrt(psi.shape[1])
    own_rows = lax.axis_index("blk") * slab_rows + jnp.arange(slab_rows, dtype=jnp.int32)
    columns = jnp.arange(batch_rows, dtype=jnp.int32)
    diagonal = own_rows[:, None] == columns[None, :]
    excluded = (episode_own[:, None] == episode_all[None, :]) & ~diagonal
    scores = jnp.einsum("ie,je->ij", phi, psi_all, preferred_element_type=jnp.float32) * logit_scale
    exponent = jnp.where(excluded, 0.0, jnp.exp(scores))
    totals = jnp.sum(exponent, axis=1)
    delta = (exponent / totals[:, None] - diagonal.astype(jnp.float32)).astype(jnp.bfloat16)
    phi_grad = (jnp.dot(delta, psi_all, preferred_element_type=jnp.float32) * logit_scale).astype(
        jnp.bfloat16
    )
    psi_grad = lax.psum_scatter(
        jnp.einsum("ij,ie->je", delta, phi, preferred_element_type=jnp.float32) * logit_scale,
        "blk",
        scatter_dimension=0,
        tiled=True,
    ).astype(jnp.bfloat16)
    phi_full, psi_full = (
        lax.all_gather(phi_grad, "rep", axis=0, tiled=True),
        lax.all_gather(psi_grad, "rep", axis=0, tiled=True),
    )
    state_parts = encoder_grads(states, state_hidden, state_active, state_second, phi_full)
    goal_parts = encoder_grads(goal_states, goal_hidden, goal_active, goal_second, psi_full)
    summed = lax.psum(
        (state_parts[0], state_parts[1], goal_parts[0], goal_parts[1]), ("blk", "sub")
    )
    return (summed[0], summed[1], summed[2], summed[3])


def solution(mesh):
    in_specs = (
        P(("grp", "blk", "sub"), None),
        P(("grp", "blk", "sub"), None),
        P(("grp", "blk", "sub")),
        P(("grp", "blk", "sub")),
        P(None, "rep"),
        P("rep", None),
        P(None, "rep"),
        P("rep", None),
    )
    out_specs = (P("grp", "rep"), P(("grp", "rep"), None), P("grp", "rep"), P(("grp", "rep"), None))
    shape = mesh.shape
    local = gathered if (shape["blk"], shape["rep"], shape["sub"]) == (4, 2, 2) else exchanged
    return jax.shard_map(local, mesh=mesh, in_specs=in_specs, out_specs=out_specs, check_vma=False)
```

```python
import functools
import math

import jax
import jax.numpy as jnp
from jax import lax
from jax.experimental import pallas as pl
from jax.experimental.pallas import tpu as pltpu
from jax.sharding import PartitionSpec as P

BF = jnp.bfloat16
F32 = jnp.float32
MIB = 1024 * 1024


def dot(a, b):
    return jnp.dot(a, b, preferred_element_type=F32)


def sigmoid(v):
    return 0.5 * jnp.tanh(0.5 * v) + 0.5


HBM = pl.BlockSpec(memory_space=pltpu.HBM)
VMEM = pl.BlockSpec(memory_space=pltpu.VMEM)
SMEM = pl.BlockSpec(memory_space=pltpu.SMEM)


def kernel(body, name, outs, args, scratch=(), limit=16, pos=False, flops=0, hbm=(), hbm_out=(), aliases={}):
    specs = [HBM if i in hbm else VMEM for i in range(len(args))]
    if pos:
        inner = body

        def body(*refs):
            inner((lax.axis_index("blk"), lax.axis_index("sub")), *refs)

    return pl.pallas_call(
        body,
        in_specs=specs,
        out_specs=[HBM if i in hbm_out else VMEM for i in range(len(outs))],
        out_shape=[jax.ShapeDtypeStruct(shape, dtype) for shape, dtype in outs],
        scratch_shapes=scratch,
        input_output_aliases=aliases,
        compiler_params=pltpu.CompilerParams(vmem_limit_bytes=int(limit * MIB)),
        cost_estimate=pl.CostEstimate(flops=flops, bytes_accessed=0, transcendentals=0),
        name=name,
    )(*args)


def encode(x_ref, weights, out_ref, active, ready=lambda i: None):
    emb = weights[2].shape[1]
    for k in range(2):
        first, second = weights[k], weights[2 + k]
        ready(k)
        for c in range(0, active.shape[1], 512):
            hidden = dot(x_ref[...], first[:, c : c + 512])
            active[:, c : c + 512] = (hidden * sigmoid(hidden)).astype(BF)
        ready(2 + k)
        out_ref[:, k * emb : (k + 1) * emb] = dot(active[...], second[...]).astype(BF)


def pack_kernel(n_blk, n_sub, pos, x_ref, own_ref, pack_ref):
    rows = x_ref.shape[0]
    owner = (pos[0] * n_sub + pos[1] + own_ref[0:1, :]) & (n_blk * n_sub - 1)
    digits = (owner, own_ref[1:2, :], own_ref[2:3, :])
    table = jnp.concatenate([d.astype(F32) for d in digits] + [jnp.zeros((13, rows), F32)], axis=0)
    pack_ref[:rows, :] = x_ref[...]
    pack_ref[rows:, :] = table.astype(BF)


def forward_kernel(x_ref, *refs):
    encode(x_ref.at[: refs[4].shape[0]], refs[:4], refs[4], refs[5])


def forward(x, weights, rows):
    hid, emb = weights[2].shape
    return kernel(
        forward_kernel,
        "forward",
        [((rows, 2 * emb), BF)],
        (x, *weights),
        [pltpu.VMEM((rows, hid), BF)],
        limit=8,
    )[0]


def add_kernel(a_ref, b_ref, out_ref):
    out_ref[...] = (a_ref[...].astype(F32) + b_ref[...].astype(F32)).astype(BF)


def both(part, there):
    return kernel(add_kernel, "both", [(part.shape, BF)], (part, there), limit=4)[0]


def place_blocks(pos, blocks, put, n_blk, n_rep, slab):
    for k, block in enumerate(blocks):
        at = jnp.bitwise_xor(pos[0], k)
        for r in range(n_rep):
            off = (r * n_blk + at) * slab
            put(pl.multiple_of(off, slab), block[r * slab : (r + 1) * slab, :])


def column(row):
    return jnp.broadcast_to(row, (128, row.shape[1])).T[:, :1]


def place_in_turn(k, n_blk):
    return -k & (n_blk - 1)


def arrange_kernel(n_blk, n_rep, slab, pos, *refs):
    mine, other = refs[:n_blk], refs[n_blk : 2 * n_blk]
    rows_mine, rows_other, goals_ref, pick_ref, ep_ref, both_sides, meta = refs[2 * n_blk :]
    rows = both_sides.shape[0]
    batch, rows_dev = n_blk * slab, n_rep * slab
    for i, (blocks, to) in enumerate(((mine, rows_mine), (other, rows_other))):

        def put(off, value, to=to):
            to[pl.ds(off, slab), :] = value

        place_blocks(pos, blocks, put, n_blk, n_rep, slab)
        for k, block in enumerate(blocks):
            at = (i * n_blk + place_in_turn(k, n_blk)) * rows_dev
            both_sides[at : at + rows_dev, :] = block[:rows_dev, :]
    for k, block in enumerate(mine):
        at = jnp.bitwise_xor(pos[0], k)
        for r in range(n_rep):
            off = pl.multiple_of((r * n_blk + at) * slab, slab)
            meta[:, pl.ds(off, slab)] = block[rows_dev:, r * slab : (r + 1) * slab].astype(F32)
    ep_ref[...] = meta[2:3, :]
    for r in range(n_rep):
        own = slice(r * batch, (r + 1) * batch)
        owner, place = meta[0:1, own].astype(jnp.int32), meta[1:2, own].astype(jnp.int32)
        side = (owner & 1) ^ pos[1]
        column_of = (side * n_blk + place_in_turn((owner >> 1) ^ pos[0], n_blk)) * rows_dev + place
        goal = column(column_of.astype(F32)).astype(jnp.int32)
        pick_ref[own, :] = jnp.where(
            goal == lax.broadcasted_iota(jnp.int32, (batch, rows), 1), 1.0, 0.0
        ).astype(BF)
    goals_ref[...] = dot(pick_ref[...], both_sides[...]).astype(BF)


def gather_kernel(n_blk, n_rep, slab, pos, *refs):
    mine, extra, other, pick_ref = refs[:n_blk], refs[n_blk], refs[n_blk + 1 : n_blk + 3], refs[n_blk + 3]
    phi_ref, psi_ref, early = refs[n_blk + 4 :]
    emb = phi_ref.shape[1]
    rows_dev = n_rep * slab
    blocks = list(mine)
    blocks[n_blk - 2] = (mine[n_blk - 2][...].astype(F32) + extra[...].astype(F32)).astype(BF)

    def put(off, value):
        phi_ref[pl.ds(off, slab), :] = value[:, :emb]

    place_blocks(pos, blocks, put, n_blk, n_rep, slab)
    for k, block in enumerate(blocks):
        at = place_in_turn(k, n_blk) * rows_dev
        early[at : at + rows_dev, :] = block[:, emb:]
    for i, block in enumerate(other):
        at = (n_blk + i) * rows_dev
        early[at : at + rows_dev, :] = block[:, emb:]
    psi_ref[...] = dot(pick_ref[:, : early.shape[0]], early[...])


def contrast_kernel(n_rep, scale, phi_ref, psi_ref, part_ref, there_ref, sums_ref, ep_ref, pick_ref, grads_ref, late, psi_all):
    half, emb = phi_ref.shape
    batch = half // n_rep
    rows_dev = sums_ref.shape[0]
    late[:rows_dev, :] = (part_ref[:, emb:].astype(F32) + there_ref[:, emb:].astype(F32)).astype(BF)
    late[rows_dev:, :] = sums_ref[:, emb:]
    psi_all[...] = (psi_ref[...] + dot(pick_ref[:, pick_ref.shape[1] - 2 * rows_dev :], late[...])).astype(BF)
    diagonal = lax.broadcasted_iota(jnp.int32, (batch, batch), 0) == lax.broadcasted_iota(
        jnp.int32, (batch, batch), 1
    )
    for r in range(n_rep):
        own = slice(r * batch, (r + 1) * batch)
        ep_row = ep_ref[:, own]
        psi = psi_all[own, :]
        phi = phi_ref[own, :]
        scores = lax.dot_general(phi, psi, (((1,), (1,)), ((), ())), preferred_element_type=F32)
        kept = (column(ep_row) != ep_row) | diagonal
        exponent = jnp.where(kept, jnp.exp(scores * scale), 0.0)
        totals = jnp.sum(exponent, axis=1, keepdims=True)
        power = jnp.where(totals > 1.0, 2.0**-32, 1.0)
        shares = (exponent * power) * (1.0 / (totals * power))
        delta = jnp.where(diagonal, shares - 1.0, shares).astype(BF)
        grads_ref[own, :emb] = (dot(delta, psi) * scale).astype(BF)
        grads_ref[own, emb:] = (dot(delta.T, phi) * scale).astype(BF)


def rows_grads(at, first_ref, second_ref, grads_ref, k, rows_ref, active, back):
    quarter, rows = active.shape
    emb = second_ref.shape[1]
    first_t = first_ref[:, pl.ds(at, quarter)].T
    second = second_ref[pl.ds(at, quarter), :]
    grad = grads_ref[:, k * emb : (k + 1) * emb]
    chunk = 256
    for c in range(0, rows, chunk):
        cols = slice(c, c + chunk)
        hidden = dot(first_t, rows_ref[cols, :].T)
        sig = sigmoid(hidden)
        act = hidden * sig
        active[:, cols] = act.astype(BF)
        slope = sig + act * (1.0 - sig)
        back[:, cols] = (dot(second, grad[cols, :].T) * slope).astype(BF)
    return dot(active[...], grad), dot(back[...], rows_ref[...])


def hidden_kernel(pos, sf, gf, rows_ref, goals_ref, *outs):
    quarter, rows = outs[0].shape
    at = pl.multiple_of(pos[1] * quarter, quarter)
    for k, (first, x_ref) in enumerate(((sf, rows_ref), (gf, goals_ref))):
        first_t = first[:, pl.ds(at, quarter)].T
        for c in range(0, rows, 256):
            cols = slice(c, c + 256)
            hidden = dot(first_t, x_ref[cols, :].T)
            sig = sigmoid(hidden)
            act = hidden * sig
            outs[2 * k][:, cols] = act.astype(BF)
            outs[2 * k + 1][:, cols] = (sig + act * (1.0 - sig)).astype(BF)


def mine_kernel(pos, ss, gs, grads_ref, rows_ref, goals_ref, *refs):
    hidden, outs, back = refs[:4], refs[4:8], refs[8]
    quarter, rows = back.shape
    emb = ss.shape[1]
    at = pl.multiple_of(pos[1] * quarter, quarter)
    for k, (second_ref, x_ref) in enumerate(((ss, rows_ref), (gs, goals_ref))):
        second = second_ref[pl.ds(at, quarter), :]
        grad = grads_ref[:, k * emb : (k + 1) * emb]
        for c in range(0, rows, 256):
            cols = slice(c, c + 256)
            back[:, cols] = (dot(second, grad[cols, :].T) * hidden[2 * k + 1][:, cols].astype(F32)).astype(BF)
        outs[2 * k][...] = dot(hidden[2 * k][...], grad)
        outs[2 * k + 1][...] = dot(back[...], x_ref[...])


def other_kernel(k, n_put, pos, first, second, grads_ref, rows_ref, sum_second, sum_first, *refs):
    done, outs, puts, (active, back), sems = (
        refs[:n_put],
        refs[n_put : n_put + 4],
        refs[n_put + 4 : 2 * n_put + 4],
        refs[2 * n_put + 4 : 2 * n_put + 6],
        refs[2 * n_put + 6 :],
    )
    copies = [put_half(pos[1], x, o, sems[0].at[i]) for i, (x, o) in enumerate(zip(done, puts))]
    for c in copies:
        c.start()
    quarter = active.shape[0]
    at = pl.multiple_of(pos[1] * quarter, quarter)
    grad_second, grad_first = rows_grads(at, first, second, grads_ref, k, rows_ref, active, back)
    halves = ((sum_first[...] + grad_first).astype(BF).T, (sum_second[...] + grad_second).astype(BF))
    for half, out16, out32 in zip(halves, outs[:2], outs[2:]):
        out16[...] = half
        out32[...] = half.astype(F32)
    for c in copies:
        c.wait()


def put_half(side, half, out, sem):
    n, m = half.shape
    if out.shape[0] == n:
        to = out.at[:, pl.ds(pl.multiple_of(side * m, m), m)]
    else:
        to = out.at[pl.ds(pl.multiple_of(side * n, n), n), :]
    return pltpu.make_async_copy(half, to, sem)


def finish_kernel(old, new, pos, *refs):
    n = old + new
    halves, outs, scratch, sems = refs[:n], refs[n + old : 2 * n + old], refs[2 * n + old : -1], refs[-1]
    copies = [put_half(pos[1], x, o, sems.at[old + i]) for i, (x, o) in enumerate(zip(halves[old:], outs[old:]))]
    for c in copies:
        c.start()
    for i in range(old):
        scratch[i][...] = halves[i][...].astype(F32)
        copies.append(put_half(1 - pos[1], scratch[i], outs[i], sems.at[i]))
        copies[-1].start()
    for c in copies:
        c.wait()


def finish(there, own, wholes, shapes):
    old, new = len(wholes), len(shapes)
    n = old + new
    return kernel(
        functools.partial(finish_kernel, old, new),
        "finish",
        [(w.shape, w.dtype) for w in wholes] + shapes,
        (*there, *own, *wholes),
        [*(pltpu.VMEM(x.shape, F32) for x in there), pltpu.SemaphoreType.DMA((n,))],
        pos=True,
        hbm=range(n, n + old),
        hbm_out=range(n),
        aliases={n + i: i for i in range(old)},
    )


def gathered(
    states, goal_distance, goal_row, episode, state_first, state_second, goal_first, goal_second
):
    rows_dev, width = states.shape
    n_blk, n_rep, n_sub = (lax.axis_size(a) for a in ("blk", "rep", "sub"))
    slab = rows_dev // n_rep
    rows_all = n_blk * n_sub * rows_dev
    hid, emb = state_second.shape
    quarter = hid // n_sub

    def across(x, k):
        return lax.ppermute(x, "blk", [(i, i ^ k) for i in range(n_blk)])

    def swap(x, axis):
        return lax.ppermute(x, axis, [(0, 1), (1, 0)])

    def after(x, *first):
        return lax.optimization_barrier((x, *first))[0]

    weights = (state_first, goal_first, state_second, goal_second)
    (pack,) = kernel(
        functools.partial(pack_kernel, n_blk, n_sub),
        "pack",
        [((rows_dev + 16, width), BF)],
        (states, jnp.stack([goal_distance.reshape(rows_dev), goal_row, episode])),
        pos=True,
        limit=4,
        flops=2**32,
    )
    got = {0: pack, 3: across(pack, 3)}
    held = weights
    part0 = forward(pack, held, rows_dev)
    got[1] = across(after(pack, part0), 1)
    got[2] = across(after(pack, got[3]), 2)
    there0 = swap(part0, "rep")
    part3 = forward(got[3], held, rows_dev)
    there3 = swap(part3, "rep")

    sums = {0: both(part0, there0)}
    sums[1] = across(after(sums[0], got[2]), 1)
    part2 = forward(after(got[2], sums[0]), held, rows_dev)
    there2 = swap(part2, "rep")
    sums[3] = both(part3, there3)

    side = ((rows_all // 2, width), BF)
    mine, other, goals_mine, pick, episodes = kernel(
        functools.partial(arrange_kernel, n_blk, n_rep, slab),
        "arrange",
        [side, side, side, ((rows_all // 2, rows_all), BF), ((1, rows_all // 2), F32)],
        (*(got[k] for k in range(n_blk)), *(swap(got[k], "sub") for k in range(n_blk))),
        [
            pltpu.VMEM((rows_all, width), BF),
            pltpu.VMEM((16, rows_all // 2), F32),
        ],
        pos=True,
    )
    sf, gf, ss, gs = held
    hidden = kernel(
        hidden_kernel,
        "hidden",
        [((quarter, rows_all // 2), BF)] * 4,
        (sf, gf, mine, goals_mine),
        pos=True,
    )
    there2 = after(there2, hidden[3])
    late = [swap(x, "sub") for x in (part2, there2, sums[1])]
    half = rows_all // 2
    phi, psi = kernel(
        functools.partial(gather_kernel, n_blk, n_rep, slab),
        "gather",
        [((half, emb), BF), ((half, emb), F32)],
        (sums[0], sums[1], part2, sums[3], there2, swap(sums[0], "sub"), swap(sums[3], "sub"), pick),
        [pltpu.VMEM((rows_all - 2 * rows_dev, emb), BF)],
        pos=True,
    )
    (grads_mine,) = kernel(
        functools.partial(contrast_kernel, n_rep, 4.0 / math.sqrt(emb)),
        "contrast",
        [((half, 2 * emb), BF)],
        (phi, psi, *late, episodes, pick),
        [pltpu.VMEM((2 * rows_dev, emb), BF), pltpu.VMEM((half, emb), BF)],
    )
    grads_other = swap(grads_mine, "sub")
    goals_other = swap(goals_mine, "sub")

    sf, gf, ss, gs = weights
    work = [pltpu.VMEM((quarter, rows_all // 2), BF), pltpu.VMEM((quarter, rows_all // 2), BF)]
    flops = 4 * rows_all * width * quarter
    sums_s2, sums_s1, sums_g2, sums_g1 = kernel(
        mine_kernel,
        "mine",
        [((quarter, emb), F32), ((quarter, width), F32)] * 2,
        (ss, gs, grads_mine, mine, goals_mine, *hidden),
        work[:1],
        pos=True,
        flops=2 * flops,
    )
    halves = [(shape, kind) for kind in (BF, F32) for shape in ((width, quarter), (quarter, emb))]
    wholes = [((width, hid), F32), ((hid, emb), F32)]
    *state_halves, state_first_own, state_second_own = kernel(
        functools.partial(other_kernel, 0, 0),
        "other_state",
        halves,
        (sf, ss, grads_other, other, sums_s2, sums_s1),
        work,
        pos=True,
        flops=flops,
    )
    state_there = [swap(x, "sub") for x in state_halves]
    *goal_halves, goal_first_own, goal_second_own, out0, out1 = kernel(
        functools.partial(other_kernel, 1, 2),
        "other_goal",
        halves + wholes,
        (gf, gs, grads_other, goals_other, sums_g2, sums_g1, state_first_own, state_second_own),
        work + [pltpu.SemaphoreType.DMA((2,))],
        pos=True,
        flops=flops,
        hbm_out=(4, 5),
    )
    goal_there = [swap(x, "sub") for x in goal_halves]
    out0, out1, out2, out3 = finish(state_there, (goal_first_own, goal_second_own), (out0, out1), wholes)
    out2, out3 = finish(goal_there, (), (out2, out3), [])
    return (out0, out1, out2, out3)


def silu_slope(hidden):
    sig = jax.nn.sigmoid(hidden)
    return sig * (1.0 + hidden * (1.0 - sig))


def encoder_grads(rows_in, hidden, active, second, emb_grad):
    grad_second = jnp.einsum("nh,ne->he", active, emb_grad, preferred_element_type=jnp.float32)
    back = jnp.einsum("ne,he->nh", emb_grad, second, preferred_element_type=jnp.float32)
    back_rows = (back * silu_slope(hidden)).astype(jnp.bfloat16)
    grad_first = jnp.einsum("ns,nh->sh", rows_in, back_rows, preferred_element_type=jnp.float32)
    return (grad_first, grad_second)


def exchanged(
    states, goal_distance, goal_row, episode, state_first, state_second, goal_first, goal_second
):
    rows_dev, width = states.shape
    owners = lax.axis_size(("blk", "sub"))
    position = lax.axis_index(("blk", "sub"))
    capacity = 4 * rows_dev // owners
    target = (position + goal_distance[:, 0]) % owners
    onehot = (target[:, None] == jnp.arange(owners, dtype=jnp.int32)[None, :]).astype(jnp.int32)
    slot_rank = jnp.sum((jnp.cumsum(onehot, axis=0) - onehot) * onehot, axis=1)
    requests = jnp.zeros((owners, capacity), jnp.int32).at[target, slot_rank].set(goal_row)
    wanted = lax.all_to_all(requests, ("blk", "sub"), split_axis=0, concat_axis=0, tiled=True)
    fetched = jnp.take(states, wanted.reshape(-1), axis=0).reshape(wanted.shape + (width,))
    replies = lax.all_to_all(fetched, ("blk", "sub"), split_axis=0, concat_axis=0, tiled=True)
    goal_states = jnp.take(
        replies.reshape(owners * capacity, width), target * capacity + slot_rank, axis=0
    )
    slab_rows = rows_dev // lax.axis_size("rep")
    state_hidden = jnp.dot(states, state_first, preferred_element_type=jnp.float32)
    state_active = jax.nn.silu(state_hidden).astype(jnp.bfloat16)
    goal_hidden = jnp.dot(goal_states, goal_first, preferred_element_type=jnp.float32)
    goal_active = jax.nn.silu(goal_hidden).astype(jnp.bfloat16)
    phi = lax.psum_scatter(
        jnp.dot(state_active, state_second, preferred_element_type=jnp.float32),
        "rep",
        scatter_dimension=0,
        tiled=True,
    ).astype(jnp.bfloat16)
    psi = lax.psum_scatter(
        jnp.dot(goal_active, goal_second, preferred_element_type=jnp.float32),
        "rep",
        scatter_dimension=0,
        tiled=True,
    ).astype(jnp.bfloat16)
    episode_own = lax.dynamic_slice_in_dim(episode, lax.axis_index("rep") * slab_rows, slab_rows, 0)
    psi_all, episode_all = (
        lax.all_gather(psi, "blk", axis=0, tiled=True),
        lax.all_gather(episode_own, "blk", axis=0, tiled=True),
    )
    batch_rows = psi_all.shape[0]
    logit_scale = 4.0 / math.sqrt(psi.shape[1])
    own_rows = lax.axis_index("blk") * slab_rows + jnp.arange(slab_rows, dtype=jnp.int32)
    columns = jnp.arange(batch_rows, dtype=jnp.int32)
    diagonal = own_rows[:, None] == columns[None, :]
    excluded = (episode_own[:, None] == episode_all[None, :]) & ~diagonal
    scores = jnp.einsum("ie,je->ij", phi, psi_all, preferred_element_type=jnp.float32) * logit_scale
    exponent = jnp.where(excluded, 0.0, jnp.exp(scores))
    totals = jnp.sum(exponent, axis=1)
    delta = (exponent / totals[:, None] - diagonal.astype(jnp.float32)).astype(jnp.bfloat16)
    phi_grad = (jnp.dot(delta, psi_all, preferred_element_type=jnp.float32) * logit_scale).astype(
        jnp.bfloat16
    )
    psi_grad = lax.psum_scatter(
        jnp.einsum("ij,ie->je", delta, phi, preferred_element_type=jnp.float32) * logit_scale,
        "blk",
        scatter_dimension=0,
        tiled=True,
    ).astype(jnp.bfloat16)
    phi_full, psi_full = (
        lax.all_gather(phi_grad, "rep", axis=0, tiled=True),
        lax.all_gather(psi_grad, "rep", axis=0, tiled=True),
    )
    state_parts = encoder_grads(states, state_hidden, state_active, state_second, phi_full)
    goal_parts = encoder_grads(goal_states, goal_hidden, goal_active, goal_second, psi_full)
    summed = lax.psum(
        (state_parts[0], state_parts[1], goal_parts[0], goal_parts[1]), ("blk", "sub")
    )
    return (summed[0], summed[1], summed[2], summed[3])


def solution(mesh):
    in_specs = (
        P(("grp", "blk", "sub"), None),
        P(("grp", "blk", "sub"), None),
        P(("grp", "blk", "sub")),
        P(("grp", "blk", "sub")),
        P(None, "rep"),
        P("rep", None),
        P(None, "rep"),
        P("rep", None),
    )
    out_specs = (P("grp", "rep"), P(("grp", "rep"), None), P("grp", "rep"), P(("grp", "rep"), None))

    def local(states, *others):
        small = (mesh.shape["blk"], mesh.shape["rep"], mesh.shape["sub"]) == (4, 2, 2)
        plan = gathered if small and states.shape[0] == states.shape[1] == 256 else exchanged
        return plan(states, *others)

    return jax.shard_map(local, mesh=mesh, in_specs=in_specs, out_specs=out_specs, check_vma=False)
```

```python
import functools
import math

import jax
import jax.numpy as jnp
from jax import lax
from jax.experimental import pallas as pl
from jax.experimental.pallas import tpu as pltpu
from jax.sharding import PartitionSpec as P

BF = jnp.bfloat16
F32 = jnp.float32
MIB = 1024 * 1024


def dot(a, b):
    return jnp.dot(a, b, preferred_element_type=F32)


def sigmoid(v):
    return 0.5 * jnp.tanh(0.5 * v) + 0.5


HBM = pl.BlockSpec(memory_space=pltpu.HBM)
VMEM = pl.BlockSpec(memory_space=pltpu.VMEM)
SMEM = pl.BlockSpec(memory_space=pltpu.SMEM)


def kernel(body, name, outs, args, scratch=(), limit=16, pos=False, flops=0, hbm=(), hbm_out=(), aliases={}):
    specs = [HBM if i in hbm else VMEM for i in range(len(args))]
    if pos:
        inner = body

        def body(*refs):
            inner((lax.axis_index("blk"), lax.axis_index("sub")), *refs)

    return pl.pallas_call(
        body,
        in_specs=specs,
        out_specs=[HBM if i in hbm_out else VMEM for i in range(len(outs))],
        out_shape=[jax.ShapeDtypeStruct(shape, dtype) for shape, dtype in outs],
        scratch_shapes=scratch,
        input_output_aliases=aliases,
        compiler_params=pltpu.CompilerParams(vmem_limit_bytes=int(limit * MIB)),
        cost_estimate=pl.CostEstimate(flops=flops, bytes_accessed=0, transcendentals=0),
        name=name,
    )(*args)


def encode(x_ref, weights, out_ref, active, ready=lambda i: None):
    emb = weights[2].shape[1]
    for k in range(2):
        first, second = weights[k], weights[2 + k]
        ready(k)
        for c in range(0, active.shape[1], 512):
            hidden = dot(x_ref[...], first[:, c : c + 512])
            active[:, c : c + 512] = (hidden * sigmoid(hidden)).astype(BF)
        ready(2 + k)
        out_ref[:, k * emb : (k + 1) * emb] = dot(active[...], second[...]).astype(BF)


def pack_kernel(n_blk, n_sub, pos, x_ref, own_ref, pack_ref):
    rows = x_ref.shape[0]
    owner = (pos[0] * n_sub + pos[1] + own_ref[0:1, :]) & (n_blk * n_sub - 1)
    digits = (owner, own_ref[1:2, :], own_ref[2:3, :])
    table = jnp.concatenate([d.astype(F32) for d in digits] + [jnp.zeros((13, rows), F32)], axis=0)
    pack_ref[:rows, :] = x_ref[...]
    pack_ref[rows:, :] = table.astype(BF)


def forward_kernel(x_ref, *refs):
    encode(x_ref.at[: refs[4].shape[0]], refs[:4], refs[4], refs[5])


def forward(x, weights, rows):
    hid, emb = weights[2].shape
    return kernel(
        forward_kernel,
        "forward",
        [((rows, 2 * emb), BF)],
        (x, *weights),
        [pltpu.VMEM((rows, hid), BF)],
        limit=8,
    )[0]


def add_kernel(a_ref, b_ref, out_ref):
    out_ref[...] = (a_ref[...].astype(F32) + b_ref[...].astype(F32)).astype(BF)


def both(part, there):
    return kernel(add_kernel, "both", [(part.shape, BF)], (part, there), limit=4)[0]


def place_blocks(pos, blocks, put, n_blk, n_rep, slab):
    for k, block in enumerate(blocks):
        at = jnp.bitwise_xor(pos[0], k)
        for r in range(n_rep):
            off = (r * n_blk + at) * slab
            put(pl.multiple_of(off, slab), block[r * slab : (r + 1) * slab, :])


def column(row):
    return jnp.broadcast_to(row, (128, row.shape[1])).T[:, :1]


def place_in_turn(k, n_blk):
    return -k & (n_blk - 1)


def arrange_kernel(n_blk, n_rep, slab, pos, *refs):
    mine, other, firsts = refs[:n_blk], refs[n_blk : 2 * n_blk], refs[2 * n_blk : 2 * n_blk + 2]
    rows_mine, rows_other, goals_ref, pick_ref, ep_ref, *hidden, both_sides, meta = refs[2 * n_blk + 2 :]
    rows = both_sides.shape[0]
    batch, rows_dev = n_blk * slab, n_rep * slab
    for i, (blocks, to) in enumerate(((mine, rows_mine), (other, rows_other))):

        def put(off, value, to=to):
            to[pl.ds(off, slab), :] = value

        place_blocks(pos, blocks, put, n_blk, n_rep, slab)
        for k, block in enumerate(blocks):
            at = (i * n_blk + place_in_turn(k, n_blk)) * rows_dev
            both_sides[at : at + rows_dev, :] = block[:rows_dev, :]
    for k, block in enumerate(mine):
        at = jnp.bitwise_xor(pos[0], k)
        for r in range(n_rep):
            off = pl.multiple_of((r * n_blk + at) * slab, slab)
            meta[:, pl.ds(off, slab)] = block[rows_dev:, r * slab : (r + 1) * slab].astype(F32)
    ep_ref[...] = meta[2:3, :]
    for r in range(n_rep):
        own = slice(r * batch, (r + 1) * batch)
        owner, place = meta[0:1, own].astype(jnp.int32), meta[1:2, own].astype(jnp.int32)
        side = (owner & 1) ^ pos[1]
        column_of = (side * n_blk + place_in_turn((owner >> 1) ^ pos[0], n_blk)) * rows_dev + place
        goal = column(column_of.astype(F32)).astype(jnp.int32)
        pick_ref[own, :] = jnp.where(
            goal == lax.broadcasted_iota(jnp.int32, (batch, rows), 1), 1.0, 0.0
        ).astype(BF)
    goals_ref[...] = dot(pick_ref[...], both_sides[...]).astype(BF)
    activate(pos, firsts, (rows_mine, goals_ref), hidden)


def gather_kernel(n_blk, n_rep, slab, pos, *refs):
    mine, extra, other, pick_ref = refs[:n_blk], refs[n_blk], refs[n_blk + 1 : n_blk + 3], refs[n_blk + 3]
    phi_ref, psi_ref, early = refs[n_blk + 4 :]
    emb = phi_ref.shape[1]
    rows_dev = n_rep * slab
    blocks = list(mine)
    blocks[n_blk - 2] = (mine[n_blk - 2][...].astype(F32) + extra[...].astype(F32)).astype(BF)

    def put(off, value):
        phi_ref[pl.ds(off, slab), :] = value[:, :emb]

    place_blocks(pos, blocks, put, n_blk, n_rep, slab)
    for k, block in enumerate(blocks):
        at = place_in_turn(k, n_blk) * rows_dev
        early[at : at + rows_dev, :] = block[:, emb:]
    for i, block in enumerate(other):
        at = (n_blk + i) * rows_dev
        early[at : at + rows_dev, :] = block[:, emb:]
    psi_ref[...] = dot(pick_ref[:, : early.shape[0]], early[...])


def contrast_kernel(n_rep, scale, phi_ref, psi_ref, part_ref, there_ref, sums_ref, ep_ref, pick_ref, grads_ref, late, psi_all):
    half, emb = phi_ref.shape
    batch = half // n_rep
    rows_dev = sums_ref.shape[0]
    late[:rows_dev, :] = (part_ref[:, emb:].astype(F32) + there_ref[:, emb:].astype(F32)).astype(BF)
    late[rows_dev:, :] = sums_ref[:, emb:]
    psi_all[...] = (psi_ref[...] + dot(pick_ref[:, pick_ref.shape[1] - 2 * rows_dev :], late[...])).astype(BF)
    diagonal = lax.broadcasted_iota(jnp.int32, (batch, batch), 0) == lax.broadcasted_iota(
        jnp.int32, (batch, batch), 1
    )
    for r in range(n_rep):
        own = slice(r * batch, (r + 1) * batch)
        ep_row = ep_ref[:, own]
        psi = psi_all[own, :]
        phi = phi_ref[own, :]
        scores = lax.dot_general(phi, psi, (((1,), (1,)), ((), ())), preferred_element_type=F32)
        kept = (column(ep_row) != ep_row) | diagonal
        exponent = jnp.where(kept, jnp.exp(scores * scale), 0.0)
        totals = jnp.sum(exponent, axis=1, keepdims=True)
        power = jnp.where(totals > 1.0, 2.0**-32, 1.0)
        shares = (exponent * power) * (1.0 / (totals * power))
        delta = jnp.where(diagonal, shares - 1.0, shares).astype(BF)
        grads_ref[own, :emb] = (dot(delta, psi) * scale).astype(BF)
        grads_ref[own, emb:] = (dot(delta.T, phi) * scale).astype(BF)


def rows_grads(at, first_ref, second_ref, grads_ref, k, rows_ref, active, back):
    quarter, rows = active.shape
    emb = second_ref.shape[1]
    first_t = first_ref[:, pl.ds(at, quarter)].T
    second = second_ref[pl.ds(at, quarter), :]
    grad = grads_ref[:, k * emb : (k + 1) * emb]
    chunk = 256
    for c in range(0, rows, chunk):
        cols = slice(c, c + chunk)
        hidden = dot(first_t, rows_ref[cols, :].T)
        sig = sigmoid(hidden)
        act = hidden * sig
        active[:, cols] = act.astype(BF)
        slope = sig + act * (1.0 - sig)
        back[:, cols] = (dot(second, grad[cols, :].T) * slope).astype(BF)
    return dot(active[...], grad), dot(back[...], rows_ref[...])


def activate(pos, firsts, inputs, outs):
    quarter, rows = outs[0].shape
    at = pl.multiple_of(pos[1] * quarter, quarter)
    for k, (first, x_ref) in enumerate(zip(firsts, inputs)):
        first_t = first[:, pl.ds(at, quarter)].T
        for c in range(0, rows, 256):
            cols = slice(c, c + 256)
            hidden = dot(first_t, x_ref[cols, :].T)
            sig = sigmoid(hidden)
            act = hidden * sig
            outs[2 * k][:, cols] = act.astype(BF)
            outs[2 * k + 1][:, cols] = (sig + act * (1.0 - sig)).astype(BF)


def mine_kernel(pos, ss, gs, grads_ref, rows_ref, goals_ref, *refs):
    hidden, outs, back = refs[:4], refs[4:8], refs[8]
    quarter, rows = back.shape
    emb = ss.shape[1]
    at = pl.multiple_of(pos[1] * quarter, quarter)
    for k, (second_ref, x_ref) in enumerate(((ss, rows_ref), (gs, goals_ref))):
        second = second_ref[pl.ds(at, quarter), :]
        grad = grads_ref[:, k * emb : (k + 1) * emb]
        for c in range(0, rows, 256):
            cols = slice(c, c + 256)
            back[:, cols] = (dot(second, grad[cols, :].T) * hidden[2 * k + 1][:, cols].astype(F32)).astype(BF)
        outs[2 * k][...] = dot(hidden[2 * k][...], grad)
        outs[2 * k + 1][...] = dot(back[...], x_ref[...])


def other_kernel(k, n_put, pos, first, second, grads_ref, rows_ref, sum_second, sum_first, *refs):
    done, outs, puts, (active, back), sems = (
        refs[:n_put],
        refs[n_put : n_put + 4],
        refs[n_put + 4 : 2 * n_put + 4],
        refs[2 * n_put + 4 : 2 * n_put + 6],
        refs[2 * n_put + 6 :],
    )
    copies = [put_half(pos[1], x, o, sems[0].at[i]) for i, (x, o) in enumerate(zip(done, puts))]
    for c in copies:
        c.start()
    quarter = active.shape[0]
    at = pl.multiple_of(pos[1] * quarter, quarter)
    grad_second, grad_first = rows_grads(at, first, second, grads_ref, k, rows_ref, active, back)
    halves = ((sum_first[...] + grad_first).astype(BF).T, (sum_second[...] + grad_second).astype(BF))
    for half, out16, out32 in zip(halves, outs[:2], outs[2:]):
        out16[...] = half
        out32[...] = half.astype(F32)
    for c in copies:
        c.wait()


def put_half(side, half, out, sem):
    n, m = half.shape
    if out.shape[0] == n:
        to = out.at[:, pl.ds(pl.multiple_of(side * m, m), m)]
    else:
        to = out.at[pl.ds(pl.multiple_of(side * n, n), n), :]
    return pltpu.make_async_copy(half, to, sem)


def finish_kernel(old, new, pos, *refs):
    n = old + new
    halves, outs, scratch, sems = refs[:n], refs[n + old : 2 * n + old], refs[2 * n + old : -1], refs[-1]
    copies = [put_half(pos[1], x, o, sems.at[old + i]) for i, (x, o) in enumerate(zip(halves[old:], outs[old:]))]
    for c in copies:
        c.start()
    for i in range(old):
        scratch[i][...] = halves[i][...].astype(F32)
        copies.append(put_half(1 - pos[1], scratch[i], outs[i], sems.at[i]))
        copies[-1].start()
    for c in copies:
        c.wait()


def finish(there, own, wholes, shapes):
    old, new = len(wholes), len(shapes)
    n = old + new
    return kernel(
        functools.partial(finish_kernel, old, new),
        "finish",
        [(w.shape, w.dtype) for w in wholes] + shapes,
        (*there, *own, *wholes),
        [*(pltpu.VMEM(x.shape, F32) for x in there), pltpu.SemaphoreType.DMA((n,))],
        pos=True,
        hbm=range(n, n + old),
        hbm_out=range(n),
        aliases={n + i: i for i in range(old)},
    )


def gathered(
    states, goal_distance, goal_row, episode, state_first, state_second, goal_first, goal_second
):
    rows_dev, width = states.shape
    n_blk, n_rep, n_sub = (lax.axis_size(a) for a in ("blk", "rep", "sub"))
    slab = rows_dev // n_rep
    rows_all = n_blk * n_sub * rows_dev
    hid, emb = state_second.shape
    quarter = hid // n_sub

    def across(x, k):
        return lax.ppermute(x, "blk", [(i, i ^ k) for i in range(n_blk)])

    def swap(x, axis):
        return lax.ppermute(x, axis, [(0, 1), (1, 0)])

    def after(x, *first):
        return lax.optimization_barrier((x, *first))[0]

    weights = (state_first, goal_first, state_second, goal_second)
    (pack,) = kernel(
        functools.partial(pack_kernel, n_blk, n_sub),
        "pack",
        [((rows_dev + 16, width), BF)],
        (states, jnp.stack([goal_distance.reshape(rows_dev), goal_row, episode])),
        pos=True,
        limit=4,
        flops=2**32,
    )
    got = {0: pack, 3: across(pack, 3)}
    held = weights
    part0 = forward(pack, held, rows_dev)
    got[1] = across(after(pack, part0), 1)
    got[2] = across(after(pack, got[3]), 2)
    there0 = swap(part0, "rep")
    part3 = forward(got[3], held, rows_dev)
    there3 = swap(part3, "rep")

    sums = {0: both(part0, there0)}
    sums[1] = across(after(sums[0], got[2]), 1)
    part2 = forward(after(got[2], sums[0]), held, rows_dev)
    there2 = swap(part2, "rep")
    sums[3] = both(part3, there3)

    side = ((rows_all // 2, width), BF)
    sf, gf, ss, gs = held
    mine, other, goals_mine, pick, episodes, *hidden = kernel(
        functools.partial(arrange_kernel, n_blk, n_rep, slab),
        "arrange",
        [side, side, side, ((rows_all // 2, rows_all), BF), ((1, rows_all // 2), F32)]
        + [((quarter, rows_all // 2), BF)] * 4,
        (*(got[k] for k in range(n_blk)), *(swap(got[k], "sub") for k in range(n_blk)), sf, gf),
        [
            pltpu.VMEM((rows_all, width), BF),
            pltpu.VMEM((16, rows_all // 2), F32),
        ],
        pos=True,
    )
    there2 = after(there2, pick)
    late = [swap(x, "sub") for x in (part2, there2, sums[1])]
    half = rows_all // 2
    phi, psi = kernel(
        functools.partial(gather_kernel, n_blk, n_rep, slab),
        "gather",
        [((half, emb), BF), ((half, emb), F32)],
        (sums[0], sums[1], part2, sums[3], there2, swap(sums[0], "sub"), swap(sums[3], "sub"), pick),
        [pltpu.VMEM((rows_all - 2 * rows_dev, emb), BF)],
        pos=True,
    )
    (grads_mine,) = kernel(
        functools.partial(contrast_kernel, n_rep, 4.0 / math.sqrt(emb)),
        "contrast",
        [((half, 2 * emb), BF)],
        (phi, psi, *late, episodes, pick),
        [pltpu.VMEM((2 * rows_dev, emb), BF), pltpu.VMEM((half, emb), BF)],
    )
    grads_other = swap(grads_mine, "sub")
    goals_other = swap(goals_mine, "sub")

    sf, gf, ss, gs = weights
    work = [pltpu.VMEM((quarter, rows_all // 2), BF), pltpu.VMEM((quarter, rows_all // 2), BF)]
    flops = 4 * rows_all * width * quarter
    sums_s2, sums_s1, sums_g2, sums_g1 = kernel(
        mine_kernel,
        "mine",
        [((quarter, emb), F32), ((quarter, width), F32)] * 2,
        (ss, gs, grads_mine, mine, goals_mine, *hidden),
        work[:1],
        pos=True,
        flops=2 * flops,
    )
    halves = [(shape, kind) for kind in (BF, F32) for shape in ((width, quarter), (quarter, emb))]
    wholes = [((width, hid), F32), ((hid, emb), F32)]
    *state_halves, state_first_own, state_second_own = kernel(
        functools.partial(other_kernel, 0, 0),
        "other_state",
        halves,
        (sf, ss, grads_other, other, sums_s2, sums_s1),
        work,
        pos=True,
        flops=flops,
    )
    state_there = [swap(x, "sub") for x in state_halves]
    *goal_halves, goal_first_own, goal_second_own, out0, out1 = kernel(
        functools.partial(other_kernel, 1, 2),
        "other_goal",
        halves + wholes,
        (gf, gs, grads_other, goals_other, sums_g2, sums_g1, state_first_own, state_second_own),
        work + [pltpu.SemaphoreType.DMA((2,))],
        pos=True,
        flops=flops,
        hbm_out=(4, 5),
    )
    goal_there = [swap(x, "sub") for x in goal_halves]
    out0, out1, out2, out3 = finish(state_there, (goal_first_own, goal_second_own), (out0, out1), wholes)
    out2, out3 = finish(goal_there, (), (out2, out3), [])
    return (out0, out1, out2, out3)


def silu_slope(hidden):
    sig = jax.nn.sigmoid(hidden)
    return sig * (1.0 + hidden * (1.0 - sig))


def encoder_grads(rows_in, hidden, active, second, emb_grad):
    grad_second = jnp.einsum("nh,ne->he", active, emb_grad, preferred_element_type=jnp.float32)
    back = jnp.einsum("ne,he->nh", emb_grad, second, preferred_element_type=jnp.float32)
    back_rows = (back * silu_slope(hidden)).astype(jnp.bfloat16)
    grad_first = jnp.einsum("ns,nh->sh", rows_in, back_rows, preferred_element_type=jnp.float32)
    return (grad_first, grad_second)


def exchanged(
    states, goal_distance, goal_row, episode, state_first, state_second, goal_first, goal_second
):
    rows_dev, width = states.shape
    owners = lax.axis_size(("blk", "sub"))
    position = lax.axis_index(("blk", "sub"))
    capacity = 4 * rows_dev // owners
    target = (position + goal_distance[:, 0]) % owners
    onehot = (target[:, None] == jnp.arange(owners, dtype=jnp.int32)[None, :]).astype(jnp.int32)
    slot_rank = jnp.sum((jnp.cumsum(onehot, axis=0) - onehot) * onehot, axis=1)
    requests = jnp.zeros((owners, capacity), jnp.int32).at[target, slot_rank].set(goal_row)
    wanted = lax.all_to_all(requests, ("blk", "sub"), split_axis=0, concat_axis=0, tiled=True)
    fetched = jnp.take(states, wanted.reshape(-1), axis=0).reshape(wanted.shape + (width,))
    replies = lax.all_to_all(fetched, ("blk", "sub"), split_axis=0, concat_axis=0, tiled=True)
    goal_states = jnp.take(
        replies.reshape(owners * capacity, width), target * capacity + slot_rank, axis=0
    )
    slab_rows = rows_dev // lax.axis_size("rep")
    state_hidden = jnp.dot(states, state_first, preferred_element_type=jnp.float32)
    state_active = jax.nn.silu(state_hidden).astype(jnp.bfloat16)
    goal_hidden = jnp.dot(goal_states, goal_first, preferred_element_type=jnp.float32)
    goal_active = jax.nn.silu(goal_hidden).astype(jnp.bfloat16)
    phi = lax.psum_scatter(
        jnp.dot(state_active, state_second, preferred_element_type=jnp.float32),
        "rep",
        scatter_dimension=0,
        tiled=True,
    ).astype(jnp.bfloat16)
    psi = lax.psum_scatter(
        jnp.dot(goal_active, goal_second, preferred_element_type=jnp.float32),
        "rep",
        scatter_dimension=0,
        tiled=True,
    ).astype(jnp.bfloat16)
    episode_own = lax.dynamic_slice_in_dim(episode, lax.axis_index("rep") * slab_rows, slab_rows, 0)
    psi_all, episode_all = (
        lax.all_gather(psi, "blk", axis=0, tiled=True),
        lax.all_gather(episode_own, "blk", axis=0, tiled=True),
    )
    batch_rows = psi_all.shape[0]
    logit_scale = 4.0 / math.sqrt(psi.shape[1])
    own_rows = lax.axis_index("blk") * slab_rows + jnp.arange(slab_rows, dtype=jnp.int32)
    columns = jnp.arange(batch_rows, dtype=jnp.int32)
    diagonal = own_rows[:, None] == columns[None, :]
    excluded = (episode_own[:, None] == episode_all[None, :]) & ~diagonal
    scores = jnp.einsum("ie,je->ij", phi, psi_all, preferred_element_type=jnp.float32) * logit_scale
    exponent = jnp.where(excluded, 0.0, jnp.exp(scores))
    totals = jnp.sum(exponent, axis=1)
    delta = (exponent / totals[:, None] - diagonal.astype(jnp.float32)).astype(jnp.bfloat16)
    phi_grad = (jnp.dot(delta, psi_all, preferred_element_type=jnp.float32) * logit_scale).astype(
        jnp.bfloat16
    )
    psi_grad = lax.psum_scatter(
        jnp.einsum("ij,ie->je", delta, phi, preferred_element_type=jnp.float32) * logit_scale,
        "blk",
        scatter_dimension=0,
        tiled=True,
    ).astype(jnp.bfloat16)
    phi_full, psi_full = (
        lax.all_gather(phi_grad, "rep", axis=0, tiled=True),
        lax.all_gather(psi_grad, "rep", axis=0, tiled=True),
    )
    state_parts = encoder_grads(states, state_hidden, state_active, state_second, phi_full)
    goal_parts = encoder_grads(goal_states, goal_hidden, goal_active, goal_second, psi_full)
    summed = lax.psum(
        (state_parts[0], state_parts[1], goal_parts[0], goal_parts[1]), ("blk", "sub")
    )
    return (summed[0], summed[1], summed[2], summed[3])


def solution(mesh):
    in_specs = (
        P(("grp", "blk", "sub"), None),
        P(("grp", "blk", "sub"), None),
        P(("grp", "blk", "sub")),
        P(("grp", "blk", "sub")),
        P(None, "rep"),
        P("rep", None),
        P(None, "rep"),
        P("rep", None),
    )
    out_specs = (P("grp", "rep"), P(("grp", "rep"), None), P("grp", "rep"), P(("grp", "rep"), None))

    def local(states, *others):
        small = (mesh.shape["blk"], mesh.shape["rep"], mesh.shape["sub"]) == (4, 2, 2)
        plan = gathered if small and states.shape[0] == states.shape[1] == 256 else exchanged
        return plan(states, *others)

    return jax.shard_map(local, mesh=mesh, in_specs=in_specs, out_specs=out_specs, check_vma=False)
```

```python
import functools
import math

import jax
import jax.numpy as jnp
from jax import lax
from jax.experimental import pallas as pl
from jax.experimental.pallas import tpu as pltpu
from jax.sharding import PartitionSpec as P

BF = jnp.bfloat16
F32 = jnp.float32
MIB = 1024 * 1024


def dot(a, b):
    return jnp.dot(a, b, preferred_element_type=F32)


def sigmoid(v):
    return 0.5 * jnp.tanh(0.5 * v) + 0.5


HBM = pl.BlockSpec(memory_space=pltpu.HBM)
VMEM = pl.BlockSpec(memory_space=pltpu.VMEM)
SMEM = pl.BlockSpec(memory_space=pltpu.SMEM)


def kernel(body, name, outs, args, scratch=(), limit=16, pos=False, flops=0, hbm=(), hbm_out=(), aliases={}):
    specs = [HBM if i in hbm else VMEM for i in range(len(args))]
    if pos:
        inner = body

        def body(*refs):
            inner((lax.axis_index("blk"), lax.axis_index("sub")), *refs)

    return pl.pallas_call(
        body,
        in_specs=specs,
        out_specs=[HBM if i in hbm_out else VMEM for i in range(len(outs))],
        out_shape=[jax.ShapeDtypeStruct(shape, dtype) for shape, dtype in outs],
        scratch_shapes=scratch,
        input_output_aliases=aliases,
        compiler_params=pltpu.CompilerParams(vmem_limit_bytes=int(limit * MIB)),
        cost_estimate=pl.CostEstimate(flops=flops, bytes_accessed=0, transcendentals=0),
        name=name,
    )(*args)


def encode(x_ref, weights, out_ref, active, ready=lambda i: None):
    emb = weights[2].shape[1]
    for k in range(2):
        first, second = weights[k], weights[2 + k]
        ready(k)
        for c in range(0, active.shape[1], 512):
            hidden = dot(x_ref[...], first[:, c : c + 512])
            active[:, c : c + 512] = (hidden * sigmoid(hidden)).astype(BF)
        ready(2 + k)
        out_ref[:, k * emb : (k + 1) * emb] = dot(active[...], second[...]).astype(BF)


def blank_kernel(out_ref):
    out_ref[...] = jnp.zeros_like(out_ref)


def pack_kernel(n_blk, n_sub, pos, blank_ref, x_ref, distance_ref, place_ref, episode_ref, pack_ref):
    rows = x_ref.shape[0]
    owner = (pos[0] * n_sub + pos[1] + distance_ref[...]) & (n_blk * n_sub - 1)
    digits = (owner, place_ref[...], episode_ref[...])
    table = jnp.concatenate([d.astype(F32) for d in digits] + [blank_ref[3:, :]], axis=0)
    pack_ref[:rows, :] = x_ref[...]
    pack_ref[rows:, :] = table.astype(BF)


def forward_kernel(x_ref, *refs):
    encode(x_ref.at[: refs[4].shape[0]], refs[:4], refs[4], refs[5])


def forward(x, weights, rows):
    hid, emb = weights[2].shape
    return kernel(
        forward_kernel,
        "forward",
        [((rows, 2 * emb), BF)],
        (x, *weights),
        [pltpu.VMEM((rows, hid), BF)],
        limit=8,
    )[0]


def add_kernel(a_ref, b_ref, out_ref):
    out_ref[...] = (a_ref[...].astype(F32) + b_ref[...].astype(F32)).astype(BF)


def both(part, there):
    return kernel(add_kernel, "both", [(part.shape, BF)], (part, there), limit=4)[0]


def place_blocks(pos, blocks, put, n_blk, n_rep, slab):
    for k, block in enumerate(blocks):
        at = jnp.bitwise_xor(pos[0], k)
        for r in range(n_rep):
            off = (r * n_blk + at) * slab
            put(pl.multiple_of(off, slab), block[r * slab : (r + 1) * slab, :])


def column(row):
    return jnp.broadcast_to(row, (128, row.shape[1])).T[:, :1]


def place_in_turn(k, n_blk):
    return -k & (n_blk - 1)


def arrange_kernel(n_blk, n_rep, slab, pos, *refs):
    mine, other, firsts = refs[:n_blk], refs[n_blk : 2 * n_blk], refs[2 * n_blk : 2 * n_blk + 2]
    rows_mine, rows_other, goals_ref, pick_ref, ep_ref, *hidden, both_sides, meta = refs[2 * n_blk + 2 :]
    rows = both_sides.shape[0]
    batch, rows_dev = n_blk * slab, n_rep * slab
    for i, (blocks, to) in enumerate(((mine, rows_mine), (other, rows_other))):

        def put(off, value, to=to):
            to[pl.ds(off, slab), :] = value

        place_blocks(pos, blocks, put, n_blk, n_rep, slab)
        for k, block in enumerate(blocks):
            at = (i * n_blk + place_in_turn(k, n_blk)) * rows_dev
            both_sides[at : at + rows_dev, :] = block[:rows_dev, :]
    for k, block in enumerate(mine):
        at = jnp.bitwise_xor(pos[0], k)
        for r in range(n_rep):
            off = pl.multiple_of((r * n_blk + at) * slab, slab)
            meta[:, pl.ds(off, slab)] = block[rows_dev:, r * slab : (r + 1) * slab].astype(F32)
    ep_ref[...] = meta[2:3, :]
    for r in range(n_rep):
        own = slice(r * batch, (r + 1) * batch)
        owner, place = meta[0:1, own].astype(jnp.int32), meta[1:2, own].astype(jnp.int32)
        side = (owner & 1) ^ pos[1]
        column_of = (side * n_blk + place_in_turn((owner >> 1) ^ pos[0], n_blk)) * rows_dev + place
        goal = column(column_of.astype(F32)).astype(jnp.int32)
        pick_ref[own, :] = jnp.where(
            goal == lax.broadcasted_iota(jnp.int32, (batch, rows), 1), 1.0, 0.0
        ).astype(BF)
    goals_ref[...] = dot(pick_ref[...], both_sides[...]).astype(BF)
    activate(pos, firsts, (rows_mine, goals_ref), hidden)


def gather_kernel(n_blk, n_rep, slab, pos, *refs):
    mine, extra, other, pick_ref = refs[:n_blk], refs[n_blk], refs[n_blk + 1 : n_blk + 3], refs[n_blk + 3]
    phi_ref, psi_ref, early = refs[n_blk + 4 :]
    emb = phi_ref.shape[1]
    rows_dev = n_rep * slab
    blocks = list(mine)
    blocks[n_blk - 2] = (mine[n_blk - 2][...].astype(F32) + extra[...].astype(F32)).astype(BF)

    def put(off, value):
        phi_ref[pl.ds(off, slab), :] = value[:, :emb]

    place_blocks(pos, blocks, put, n_blk, n_rep, slab)
    for k, block in enumerate(blocks):
        at = place_in_turn(k, n_blk) * rows_dev
        early[at : at + rows_dev, :] = block[:, emb:]
    for i, block in enumerate(other):
        at = (n_blk + i) * rows_dev
        early[at : at + rows_dev, :] = block[:, emb:]
    psi_ref[...] = dot(pick_ref[:, : early.shape[0]], early[...])


def contrast_kernel(n_rep, scale, phi_ref, psi_ref, part_ref, there_ref, sums_ref, ep_ref, pick_ref, grads_ref, late, psi_all):
    half, emb = phi_ref.shape
    batch = half // n_rep
    rows_dev = sums_ref.shape[0]
    late[:rows_dev, :] = (part_ref[:, emb:].astype(F32) + there_ref[:, emb:].astype(F32)).astype(BF)
    late[rows_dev:, :] = sums_ref[:, emb:]
    psi_all[...] = (psi_ref[...] + dot(pick_ref[:, pick_ref.shape[1] - 2 * rows_dev :], late[...])).astype(BF)
    diagonal = lax.broadcasted_iota(jnp.int32, (batch, batch), 0) == lax.broadcasted_iota(
        jnp.int32, (batch, batch), 1
    )
    for r in range(n_rep):
        own = slice(r * batch, (r + 1) * batch)
        ep_row = ep_ref[:, own]
        psi = psi_all[own, :]
        phi = phi_ref[own, :]
        scores = lax.dot_general(phi, psi, (((1,), (1,)), ((), ())), preferred_element_type=F32)
        kept = (column(ep_row) != ep_row) | diagonal
        exponent = jnp.where(kept, jnp.exp(scores * scale), 0.0)
        totals = jnp.sum(exponent, axis=1, keepdims=True)
        power = jnp.where(totals > 1.0, 2.0**-32, 1.0)
        shares = (exponent * power) * (1.0 / (totals * power))
        delta = jnp.where(diagonal, shares - 1.0, shares).astype(BF)
        grads_ref[own, :emb] = (dot(delta, psi) * scale).astype(BF)
        grads_ref[own, emb:] = (dot(delta.T, phi) * scale).astype(BF)


def rows_grads(at, first_ref, second_ref, grads_ref, k, rows_ref, active, back):
    quarter, rows = active.shape
    emb = second_ref.shape[1]
    first_t = first_ref[:, pl.ds(at, quarter)].T
    second = second_ref[pl.ds(at, quarter), :]
    grad = grads_ref[:, k * emb : (k + 1) * emb]
    chunk = 256
    for c in range(0, rows, chunk):
        cols = slice(c, c + chunk)
        hidden = dot(first_t, rows_ref[cols, :].T)
        sig = sigmoid(hidden)
        act = hidden * sig
        active[:, cols] = act.astype(BF)
        slope = sig + act * (1.0 - sig)
        back[:, cols] = (dot(second, grad[cols, :].T) * slope).astype(BF)
    return dot(active[...], grad), dot(back[...], rows_ref[...])


def activate(pos, firsts, inputs, outs):
    quarter, rows = outs[0].shape
    at = pl.multiple_of(pos[1] * quarter, quarter)
    for k, (first, x_ref) in enumerate(zip(firsts, inputs)):
        first_t = first[:, pl.ds(at, quarter)].T
        for c in range(0, rows, 256):
            cols = slice(c, c + 256)
            hidden = dot(first_t, x_ref[cols, :].T)
            sig = sigmoid(hidden)
            act = hidden * sig
            outs[2 * k][:, cols] = act.astype(BF)
            outs[2 * k + 1][:, cols] = (sig + act * (1.0 - sig)).astype(BF)


def mine_kernel(pos, ss, gs, grads_ref, rows_ref, goals_ref, *refs):
    hidden, outs, back = refs[:4], refs[4:8], refs[8]
    quarter, rows = back.shape
    emb = ss.shape[1]
    at = pl.multiple_of(pos[1] * quarter, quarter)
    for k, (second_ref, x_ref) in enumerate(((ss, rows_ref), (gs, goals_ref))):
        second = second_ref[pl.ds(at, quarter), :]
        grad = grads_ref[:, k * emb : (k + 1) * emb]
        for c in range(0, rows, 256):
            cols = slice(c, c + 256)
            back[:, cols] = (dot(second, grad[cols, :].T) * hidden[2 * k + 1][:, cols].astype(F32)).astype(BF)
        outs[2 * k][...] = dot(hidden[2 * k][...], grad)
        outs[2 * k + 1][...] = dot(back[...], x_ref[...])


def column_blocks(shape):
    n, m = shape
    return [(at, slice(at, at + n)) for at in range(0, m, n)]


def other_kernel(k, n_put, pos, first, second, grads_ref, rows_ref, sum_second, sum_first, *refs):
    done, outs, puts, (active, back), sems = (
        refs[:n_put],
        refs[n_put : n_put + 3],
        refs[n_put + 3 : 2 * n_put + 3],
        refs[2 * n_put + 3 : 2 * n_put + 5],
        refs[2 * n_put + 5 :],
    )
    copies = [put_half(pos[1], x, o, sems[0].at[i]) for i, (x, o) in enumerate(zip(done, puts))]
    for c in copies:
        c.start()
    quarter = active.shape[0]
    at = pl.multiple_of(pos[1] * quarter, quarter)
    grad_second, grad_first = rows_grads(at, first, second, grads_ref, k, rows_ref, active, back)
    first_half, second_half = (sum_first[...] + grad_first).astype(BF).T, (sum_second[...] + grad_second).astype(BF)
    sent, first_out, second_out = outs
    sent[:quarter, :] = second_half
    for at, cols in column_blocks(first_half.shape):
        sent[quarter + at : quarter + at + first_half.shape[0], :] = first_half[:, cols]
    first_out[...] = first_half.astype(F32)
    second_out[...] = second_half.astype(F32)
    for c in copies:
        c.wait()


def put_half(side, half, out, sem):
    n, m = half.shape
    if out.shape[0] == n:
        to = out.at[:, pl.ds(pl.multiple_of(side * m, m), m)]
    else:
        to = out.at[pl.ds(pl.multiple_of(side * n, n), n), :]
    return pltpu.make_async_copy(half, to, sem)


def finish_kernel(new, pos, there_ref, *refs):
    own, outs, (first, second), sems = refs[:new], refs[new + 2 : 2 * new + 4], refs[2 * new + 4 : 2 * new + 6], refs[-1]
    copies = [put_half(pos[1], x, o, sems.at[2 + i]) for i, (x, o) in enumerate(zip(own, outs[2:]))]
    for c in copies:
        c.start()
    quarter = second.shape[0]
    second[...] = there_ref[:quarter, :].astype(F32)
    copies.append(put_half(1 - pos[1], second, outs[1], sems.at[1]))
    copies[-1].start()
    for at, cols in column_blocks(first.shape):
        first[:, cols] = there_ref[quarter + at : quarter + at + first.shape[0], :].astype(F32)
    copies.append(put_half(1 - pos[1], first, outs[0], sems.at[0]))
    copies[-1].start()
    for c in copies:
        c.wait()


def finish(there, own, wholes, shapes):
    new = len(shapes)
    (width, hid), (_, emb) = (w.shape for w in wholes)
    return kernel(
        functools.partial(finish_kernel, new),
        "finish",
        [(w.shape, w.dtype) for w in wholes] + shapes,
        (there, *own, *wholes),
        [
            pltpu.VMEM((width, hid // 2), F32),
            pltpu.VMEM((hid // 2, emb), F32),
            pltpu.SemaphoreType.DMA((2 + new,)),
        ],
        pos=True,
        hbm=(1 + new, 2 + new),
        hbm_out=range(2 + new),
        aliases={1 + new: 0, 2 + new: 1},
    )


def gathered(
    states, goal_distance, goal_row, episode, state_first, state_second, goal_first, goal_second
):
    rows_dev, width = states.shape
    n_blk, n_rep, n_sub = (lax.axis_size(a) for a in ("blk", "rep", "sub"))
    slab = rows_dev // n_rep
    rows_all = n_blk * n_sub * rows_dev
    hid, emb = state_second.shape
    quarter = hid // n_sub

    def across(x, k):
        return lax.ppermute(x, "blk", [(i, i ^ k) for i in range(n_blk)])

    def swap(x, axis):
        return lax.ppermute(x, axis, [(0, 1), (1, 0)])

    def after(x, *first):
        return lax.optimization_barrier((x, *first))[0]

    weights = (state_first, goal_first, state_second, goal_second)
    (blank,) = kernel(blank_kernel, "blank", [((16, rows_dev), F32)], (), limit=1, flops=2**32)
    (pack,) = kernel(
        functools.partial(pack_kernel, n_blk, n_sub),
        "pack",
        [((rows_dev + 16, width), BF)],
        (blank, states, *(x.reshape(1, rows_dev) for x in (goal_distance, goal_row, episode))),
        pos=True,
        limit=4,
        flops=2**32,
    )
    got = {0: pack, 3: across(pack, 3)}
    held = weights
    part0 = forward(pack, held, rows_dev)
    got[1] = across(after(pack, part0), 1)
    got[2] = across(after(pack, got[3]), 2)
    there0 = swap(part0, "rep")
    part3 = forward(got[3], held, rows_dev)
    there3 = swap(part3, "rep")

    sums = {0: both(part0, there0)}
    sums[1] = across(after(sums[0], got[2]), 1)
    part2 = forward(after(got[2], sums[0]), held, rows_dev)
    there2 = swap(part2, "rep")
    sums[3] = both(part3, there3)

    side = ((rows_all // 2, width), BF)
    sf, gf, ss, gs = held
    mine, other, goals_mine, pick, episodes, *hidden = kernel(
        functools.partial(arrange_kernel, n_blk, n_rep, slab),
        "arrange",
        [side, side, side, ((rows_all // 2, rows_all), BF), ((1, rows_all // 2), F32)]
        + [((quarter, rows_all // 2), BF)] * 4,
        (*(got[k] for k in range(n_blk)), *(swap(got[k], "sub") for k in range(n_blk)), sf, gf),
        [
            pltpu.VMEM((rows_all, width), BF),
            pltpu.VMEM((16, rows_all // 2), F32),
        ],
        pos=True,
    )
    there2 = after(there2, pick)
    late = [swap(x, "sub") for x in (part2, there2, sums[1])]
    half = rows_all // 2
    phi, psi = kernel(
        functools.partial(gather_kernel, n_blk, n_rep, slab),
        "gather",
        [((half, emb), BF), ((half, emb), F32)],
        (sums[0], sums[1], part2, sums[3], there2, swap(sums[0], "sub"), swap(sums[3], "sub"), pick),
        [pltpu.VMEM((rows_all - 2 * rows_dev, emb), BF)],
        pos=True,
    )
    (grads_mine,) = kernel(
        functools.partial(contrast_kernel, n_rep, 4.0 / math.sqrt(emb)),
        "contrast",
        [((half, 2 * emb), BF)],
        (phi, psi, *late, episodes, pick),
        [pltpu.VMEM((2 * rows_dev, emb), BF), pltpu.VMEM((half, emb), BF)],
    )
    grads_other = swap(grads_mine, "sub")
    goals_other = swap(goals_mine, "sub")

    sf, gf, ss, gs = weights
    work = [pltpu.VMEM((quarter, rows_all // 2), BF), pltpu.VMEM((quarter, rows_all // 2), BF)]
    flops = 4 * rows_all * width * quarter
    sums_s2, sums_s1, sums_g2, sums_g1 = kernel(
        mine_kernel,
        "mine",
        [((quarter, emb), F32), ((quarter, width), F32)] * 2,
        (ss, gs, grads_mine, mine, goals_mine, *hidden),
        work[:1],
        pos=True,
        flops=2 * flops,
    )
    halves = [((2 * quarter, emb), BF), ((width, quarter), F32), ((quarter, emb), F32)]
    wholes = [((width, hid), F32), ((hid, emb), F32)]
    state_halves, state_first_own, state_second_own = kernel(
        functools.partial(other_kernel, 0, 0),
        "other_state",
        halves,
        (sf, ss, grads_other, other, sums_s2, sums_s1),
        work,
        pos=True,
        flops=flops,
    )
    state_there = swap(state_halves, "sub")
    goal_halves, goal_first_own, goal_second_own, out0, out1 = kernel(
        functools.partial(other_kernel, 1, 2),
        "other_goal",
        halves + wholes,
        (gf, gs, grads_other, goals_other, sums_g2, sums_g1, state_first_own, state_second_own),
        work + [pltpu.SemaphoreType.DMA((2,))],
        pos=True,
        flops=flops,
        hbm_out=(3, 4),
    )
    goal_there = swap(goal_halves, "sub")
    out0, out1, out2, out3 = finish(state_there, (goal_first_own, goal_second_own), (out0, out1), wholes)
    out2, out3 = finish(goal_there, (), (out2, out3), [])
    return (out0, out1, out2, out3)


def silu_slope(hidden):
    sig = jax.nn.sigmoid(hidden)
    return sig * (1.0 + hidden * (1.0 - sig))


def encoder_grads(rows_in, hidden, active, second, emb_grad):
    grad_second = jnp.einsum("nh,ne->he", active, emb_grad, preferred_element_type=jnp.float32)
    back = jnp.einsum("ne,he->nh", emb_grad, second, preferred_element_type=jnp.float32)
    back_rows = (back * silu_slope(hidden)).astype(jnp.bfloat16)
    grad_first = jnp.einsum("ns,nh->sh", rows_in, back_rows, preferred_element_type=jnp.float32)
    return (grad_first, grad_second)


def exchanged(
    states, goal_distance, goal_row, episode, state_first, state_second, goal_first, goal_second
):
    rows_dev, width = states.shape
    owners = lax.axis_size(("blk", "sub"))
    position = lax.axis_index(("blk", "sub"))
    capacity = 4 * rows_dev // owners
    target = (position + goal_distance[:, 0]) % owners
    onehot = (target[:, None] == jnp.arange(owners, dtype=jnp.int32)[None, :]).astype(jnp.int32)
    slot_rank = jnp.sum((jnp.cumsum(onehot, axis=0) - onehot) * onehot, axis=1)
    requests = jnp.zeros((owners, capacity), jnp.int32).at[target, slot_rank].set(goal_row)
    wanted = lax.all_to_all(requests, ("blk", "sub"), split_axis=0, concat_axis=0, tiled=True)
    fetched = jnp.take(states, wanted.reshape(-1), axis=0).reshape(wanted.shape + (width,))
    replies = lax.all_to_all(fetched, ("blk", "sub"), split_axis=0, concat_axis=0, tiled=True)
    goal_states = jnp.take(
        replies.reshape(owners * capacity, width), target * capacity + slot_rank, axis=0
    )
    slab_rows = rows_dev // lax.axis_size("rep")
    state_hidden = jnp.dot(states, state_first, preferred_element_type=jnp.float32)
    state_active = jax.nn.silu(state_hidden).astype(jnp.bfloat16)
    goal_hidden = jnp.dot(goal_states, goal_first, preferred_element_type=jnp.float32)
    goal_active = jax.nn.silu(goal_hidden).astype(jnp.bfloat16)
    phi = lax.psum_scatter(
        jnp.dot(state_active, state_second, preferred_element_type=jnp.float32),
        "rep",
        scatter_dimension=0,
        tiled=True,
    ).astype(jnp.bfloat16)
    psi = lax.psum_scatter(
        jnp.dot(goal_active, goal_second, preferred_element_type=jnp.float32),
        "rep",
        scatter_dimension=0,
        tiled=True,
    ).astype(jnp.bfloat16)
    episode_own = lax.dynamic_slice_in_dim(episode, lax.axis_index("rep") * slab_rows, slab_rows, 0)
    psi_all, episode_all = (
        lax.all_gather(psi, "blk", axis=0, tiled=True),
        lax.all_gather(episode_own, "blk", axis=0, tiled=True),
    )
    batch_rows = psi_all.shape[0]
    logit_scale = 4.0 / math.sqrt(psi.shape[1])
    own_rows = lax.axis_index("blk") * slab_rows + jnp.arange(slab_rows, dtype=jnp.int32)
    columns = jnp.arange(batch_rows, dtype=jnp.int32)
    diagonal = own_rows[:, None] == columns[None, :]
    excluded = (episode_own[:, None] == episode_all[None, :]) & ~diagonal
    scores = jnp.einsum("ie,je->ij", phi, psi_all, preferred_element_type=jnp.float32) * logit_scale
    exponent = jnp.where(excluded, 0.0, jnp.exp(scores))
    totals = jnp.sum(exponent, axis=1)
    delta = (exponent / totals[:, None] - diagonal.astype(jnp.float32)).astype(jnp.bfloat16)
    phi_grad = (jnp.dot(delta, psi_all, preferred_element_type=jnp.float32) * logit_scale).astype(
        jnp.bfloat16
    )
    psi_grad = lax.psum_scatter(
        jnp.einsum("ij,ie->je", delta, phi, preferred_element_type=jnp.float32) * logit_scale,
        "blk",
        scatter_dimension=0,
        tiled=True,
    ).astype(jnp.bfloat16)
    phi_full, psi_full = (
        lax.all_gather(phi_grad, "rep", axis=0, tiled=True),
        lax.all_gather(psi_grad, "rep", axis=0, tiled=True),
    )
    state_parts = encoder_grads(states, state_hidden, state_active, state_second, phi_full)
    goal_parts = encoder_grads(goal_states, goal_hidden, goal_active, goal_second, psi_full)
    summed = lax.psum(
        (state_parts[0], state_parts[1], goal_parts[0], goal_parts[1]), ("blk", "sub")
    )
    return (summed[0], summed[1], summed[2], summed[3])


def solution(mesh):
    in_specs = (
        P(("grp", "blk", "sub"), None),
        P(("grp", "blk", "sub"), None),
        P(("grp", "blk", "sub")),
        P(("grp", "blk", "sub")),
        P(None, "rep"),
        P("rep", None),
        P(None, "rep"),
        P("rep", None),
    )
    out_specs = (P("grp", "rep"), P(("grp", "rep"), None), P("grp", "rep"), P(("grp", "rep"), None))

    def local(states, *others):
        small = (mesh.shape["blk"], mesh.shape["rep"], mesh.shape["sub"]) == (4, 2, 2)
        plan = gathered if small and states.shape[0] == states.shape[1] == 256 else exchanged
        return plan(states, *others)

    return jax.shard_map(local, mesh=mesh, in_specs=in_specs, out_specs=out_specs, check_vma=False)
```

```python
import functools
import math

import jax
import jax.numpy as jnp
from jax import lax
from jax.experimental import pallas as pl
from jax.experimental.pallas import tpu as pltpu
from jax.sharding import PartitionSpec as P

BF = jnp.bfloat16
F32 = jnp.float32
MIB = 1024 * 1024


def dot(a, b):
    return jnp.dot(a, b, preferred_element_type=F32)


def sigmoid(v):
    return 0.5 * jnp.tanh(0.5 * v) + 0.5


HBM = pl.BlockSpec(memory_space=pltpu.HBM)
VMEM = pl.BlockSpec(memory_space=pltpu.VMEM)
SMEM = pl.BlockSpec(memory_space=pltpu.SMEM)


def kernel(body, name, outs, args, scratch=(), limit=16, pos=False, flops=0, hbm=(), hbm_out=(), aliases={}):
    specs = [HBM if i in hbm else VMEM for i in range(len(args))]
    if pos:
        inner = body

        def body(*refs):
            inner((lax.axis_index("blk"), lax.axis_index("sub")), *refs)

    return pl.pallas_call(
        body,
        in_specs=specs,
        out_specs=[HBM if i in hbm_out else VMEM for i in range(len(outs))],
        out_shape=[jax.ShapeDtypeStruct(shape, dtype) for shape, dtype in outs],
        scratch_shapes=scratch,
        input_output_aliases=aliases,
        compiler_params=pltpu.CompilerParams(vmem_limit_bytes=int(limit * MIB)),
        cost_estimate=pl.CostEstimate(flops=flops, bytes_accessed=0, transcendentals=0),
        name=name,
    )(*args)


def encode(x_ref, weights, out_ref, active, ready=lambda i: None):
    emb = weights[2].shape[1]
    for k in range(2):
        first, second = weights[k], weights[2 + k]
        ready(k)
        for c in range(0, active.shape[1], 512):
            hidden = dot(x_ref[...], first[:, c : c + 512])
            active[:, c : c + 512] = (hidden * sigmoid(hidden)).astype(BF)
        ready(2 + k)
        out_ref[:, k * emb : (k + 1) * emb] = dot(active[...], second[...]).astype(BF)


def blank_kernel(out_ref):
    out_ref[...] = jnp.zeros_like(out_ref)


def pack_kernel(n_blk, n_sub, pos, blank_ref, x_ref, distance_ref, place_ref, episode_ref, pack_ref):
    rows = x_ref.shape[0]
    owner = (pos[0] * n_sub + pos[1] + distance_ref[...]) & (n_blk * n_sub - 1)
    digits = (owner, place_ref[...], episode_ref[...])
    table = jnp.concatenate([d.astype(F32) for d in digits] + [blank_ref[3:, :]], axis=0)
    pack_ref[:rows, :] = x_ref[...]
    pack_ref[rows:, :] = table.astype(BF)


def forward_kernel(x_ref, *refs):
    encode(x_ref.at[: refs[4].shape[0]], refs[:4], refs[4], refs[5])


def forward(x, weights, rows):
    hid, emb = weights[2].shape
    return kernel(
        forward_kernel,
        "forward",
        [((rows, 2 * emb), BF)],
        (x, *weights),
        [pltpu.VMEM((rows, hid), BF)],
        limit=8,
    )[0]


def add_kernel(a_ref, b_ref, out_ref):
    out_ref[...] = (a_ref[...].astype(F32) + b_ref[...].astype(F32)).astype(BF)


def both(part, there):
    return kernel(add_kernel, "both", [(part.shape, BF)], (part, there), limit=4)[0]


def place_blocks(pos, blocks, put, n_blk, n_rep, slab):
    for k, block in enumerate(blocks):
        at = jnp.bitwise_xor(pos[0], k)
        for r in range(n_rep):
            off = (r * n_blk + at) * slab
            put(pl.multiple_of(off, slab), block[r * slab : (r + 1) * slab, :])


def column(row):
    return jnp.broadcast_to(row, (128, row.shape[1])).T[:, :1]


def place_in_turn(k, n_blk):
    return -k & (n_blk - 1)


def arrange_kernel(n_blk, n_rep, slab, pos, *refs):
    mine, other, firsts = refs[:n_blk], refs[n_blk : 2 * n_blk], refs[2 * n_blk : 2 * n_blk + 2]
    rows_mine, rows_other, goals_ref, pick_ref, ep_ref, *hidden, both_sides, meta = refs[2 * n_blk + 2 :]
    rows = both_sides.shape[0]
    batch, rows_dev = n_blk * slab, n_rep * slab
    for i, (blocks, to) in enumerate(((mine, rows_mine), (other, rows_other))):

        def put(off, value, to=to):
            to[pl.ds(off, slab), :] = value

        place_blocks(pos, blocks, put, n_blk, n_rep, slab)
        for k, block in enumerate(blocks):
            at = (i * n_blk + place_in_turn(k, n_blk)) * rows_dev
            both_sides[at : at + rows_dev, :] = block[:rows_dev, :]
    for k, block in enumerate(mine):
        at = jnp.bitwise_xor(pos[0], k)
        for r in range(n_rep):
            off = pl.multiple_of((r * n_blk + at) * slab, slab)
            meta[:, pl.ds(off, slab)] = block[rows_dev:, r * slab : (r + 1) * slab].astype(F32)
    ep_ref[...] = meta[2:3, :]
    for r in range(n_rep):
        own = slice(r * batch, (r + 1) * batch)
        owner, place = meta[0:1, own].astype(jnp.int32), meta[1:2, own].astype(jnp.int32)
        side = (owner & 1) ^ pos[1]
        column_of = (side * n_blk + place_in_turn((owner >> 1) ^ pos[0], n_blk)) * rows_dev + place
        goal = column(column_of.astype(F32)).astype(jnp.int32)
        pick_ref[own, :] = jnp.where(
            goal == lax.broadcasted_iota(jnp.int32, (batch, rows), 1), 1.0, 0.0
        ).astype(BF)
    goals_ref[...] = dot(pick_ref[...], both_sides[...]).astype(BF)
    activate(pos, firsts, (rows_mine, goals_ref), hidden)


def gather_kernel(n_blk, n_rep, slab, pos, *refs):
    mine, extra, other, pick_ref = refs[:n_blk], refs[n_blk], refs[n_blk + 1 : n_blk + 3], refs[n_blk + 3]
    phi_ref, psi_ref, early = refs[n_blk + 4 :]
    emb = phi_ref.shape[1]
    rows_dev = n_rep * slab
    blocks = list(mine)
    blocks[n_blk - 2] = (mine[n_blk - 2][...].astype(F32) + extra[...].astype(F32)).astype(BF)

    def put(off, value):
        phi_ref[pl.ds(off, slab), :] = value[:, :emb]

    place_blocks(pos, blocks, put, n_blk, n_rep, slab)
    for k, block in enumerate(blocks):
        at = place_in_turn(k, n_blk) * rows_dev
        early[at : at + rows_dev, :] = block[:, emb:]
    for i, block in enumerate(other):
        at = (n_blk + i) * rows_dev
        early[at : at + rows_dev, :] = block[:, emb:]
    psi_ref[...] = dot(pick_ref[:, : early.shape[0]], early[...])


def contrast_kernel(n_rep, scale, phi_ref, psi_ref, part_ref, there_ref, sums_ref, ep_ref, pick_ref, grads_ref, late, psi_all):
    half, emb = phi_ref.shape
    batch = half // n_rep
    rows_dev = sums_ref.shape[0]
    late[:rows_dev, :] = (part_ref[:, emb:].astype(F32) + there_ref[:, emb:].astype(F32)).astype(BF)
    late[rows_dev:, :] = sums_ref[:, emb:]
    psi_all[...] = (psi_ref[...] + dot(pick_ref[:, pick_ref.shape[1] - 2 * rows_dev :], late[...])).astype(BF)
    diagonal = lax.broadcasted_iota(jnp.int32, (batch, batch), 0) == lax.broadcasted_iota(
        jnp.int32, (batch, batch), 1
    )
    for r in range(n_rep):
        own = slice(r * batch, (r + 1) * batch)
        ep_row = ep_ref[:, own]
        psi = psi_all[own, :]
        phi = phi_ref[own, :]
        scores = lax.dot_general(phi, psi, (((1,), (1,)), ((), ())), preferred_element_type=F32)
        kept = (column(ep_row) != ep_row) | diagonal
        exponent = jnp.where(kept, jnp.exp(scores * scale), 0.0)
        totals = jnp.sum(exponent, axis=1, keepdims=True)
        power = jnp.where(totals > 1.0, 2.0**-32, 1.0)
        shares = (exponent * power) * (1.0 / (totals * power))
        delta = jnp.where(diagonal, shares - 1.0, shares).astype(BF)
        grads_ref[own, :emb] = (dot(delta, psi) * scale).astype(BF)
        grads_ref[own, emb:] = (dot(delta.T, phi) * scale).astype(BF)


def rows_grads(at, first_ref, second_ref, grads_ref, k, rows_ref, active, back):
    quarter, rows = active.shape
    emb = second_ref.shape[1]
    first_t = first_ref[:, pl.ds(at, quarter)].T
    second = second_ref[pl.ds(at, quarter), :]
    grad = grads_ref[:, k * emb : (k + 1) * emb]
    chunk = 256
    for c in range(0, rows, chunk):
        cols = slice(c, c + chunk)
        hidden = dot(first_t, rows_ref[cols, :].T)
        sig = sigmoid(hidden)
        act = hidden * sig
        active[:, cols] = act.astype(BF)
        slope = sig + act * (1.0 - sig)
        back[:, cols] = (dot(second, grad[cols, :].T) * slope).astype(BF)
    return dot(active[...], grad), dot(back[...], rows_ref[...])


def activate(pos, firsts, inputs, outs):
    quarter, rows = outs[0].shape
    at = pl.multiple_of(pos[1] * quarter, quarter)
    for k, (first, x_ref) in enumerate(zip(firsts, inputs)):
        first_t = first[:, pl.ds(at, quarter)].T
        for c in range(0, rows, 256):
            cols = slice(c, c + 256)
            hidden = dot(first_t, x_ref[cols, :].T)
            sig = sigmoid(hidden)
            act = hidden * sig
            outs[2 * k][:, cols] = act.astype(BF)
            outs[2 * k + 1][:, cols] = (sig + act * (1.0 - sig)).astype(BF)


def mine_kernel(pos, ss, gs, grads_ref, rows_ref, goals_ref, *refs):
    hidden, outs, back = refs[:4], refs[4:8], refs[8]
    quarter, rows = back.shape
    emb = ss.shape[1]
    at = pl.multiple_of(pos[1] * quarter, quarter)
    for k, (second_ref, x_ref) in enumerate(((ss, rows_ref), (gs, goals_ref))):
        second = second_ref[pl.ds(at, quarter), :]
        grad = grads_ref[:, k * emb : (k + 1) * emb]
        for c in range(0, rows, 256):
            cols = slice(c, c + 256)
            back[:, cols] = (dot(second, grad[cols, :].T) * hidden[2 * k + 1][:, cols].astype(F32)).astype(BF)
        outs[2 * k][...] = dot(hidden[2 * k][...], grad)
        outs[2 * k + 1][...] = dot(back[...], x_ref[...])


def other_kernel(k, n_put, pos, first, second, grads_ref, rows_ref, sum_second, sum_first, *refs):
    done, outs, puts, (active, back), sems = (
        refs[:n_put],
        refs[n_put : n_put + 4],
        refs[n_put + 4 : 2 * n_put + 4],
        refs[2 * n_put + 4 : 2 * n_put + 6],
        refs[2 * n_put + 6 :],
    )
    copies = [put_half(pos[1], x, o, sems[0].at[i]) for i, (x, o) in enumerate(zip(done, puts))]
    for c in copies:
        c.start()
    quarter = active.shape[0]
    at = pl.multiple_of(pos[1] * quarter, quarter)
    grad_second, grad_first = rows_grads(at, first, second, grads_ref, k, rows_ref, active, back)
    halves = ((sum_first[...] + grad_first).astype(BF).T, (sum_second[...] + grad_second).astype(BF))
    for half, out16, out32 in zip(halves, outs[:2], outs[2:]):
        out16[...] = half
        out32[...] = half.astype(F32)
    for c in copies:
        c.wait()


def put_half(side, half, out, sem):
    n, m = half.shape
    if out.shape[0] == n:
        to = out.at[:, pl.ds(pl.multiple_of(side * m, m), m)]
    else:
        to = out.at[pl.ds(pl.multiple_of(side * n, n), n), :]
    return pltpu.make_async_copy(half, to, sem)


def finish_kernel(old, new, pos, *refs):
    n = old + new
    halves, outs, scratch, sems = refs[:n], refs[n + old : 2 * n + old], refs[2 * n + old : -1], refs[-1]
    copies = [put_half(pos[1], x, o, sems.at[old + i]) for i, (x, o) in enumerate(zip(halves[old:], outs[old:]))]
    for c in copies:
        c.start()
    for i in range(old):
        scratch[i][...] = halves[i][...].astype(F32)
        copies.append(put_half(1 - pos[1], scratch[i], outs[i], sems.at[i]))
        copies[-1].start()
    for c in copies:
        c.wait()


def finish(there, own, wholes, shapes):
    old, new = len(wholes), len(shapes)
    n = old + new
    return kernel(
        functools.partial(finish_kernel, old, new),
        "finish",
        [(w.shape, w.dtype) for w in wholes] + shapes,
        (*there, *own, *wholes),
        [*(pltpu.VMEM(x.shape, F32) for x in there), pltpu.SemaphoreType.DMA((n,))],
        pos=True,
        hbm=range(n, n + old),
        hbm_out=range(n),
        aliases={n + i: i for i in range(old)},
    )


def gathered(
    states, goal_distance, goal_row, episode, state_first, state_second, goal_first, goal_second
):
    rows_dev, width = states.shape
    n_blk, n_rep, n_sub = (lax.axis_size(a) for a in ("blk", "rep", "sub"))
    slab = rows_dev // n_rep
    rows_all = n_blk * n_sub * rows_dev
    hid, emb = state_second.shape
    quarter = hid // n_sub

    def across(x, k):
        return lax.ppermute(x, "blk", [(i, i ^ k) for i in range(n_blk)])

    def swap(x, axis):
        return lax.ppermute(x, axis, [(0, 1), (1, 0)])

    def after(x, *first):
        return lax.optimization_barrier((x, *first))[0]

    weights = (state_first, goal_first, state_second, goal_second)
    (blank,) = kernel(blank_kernel, "blank", [((16, rows_dev), F32)], (), limit=1, flops=2**32)
    (pack,) = kernel(
        functools.partial(pack_kernel, n_blk, n_sub),
        "pack",
        [((rows_dev + 16, width), BF)],
        (blank, states, *(x.reshape(1, rows_dev) for x in (goal_distance, goal_row, episode))),
        pos=True,
        limit=4,
        flops=2**32,
    )
    got = {0: pack, 3: across(pack, 3)}
    held = weights
    part0 = forward(pack, held, rows_dev)
    got[1] = across(after(pack, part0), 1)
    got[2] = across(after(pack, got[3]), 2)
    there0 = swap(part0, "rep")
    part3 = forward(got[3], held, rows_dev)
    there3 = swap(part3, "rep")

    sums = {0: both(part0, there0)}
    sums[1] = across(after(sums[0], got[2]), 1)
    others = {k: swap(got[k], "sub") for k in (0, 3)}
    part2 = forward(after(got[2], sums[0], others[0], others[3]), held, rows_dev)
    others.update({k: swap(got[k], "sub") for k in (1, 2)})
    there2 = swap(part2, "rep")
    sums[3] = both(part3, there3)

    side = ((rows_all // 2, width), BF)
    sf, gf, ss, gs = held
    mine, other, goals_mine, pick, episodes, *hidden = kernel(
        functools.partial(arrange_kernel, n_blk, n_rep, slab),
        "arrange",
        [side, side, side, ((rows_all // 2, rows_all), BF), ((1, rows_all // 2), F32)]
        + [((quarter, rows_all // 2), BF)] * 4,
        (*(got[k] for k in range(n_blk)), *(others[k] for k in range(n_blk)), sf, gf),
        [
            pltpu.VMEM((rows_all, width), BF),
            pltpu.VMEM((16, rows_all // 2), F32),
        ],
        pos=True,
    )
    there2 = after(there2, pick)
    late = [swap(x, "sub") for x in (part2, there2, sums[1])]
    half = rows_all // 2
    phi, psi = kernel(
        functools.partial(gather_kernel, n_blk, n_rep, slab),
        "gather",
        [((half, emb), BF), ((half, emb), F32)],
        (sums[0], sums[1], part2, sums[3], there2, swap(sums[0], "sub"), swap(sums[3], "sub"), pick),
        [pltpu.VMEM((rows_all - 2 * rows_dev, emb), BF)],
        pos=True,
    )
    (grads_mine,) = kernel(
        functools.partial(contrast_kernel, n_rep, 4.0 / math.sqrt(emb)),
        "contrast",
        [((half, 2 * emb), BF)],
        (phi, psi, *late, episodes, pick),
        [pltpu.VMEM((2 * rows_dev, emb), BF), pltpu.VMEM((half, emb), BF)],
    )
    grads_other = swap(grads_mine, "sub")
    goals_other = swap(goals_mine, "sub")

    sf, gf, ss, gs = weights
    work = [pltpu.VMEM((quarter, rows_all // 2), BF), pltpu.VMEM((quarter, rows_all // 2), BF)]
    flops = 4 * rows_all * width * quarter
    sums_s2, sums_s1, sums_g2, sums_g1 = kernel(
        mine_kernel,
        "mine",
        [((quarter, emb), F32), ((quarter, width), F32)] * 2,
        (ss, gs, grads_mine, mine, goals_mine, *hidden),
        work[:1],
        pos=True,
        flops=2 * flops,
    )
    halves = [(shape, kind) for kind in (BF, F32) for shape in ((width, quarter), (quarter, emb))]
    wholes = [((width, hid), F32), ((hid, emb), F32)]
    *state_halves, state_first_own, state_second_own = kernel(
        functools.partial(other_kernel, 0, 0),
        "other_state",
        halves,
        (sf, ss, grads_other, other, sums_s2, sums_s1),
        work,
        pos=True,
        flops=flops,
    )
    state_there = [swap(x, "sub") for x in state_halves]
    *goal_halves, goal_first_own, goal_second_own, out0, out1 = kernel(
        functools.partial(other_kernel, 1, 2),
        "other_goal",
        halves + wholes,
        (gf, gs, grads_other, goals_other, sums_g2, sums_g1, state_first_own, state_second_own),
        work + [pltpu.SemaphoreType.DMA((2,))],
        pos=True,
        flops=flops,
        hbm_out=(4, 5),
    )
    goal_there = [swap(x, "sub") for x in goal_halves]
    out0, out1, out2, out3 = finish(state_there, (goal_first_own, goal_second_own), (out0, out1), wholes)
    out2, out3 = finish(goal_there, (), (out2, out3), [])
    return (out0, out1, out2, out3)


def silu_slope(hidden):
    sig = jax.nn.sigmoid(hidden)
    return sig * (1.0 + hidden * (1.0 - sig))


def encoder_grads(rows_in, hidden, active, second, emb_grad):
    grad_second = jnp.einsum("nh,ne->he", active, emb_grad, preferred_element_type=jnp.float32)
    back = jnp.einsum("ne,he->nh", emb_grad, second, preferred_element_type=jnp.float32)
    back_rows = (back * silu_slope(hidden)).astype(jnp.bfloat16)
    grad_first = jnp.einsum("ns,nh->sh", rows_in, back_rows, preferred_element_type=jnp.float32)
    return (grad_first, grad_second)


def exchanged(
    states, goal_distance, goal_row, episode, state_first, state_second, goal_first, goal_second
):
    rows_dev, width = states.shape
    owners = lax.axis_size(("blk", "sub"))
    position = lax.axis_index(("blk", "sub"))
    capacity = 4 * rows_dev // owners
    target = (position + goal_distance[:, 0]) % owners
    onehot = (target[:, None] == jnp.arange(owners, dtype=jnp.int32)[None, :]).astype(jnp.int32)
    slot_rank = jnp.sum((jnp.cumsum(onehot, axis=0) - onehot) * onehot, axis=1)
    requests = jnp.zeros((owners, capacity), jnp.int32).at[target, slot_rank].set(goal_row)
    wanted = lax.all_to_all(requests, ("blk", "sub"), split_axis=0, concat_axis=0, tiled=True)
    fetched = jnp.take(states, wanted.reshape(-1), axis=0).reshape(wanted.shape + (width,))
    replies = lax.all_to_all(fetched, ("blk", "sub"), split_axis=0, concat_axis=0, tiled=True)
    goal_states = jnp.take(
        replies.reshape(owners * capacity, width), target * capacity + slot_rank, axis=0
    )
    slab_rows = rows_dev // lax.axis_size("rep")
    state_hidden = jnp.dot(states, state_first, preferred_element_type=jnp.float32)
    state_active = jax.nn.silu(state_hidden).astype(jnp.bfloat16)
    goal_hidden = jnp.dot(goal_states, goal_first, preferred_element_type=jnp.float32)
    goal_active = jax.nn.silu(goal_hidden).astype(jnp.bfloat16)
    phi = lax.psum_scatter(
        jnp.dot(state_active, state_second, preferred_element_type=jnp.float32),
        "rep",
        scatter_dimension=0,
        tiled=True,
    ).astype(jnp.bfloat16)
    psi = lax.psum_scatter(
        jnp.dot(goal_active, goal_second, preferred_element_type=jnp.float32),
        "rep",
        scatter_dimension=0,
        tiled=True,
    ).astype(jnp.bfloat16)
    episode_own = lax.dynamic_slice_in_dim(episode, lax.axis_index("rep") * slab_rows, slab_rows, 0)
    psi_all, episode_all = (
        lax.all_gather(psi, "blk", axis=0, tiled=True),
        lax.all_gather(episode_own, "blk", axis=0, tiled=True),
    )
    batch_rows = psi_all.shape[0]
    logit_scale = 4.0 / math.sqrt(psi.shape[1])
    own_rows = lax.axis_index("blk") * slab_rows + jnp.arange(slab_rows, dtype=jnp.int32)
    columns = jnp.arange(batch_rows, dtype=jnp.int32)
    diagonal = own_rows[:, None] == columns[None, :]
    excluded = (episode_own[:, None] == episode_all[None, :]) & ~diagonal
    scores = jnp.einsum("ie,je->ij", phi, psi_all, preferred_element_type=jnp.float32) * logit_scale
    exponent = jnp.where(excluded, 0.0, jnp.exp(scores))
    totals = jnp.sum(exponent, axis=1)
    delta = (exponent / totals[:, None] - diagonal.astype(jnp.float32)).astype(jnp.bfloat16)
    phi_grad = (jnp.dot(delta, psi_all, preferred_element_type=jnp.float32) * logit_scale).astype(
        jnp.bfloat16
    )
    psi_grad = lax.psum_scatter(
        jnp.einsum("ij,ie->je", delta, phi, preferred_element_type=jnp.float32) * logit_scale,
        "blk",
        scatter_dimension=0,
        tiled=True,
    ).astype(jnp.bfloat16)
    phi_full, psi_full = (
        lax.all_gather(phi_grad, "rep", axis=0, tiled=True),
        lax.all_gather(psi_grad, "rep", axis=0, tiled=True),
    )
    state_parts = encoder_grads(states, state_hidden, state_active, state_second, phi_full)
    goal_parts = encoder_grads(goal_states, goal_hidden, goal_active, goal_second, psi_full)
    summed = lax.psum(
        (state_parts[0], state_parts[1], goal_parts[0], goal_parts[1]), ("blk", "sub")
    )
    return (summed[0], summed[1], summed[2], summed[3])


def solution(mesh):
    in_specs = (
        P(("grp", "blk", "sub"), None),
        P(("grp", "blk", "sub"), None),
        P(("grp", "blk", "sub")),
        P(("grp", "blk", "sub")),
        P(None, "rep"),
        P("rep", None),
        P(None, "rep"),
        P("rep", None),
    )
    out_specs = (P("grp", "rep"), P(("grp", "rep"), None), P("grp", "rep"), P(("grp", "rep"), None))

    def local(states, *others):
        small = (mesh.shape["blk"], mesh.shape["rep"], mesh.shape["sub"]) == (4, 2, 2)
        plan = gathered if small and states.shape[0] == states.shape[1] == 256 else exchanged
        return plan(states, *others)

    return jax.shard_map(local, mesh=mesh, in_specs=in_specs, out_specs=out_specs, check_vma=False)
```

```python
import functools
import math

import jax
import jax.numpy as jnp
from jax import lax
from jax.experimental import pallas as pl
from jax.experimental.pallas import tpu as pltpu
from jax.sharding import PartitionSpec as P

BF = jnp.bfloat16
F32 = jnp.float32
MIB = 1024 * 1024


def dot(a, b):
    return jnp.dot(a, b, preferred_element_type=F32)


def sigmoid(v):
    return 0.5 * jnp.tanh(0.5 * v) + 0.5


HBM = pl.BlockSpec(memory_space=pltpu.HBM)
VMEM = pl.BlockSpec(memory_space=pltpu.VMEM)
SMEM = pl.BlockSpec(memory_space=pltpu.SMEM)


def kernel(body, name, outs, args, scratch=(), limit=16, pos=False, flops=0, hbm=(), hbm_out=(), aliases={}):
    specs = [HBM if i in hbm else VMEM for i in range(len(args))]
    if pos:
        inner = body

        def body(*refs):
            inner((lax.axis_index("blk"), lax.axis_index("sub")), *refs)

    return pl.pallas_call(
        body,
        in_specs=specs,
        out_specs=[HBM if i in hbm_out else VMEM for i in range(len(outs))],
        out_shape=[jax.ShapeDtypeStruct(shape, dtype) for shape, dtype in outs],
        scratch_shapes=scratch,
        input_output_aliases=aliases,
        compiler_params=pltpu.CompilerParams(vmem_limit_bytes=int(limit * MIB)),
        cost_estimate=pl.CostEstimate(flops=flops, bytes_accessed=0, transcendentals=0),
        name=name,
    )(*args)


def encode(x_ref, weights, out_ref, active, ready=lambda i: None):
    emb = weights[2].shape[1]
    for k in range(2):
        first, second = weights[k], weights[2 + k]
        ready(k)
        for c in range(0, active.shape[1], 512):
            hidden = dot(x_ref[...], first[:, c : c + 512])
            active[:, c : c + 512] = (hidden * sigmoid(hidden)).astype(BF)
        ready(2 + k)
        out_ref[:, k * emb : (k + 1) * emb] = dot(active[...], second[...]).astype(BF)


def blank_kernel(out_ref):
    out_ref[...] = jnp.zeros_like(out_ref)


def pack_kernel(n_blk, n_sub, pos, blank_ref, x_ref, distance_ref, place_ref, episode_ref, pack_ref):
    rows = x_ref.shape[0]
    owner = (pos[0] * n_sub + pos[1] + distance_ref[...]) & (n_blk * n_sub - 1)
    digits = (owner, place_ref[...], episode_ref[...])
    table = jnp.concatenate([d.astype(F32) for d in digits] + [blank_ref[3:, :]], axis=0)
    pack_ref[:rows, :] = x_ref[...]
    pack_ref[rows:, :] = table.astype(BF)


def forward_kernel(x_ref, *refs):
    encode(x_ref.at[: refs[4].shape[0]], refs[:4], refs[4], refs[5])


def forward(x, weights, rows):
    hid, emb = weights[2].shape
    return kernel(
        forward_kernel,
        "forward",
        [((rows, 2 * emb), BF)],
        (x, *weights),
        [pltpu.VMEM((rows, hid), BF)],
        limit=8,
    )[0]


def add_kernel(a_ref, b_ref, out_ref):
    out_ref[...] = (a_ref[...].astype(F32) + b_ref[...].astype(F32)).astype(BF)


def both(part, there):
    return kernel(add_kernel, "both", [(part.shape, BF)], (part, there), limit=4)[0]


def place_blocks(pos, blocks, put, n_blk, n_rep, slab):
    for k, block in enumerate(blocks):
        at = jnp.bitwise_xor(pos[0], k)
        for r in range(n_rep):
            off = (r * n_blk + at) * slab
            put(pl.multiple_of(off, slab), block[r * slab : (r + 1) * slab, :])


def column(row):
    return jnp.broadcast_to(row, (128, row.shape[1])).T[:, :1]


def place_in_turn(k, n_blk):
    return -k & (n_blk - 1)


def arrange_kernel(n_blk, n_rep, slab, pos, *refs):
    mine, other, firsts = refs[:n_blk], refs[n_blk : 2 * n_blk], refs[2 * n_blk : 2 * n_blk + 2]
    rows_mine, rows_other, goals_ref, pick_ref, ep_ref, *hidden, both_sides, meta = refs[2 * n_blk + 2 :]
    rows = both_sides.shape[0]
    batch, rows_dev = n_blk * slab, n_rep * slab
    for i, (blocks, to) in enumerate(((mine, rows_mine), (other, rows_other))):

        def put(off, value, to=to):
            to[pl.ds(off, slab), :] = value

        place_blocks(pos, blocks, put, n_blk, n_rep, slab)
        for k, block in enumerate(blocks):
            at = (i * n_blk + place_in_turn(k, n_blk)) * rows_dev
            both_sides[at : at + rows_dev, :] = block[:rows_dev, :]
    for k, block in enumerate(mine):
        at = jnp.bitwise_xor(pos[0], k)
        for r in range(n_rep):
            off = pl.multiple_of((r * n_blk + at) * slab, slab)
            meta[:, pl.ds(off, slab)] = block[rows_dev:, r * slab : (r + 1) * slab].astype(F32)
    ep_ref[...] = meta[2:3, :]
    for r in range(n_rep):
        own = slice(r * batch, (r + 1) * batch)
        owner, place = meta[0:1, own].astype(jnp.int32), meta[1:2, own].astype(jnp.int32)
        side = (owner & 1) ^ pos[1]
        column_of = (side * n_blk + place_in_turn((owner >> 1) ^ pos[0], n_blk)) * rows_dev + place
        goal = column(column_of.astype(F32)).astype(jnp.int32)
        pick_ref[own, :] = jnp.where(
            goal == lax.broadcasted_iota(jnp.int32, (batch, rows), 1), 1.0, 0.0
        ).astype(BF)
    goals_ref[...] = dot(pick_ref[...], both_sides[...]).astype(BF)
    activate(pos, firsts, (rows_mine, goals_ref), hidden)


def gather_kernel(n_blk, n_rep, slab, pos, *refs):
    mine, extra, other, pick_ref = refs[:n_blk], refs[n_blk], refs[n_blk + 1 : n_blk + 3], refs[n_blk + 3]
    phi_ref, psi_ref, early = refs[n_blk + 4 :]
    emb = phi_ref.shape[1]
    rows_dev = n_rep * slab
    blocks = list(mine)
    blocks[n_blk - 2] = (mine[n_blk - 2][...].astype(F32) + extra[...].astype(F32)).astype(BF)

    def put(off, value):
        phi_ref[pl.ds(off, slab), :] = value[:, :emb]

    place_blocks(pos, blocks, put, n_blk, n_rep, slab)
    for k, block in enumerate(blocks):
        at = place_in_turn(k, n_blk) * rows_dev
        early[at : at + rows_dev, :] = block[:, emb:]
    for i, block in enumerate(other):
        at = (n_blk + i) * rows_dev
        early[at : at + rows_dev, :] = block[:, emb:]
    psi_ref[...] = dot(pick_ref[:, : early.shape[0]], early[...])


def contrast_kernel(n_rep, scale, phi_ref, psi_ref, part_ref, there_ref, sums_ref, ep_ref, pick_ref, grads_ref, late, psi_all):
    half, emb = phi_ref.shape
    batch = half // n_rep
    rows_dev = sums_ref.shape[0]
    late[:rows_dev, :] = (part_ref[:, emb:].astype(F32) + there_ref[:, emb:].astype(F32)).astype(BF)
    late[rows_dev:, :] = sums_ref[:, emb:]
    psi_all[...] = (psi_ref[...] + dot(pick_ref[:, pick_ref.shape[1] - 2 * rows_dev :], late[...])).astype(BF)
    diagonal = lax.broadcasted_iota(jnp.int32, (batch, batch), 0) == lax.broadcasted_iota(
        jnp.int32, (batch, batch), 1
    )
    for r in range(n_rep):
        own = slice(r * batch, (r + 1) * batch)
        ep_row = ep_ref[:, own]
        psi = psi_all[own, :]
        phi = phi_ref[own, :]
        scores = lax.dot_general(phi, psi, (((1,), (1,)), ((), ())), preferred_element_type=F32)
        kept = (column(ep_row) != ep_row) | diagonal
        exponent = jnp.where(kept, jnp.exp(scores * scale), 0.0)
        totals = jnp.sum(exponent, axis=1, keepdims=True)
        power = jnp.where(totals > 1.0, 2.0**-32, 1.0)
        shares = (exponent * power) * (1.0 / (totals * power))
        delta = jnp.where(diagonal, shares - 1.0, shares).astype(BF)
        grads_ref[own, :emb] = (dot(delta, psi) * scale).astype(BF)
        grads_ref[own, emb:] = (dot(delta.T, phi) * scale).astype(BF)


def rows_grads(at, first_ref, second_ref, grads_ref, k, rows_ref, active, back):
    quarter, rows = active.shape
    emb = second_ref.shape[1]
    first_t = first_ref[:, pl.ds(at, quarter)].T
    second = second_ref[pl.ds(at, quarter), :]
    grad = grads_ref[:, k * emb : (k + 1) * emb]
    chunk = 256
    for c in range(0, rows, chunk):
        cols = slice(c, c + chunk)
        hidden = dot(first_t, rows_ref[cols, :].T)
        sig = sigmoid(hidden)
        act = hidden * sig
        active[:, cols] = act.astype(BF)
        slope = sig + act * (1.0 - sig)
        back[:, cols] = (dot(second, grad[cols, :].T) * slope).astype(BF)
    return dot(active[...], grad), dot(back[...], rows_ref[...])


def activate(pos, firsts, inputs, outs):
    quarter, rows = outs[0].shape
    at = pl.multiple_of(pos[1] * quarter, quarter)
    for k, (first, x_ref) in enumerate(zip(firsts, inputs)):
        first_t = first[:, pl.ds(at, quarter)].T
        for c in range(0, rows, 256):
            cols = slice(c, c + 256)
            hidden = dot(first_t, x_ref[cols, :].T)
            sig = sigmoid(hidden)
            act = hidden * sig
            outs[2 * k][:, cols] = act.astype(BF)
            outs[2 * k + 1][:, cols] = (sig + act * (1.0 - sig)).astype(BF)


def mine_kernel(pos, ss, gs, grads_ref, rows_ref, goals_ref, *refs):
    hidden, outs, back = refs[:4], refs[4:8], refs[8]
    quarter, rows = back.shape
    emb = ss.shape[1]
    at = pl.multiple_of(pos[1] * quarter, quarter)
    for k, (second_ref, x_ref) in enumerate(((ss, rows_ref), (gs, goals_ref))):
        second = second_ref[pl.ds(at, quarter), :]
        grad = grads_ref[:, k * emb : (k + 1) * emb]
        for c in range(0, rows, 256):
            cols = slice(c, c + 256)
            back[:, cols] = (dot(second, grad[cols, :].T) * hidden[2 * k + 1][:, cols].astype(F32)).astype(BF)
        outs[2 * k][...] = dot(hidden[2 * k][...], grad)
        outs[2 * k + 1][...] = dot(back[...], x_ref[...])


def other_kernel(k, n_put, pos, first, second, grads_ref, rows_ref, sum_second, sum_first, *refs):
    done, outs, puts, (active, back), sems = (
        refs[:n_put],
        refs[n_put : n_put + 4],
        refs[n_put + 4 : 2 * n_put + 4],
        refs[2 * n_put + 4 : 2 * n_put + 6],
        refs[2 * n_put + 6 :],
    )
    copies = [put_half(pos[1], x, o, sems[0].at[i]) for i, (x, o) in enumerate(zip(done, puts))]
    for c in copies:
        c.start()
    quarter = active.shape[0]
    at = pl.multiple_of(pos[1] * quarter, quarter)
    grad_second, grad_first = rows_grads(at, first, second, grads_ref, k, rows_ref, active, back)
    halves = ((sum_first[...] + grad_first).astype(BF).T, (sum_second[...] + grad_second).astype(BF))
    for half, out16, out32 in zip(halves, outs[:2], outs[2:]):
        out16[...] = half
        out32[...] = half.astype(F32)
    for c in copies:
        c.wait()


def put_half(side, half, out, sem):
    n, m = half.shape
    if out.shape[0] == n:
        to = out.at[:, pl.ds(pl.multiple_of(side * m, m), m)]
    else:
        to = out.at[pl.ds(pl.multiple_of(side * n, n), n), :]
    return pltpu.make_async_copy(half, to, sem)


def finish_kernel(old, new, pos, *refs):
    n = old + new
    halves, outs, scratch, sems = refs[:n], refs[n + old : 2 * n + old], refs[2 * n + old : -1], refs[-1]
    copies = [put_half(pos[1], x, o, sems.at[old + i]) for i, (x, o) in enumerate(zip(halves[old:], outs[old:]))]
    for c in copies:
        c.start()
    for i in range(old):
        scratch[i][...] = halves[i][...].astype(F32)
        copies.append(put_half(1 - pos[1], scratch[i], outs[i], sems.at[i]))
        copies[-1].start()
    for c in copies:
        c.wait()


def finish(there, own, wholes, shapes):
    old, new = len(wholes), len(shapes)
    n = old + new
    return kernel(
        functools.partial(finish_kernel, old, new),
        "finish",
        [(w.shape, w.dtype) for w in wholes] + shapes,
        (*there, *own, *wholes),
        [*(pltpu.VMEM(x.shape, F32) for x in there), pltpu.SemaphoreType.DMA((n,))],
        pos=True,
        hbm=range(n, n + old),
        hbm_out=range(n),
        aliases={n + i: i for i in range(old)},
    )


def gathered(
    states, goal_distance, goal_row, episode, state_first, state_second, goal_first, goal_second
):
    rows_dev, width = states.shape
    n_blk, n_rep, n_sub = (lax.axis_size(a) for a in ("blk", "rep", "sub"))
    slab = rows_dev // n_rep
    rows_all = n_blk * n_sub * rows_dev
    hid, emb = state_second.shape
    quarter = hid // n_sub

    def across(x, k):
        return lax.ppermute(x, "blk", [(i, i ^ k) for i in range(n_blk)])

    def swap(x, axis):
        return lax.ppermute(x, axis, [(0, 1), (1, 0)])

    def after(x, *first):
        return lax.optimization_barrier((x, *first))[0]

    weights = (state_first, goal_first, state_second, goal_second)
    (blank,) = kernel(blank_kernel, "blank", [((16, rows_dev), F32)], (), limit=1, flops=2**32)
    (pack,) = kernel(
        functools.partial(pack_kernel, n_blk, n_sub),
        "pack",
        [((rows_dev + 16, width), BF)],
        (blank, states, *(x.reshape(1, rows_dev) for x in (goal_distance, goal_row, episode))),
        pos=True,
        limit=4,
        flops=2**32,
    )
    got = {0: pack, 3: across(pack, 3)}
    held = weights
    part0 = forward(pack, held, rows_dev)
    got[1] = across(after(pack, part0), 1)
    got[2] = across(after(pack, got[3]), 2)
    there0 = swap(part0, "rep")
    part3 = forward(got[3], held, rows_dev)
    there3 = swap(part3, "rep")

    sums = {0: both(part0, there0)}
    sums[1] = across(after(sums[0], got[2]), 1)
    part2 = forward(after(got[2], sums[0]), held, rows_dev)
    there2 = swap(part2, "rep")
    sums[3] = both(part3, there3)

    side = ((rows_all // 2, width), BF)
    sf, gf, ss, gs = held
    mine, other, goals_mine, pick, episodes, *hidden = kernel(
        functools.partial(arrange_kernel, n_blk, n_rep, slab),
        "arrange",
        [side, side, side, ((rows_all // 2, rows_all), BF), ((1, rows_all // 2), F32)]
        + [((quarter, rows_all // 2), BF)] * 4,
        (*(got[k] for k in range(n_blk)), *(swap(got[k], "sub") for k in range(n_blk)), sf, gf),
        [
            pltpu.VMEM((rows_all, width), BF),
            pltpu.VMEM((16, rows_all // 2), F32),
        ],
        pos=True,
    )
    there2 = after(there2, pick)
    late = [swap(x, "sub") for x in (part2, there2, sums[1])]
    half = rows_all // 2
    phi, psi = kernel(
        functools.partial(gather_kernel, n_blk, n_rep, slab),
        "gather",
        [((half, emb), BF), ((half, emb), F32)],
        (sums[0], sums[1], part2, sums[3], there2, swap(sums[0], "sub"), swap(sums[3], "sub"), pick),
        [pltpu.VMEM((rows_all - 2 * rows_dev, emb), BF)],
        pos=True,
    )
    (grads_mine,) = kernel(
        functools.partial(contrast_kernel, n_rep, 4.0 / math.sqrt(emb)),
        "contrast",
        [((half, 2 * emb), BF)],
        (phi, psi, *late, episodes, pick),
        [pltpu.VMEM((2 * rows_dev, emb), BF), pltpu.VMEM((half, emb), BF)],
    )
    grads_other = swap(grads_mine, "sub")
    goals_other = swap(goals_mine, "sub")

    sf, gf, ss, gs = weights
    work = [pltpu.VMEM((quarter, rows_all // 2), BF), pltpu.VMEM((quarter, rows_all // 2), BF)]
    flops = 4 * rows_all * width * quarter
    sums_s2, sums_s1, sums_g2, sums_g1 = kernel(
        mine_kernel,
        "mine",
        [((quarter, emb), F32), ((quarter, width), F32)] * 2,
        (ss, gs, grads_mine, mine, goals_mine, *hidden),
        work[:1],
        pos=True,
        flops=2 * flops,
    )
    halves = [(shape, kind) for kind in (BF, F32) for shape in ((width, quarter), (quarter, emb))]
    wholes = [((width, hid), F32), ((hid, emb), F32)]
    *state_halves, state_first_own, state_second_own = kernel(
        functools.partial(other_kernel, 0, 0),
        "other_state",
        halves,
        (sf, ss, grads_other, other, sums_s2, sums_s1),
        work,
        pos=True,
        flops=flops,
    )
    state_there = [swap(x, "sub") for x in state_halves]
    *goal_halves, goal_first_own, goal_second_own, out0, out1 = kernel(
        functools.partial(other_kernel, 1, 2),
        "other_goal",
        halves + wholes,
        (gf, gs, grads_other, goals_other, sums_g2, sums_g1, state_first_own, state_second_own),
        work + [pltpu.SemaphoreType.DMA((2,))],
        pos=True,
        flops=flops,
        hbm_out=(4, 5),
    )
    goal_there = [swap(x, "sub") for x in goal_halves]
    out0, out1, out2, out3 = finish(state_there, (goal_first_own, goal_second_own), (out0, out1), wholes)
    out2, out3 = finish(goal_there, (), (out2, out3), [])
    return (out0, out1, out2, out3)


def silu_slope(hidden):
    sig = jax.nn.sigmoid(hidden)
    return sig * (1.0 + hidden * (1.0 - sig))


def encoder_grads(rows_in, hidden, active, second, emb_grad):
    grad_second = jnp.einsum("nh,ne->he", active, emb_grad, preferred_element_type=jnp.float32)
    back = jnp.einsum("ne,he->nh", emb_grad, second, preferred_element_type=jnp.float32)
    back_rows = (back * silu_slope(hidden)).astype(jnp.bfloat16)
    grad_first = jnp.einsum("ns,nh->sh", rows_in, back_rows, preferred_element_type=jnp.float32)
    return (grad_first, grad_second)


def exchanged(
    states, goal_distance, goal_row, episode, state_first, state_second, goal_first, goal_second
):
    rows_dev, width = states.shape
    owners = lax.axis_size(("blk", "sub"))
    position = lax.axis_index(("blk", "sub"))
    capacity = 4 * rows_dev // owners
    target = (position + goal_distance[:, 0]) % owners
    onehot = (target[:, None] == jnp.arange(owners, dtype=jnp.int32)[None, :]).astype(jnp.int32)
    slot_rank = jnp.sum((jnp.cumsum(onehot, axis=0) - onehot) * onehot, axis=1)
    requests = jnp.zeros((owners, capacity), jnp.int32).at[target, slot_rank].set(goal_row)
    wanted = lax.all_to_all(requests, ("blk", "sub"), split_axis=0, concat_axis=0, tiled=True)
    fetched = jnp.take(states, wanted.reshape(-1), axis=0).reshape(wanted.shape + (width,))
    replies = lax.all_to_all(fetched, ("blk", "sub"), split_axis=0, concat_axis=0, tiled=True)
    goal_states = jnp.take(
        replies.reshape(owners * capacity, width), target * capacity + slot_rank, axis=0
    )
    slab_rows = rows_dev // lax.axis_size("rep")
    state_hidden = jnp.dot(states, state_first, preferred_element_type=jnp.float32)
    state_active = jax.nn.silu(state_hidden).astype(jnp.bfloat16)
    goal_hidden = jnp.dot(goal_states, goal_first, preferred_element_type=jnp.float32)
    goal_active = jax.nn.silu(goal_hidden).astype(jnp.bfloat16)
    phi = lax.psum_scatter(
        jnp.dot(state_active, state_second, preferred_element_type=jnp.float32),
        "rep",
        scatter_dimension=0,
        tiled=True,
    ).astype(jnp.bfloat16)
    psi = lax.psum_scatter(
        jnp.dot(goal_active, goal_second, preferred_element_type=jnp.float32),
        "rep",
        scatter_dimension=0,
        tiled=True,
    ).astype(jnp.bfloat16)
    episode_own = lax.dynamic_slice_in_dim(episode, lax.axis_index("rep") * slab_rows, slab_rows, 0)
    psi_all, episode_all = (
        lax.all_gather(psi, "blk", axis=0, tiled=True),
        lax.all_gather(episode_own, "blk", axis=0, tiled=True),
    )
    batch_rows = psi_all.shape[0]
    logit_scale = 4.0 / math.sqrt(psi.shape[1])
    own_rows = lax.axis_index("blk") * slab_rows + jnp.arange(slab_rows, dtype=jnp.int32)
    columns = jnp.arange(batch_rows, dtype=jnp.int32)
    diagonal = own_rows[:, None] == columns[None, :]
    excluded = (episode_own[:, None] == episode_all[None, :]) & ~diagonal
    scores = jnp.einsum("ie,je->ij", phi, psi_all, preferred_element_type=jnp.float32) * logit_scale
    exponent = jnp.where(excluded, 0.0, jnp.exp(scores))
    totals = jnp.sum(exponent, axis=1)
    delta = (exponent / totals[:, None] - diagonal.astype(jnp.float32)).astype(jnp.bfloat16)
    phi_grad = (jnp.dot(delta, psi_all, preferred_element_type=jnp.float32) * logit_scale).astype(
        jnp.bfloat16
    )
    psi_grad = lax.psum_scatter(
        jnp.einsum("ij,ie->je", delta, phi, preferred_element_type=jnp.float32) * logit_scale,
        "blk",
        scatter_dimension=0,
        tiled=True,
    ).astype(jnp.bfloat16)
    phi_full, psi_full = (
        lax.all_gather(phi_grad, "rep", axis=0, tiled=True),
        lax.all_gather(psi_grad, "rep", axis=0, tiled=True),
    )
    state_parts = encoder_grads(states, state_hidden, state_active, state_second, phi_full)
    goal_parts = encoder_grads(goal_states, goal_hidden, goal_active, goal_second, psi_full)
    summed = lax.psum(
        (state_parts[0], state_parts[1], goal_parts[0], goal_parts[1]), ("blk", "sub")
    )
    return (summed[0], summed[1], summed[2], summed[3])


def solution(mesh):
    in_specs = (
        P(("grp", "blk", "sub"), None),
        P(("grp", "blk", "sub"), None),
        P(("grp", "blk", "sub")),
        P(("grp", "blk", "sub")),
        P(None, "rep"),
        P("rep", None),
        P(None, "rep"),
        P("rep", None),
    )
    out_specs = (P("grp", "rep"), P(("grp", "rep"), None), P("grp", "rep"), P(("grp", "rep"), None))

    def local(states, *others):
        small = (mesh.shape["blk"], mesh.shape["rep"], mesh.shape["sub"]) == (4, 2, 2)
        plan = gathered if small and states.shape[0] == states.shape[1] == 256 else exchanged
        return plan(states, *others)

    return jax.shard_map(local, mesh=mesh, in_specs=in_specs, out_specs=out_specs, check_vma=False)
```

```python
import functools
import math

import jax
import jax.numpy as jnp
from jax import lax
from jax.experimental import pallas as pl
from jax.experimental.pallas import tpu as pltpu
from jax.sharding import PartitionSpec as P

BF = jnp.bfloat16
F32 = jnp.float32
MIB = 1024 * 1024


def dot(a, b):
    return jnp.dot(a, b, preferred_element_type=F32)


def sigmoid(v):
    return 0.5 * jnp.tanh(0.5 * v) + 0.5


HBM = pl.BlockSpec(memory_space=pltpu.HBM)
VMEM = pl.BlockSpec(memory_space=pltpu.VMEM)
SMEM = pl.BlockSpec(memory_space=pltpu.SMEM)


def kernel(body, name, outs, args, scratch=(), limit=16, pos=False, flops=0, hbm=(), hbm_out=(), aliases={}):
    specs = [HBM if i in hbm else VMEM for i in range(len(args))]
    if pos:
        inner = body

        def body(*refs):
            inner((lax.axis_index("blk"), lax.axis_index("sub")), *refs)

    return pl.pallas_call(
        body,
        in_specs=specs,
        out_specs=[HBM if i in hbm_out else VMEM for i in range(len(outs))],
        out_shape=[jax.ShapeDtypeStruct(shape, dtype) for shape, dtype in outs],
        scratch_shapes=scratch,
        input_output_aliases=aliases,
        compiler_params=pltpu.CompilerParams(vmem_limit_bytes=int(limit * MIB)),
        cost_estimate=pl.CostEstimate(flops=flops, bytes_accessed=0, transcendentals=0),
        name=name,
    )(*args)


def encode(x_ref, weights, out_ref, active, ready=lambda i: None):
    emb = weights[2].shape[1]
    for k in range(2):
        first, second = weights[k], weights[2 + k]
        ready(k)
        for c in range(0, active.shape[1], 512):
            hidden = dot(x_ref[...], first[:, c : c + 512])
            active[:, c : c + 512] = (hidden * sigmoid(hidden)).astype(BF)
        ready(2 + k)
        out_ref[:, k * emb : (k + 1) * emb] = dot(active[...], second[...]).astype(BF)


def blank_kernel(out_ref):
    out_ref[...] = jnp.zeros_like(out_ref)


def pack_kernel(n_blk, n_sub, pos, blank_ref, x_ref, distance_ref, place_ref, episode_ref, pack_ref):
    rows = x_ref.shape[0]
    owner = (pos[0] * n_sub + pos[1] + distance_ref[...]) & (n_blk * n_sub - 1)
    digits = (owner, place_ref[...], episode_ref[...])
    table = jnp.concatenate([d.astype(F32) for d in digits] + [blank_ref[3:, :]], axis=0)
    pack_ref[:rows, :] = x_ref[...]
    pack_ref[rows:, :] = table.astype(BF)


def forward_kernel(x_ref, *refs):
    encode(x_ref.at[: refs[4].shape[0]], refs[:4], refs[4], refs[5])


def forward(x, weights, rows):
    hid, emb = weights[2].shape
    return kernel(
        forward_kernel,
        "forward",
        [((rows, 2 * emb), BF)],
        (x, *weights),
        [pltpu.VMEM((rows, hid), BF)],
        limit=8,
    )[0]


def add_kernel(a_ref, b_ref, out_ref):
    out_ref[...] = (a_ref[...].astype(F32) + b_ref[...].astype(F32)).astype(BF)


def both(part, there):
    return kernel(add_kernel, "both", [(part.shape, BF)], (part, there), limit=4)[0]


def place_blocks(pos, blocks, put, n_blk, n_rep, slab):
    for k, block in enumerate(blocks):
        at = jnp.bitwise_xor(pos[0], k)
        for r in range(n_rep):
            off = (r * n_blk + at) * slab
            put(pl.multiple_of(off, slab), block[r * slab : (r + 1) * slab, :])


def column(row):
    return jnp.broadcast_to(row, (128, row.shape[1])).T[:, :1]


def place_in_turn(k, n_blk):
    return -k & (n_blk - 1)


def arrange_kernel(n_blk, n_rep, slab, pos, *refs):
    mine, other, firsts = refs[:n_blk], refs[n_blk : 2 * n_blk], refs[2 * n_blk : 2 * n_blk + 2]
    rows_mine, rows_other, goals_ref, pick_ref, ep_ref, *hidden, both_sides, meta = refs[2 * n_blk + 2 :]
    rows = both_sides.shape[0]
    batch, rows_dev = n_blk * slab, n_rep * slab
    for i, (blocks, to) in enumerate(((mine, rows_mine), (other, rows_other))):

        def put(off, value, to=to):
            to[pl.ds(off, slab), :] = value

        place_blocks(pos, blocks, put, n_blk, n_rep, slab)
        for k, block in enumerate(blocks):
            at = (i * n_blk + place_in_turn(k, n_blk)) * rows_dev
            both_sides[at : at + rows_dev, :] = block[:rows_dev, :]
    for k, block in enumerate(mine):
        at = jnp.bitwise_xor(pos[0], k)
        for r in range(n_rep):
            off = pl.multiple_of((r * n_blk + at) * slab, slab)
            meta[:, pl.ds(off, slab)] = block[rows_dev:, r * slab : (r + 1) * slab].astype(F32)
    ep_ref[...] = meta[2:3, :]
    for r in range(n_rep):
        own = slice(r * batch, (r + 1) * batch)
        owner, place = meta[0:1, own].astype(jnp.int32), meta[1:2, own].astype(jnp.int32)
        side = (owner & 1) ^ pos[1]
        column_of = (side * n_blk + place_in_turn((owner >> 1) ^ pos[0], n_blk)) * rows_dev + place
        goal = column(column_of.astype(F32)).astype(jnp.int32)
        pick_ref[own, :] = jnp.where(
            goal == lax.broadcasted_iota(jnp.int32, (batch, rows), 1), 1.0, 0.0
        ).astype(BF)
    goals_ref[...] = dot(pick_ref[...], both_sides[...]).astype(BF)
    activate(pos, firsts, (rows_mine, goals_ref), hidden)


def gather_kernel(n_blk, n_rep, slab, pos, *refs):
    mine, extra, other, pick_ref = refs[:n_blk], refs[n_blk], refs[n_blk + 1 : n_blk + 3], refs[n_blk + 3]
    phi_ref, psi_ref, early = refs[n_blk + 4 :]
    emb = phi_ref.shape[1]
    rows_dev = n_rep * slab
    blocks = list(mine)
    blocks[n_blk - 2] = (mine[n_blk - 2][...].astype(F32) + extra[...].astype(F32)).astype(BF)

    def put(off, value):
        phi_ref[pl.ds(off, slab), :] = value[:, :emb]

    place_blocks(pos, blocks, put, n_blk, n_rep, slab)
    for k, block in enumerate(blocks):
        at = place_in_turn(k, n_blk) * rows_dev
        early[at : at + rows_dev, :] = block[:, emb:]
    for i, block in enumerate(other):
        at = (n_blk + i) * rows_dev
        early[at : at + rows_dev, :] = block[:, emb:]
    psi_ref[...] = dot(pick_ref[:, : early.shape[0]], early[...])


def contrast_kernel(n_rep, scale, phi_ref, psi_ref, part_ref, there_ref, sums_ref, ep_ref, pick_ref, grads_ref, late, psi_all):
    half, emb = phi_ref.shape
    batch = half // n_rep
    rows_dev = sums_ref.shape[0]
    late[:rows_dev, :] = (part_ref[:, emb:].astype(F32) + there_ref[:, emb:].astype(F32)).astype(BF)
    late[rows_dev:, :] = sums_ref[:, emb:]
    psi_all[...] = (psi_ref[...] + dot(pick_ref[:, pick_ref.shape[1] - 2 * rows_dev :], late[...])).astype(BF)
    diagonal = lax.broadcasted_iota(jnp.int32, (batch, batch), 0) == lax.broadcasted_iota(
        jnp.int32, (batch, batch), 1
    )
    batches = [slice(r * batch, (r + 1) * batch) for r in range(n_rep)]
    scores = [
        lax.dot_general(phi_ref[own, :], psi_all[own, :], (((1,), (1,)), ((), ())), preferred_element_type=F32)
        for own in batches
    ]
    deltas = []
    for own, score in zip(batches, scores):
        ep_row = ep_ref[:, own]
        kept = (column(ep_row) != ep_row) | diagonal
        exponent = jnp.where(kept, jnp.exp(score * scale), 0.0)
        totals = jnp.sum(exponent, axis=1, keepdims=True)
        power = jnp.where(totals > 1.0, 2.0**-32, 1.0)
        shares = (exponent * power) * (1.0 / (totals * power))
        deltas.append(jnp.where(diagonal, shares - 1.0, shares).astype(BF))
    for own, delta in zip(batches, deltas):
        grads_ref[own, :emb] = (dot(delta, psi_all[own, :]) * scale).astype(BF)
    for own, delta in zip(batches, deltas):
        grads_ref[own, emb:] = (dot(delta.T, phi_ref[own, :]) * scale).astype(BF)


def rows_grads(at, first_ref, second_ref, grads_ref, k, rows_ref, active, back):
    quarter, rows = active.shape
    emb = second_ref.shape[1]
    first_t = first_ref[:, pl.ds(at, quarter)].T
    second = second_ref[pl.ds(at, quarter), :]
    grad = grads_ref[:, k * emb : (k + 1) * emb]
    chunk = 256
    for c in range(0, rows, chunk):
        cols = slice(c, c + chunk)
        hidden = dot(first_t, rows_ref[cols, :].T)
        sig = sigmoid(hidden)
        act = hidden * sig
        active[:, cols] = act.astype(BF)
        slope = sig + act * (1.0 - sig)
        back[:, cols] = (dot(second, grad[cols, :].T) * slope).astype(BF)
    return dot(active[...], grad), dot(back[...], rows_ref[...])


def activate(pos, firsts, inputs, outs):
    quarter, rows = outs[0].shape
    at = pl.multiple_of(pos[1] * quarter, quarter)
    for k, (first, x_ref) in enumerate(zip(firsts, inputs)):
        first_t = first[:, pl.ds(at, quarter)].T
        for c in range(0, rows, 256):
            cols = slice(c, c + 256)
            hidden = dot(first_t, x_ref[cols, :].T)
            sig = sigmoid(hidden)
            act = hidden * sig
            outs[2 * k][:, cols] = act.astype(BF)
            outs[2 * k + 1][:, cols] = (sig + act * (1.0 - sig)).astype(BF)


def mine_kernel(pos, ss, gs, grads_ref, rows_ref, goals_ref, *refs):
    hidden, outs, back = refs[:4], refs[4:8], refs[8]
    quarter, rows = back.shape
    emb = ss.shape[1]
    at = pl.multiple_of(pos[1] * quarter, quarter)
    for k, (second_ref, x_ref) in enumerate(((ss, rows_ref), (gs, goals_ref))):
        second = second_ref[pl.ds(at, quarter), :]
        grad = grads_ref[:, k * emb : (k + 1) * emb]
        for c in range(0, rows, 256):
            cols = slice(c, c + 256)
            back[:, cols] = (dot(second, grad[cols, :].T) * hidden[2 * k + 1][:, cols].astype(F32)).astype(BF)
        outs[2 * k][...] = dot(hidden[2 * k][...], grad)
        outs[2 * k + 1][...] = dot(back[...], x_ref[...])


def other_kernel(k, n_put, pos, first, second, grads_ref, rows_ref, sum_second, sum_first, *refs):
    done, outs, puts, (active, back), sems = (
        refs[:n_put],
        refs[n_put : n_put + 4],
        refs[n_put + 4 : 2 * n_put + 4],
        refs[2 * n_put + 4 : 2 * n_put + 6],
        refs[2 * n_put + 6 :],
    )
    copies = [put_half(pos[1], x, o, sems[0].at[i]) for i, (x, o) in enumerate(zip(done, puts))]
    for c in copies:
        c.start()
    quarter = active.shape[0]
    at = pl.multiple_of(pos[1] * quarter, quarter)
    grad_second, grad_first = rows_grads(at, first, second, grads_ref, k, rows_ref, active, back)
    halves = ((sum_first[...] + grad_first).astype(BF).T, (sum_second[...] + grad_second).astype(BF))
    for half, out16, out32 in zip(halves, outs[:2], outs[2:]):
        out16[...] = half
        out32[...] = half.astype(F32)
    for c in copies:
        c.wait()


def put_half(side, half, out, sem):
    n, m = half.shape
    if out.shape[0] == n:
        to = out.at[:, pl.ds(pl.multiple_of(side * m, m), m)]
    else:
        to = out.at[pl.ds(pl.multiple_of(side * n, n), n), :]
    return pltpu.make_async_copy(half, to, sem)


def finish_kernel(old, new, pos, *refs):
    n = old + new
    halves, outs, scratch, sems = refs[:n], refs[n + old : 2 * n + old], refs[2 * n + old : -1], refs[-1]
    copies = [put_half(pos[1], x, o, sems.at[old + i]) for i, (x, o) in enumerate(zip(halves[old:], outs[old:]))]
    for c in copies:
        c.start()
    for i in range(old):
        scratch[i][...] = halves[i][...].astype(F32)
        copies.append(put_half(1 - pos[1], scratch[i], outs[i], sems.at[i]))
        copies[-1].start()
    for c in copies:
        c.wait()


def finish(there, own, wholes, shapes):
    old, new = len(wholes), len(shapes)
    n = old + new
    return kernel(
        functools.partial(finish_kernel, old, new),
        "finish",
        [(w.shape, w.dtype) for w in wholes] + shapes,
        (*there, *own, *wholes),
        [*(pltpu.VMEM(x.shape, F32) for x in there), pltpu.SemaphoreType.DMA((n,))],
        pos=True,
        hbm=range(n, n + old),
        hbm_out=range(n),
        aliases={n + i: i for i in range(old)},
    )


def gathered(
    states, goal_distance, goal_row, episode, state_first, state_second, goal_first, goal_second
):
    rows_dev, width = states.shape
    n_blk, n_rep, n_sub = (lax.axis_size(a) for a in ("blk", "rep", "sub"))
    slab = rows_dev // n_rep
    rows_all = n_blk * n_sub * rows_dev
    hid, emb = state_second.shape
    quarter = hid // n_sub

    def across(x, k):
        return lax.ppermute(x, "blk", [(i, i ^ k) for i in range(n_blk)])

    def swap(x, axis):
        return lax.ppermute(x, axis, [(0, 1), (1, 0)])

    def after(x, *first):
        return lax.optimization_barrier((x, *first))[0]

    weights = (state_first, goal_first, state_second, goal_second)
    (blank,) = kernel(blank_kernel, "blank", [((16, rows_dev), F32)], (), limit=1, flops=2**32)
    (pack,) = kernel(
        functools.partial(pack_kernel, n_blk, n_sub),
        "pack",
        [((rows_dev + 16, width), BF)],
        (blank, states, *(x.reshape(1, rows_dev) for x in (goal_distance, goal_row, episode))),
        pos=True,
        limit=4,
        flops=2**32,
    )
    got = {0: pack, 3: across(pack, 3)}
    held = weights
    part0 = forward(pack, held, rows_dev)
    got[1] = across(after(pack, part0), 1)
    got[2] = across(after(pack, got[3]), 2)
    there0 = swap(part0, "rep")
    part3 = forward(got[3], held, rows_dev)
    there3 = swap(part3, "rep")

    sums = {0: both(part0, there0)}
    sums[1] = across(after(sums[0], got[2]), 1)
    part2 = forward(after(got[2], sums[0]), held, rows_dev)
    there2 = swap(part2, "rep")
    sums[3] = both(part3, there3)

    side = ((rows_all // 2, width), BF)
    sf, gf, ss, gs = held
    mine, other, goals_mine, pick, episodes, *hidden = kernel(
        functools.partial(arrange_kernel, n_blk, n_rep, slab),
        "arrange",
        [side, side, side, ((rows_all // 2, rows_all), BF), ((1, rows_all // 2), F32)]
        + [((quarter, rows_all // 2), BF)] * 4,
        (*(got[k] for k in range(n_blk)), *(swap(got[k], "sub") for k in range(n_blk)), sf, gf),
        [
            pltpu.VMEM((rows_all, width), BF),
            pltpu.VMEM((16, rows_all // 2), F32),
        ],
        pos=True,
    )
    there2 = after(there2, pick)
    late = [swap(x, "sub") for x in (part2, there2, sums[1])]
    half = rows_all // 2
    phi, psi = kernel(
        functools.partial(gather_kernel, n_blk, n_rep, slab),
        "gather",
        [((half, emb), BF), ((half, emb), F32)],
        (sums[0], sums[1], part2, sums[3], there2, swap(sums[0], "sub"), swap(sums[3], "sub"), pick),
        [pltpu.VMEM((rows_all - 2 * rows_dev, emb), BF)],
        pos=True,
    )
    (grads_mine,) = kernel(
        functools.partial(contrast_kernel, n_rep, 4.0 / math.sqrt(emb)),
        "contrast",
        [((half, 2 * emb), BF)],
        (phi, psi, *late, episodes, pick),
        [pltpu.VMEM((2 * rows_dev, emb), BF), pltpu.VMEM((half, emb), BF)],
    )
    grads_other = swap(grads_mine, "sub")
    goals_other = swap(goals_mine, "sub")

    sf, gf, ss, gs = weights
    work = [pltpu.VMEM((quarter, rows_all // 2), BF), pltpu.VMEM((quarter, rows_all // 2), BF)]
    flops = 4 * rows_all * width * quarter
    sums_s2, sums_s1, sums_g2, sums_g1 = kernel(
        mine_kernel,
        "mine",
        [((quarter, emb), F32), ((quarter, width), F32)] * 2,
        (ss, gs, grads_mine, mine, goals_mine, *hidden),
        work[:1],
        pos=True,
        flops=2 * flops,
    )
    halves = [(shape, kind) for kind in (BF, F32) for shape in ((width, quarter), (quarter, emb))]
    wholes = [((width, hid), F32), ((hid, emb), F32)]
    *state_halves, state_first_own, state_second_own = kernel(
        functools.partial(other_kernel, 0, 0),
        "other_state",
        halves,
        (sf, ss, grads_other, other, sums_s2, sums_s1),
        work,
        pos=True,
        flops=flops,
    )
    state_there = [swap(x, "sub") for x in state_halves]
    *goal_halves, goal_first_own, goal_second_own, out0, out1 = kernel(
        functools.partial(other_kernel, 1, 2),
        "other_goal",
        halves + wholes,
        (gf, gs, grads_other, goals_other, sums_g2, sums_g1, state_first_own, state_second_own),
        work + [pltpu.SemaphoreType.DMA((2,))],
        pos=True,
        flops=flops,
        hbm_out=(4, 5),
    )
    goal_there = [swap(x, "sub") for x in goal_halves]
    out0, out1, out2, out3 = finish(state_there, (goal_first_own, goal_second_own), (out0, out1), wholes)
    out2, out3 = finish(goal_there, (), (out2, out3), [])
    return (out0, out1, out2, out3)


def silu_slope(hidden):
    sig = jax.nn.sigmoid(hidden)
    return sig * (1.0 + hidden * (1.0 - sig))


def encoder_grads(rows_in, hidden, active, second, emb_grad):
    grad_second = jnp.einsum("nh,ne->he", active, emb_grad, preferred_element_type=jnp.float32)
    back = jnp.einsum("ne,he->nh", emb_grad, second, preferred_element_type=jnp.float32)
    back_rows = (back * silu_slope(hidden)).astype(jnp.bfloat16)
    grad_first = jnp.einsum("ns,nh->sh", rows_in, back_rows, preferred_element_type=jnp.float32)
    return (grad_first, grad_second)


def exchanged(
    states, goal_distance, goal_row, episode, state_first, state_second, goal_first, goal_second
):
    rows_dev, width = states.shape
    owners = lax.axis_size(("blk", "sub"))
    position = lax.axis_index(("blk", "sub"))
    capacity = 4 * rows_dev // owners
    target = (position + goal_distance[:, 0]) % owners
    onehot = (target[:, None] == jnp.arange(owners, dtype=jnp.int32)[None, :]).astype(jnp.int32)
    slot_rank = jnp.sum((jnp.cumsum(onehot, axis=0) - onehot) * onehot, axis=1)
    requests = jnp.zeros((owners, capacity), jnp.int32).at[target, slot_rank].set(goal_row)
    wanted = lax.all_to_all(requests, ("blk", "sub"), split_axis=0, concat_axis=0, tiled=True)
    fetched = jnp.take(states, wanted.reshape(-1), axis=0).reshape(wanted.shape + (width,))
    replies = lax.all_to_all(fetched, ("blk", "sub"), split_axis=0, concat_axis=0, tiled=True)
    goal_states = jnp.take(
        replies.reshape(owners * capacity, width), target * capacity + slot_rank, axis=0
    )
    slab_rows = rows_dev // lax.axis_size("rep")
    state_hidden = jnp.dot(states, state_first, preferred_element_type=jnp.float32)
    state_active = jax.nn.silu(state_hidden).astype(jnp.bfloat16)
    goal_hidden = jnp.dot(goal_states, goal_first, preferred_element_type=jnp.float32)
    goal_active = jax.nn.silu(goal_hidden).astype(jnp.bfloat16)
    phi = lax.psum_scatter(
        jnp.dot(state_active, state_second, preferred_element_type=jnp.float32),
        "rep",
        scatter_dimension=0,
        tiled=True,
    ).astype(jnp.bfloat16)
    psi = lax.psum_scatter(
        jnp.dot(goal_active, goal_second, preferred_element_type=jnp.float32),
        "rep",
        scatter_dimension=0,
        tiled=True,
    ).astype(jnp.bfloat16)
    episode_own = lax.dynamic_slice_in_dim(episode, lax.axis_index("rep") * slab_rows, slab_rows, 0)
    psi_all, episode_all = (
        lax.all_gather(psi, "blk", axis=0, tiled=True),
        lax.all_gather(episode_own, "blk", axis=0, tiled=True),
    )
    batch_rows = psi_all.shape[0]
    logit_scale = 4.0 / math.sqrt(psi.shape[1])
    own_rows = lax.axis_index("blk") * slab_rows + jnp.arange(slab_rows, dtype=jnp.int32)
    columns = jnp.arange(batch_rows, dtype=jnp.int32)
    diagonal = own_rows[:, None] == columns[None, :]
    excluded = (episode_own[:, None] == episode_all[None, :]) & ~diagonal
    scores = jnp.einsum("ie,je->ij", phi, psi_all, preferred_element_type=jnp.float32) * logit_scale
    exponent = jnp.where(excluded, 0.0, jnp.exp(scores))
    totals = jnp.sum(exponent, axis=1)
    delta = (exponent / totals[:, None] - diagonal.astype(jnp.float32)).astype(jnp.bfloat16)
    phi_grad = (jnp.dot(delta, psi_all, preferred_element_type=jnp.float32) * logit_scale).astype(
        jnp.bfloat16
    )
    psi_grad = lax.psum_scatter(
        jnp.einsum("ij,ie->je", delta, phi, preferred_element_type=jnp.float32) * logit_scale,
        "blk",
        scatter_dimension=0,
        tiled=True,
    ).astype(jnp.bfloat16)
    phi_full, psi_full = (
        lax.all_gather(phi_grad, "rep", axis=0, tiled=True),
        lax.all_gather(psi_grad, "rep", axis=0, tiled=True),
    )
    state_parts = encoder_grads(states, state_hidden, state_active, state_second, phi_full)
    goal_parts = encoder_grads(goal_states, goal_hidden, goal_active, goal_second, psi_full)
    summed = lax.psum(
        (state_parts[0], state_parts[1], goal_parts[0], goal_parts[1]), ("blk", "sub")
    )
    return (summed[0], summed[1], summed[2], summed[3])


def solution(mesh):
    in_specs = (
        P(("grp", "blk", "sub"), None),
        P(("grp", "blk", "sub"), None),
        P(("grp", "blk", "sub")),
        P(("grp", "blk", "sub")),
        P(None, "rep"),
        P("rep", None),
        P(None, "rep"),
        P("rep", None),
    )
    out_specs = (P("grp", "rep"), P(("grp", "rep"), None), P("grp", "rep"), P(("grp", "rep"), None))

    def local(states, *others):
        small = (mesh.shape["blk"], mesh.shape["rep"], mesh.shape["sub"]) == (4, 2, 2)
        plan = gathered if small and states.shape[0] == states.shape[1] == 256 else exchanged
        return plan(states, *others)

    return jax.shard_map(local, mesh=mesh, in_specs=in_specs, out_specs=out_specs, check_vma=False)
```

```python
import functools
import math

import jax
import jax.numpy as jnp
from jax import lax
from jax.experimental import pallas as pl
from jax.experimental.pallas import tpu as pltpu
from jax.sharding import PartitionSpec as P

BF = jnp.bfloat16
F32 = jnp.float32
MIB = 1024 * 1024


def dot(a, b):
    return jnp.dot(a, b, preferred_element_type=F32)


def sigmoid(v):
    return 0.5 * jnp.tanh(0.5 * v) + 0.5


HBM = pl.BlockSpec(memory_space=pltpu.HBM)
VMEM = pl.BlockSpec(memory_space=pltpu.VMEM)
SMEM = pl.BlockSpec(memory_space=pltpu.SMEM)


def kernel(body, name, outs, args, scratch=(), limit=16, pos=False, flops=0, hbm=(), hbm_out=(), aliases={}):
    specs = [HBM if i in hbm else VMEM for i in range(len(args))]
    if pos:
        inner = body

        def body(*refs):
            inner((lax.axis_index("blk"), lax.axis_index("sub")), *refs)

    return pl.pallas_call(
        body,
        in_specs=specs,
        out_specs=[HBM if i in hbm_out else VMEM for i in range(len(outs))],
        out_shape=[jax.ShapeDtypeStruct(shape, dtype) for shape, dtype in outs],
        scratch_shapes=scratch,
        input_output_aliases=aliases,
        compiler_params=pltpu.CompilerParams(vmem_limit_bytes=int(limit * MIB)),
        cost_estimate=pl.CostEstimate(flops=flops, bytes_accessed=0, transcendentals=0),
        name=name,
    )(*args)


def encode(x_ref, weights, out_ref, active, ready=lambda i: None):
    emb = weights[2].shape[1]
    for k in range(2):
        first, second = weights[k], weights[2 + k]
        ready(k)
        for c in range(0, active.shape[1], 512):
            hidden = dot(x_ref[...], first[:, c : c + 512])
            active[:, c : c + 512] = (hidden * sigmoid(hidden)).astype(BF)
        ready(2 + k)
        out_ref[:, k * emb : (k + 1) * emb] = dot(active[...], second[...]).astype(BF)


def blank_kernel(out_ref):
    out_ref[...] = jnp.zeros_like(out_ref)


def pack_kernel(n_blk, n_sub, pos, blank_ref, x_ref, distance_ref, place_ref, episode_ref, pack_ref):
    rows = x_ref.shape[0]
    owner = (pos[0] * n_sub + pos[1] + distance_ref[...]) & (n_blk * n_sub - 1)
    digits = (owner, place_ref[...], episode_ref[...])
    table = jnp.concatenate([d.astype(F32) for d in digits] + [blank_ref[3:, :]], axis=0)
    pack_ref[:rows, :] = x_ref[...]
    pack_ref[rows:, :] = table.astype(BF)


def forward_kernel(x_ref, *refs):
    encode(x_ref.at[: refs[4].shape[0]], refs[:4], refs[4], refs[5])


def forward(x, weights, rows):
    hid, emb = weights[2].shape
    return kernel(
        forward_kernel,
        "forward",
        [((rows, 2 * emb), BF)],
        (x, *weights),
        [pltpu.VMEM((rows, hid), BF)],
        limit=8,
    )[0]


def add_kernel(a_ref, b_ref, out_ref):
    out_ref[...] = (a_ref[...].astype(F32) + b_ref[...].astype(F32)).astype(BF)


def both(part, there):
    return kernel(add_kernel, "both", [(part.shape, BF)], (part, there), limit=4)[0]


def place_blocks(pos, blocks, put, n_blk, n_rep, slab):
    for k, block in enumerate(blocks):
        at = jnp.bitwise_xor(pos[0], k)
        for r in range(n_rep):
            off = (r * n_blk + at) * slab
            put(pl.multiple_of(off, slab), block[r * slab : (r + 1) * slab, :])


def column(row):
    return jnp.broadcast_to(row, (128, row.shape[1])).T[:, :1]


def place_in_turn(k, n_blk):
    return -k & (n_blk - 1)


def arrange_kernel(n_blk, n_rep, slab, pos, *refs):
    mine, other, firsts = refs[:n_blk], refs[n_blk : 2 * n_blk], refs[2 * n_blk : 2 * n_blk + 2]
    rows_mine, rows_other, goals_ref, pick_ref, ep_ref, *hidden, both_sides, meta = refs[2 * n_blk + 2 :]
    rows = both_sides.shape[0]
    batch, rows_dev = n_blk * slab, n_rep * slab
    for i, (blocks, to) in enumerate(((mine, rows_mine), (other, rows_other))):

        def put(off, value, to=to):
            to[pl.ds(off, slab), :] = value

        place_blocks(pos, blocks, put, n_blk, n_rep, slab)
        for k, block in enumerate(blocks):
            at = (i * n_blk + place_in_turn(k, n_blk)) * rows_dev
            both_sides[at : at + rows_dev, :] = block[:rows_dev, :]
    for k, block in enumerate(mine):
        at = jnp.bitwise_xor(pos[0], k)
        for r in range(n_rep):
            off = pl.multiple_of((r * n_blk + at) * slab, slab)
            meta[:, pl.ds(off, slab)] = block[rows_dev:, r * slab : (r + 1) * slab].astype(F32)
    ep_ref[...] = meta[2:3, :]
    for r in range(n_rep):
        own = slice(r * batch, (r + 1) * batch)
        owner, place = meta[0:1, own].astype(jnp.int32), meta[1:2, own].astype(jnp.int32)
        side = (owner & 1) ^ pos[1]
        column_of = (side * n_blk + place_in_turn((owner >> 1) ^ pos[0], n_blk)) * rows_dev + place
        goal = column(column_of.astype(F32)).astype(jnp.int32)
        pick_ref[own, :] = jnp.where(
            goal == lax.broadcasted_iota(jnp.int32, (batch, rows), 1), 1.0, 0.0
        ).astype(BF)
    activate(pos, firsts[0], rows_mine, hidden[:2])
    goals_ref[...] = dot(pick_ref[...], both_sides[...]).astype(BF)
    activate(pos, firsts[1], goals_ref, hidden[2:])


def gather_kernel(n_blk, n_rep, slab, pos, *refs):
    mine, extra, other, pick_ref = refs[:n_blk], refs[n_blk], refs[n_blk + 1 : n_blk + 3], refs[n_blk + 3]
    phi_ref, psi_ref, early = refs[n_blk + 4 :]
    emb = phi_ref.shape[1]
    rows_dev = n_rep * slab
    blocks = list(mine)
    blocks[n_blk - 2] = (mine[n_blk - 2][...].astype(F32) + extra[...].astype(F32)).astype(BF)

    def put(off, value):
        phi_ref[pl.ds(off, slab), :] = value[:, :emb]

    place_blocks(pos, blocks, put, n_blk, n_rep, slab)
    for k, block in enumerate(blocks):
        at = place_in_turn(k, n_blk) * rows_dev
        early[at : at + rows_dev, :] = block[:, emb:]
    for i, block in enumerate(other):
        at = (n_blk + i) * rows_dev
        early[at : at + rows_dev, :] = block[:, emb:]
    psi_ref[...] = dot(pick_ref[:, : early.shape[0]], early[...])


def contrast_kernel(n_rep, scale, phi_ref, psi_ref, part_ref, there_ref, sums_ref, ep_ref, pick_ref, grads_ref, late, psi_all):
    half, emb = phi_ref.shape
    batch = half // n_rep
    rows_dev = sums_ref.shape[0]
    late[:rows_dev, :] = (part_ref[:, emb:].astype(F32) + there_ref[:, emb:].astype(F32)).astype(BF)
    late[rows_dev:, :] = sums_ref[:, emb:]
    psi_all[...] = (psi_ref[...] + dot(pick_ref[:, pick_ref.shape[1] - 2 * rows_dev :], late[...])).astype(BF)
    diagonal = lax.broadcasted_iota(jnp.int32, (batch, batch), 0) == lax.broadcasted_iota(
        jnp.int32, (batch, batch), 1
    )
    batches = [slice(r * batch, (r + 1) * batch) for r in range(n_rep)]
    scores = [
        lax.dot_general(phi_ref[own, :], psi_all[own, :], (((1,), (1,)), ((), ())), preferred_element_type=F32)
        for own in batches
    ]
    deltas = []
    for own, score in zip(batches, scores):
        ep_row = ep_ref[:, own]
        kept = (column(ep_row) != ep_row) | diagonal
        exponent = jnp.where(kept, jnp.exp(score * scale), 0.0)
        totals = jnp.sum(exponent, axis=1, keepdims=True)
        power = jnp.where(totals > 1.0, 2.0**-32, 1.0)
        shares = (exponent * power) * (1.0 / (totals * power))
        deltas.append(jnp.where(diagonal, shares - 1.0, shares).astype(BF))
    for own, delta in zip(batches, deltas):
        grads_ref[own, :emb] = (dot(delta, psi_all[own, :]) * scale).astype(BF)
    for own, delta in zip(batches, deltas):
        grads_ref[own, emb:] = (dot(delta.T, phi_ref[own, :]) * scale).astype(BF)


def rows_grads(at, first_ref, second_ref, grads_ref, k, rows_ref, active, back):
    quarter, rows = active.shape
    emb = second_ref.shape[1]
    first_t = first_ref[:, pl.ds(at, quarter)].T
    second = second_ref[pl.ds(at, quarter), :]
    grad = grads_ref[:, k * emb : (k + 1) * emb]
    chunk = 256
    for c in range(0, rows, chunk):
        cols = slice(c, c + chunk)
        hidden = dot(first_t, rows_ref[cols, :].T)
        sig = sigmoid(hidden)
        act = hidden * sig
        active[:, cols] = act.astype(BF)
        slope = sig + act * (1.0 - sig)
        back[:, cols] = (dot(second, grad[cols, :].T) * slope).astype(BF)
    return dot(active[...], grad), dot(back[...], rows_ref[...])


def activate(pos, first, x_ref, outs):
    quarter, rows = outs[0].shape
    at = pl.multiple_of(pos[1] * quarter, quarter)
    first_t = first[:, pl.ds(at, quarter)].T
    for c in range(0, rows, 256):
        cols = slice(c, c + 256)
        hidden = dot(first_t, x_ref[cols, :].T)
        sig = sigmoid(hidden)
        act = hidden * sig
        outs[0][:, cols] = act.astype(BF)
        outs[1][:, cols] = (sig + act * (1.0 - sig)).astype(BF)


def mine_kernel(pos, ss, gs, grads_ref, rows_ref, goals_ref, *refs):
    hidden, outs, back = refs[:4], refs[4:8], refs[8]
    quarter, rows = back.shape
    emb = ss.shape[1]
    at = pl.multiple_of(pos[1] * quarter, quarter)
    for k, (second_ref, x_ref) in enumerate(((ss, rows_ref), (gs, goals_ref))):
        second = second_ref[pl.ds(at, quarter), :]
        grad = grads_ref[:, k * emb : (k + 1) * emb]
        for c in range(0, rows, 256):
            cols = slice(c, c + 256)
            back[:, cols] = (dot(second, grad[cols, :].T) * hidden[2 * k + 1][:, cols].astype(F32)).astype(BF)
        outs[2 * k][...] = dot(hidden[2 * k][...], grad)
        outs[2 * k + 1][...] = dot(back[...], x_ref[...])


def other_kernel(k, n_put, pos, first, second, grads_ref, rows_ref, sum_second, sum_first, *refs):
    done, outs, puts, (active, back), sems = (
        refs[:n_put],
        refs[n_put : n_put + 4],
        refs[n_put + 4 : 2 * n_put + 4],
        refs[2 * n_put + 4 : 2 * n_put + 6],
        refs[2 * n_put + 6 :],
    )
    copies = [put_half(pos[1], x, o, sems[0].at[i]) for i, (x, o) in enumerate(zip(done, puts))]
    for c in copies:
        c.start()
    quarter = active.shape[0]
    at = pl.multiple_of(pos[1] * quarter, quarter)
    grad_second, grad_first = rows_grads(at, first, second, grads_ref, k, rows_ref, active, back)
    halves = ((sum_first[...] + grad_first).astype(BF).T, (sum_second[...] + grad_second).astype(BF))
    for half, out16, out32 in zip(halves, outs[:2], outs[2:]):
        out16[...] = half
        out32[...] = half.astype(F32)
    for c in copies:
        c.wait()


def put_half(side, half, out, sem):
    n, m = half.shape
    if out.shape[0] == n:
        to = out.at[:, pl.ds(pl.multiple_of(side * m, m), m)]
    else:
        to = out.at[pl.ds(pl.multiple_of(side * n, n), n), :]
    return pltpu.make_async_copy(half, to, sem)


def finish_kernel(old, new, pos, *refs):
    n = old + new
    halves, outs, scratch, sems = refs[:n], refs[n + old : 2 * n + old], refs[2 * n + old : -1], refs[-1]
    copies = [put_half(pos[1], x, o, sems.at[old + i]) for i, (x, o) in enumerate(zip(halves[old:], outs[old:]))]
    for c in copies:
        c.start()
    for i in range(old):
        scratch[i][...] = halves[i][...].astype(F32)
        copies.append(put_half(1 - pos[1], scratch[i], outs[i], sems.at[i]))
        copies[-1].start()
    for c in copies:
        c.wait()


def finish(there, own, wholes, shapes):
    old, new = len(wholes), len(shapes)
    n = old + new
    return kernel(
        functools.partial(finish_kernel, old, new),
        "finish",
        [(w.shape, w.dtype) for w in wholes] + shapes,
        (*there, *own, *wholes),
        [*(pltpu.VMEM(x.shape, F32) for x in there), pltpu.SemaphoreType.DMA((n,))],
        pos=True,
        hbm=range(n, n + old),
        hbm_out=range(n),
        aliases={n + i: i for i in range(old)},
    )


def gathered(
    states, goal_distance, goal_row, episode, state_first, state_second, goal_first, goal_second
):
    rows_dev, width = states.shape
    n_blk, n_rep, n_sub = (lax.axis_size(a) for a in ("blk", "rep", "sub"))
    slab = rows_dev // n_rep
    rows_all = n_blk * n_sub * rows_dev
    hid, emb = state_second.shape
    quarter = hid // n_sub

    def across(x, k):
        return lax.ppermute(x, "blk", [(i, i ^ k) for i in range(n_blk)])

    def swap(x, axis):
        return lax.ppermute(x, axis, [(0, 1), (1, 0)])

    def after(x, *first):
        return lax.optimization_barrier((x, *first))[0]

    weights = (state_first, goal_first, state_second, goal_second)
    (blank,) = kernel(blank_kernel, "blank", [((16, rows_dev), F32)], (), limit=1, flops=2**32)
    (pack,) = kernel(
        functools.partial(pack_kernel, n_blk, n_sub),
        "pack",
        [((rows_dev + 16, width), BF)],
        (blank, states, *(x.reshape(1, rows_dev) for x in (goal_distance, goal_row, episode))),
        pos=True,
        limit=4,
        flops=2**32,
    )
    got = {0: pack, 3: across(pack, 3)}
    held = weights
    part0 = forward(pack, held, rows_dev)
    got[1] = across(after(pack, part0), 1)
    got[2] = across(after(pack, got[3]), 2)
    there0 = swap(part0, "rep")
    part3 = forward(got[3], held, rows_dev)
    there3 = swap(part3, "rep")

    sums = {0: both(part0, there0)}
    sums[1] = across(after(sums[0], got[2]), 1)
    part2 = forward(after(got[2], sums[0]), held, rows_dev)
    there2 = swap(part2, "rep")
    sums[3] = both(part3, there3)

    side = ((rows_all // 2, width), BF)
    sf, gf, ss, gs = held
    mine, other, goals_mine, pick, episodes, *hidden = kernel(
        functools.partial(arrange_kernel, n_blk, n_rep, slab),
        "arrange",
        [side, side, side, ((rows_all // 2, rows_all), BF), ((1, rows_all // 2), F32)]
        + [((quarter, rows_all // 2), BF)] * 4,
        (*(got[k] for k in range(n_blk)), *(swap(got[k], "sub") for k in range(n_blk)), sf, gf),
        [
            pltpu.VMEM((rows_all, width), BF),
            pltpu.VMEM((16, rows_all // 2), F32),
        ],
        pos=True,
    )
    there2 = after(there2, pick)
    late = [swap(x, "sub") for x in (part2, there2, sums[1])]
    half = rows_all // 2
    phi, psi = kernel(
        functools.partial(gather_kernel, n_blk, n_rep, slab),
        "gather",
        [((half, emb), BF), ((half, emb), F32)],
        (sums[0], sums[1], part2, sums[3], there2, swap(sums[0], "sub"), swap(sums[3], "sub"), pick),
        [pltpu.VMEM((rows_all - 2 * rows_dev, emb), BF)],
        pos=True,
    )
    (grads_mine,) = kernel(
        functools.partial(contrast_kernel, n_rep, 4.0 / math.sqrt(emb)),
        "contrast",
        [((half, 2 * emb), BF)],
        (phi, psi, *late, episodes, pick),
        [pltpu.VMEM((2 * rows_dev, emb), BF), pltpu.VMEM((half, emb), BF)],
    )
    grads_other = swap(grads_mine, "sub")
    goals_other = swap(goals_mine, "sub")

    sf, gf, ss, gs = weights
    work = [pltpu.VMEM((quarter, rows_all // 2), BF), pltpu.VMEM((quarter, rows_all // 2), BF)]
    flops = 4 * rows_all * width * quarter
    sums_s2, sums_s1, sums_g2, sums_g1 = kernel(
        mine_kernel,
        "mine",
        [((quarter, emb), F32), ((quarter, width), F32)] * 2,
        (ss, gs, grads_mine, mine, goals_mine, *hidden),
        work[:1],
        pos=True,
        flops=2 * flops,
    )
    halves = [(shape, kind) for kind in (BF, F32) for shape in ((width, quarter), (quarter, emb))]
    wholes = [((width, hid), F32), ((hid, emb), F32)]
    *state_halves, state_first_own, state_second_own = kernel(
        functools.partial(other_kernel, 0, 0),
        "other_state",
        halves,
        (sf, ss, grads_other, other, sums_s2, sums_s1),
        work,
        pos=True,
        flops=flops,
    )
    state_there = [swap(x, "sub") for x in state_halves]
    *goal_halves, goal_first_own, goal_second_own, out0, out1 = kernel(
        functools.partial(other_kernel, 1, 2),
        "other_goal",
        halves + wholes,
        (gf, gs, grads_other, goals_other, sums_g2, sums_g1, state_first_own, state_second_own),
        work + [pltpu.SemaphoreType.DMA((2,))],
        pos=True,
        flops=flops,
        hbm_out=(4, 5),
    )
    goal_there = [swap(x, "sub") for x in goal_halves]
    out0, out1, out2, out3 = finish(state_there, (goal_first_own, goal_second_own), (out0, out1), wholes)
    out2, out3 = finish(goal_there, (), (out2, out3), [])
    return (out0, out1, out2, out3)


def silu_slope(hidden):
    sig = jax.nn.sigmoid(hidden)
    return sig * (1.0 + hidden * (1.0 - sig))


def encoder_grads(rows_in, hidden, active, second, emb_grad):
    grad_second = jnp.einsum("nh,ne->he", active, emb_grad, preferred_element_type=jnp.float32)
    back = jnp.einsum("ne,he->nh", emb_grad, second, preferred_element_type=jnp.float32)
    back_rows = (back * silu_slope(hidden)).astype(jnp.bfloat16)
    grad_first = jnp.einsum("ns,nh->sh", rows_in, back_rows, preferred_element_type=jnp.float32)
    return (grad_first, grad_second)


def exchanged(
    states, goal_distance, goal_row, episode, state_first, state_second, goal_first, goal_second
):
    rows_dev, width = states.shape
    owners = lax.axis_size(("blk", "sub"))
    position = lax.axis_index(("blk", "sub"))
    capacity = 4 * rows_dev // owners
    target = (position + goal_distance[:, 0]) % owners
    onehot = (target[:, None] == jnp.arange(owners, dtype=jnp.int32)[None, :]).astype(jnp.int32)
    slot_rank = jnp.sum((jnp.cumsum(onehot, axis=0) - onehot) * onehot, axis=1)
    requests = jnp.zeros((owners, capacity), jnp.int32).at[target, slot_rank].set(goal_row)
    wanted = lax.all_to_all(requests, ("blk", "sub"), split_axis=0, concat_axis=0, tiled=True)
    fetched = jnp.take(states, wanted.reshape(-1), axis=0).reshape(wanted.shape + (width,))
    replies = lax.all_to_all(fetched, ("blk", "sub"), split_axis=0, concat_axis=0, tiled=True)
    goal_states = jnp.take(
        replies.reshape(owners * capacity, width), target * capacity + slot_rank, axis=0
    )
    slab_rows = rows_dev // lax.axis_size("rep")
    state_hidden = jnp.dot(states, state_first, preferred_element_type=jnp.float32)
    state_active = jax.nn.silu(state_hidden).astype(jnp.bfloat16)
    goal_hidden = jnp.dot(goal_states, goal_first, preferred_element_type=jnp.float32)
    goal_active = jax.nn.silu(goal_hidden).astype(jnp.bfloat16)
    phi = lax.psum_scatter(
        jnp.dot(state_active, state_second, preferred_element_type=jnp.float32),
        "rep",
        scatter_dimension=0,
        tiled=True,
    ).astype(jnp.bfloat16)
    psi = lax.psum_scatter(
        jnp.dot(goal_active, goal_second, preferred_element_type=jnp.float32),
        "rep",
        scatter_dimension=0,
        tiled=True,
    ).astype(jnp.bfloat16)
    episode_own = lax.dynamic_slice_in_dim(episode, lax.axis_index("rep") * slab_rows, slab_rows, 0)
    psi_all, episode_all = (
        lax.all_gather(psi, "blk", axis=0, tiled=True),
        lax.all_gather(episode_own, "blk", axis=0, tiled=True),
    )
    batch_rows = psi_all.shape[0]
    logit_scale = 4.0 / math.sqrt(psi.shape[1])
    own_rows = lax.axis_index("blk") * slab_rows + jnp.arange(slab_rows, dtype=jnp.int32)
    columns = jnp.arange(batch_rows, dtype=jnp.int32)
    diagonal = own_rows[:, None] == columns[None, :]
    excluded = (episode_own[:, None] == episode_all[None, :]) & ~diagonal
    scores = jnp.einsum("ie,je->ij", phi, psi_all, preferred_element_type=jnp.float32) * logit_scale
    exponent = jnp.where(excluded, 0.0, jnp.exp(scores))
    totals = jnp.sum(exponent, axis=1)
    delta = (exponent / totals[:, None] - diagonal.astype(jnp.float32)).astype(jnp.bfloat16)
    phi_grad = (jnp.dot(delta, psi_all, preferred_element_type=jnp.float32) * logit_scale).astype(
        jnp.bfloat16
    )
    psi_grad = lax.psum_scatter(
        jnp.einsum("ij,ie->je", delta, phi, preferred_element_type=jnp.float32) * logit_scale,
        "blk",
        scatter_dimension=0,
        tiled=True,
    ).astype(jnp.bfloat16)
    phi_full, psi_full = (
        lax.all_gather(phi_grad, "rep", axis=0, tiled=True),
        lax.all_gather(psi_grad, "rep", axis=0, tiled=True),
    )
    state_parts = encoder_grads(states, state_hidden, state_active, state_second, phi_full)
    goal_parts = encoder_grads(goal_states, goal_hidden, goal_active, goal_second, psi_full)
    summed = lax.psum(
        (state_parts[0], state_parts[1], goal_parts[0], goal_parts[1]), ("blk", "sub")
    )
    return (summed[0], summed[1], summed[2], summed[3])


def solution(mesh):
    in_specs = (
        P(("grp", "blk", "sub"), None),
        P(("grp", "blk", "sub"), None),
        P(("grp", "blk", "sub")),
        P(("grp", "blk", "sub")),
        P(None, "rep"),
        P("rep", None),
        P(None, "rep"),
        P("rep", None),
    )
    out_specs = (P("grp", "rep"), P(("grp", "rep"), None), P("grp", "rep"), P(("grp", "rep"), None))

    def local(states, *others):
        small = (mesh.shape["blk"], mesh.shape["rep"], mesh.shape["sub"]) == (4, 2, 2)
        plan = gathered if small and states.shape[0] == states.shape[1] == 256 else exchanged
        return plan(states, *others)

    return jax.shard_map(local, mesh=mesh, in_specs=in_specs, out_specs=out_specs, check_vma=False)
```

```python
import functools
import math

import jax
import jax.numpy as jnp
from jax import lax
from jax.experimental import pallas as pl
from jax.experimental.pallas import tpu as pltpu
from jax.sharding import PartitionSpec as P

BF = jnp.bfloat16
F32 = jnp.float32
MIB = 1024 * 1024


def dot(a, b):
    return jnp.dot(a, b, preferred_element_type=F32)


def sigmoid(v):
    return 0.5 * jnp.tanh(0.5 * v) + 0.5


HBM = pl.BlockSpec(memory_space=pltpu.HBM)
VMEM = pl.BlockSpec(memory_space=pltpu.VMEM)
SMEM = pl.BlockSpec(memory_space=pltpu.SMEM)


def kernel(body, name, outs, args, scratch=(), limit=16, pos=False, flops=0, hbm=(), hbm_out=(), aliases={}):
    specs = [HBM if i in hbm else VMEM for i in range(len(args))]
    if pos:
        inner = body

        def body(*refs):
            inner((lax.axis_index("blk"), lax.axis_index("sub")), *refs)

    return pl.pallas_call(
        body,
        in_specs=specs,
        out_specs=[HBM if i in hbm_out else VMEM for i in range(len(outs))],
        out_shape=[jax.ShapeDtypeStruct(shape, dtype) for shape, dtype in outs],
        scratch_shapes=scratch,
        input_output_aliases=aliases,
        compiler_params=pltpu.CompilerParams(vmem_limit_bytes=int(limit * MIB)),
        cost_estimate=pl.CostEstimate(flops=flops, bytes_accessed=0, transcendentals=0),
        name=name,
    )(*args)


def encode(x_ref, weights, out_ref, active, ready=lambda i: None):
    emb = weights[2].shape[1]
    for k in range(2):
        first, second = weights[k], weights[2 + k]
        ready(k)
        for c in range(0, active.shape[1], 512):
            hidden = dot(x_ref[...], first[:, c : c + 512])
            active[:, c : c + 512] = (hidden * sigmoid(hidden)).astype(BF)
        ready(2 + k)
        out_ref[:, k * emb : (k + 1) * emb] = dot(active[...], second[...]).astype(BF)


def blank_kernel(out_ref):
    out_ref[...] = jnp.zeros_like(out_ref)


def pack_kernel(n_blk, n_sub, pos, blank_ref, x_ref, distance_ref, place_ref, episode_ref, pack_ref):
    rows = x_ref.shape[0]
    owner = (pos[0] * n_sub + pos[1] + distance_ref[...]) & (n_blk * n_sub - 1)
    digits = (owner, place_ref[...], episode_ref[...])
    table = jnp.concatenate([d.astype(F32) for d in digits] + [blank_ref[3:, :]], axis=0)
    pack_ref[:rows, :] = x_ref[...]
    pack_ref[rows:, :] = table.astype(BF)


def forward_kernel(x_ref, *refs):
    encode(x_ref.at[: refs[4].shape[0]], refs[:4], refs[4], refs[5])


def forward(x, weights, rows):
    hid, emb = weights[2].shape
    return kernel(
        forward_kernel,
        "forward",
        [((rows, 2 * emb), BF)],
        (x, *weights),
        [pltpu.VMEM((rows, hid), BF)],
        limit=8,
    )[0]


def add_kernel(a_ref, b_ref, out_ref):
    out_ref[...] = (a_ref[...].astype(F32) + b_ref[...].astype(F32)).astype(BF)


def both(part, there):
    return kernel(add_kernel, "both", [(part.shape, BF)], (part, there), limit=4)[0]


def place_blocks(pos, blocks, put, n_blk, n_rep, slab):
    for k, block in enumerate(blocks):
        at = jnp.bitwise_xor(pos[0], k)
        for r in range(n_rep):
            off = (r * n_blk + at) * slab
            put(pl.multiple_of(off, slab), block[r * slab : (r + 1) * slab, :])


def column(row):
    return jnp.broadcast_to(row, (128, row.shape[1])).T[:, :1]


def place_in_turn(k, n_blk):
    return -k & (n_blk - 1)


def arrange_kernel(n_blk, n_rep, slab, pos, *refs):
    mine, other, firsts = refs[:n_blk], refs[n_blk : 2 * n_blk], refs[2 * n_blk : 2 * n_blk + 2]
    rows_mine, rows_other, goals_ref, pick_ref, ep_ref, *hidden, both_sides, meta = refs[2 * n_blk + 2 :]
    rows = both_sides.shape[0]
    batch, rows_dev = n_blk * slab, n_rep * slab
    for i, (blocks, to) in enumerate(((mine, rows_mine), (other, rows_other))):

        def put(off, value, to=to):
            to[pl.ds(off, slab), :] = value

        place_blocks(pos, blocks, put, n_blk, n_rep, slab)
        for k, block in enumerate(blocks):
            at = (i * n_blk + place_in_turn(k, n_blk)) * rows_dev
            both_sides[at : at + rows_dev, :] = block[:rows_dev, :]
    for k, block in enumerate(mine):
        at = jnp.bitwise_xor(pos[0], k)
        for r in range(n_rep):
            off = pl.multiple_of((r * n_blk + at) * slab, slab)
            meta[:, pl.ds(off, slab)] = block[rows_dev:, r * slab : (r + 1) * slab].astype(F32)
    ep_ref[...] = meta[2:3, :]
    for r in range(n_rep):
        own = slice(r * batch, (r + 1) * batch)
        owner, place = meta[0:1, own].astype(jnp.int32), meta[1:2, own].astype(jnp.int32)
        side = (owner & 1) ^ pos[1]
        column_of = (side * n_blk + place_in_turn((owner >> 1) ^ pos[0], n_blk)) * rows_dev + place
        goal = column(column_of.astype(F32)).astype(jnp.int32)
        pick_ref[own, :] = jnp.where(
            goal == lax.broadcasted_iota(jnp.int32, (batch, rows), 1), 1.0, 0.0
        ).astype(BF)
    activate(pos, firsts[0], rows_mine, hidden[:2])
    goals_ref[...] = dot(pick_ref[...], both_sides[...]).astype(BF)
    activate(pos, firsts[1], goals_ref, hidden[2:])


def gather_kernel(n_blk, n_rep, slab, pos, *refs):
    mine, extra, other, pick_ref = refs[:n_blk], refs[n_blk], refs[n_blk + 1 : n_blk + 3], refs[n_blk + 3]
    phi_ref, psi_ref, early = refs[n_blk + 4 :]
    emb = phi_ref.shape[1]
    rows_dev = n_rep * slab
    blocks = list(mine)
    blocks[n_blk - 2] = (mine[n_blk - 2][...].astype(F32) + extra[...].astype(F32)).astype(BF)

    def put(off, value):
        phi_ref[pl.ds(off, slab), :] = value[:, :emb]

    place_blocks(pos, blocks, put, n_blk, n_rep, slab)
    for k, block in enumerate(blocks):
        at = place_in_turn(k, n_blk) * rows_dev
        early[at : at + rows_dev, :] = block[:, emb:]
    for i, block in enumerate(other):
        at = (n_blk + i) * rows_dev
        early[at : at + rows_dev, :] = block[:, emb:]
    psi_ref[...] = dot(pick_ref[:, : early.shape[0]], early[...])


def contrast_kernel(n_rep, scale, phi_ref, psi_ref, part_ref, there_ref, sums_ref, ep_ref, pick_ref, grads_ref, late, psi_all):
    half, emb = phi_ref.shape
    batch = half // n_rep
    rows_dev = sums_ref.shape[0]
    late[:rows_dev, :] = (part_ref[:, emb:].astype(F32) + there_ref[:, emb:].astype(F32)).astype(BF)
    late[rows_dev:, :] = sums_ref[:, emb:]
    psi_all[...] = (psi_ref[...] + dot(pick_ref[:, pick_ref.shape[1] - 2 * rows_dev :], late[...])).astype(BF)
    diagonal = lax.broadcasted_iota(jnp.int32, (batch, batch), 0) == lax.broadcasted_iota(
        jnp.int32, (batch, batch), 1
    )
    batches = [slice(r * batch, (r + 1) * batch) for r in range(n_rep)]
    scores = [
        lax.dot_general(phi_ref[own, :], psi_all[own, :], (((1,), (1,)), ((), ())), preferred_element_type=F32)
        for own in batches
    ]
    deltas = []
    for own, score in zip(batches, scores):
        ep_row = ep_ref[:, own]
        kept = (column(ep_row) != ep_row) | diagonal
        exponent = jnp.where(kept, jnp.exp(score * scale), 0.0)
        totals = jnp.sum(exponent, axis=1, keepdims=True)
        power = jnp.where(totals > 1.0, 2.0**-32, 1.0)
        shares = (exponent * power) * (1.0 / (totals * power))
        deltas.append(jnp.where(diagonal, shares - 1.0, shares).astype(BF))
    for own, delta in zip(batches, deltas):
        grads_ref[own, :emb] = (dot(delta, psi_all[own, :]) * scale).astype(BF)
    for own, delta in zip(batches, deltas):
        grads_ref[own, emb:] = (dot(delta.T, phi_ref[own, :]) * scale).astype(BF)


def rows_grads(at, first_ref, second_ref, grads_ref, k, rows_ref, active, back):
    quarter, rows = active.shape
    emb = second_ref.shape[1]
    first_t = first_ref[:, pl.ds(at, quarter)].T
    second = second_ref[pl.ds(at, quarter), :]
    grad = grads_ref[:, k * emb : (k + 1) * emb]
    chunk = 256
    for c in range(0, rows, chunk):
        cols = slice(c, c + chunk)
        hidden = dot(first_t, rows_ref[cols, :].T)
        sig = sigmoid(hidden)
        act = hidden * sig
        active[:, cols] = act.astype(BF)
        slope = sig + act * (1.0 - sig)
        back[:, cols] = (dot(second, grad[cols, :].T) * slope).astype(BF)
    return dot(active[...], grad), dot(back[...], rows_ref[...])


def activate(pos, first, x_ref, outs):
    quarter, rows = outs[0].shape
    at = pl.multiple_of(pos[1] * quarter, quarter)
    first_t = first[:, pl.ds(at, quarter)].T
    for c in range(0, rows, 256):
        cols = slice(c, c + 256)
        hidden = dot(first_t, x_ref[cols, :].T)
        sig = sigmoid(hidden)
        act = hidden * sig
        outs[0][:, cols] = act.astype(BF)
        outs[1][:, cols] = (sig + act * (1.0 - sig)).astype(BF)


def mine_kernel(pos, ss, gs, grads_ref, rows_ref, goals_ref, *refs):
    hidden, outs, back = refs[:4], refs[4:8], refs[8]
    quarter, rows = back.shape
    emb = ss.shape[1]
    at = pl.multiple_of(pos[1] * quarter, quarter)
    for k, (second_ref, x_ref) in enumerate(((ss, rows_ref), (gs, goals_ref))):
        second = second_ref[pl.ds(at, quarter), :]
        grad = grads_ref[:, k * emb : (k + 1) * emb]
        outs[2 * k][...] = dot(hidden[2 * k][...], grad)
        for c in range(0, rows, 256):
            cols = slice(c, c + 256)
            back[:, cols] = (dot(second, grad[cols, :].T) * hidden[2 * k + 1][:, cols].astype(F32)).astype(BF)
        outs[2 * k + 1][...] = dot(back[...], x_ref[...])


def other_kernel(k, n_put, pos, first, second, grads_ref, rows_ref, sum_second, sum_first, *refs):
    done, outs, puts, (active, back), sems = (
        refs[:n_put],
        refs[n_put : n_put + 4],
        refs[n_put + 4 : 2 * n_put + 4],
        refs[2 * n_put + 4 : 2 * n_put + 6],
        refs[2 * n_put + 6 :],
    )
    copies = [put_half(pos[1], x, o, sems[0].at[i]) for i, (x, o) in enumerate(zip(done, puts))]
    for c in copies:
        c.start()
    quarter = active.shape[0]
    at = pl.multiple_of(pos[1] * quarter, quarter)
    grad_second, grad_first = rows_grads(at, first, second, grads_ref, k, rows_ref, active, back)
    halves = ((sum_first[...] + grad_first).astype(BF).T, (sum_second[...] + grad_second).astype(BF))
    for half, out16, out32 in zip(halves, outs[:2], outs[2:]):
        out16[...] = half
        out32[...] = half.astype(F32)
    for c in copies:
        c.wait()


def put_half(side, half, out, sem):
    n, m = half.shape
    if out.shape[0] == n:
        to = out.at[:, pl.ds(pl.multiple_of(side * m, m), m)]
    else:
        to = out.at[pl.ds(pl.multiple_of(side * n, n), n), :]
    return pltpu.make_async_copy(half, to, sem)


def finish_kernel(old, new, pos, *refs):
    n = old + new
    halves, outs, scratch, sems = refs[:n], refs[n + old : 2 * n + old], refs[2 * n + old : -1], refs[-1]
    copies = [put_half(pos[1], x, o, sems.at[old + i]) for i, (x, o) in enumerate(zip(halves[old:], outs[old:]))]
    for c in copies:
        c.start()
    for i in range(old):
        scratch[i][...] = halves[i][...].astype(F32)
        copies.append(put_half(1 - pos[1], scratch[i], outs[i], sems.at[i]))
        copies[-1].start()
    for c in copies:
        c.wait()


def finish(there, own, wholes, shapes):
    old, new = len(wholes), len(shapes)
    n = old + new
    return kernel(
        functools.partial(finish_kernel, old, new),
        "finish",
        [(w.shape, w.dtype) for w in wholes] + shapes,
        (*there, *own, *wholes),
        [*(pltpu.VMEM(x.shape, F32) for x in there), pltpu.SemaphoreType.DMA((n,))],
        pos=True,
        hbm=range(n, n + old),
        hbm_out=range(n),
        aliases={n + i: i for i in range(old)},
    )


def gathered(
    states, goal_distance, goal_row, episode, state_first, state_second, goal_first, goal_second
):
    rows_dev, width = states.shape
    n_blk, n_rep, n_sub = (lax.axis_size(a) for a in ("blk", "rep", "sub"))
    slab = rows_dev // n_rep
    rows_all = n_blk * n_sub * rows_dev
    hid, emb = state_second.shape
    quarter = hid // n_sub

    def across(x, k):
        return lax.ppermute(x, "blk", [(i, i ^ k) for i in range(n_blk)])

    def swap(x, axis):
        return lax.ppermute(x, axis, [(0, 1), (1, 0)])

    def after(x, *first):
        return lax.optimization_barrier((x, *first))[0]

    weights = (state_first, goal_first, state_second, goal_second)
    (blank,) = kernel(blank_kernel, "blank", [((16, rows_dev), F32)], (), limit=1, flops=2**32)
    (pack,) = kernel(
        functools.partial(pack_kernel, n_blk, n_sub),
        "pack",
        [((rows_dev + 16, width), BF)],
        (blank, states, *(x.reshape(1, rows_dev) for x in (goal_distance, goal_row, episode))),
        pos=True,
        limit=4,
        flops=2**32,
    )
    got = {0: pack, 3: across(pack, 3)}
    held = weights
    part0 = forward(pack, held, rows_dev)
    got[1] = across(after(pack, part0), 1)
    got[2] = across(after(pack, got[3]), 2)
    there0 = swap(part0, "rep")
    part3 = forward(got[3], held, rows_dev)
    there3 = swap(part3, "rep")

    sums = {0: both(part0, there0)}
    sums[1] = across(after(sums[0], got[2]), 1)
    part2 = forward(after(got[2], sums[0]), held, rows_dev)
    there2 = swap(part2, "rep")
    sums[3] = both(part3, there3)

    side = ((rows_all // 2, width), BF)
    sf, gf, ss, gs = held
    mine, other, goals_mine, pick, episodes, *hidden = kernel(
        functools.partial(arrange_kernel, n_blk, n_rep, slab),
        "arrange",
        [side, side, side, ((rows_all // 2, rows_all), BF), ((1, rows_all // 2), F32)]
        + [((quarter, rows_all // 2), BF)] * 4,
        (*(got[k] for k in range(n_blk)), *(swap(got[k], "sub") for k in range(n_blk)), sf, gf),
        [
            pltpu.VMEM((rows_all, width), BF),
            pltpu.VMEM((16, rows_all // 2), F32),
        ],
        pos=True,
    )
    there2 = after(there2, pick)
    late = [swap(x, "sub") for x in (part2, there2, sums[1])]
    half = rows_all // 2
    phi, psi = kernel(
        functools.partial(gather_kernel, n_blk, n_rep, slab),
        "gather",
        [((half, emb), BF), ((half, emb), F32)],
        (sums[0], sums[1], part2, sums[3], there2, swap(sums[0], "sub"), swap(sums[3], "sub"), pick),
        [pltpu.VMEM((rows_all - 2 * rows_dev, emb), BF)],
        pos=True,
    )
    (grads_mine,) = kernel(
        functools.partial(contrast_kernel, n_rep, 4.0 / math.sqrt(emb)),
        "contrast",
        [((half, 2 * emb), BF)],
        (phi, psi, *late, episodes, pick),
        [pltpu.VMEM((2 * rows_dev, emb), BF), pltpu.VMEM((half, emb), BF)],
    )
    grads_other = swap(grads_mine, "sub")
    goals_other = swap(goals_mine, "sub")

    sf, gf, ss, gs = weights
    work = [pltpu.VMEM((quarter, rows_all // 2), BF), pltpu.VMEM((quarter, rows_all // 2), BF)]
    flops = 4 * rows_all * width * quarter
    sums_s2, sums_s1, sums_g2, sums_g1 = kernel(
        mine_kernel,
        "mine",
        [((quarter, emb), F32), ((quarter, width), F32)] * 2,
        (ss, gs, grads_mine, mine, goals_mine, *hidden),
        work[:1],
        pos=True,
        flops=2 * flops,
    )
    halves = [(shape, kind) for kind in (BF, F32) for shape in ((width, quarter), (quarter, emb))]
    wholes = [((width, hid), F32), ((hid, emb), F32)]
    *state_halves, state_first_own, state_second_own = kernel(
        functools.partial(other_kernel, 0, 0),
        "other_state",
        halves,
        (sf, ss, grads_other, other, sums_s2, sums_s1),
        work,
        pos=True,
        flops=flops,
    )
    state_there = [swap(x, "sub") for x in state_halves]
    *goal_halves, goal_first_own, goal_second_own, out0, out1 = kernel(
        functools.partial(other_kernel, 1, 2),
        "other_goal",
        halves + wholes,
        (gf, gs, grads_other, goals_other, sums_g2, sums_g1, state_first_own, state_second_own),
        work + [pltpu.SemaphoreType.DMA((2,))],
        pos=True,
        flops=flops,
        hbm_out=(4, 5),
    )
    goal_there = [swap(x, "sub") for x in goal_halves]
    out0, out1, out2, out3 = finish(state_there, (goal_first_own, goal_second_own), (out0, out1), wholes)
    out2, out3 = finish(goal_there, (), (out2, out3), [])
    return (out0, out1, out2, out3)


def silu_slope(hidden):
    sig = jax.nn.sigmoid(hidden)
    return sig * (1.0 + hidden * (1.0 - sig))


def encoder_grads(rows_in, hidden, active, second, emb_grad):
    grad_second = jnp.einsum("nh,ne->he", active, emb_grad, preferred_element_type=jnp.float32)
    back = jnp.einsum("ne,he->nh", emb_grad, second, preferred_element_type=jnp.float32)
    back_rows = (back * silu_slope(hidden)).astype(jnp.bfloat16)
    grad_first = jnp.einsum("ns,nh->sh", rows_in, back_rows, preferred_element_type=jnp.float32)
    return (grad_first, grad_second)


def exchanged(
    states, goal_distance, goal_row, episode, state_first, state_second, goal_first, goal_second
):
    rows_dev, width = states.shape
    owners = lax.axis_size(("blk", "sub"))
    position = lax.axis_index(("blk", "sub"))
    capacity = 4 * rows_dev // owners
    target = (position + goal_distance[:, 0]) % owners
    onehot = (target[:, None] == jnp.arange(owners, dtype=jnp.int32)[None, :]).astype(jnp.int32)
    slot_rank = jnp.sum((jnp.cumsum(onehot, axis=0) - onehot) * onehot, axis=1)
    requests = jnp.zeros((owners, capacity), jnp.int32).at[target, slot_rank].set(goal_row)
    wanted = lax.all_to_all(requests, ("blk", "sub"), split_axis=0, concat_axis=0, tiled=True)
    fetched = jnp.take(states, wanted.reshape(-1), axis=0).reshape(wanted.shape + (width,))
    replies = lax.all_to_all(fetched, ("blk", "sub"), split_axis=0, concat_axis=0, tiled=True)
    goal_states = jnp.take(
        replies.reshape(owners * capacity, width), target * capacity + slot_rank, axis=0
    )
    slab_rows = rows_dev // lax.axis_size("rep")
    state_hidden = jnp.dot(states, state_first, preferred_element_type=jnp.float32)
    state_active = jax.nn.silu(state_hidden).astype(jnp.bfloat16)
    goal_hidden = jnp.dot(goal_states, goal_first, preferred_element_type=jnp.float32)
    goal_active = jax.nn.silu(goal_hidden).astype(jnp.bfloat16)
    phi = lax.psum_scatter(
        jnp.dot(state_active, state_second, preferred_element_type=jnp.float32),
        "rep",
        scatter_dimension=0,
        tiled=True,
    ).astype(jnp.bfloat16)
    psi = lax.psum_scatter(
        jnp.dot(goal_active, goal_second, preferred_element_type=jnp.float32),
        "rep",
        scatter_dimension=0,
        tiled=True,
    ).astype(jnp.bfloat16)
    episode_own = lax.dynamic_slice_in_dim(episode, lax.axis_index("rep") * slab_rows, slab_rows, 0)
    psi_all, episode_all = (
        lax.all_gather(psi, "blk", axis=0, tiled=True),
        lax.all_gather(episode_own, "blk", axis=0, tiled=True),
    )
    batch_rows = psi_all.shape[0]
    logit_scale = 4.0 / math.sqrt(psi.shape[1])
    own_rows = lax.axis_index("blk") * slab_rows + jnp.arange(slab_rows, dtype=jnp.int32)
    columns = jnp.arange(batch_rows, dtype=jnp.int32)
    diagonal = own_rows[:, None] == columns[None, :]
    excluded = (episode_own[:, None] == episode_all[None, :]) & ~diagonal
    scores = jnp.einsum("ie,je->ij", phi, psi_all, preferred_element_type=jnp.float32) * logit_scale
    exponent = jnp.where(excluded, 0.0, jnp.exp(scores))
    totals = jnp.sum(exponent, axis=1)
    delta = (exponent / totals[:, None] - diagonal.astype(jnp.float32)).astype(jnp.bfloat16)
    phi_grad = (jnp.dot(delta, psi_all, preferred_element_type=jnp.float32) * logit_scale).astype(
        jnp.bfloat16
    )
    psi_grad = lax.psum_scatter(
        jnp.einsum("ij,ie->je", delta, phi, preferred_element_type=jnp.float32) * logit_scale,
        "blk",
        scatter_dimension=0,
        tiled=True,
    ).astype(jnp.bfloat16)
    phi_full, psi_full = (
        lax.all_gather(phi_grad, "rep", axis=0, tiled=True),
        lax.all_gather(psi_grad, "rep", axis=0, tiled=True),
    )
    state_parts = encoder_grads(states, state_hidden, state_active, state_second, phi_full)
    goal_parts = encoder_grads(goal_states, goal_hidden, goal_active, goal_second, psi_full)
    summed = lax.psum(
        (state_parts[0], state_parts[1], goal_parts[0], goal_parts[1]), ("blk", "sub")
    )
    return (summed[0], summed[1], summed[2], summed[3])


def solution(mesh):
    in_specs = (
        P(("grp", "blk", "sub"), None),
        P(("grp", "blk", "sub"), None),
        P(("grp", "blk", "sub")),
        P(("grp", "blk", "sub")),
        P(None, "rep"),
        P("rep", None),
        P(None, "rep"),
        P("rep", None),
    )
    out_specs = (P("grp", "rep"), P(("grp", "rep"), None), P("grp", "rep"), P(("grp", "rep"), None))

    def local(states, *others):
        small = (mesh.shape["blk"], mesh.shape["rep"], mesh.shape["sub"]) == (4, 2, 2)
        plan = gathered if small and states.shape[0] == states.shape[1] == 256 else exchanged
        return plan(states, *others)

    return jax.shard_map(local, mesh=mesh, in_specs=in_specs, out_specs=out_specs, check_vma=False)
```
